32 devices in a mesh: clus: 4 (over y, x), rep: 8 (over z, core).
Axes of the slice: x: 2, y: 2, z: 4, core: 2. Of those that a mesh axis runs over, the one named last changes fastest.
Arguments:
- descriptors: bfloat16 [8, 4, 512, 2048], P('rep', 'clus')
- request: int32 [8, 4, 4, 32], P('rep', 'clus'), may hold values from 0 to 1535
- pick: int32 [8, 4, 512, 10], P('rep', 'clus'), may hold values from 0 to 127, as said below
Outputs:
- augmented: bfloat16 [8, 4, 512, 2048], P('rep', 'clus')
The draws below stay inside these ranges and needn't reach their ends.
Inputs may be any that keep to these rules, and one draw needn't show every extreme that they name: `pick`: the 10 slots of one descriptor are distinct.
All inputs are finite; a program needn't handle non-finite values.
Results may differ from the reference program's by a relative error of at most 0.0075.
Values may be sent and summed in bfloat16 or wider, within the bound.
No kernel may reach another device: no remote copies, remote signals or barrier semaphores. Data moves between devices by JAX's collectives and lax.ppermute only.
A program may use at most 64 MiB of HBM per device.

```python
import math
import jax
import jax.numpy as jnp
import numpy as np
from jax import lax

WIDTH = 2048
ROWS_DEV = 512
NEIGHBOURS = 10
ROUNDS = 2
SLOT_CAP = 32
BUFFER = 128
GROUPS = 8
N_CLUS = 4
N_REP = 8


def draw_descriptors(key, part):
    key = jax.random.fold_in(key, 11)
    key_dir, key_amp, key_noise = jax.random.split(key, 3)
    shape = (GROUPS, N_CLUS, ROWS_DEV, WIDTH)
    common = jax.random.normal(key_dir, (WIDTH,), jnp.float32)
    amount = jax.random.uniform(key_amp, (GROUPS, N_CLUS, ROWS_DEV, 1), jnp.float32, -0.6, 1.2)
    noise = 0.7 * jax.random.normal(key_noise, shape, jnp.float32)
    return (amount * common + noise).astype(jnp.bfloat16)


def draw_pick(key, part):
    key = jax.random.fold_in(key, 23)
    upper = 2147483647 // BUFFER - 1
    scores = jax.random.randint(key, (GROUPS, N_CLUS, ROWS_DEV, BUFFER), 0, upper, jnp.int32)
    scores = scores * BUFFER + jnp.arange(BUFFER, dtype=jnp.int32)
    order = jnp.argsort(scores, axis=-1, stable=True)
    return order[..., :NEIGHBOURS].astype(jnp.int32)


def plant(result, key, low, top_value):
    spot = [jax.random.randint(jax.random.fold_in(key, axis), (), 0, length) for axis, length in enumerate(result.shape)]
    longest = result.shape.index(max(result.shape))
    next_to = spot[:longest] + [(spot[longest] + 1) % result.shape[longest]] + spot[longest + 1:]
    return result.at[tuple(spot)].set(low).at[tuple(next_to)].set(top_value)


def cumulative_ranks(count, skew):
    weights = [(1 << 20) // math.isqrt(standing ** skew) + 1 for standing in range(1, count + 1)]
    deviation = 1 + sum(weights) // (1 << 30)
    return np.cumsum(np.array([max(1, weight // deviation) for weight in weights]))


def skewed_ids(rng, shape, number_of, lean):
    listing = cumulative_ranks(number_of, lean)
    ticket = jax.random.randint(jax.random.fold_in(rng, 1), shape, 0, int(listing[number_of - 1]))
    standing = jnp.searchsorted(jnp.asarray(listing, jnp.int32), ticket, side="right")
    return jax.random.permutation(jax.random.fold_in(rng, 2), number_of)[standing].astype(jnp.int32)


def setup_inputs(seed: int = 0) -> dict:
    keys = jax.random.split(jax.random.key(seed), 4)
    descriptors = draw_descriptors(jax.random.fold_in(keys[3], 71), 0)
    request = plant(skewed_ids(keys[1], (GROUPS, N_CLUS, N_CLUS, SLOT_CAP), 3 * ROWS_DEV, 2), jax.random.fold_in(keys[1], 3), 0, (3 * ROWS_DEV) - 1).astype(jnp.int32)
    pick = draw_pick(jax.random.fold_in(keys[3], 71), 0)
    return {"descriptors": descriptors, "request": request, "pick": pick}


def normalize(value):
    return value * lax.rsqrt(lax.optimization_barrier(jnp.mean(value * value, axis=-1, keepdims=True)) + 1e-06)

def reference(descriptors, request, pick):
    current = normalize(descriptors.astype(jnp.float32)).astype(jnp.bfloat16)
    clus_index = jnp.arange(N_CLUS, dtype=jnp.int32)

    def one_round(state):

        def per_group(group):
            own = state[group]
            slots = pick[group]
            server = slots // SLOT_CAP
            place = slots % SLOT_CAP
            wanted = request[group][clus_index[:, None, None], server, place]
            source = (group + wanted // ROWS_DEV - 1 + N_REP) % N_REP
            fetched = state[source, server, wanted % ROWS_DEV]
            own_wide = own.astype(jnp.float32)
            fetched_wide = fetched.astype(jnp.float32)
            sims = jnp.einsum('crd,crkd->crk', own_wide, fetched_wide) / WIDTH
            positive = jnp.maximum(sims, 0.0)
            weights = (positive * positive * positive).astype(jnp.bfloat16)
            mixed = own_wide + jnp.einsum('crk,crkd->crd', weights.astype(jnp.float32), fetched_wide)
            return normalize(mixed).astype(jnp.bfloat16)
        return lax.map(per_group, jnp.arange(N_REP, dtype=jnp.int32))
    for step in range(ROUNDS):
        current = one_round(current)
    return current
```

```python
import functools

import jax
import jax.numpy as jnp
from jax import lax
from jax.experimental import pallas as pl
from jax.experimental.pallas import tpu as pltpu
from jax.sharding import PartitionSpec as P

ROUNDS = 2
LANES = 128
BLOCK = 128


def params():
    return pltpu.CompilerParams(vmem_limit_bytes=32 * 1024 * 1024)


def normalize(value):
    return value * lax.rsqrt(jnp.mean(value * value, axis=-1, keepdims=True) + 1e-06)


def normalize_kernel(slot_cap, x_ref, pick_ref, out_ref, mask_ref):
    out_ref[...] = normalize(x_ref[...].astype(jnp.float32)).astype(jnp.bfloat16)
    rows, total = x_ref.shape[0], mask_ref.shape[1] // 2
    slot = lax.broadcasted_iota(jnp.int32, (rows, 2 * total), 1)
    turned = lax.axis_index("clus") * slot_cap
    slot = jnp.where(slot < total, slot, (slot - total) ^ turned)
    chosen = jnp.zeros((rows, 2 * total), jnp.float32)
    for k in range(pick_ref.shape[1]):
        chosen = jnp.where(pick_ref[:, k : k + 1] == slot, 1.0, chosen)
    mask_ref[...] = chosen.astype(jnp.bfloat16)


def normalize_call(descriptors, slots, total, slot_cap):
    rows, width = descriptors.shape
    return pl.pallas_call(
        functools.partial(normalize_kernel, slot_cap),
        grid=(rows // BLOCK,),
        in_specs=[
            pl.BlockSpec((BLOCK, width), lambda i: (i, 0)),
            pl.BlockSpec((BLOCK, slots.shape[1]), lambda i: (i, 0)),
        ],
        out_specs=[
            pl.BlockSpec((BLOCK, width), lambda i: (i, 0)),
            pl.BlockSpec((BLOCK, 2 * total), lambda i: (i, 0)),
        ],
        out_shape=[
            jax.ShapeDtypeStruct((rows, width), jnp.bfloat16),
            jax.ShapeDtypeStruct((rows, 2 * total), jnp.bfloat16),
        ],
        compiler_params=params(),
        cost_estimate=pl.CostEstimate(
            flops=6 * rows * width, bytes_accessed=4 * rows * width, transcendentals=rows
        ),
        name="normalize",
    )(descriptors, slots)


def serve(x, select, out_core, out_own, out_across):
    total = out_own.shape[0]
    cap = out_across[0].shape[0]
    fetched = jnp.dot(select, x, preferred_element_type=jnp.float32).astype(jnp.bfloat16)
    out_core[...] = fetched[:total]
    out_own[...] = fetched[total : 2 * total]
    for d, out in enumerate(out_across):
        out[...] = fetched[2 * total + d * cap : 2 * total + (d + 1) * cap]


def serve_kernel(x_ref, asked_ref, select_ref, core_ref, own_ref, *across_refs):
    rows = x_ref.shape[0]
    total = asked_ref.shape[2]
    asked = jnp.sum(asked_ref[...].astype(jnp.float32), axis=0)
    odd = lax.axis_index("rep") % 2
    thirds = (2 * odd, 1, 2 - 2 * odd)
    for q in range(3):
        column = jnp.broadcast_to(asked[q : q + 1], (LANES, total)).T
        column = column.astype(jnp.int32) - thirds[q] * rows
        for t in range(rows // LANES):
            lane = lax.broadcasted_iota(jnp.int32, (total, LANES), 1) + t * LANES
            select_ref[q * total : (q + 1) * total, t * LANES : (t + 1) * LANES] = jnp.where(
                column == lane, 1.0, 0.0
            ).astype(jnp.bfloat16)
    serve(x_ref[...], select_ref[...], core_ref, own_ref, across_refs)


def served_shapes(servers, cap, width):
    total = servers * cap
    return [jax.ShapeDtypeStruct((total, width), jnp.bfloat16)] * 2 + [
        jax.ShapeDtypeStruct((cap, width), jnp.bfloat16)
    ] * servers


def serve_call(x, asked, servers, cap):
    rows, width = x.shape
    total = servers * cap
    out = pl.pallas_call(
        serve_kernel,
        out_shape=[jax.ShapeDtypeStruct((3 * total, rows), jnp.bfloat16)]
        + served_shapes(servers, cap, width),
        compiler_params=params(),
        cost_estimate=pl.CostEstimate(
            flops=6 * total * rows * width, bytes_accessed=4 * rows * width, transcendentals=0
        ),
        name="serve",
    )(x, asked)
    return out[0], out[1:]


def mix(x_ref, mask_ref, buffer):
    width = x_ref.shape[1]
    x = x_ref[...]
    sims = lax.dot_general(
        x, buffer[...], (((1,), (1,)), ((), ())), preferred_element_type=jnp.float32
    )
    positive = jnp.maximum(sims * (1.0 / width), 0.0)
    cubed = (positive * positive * positive).astype(jnp.bfloat16)
    weights = cubed * mask_ref[...]
    mixed = x.astype(jnp.float32) + jnp.dot(
        weights, buffer[...], preferred_element_type=jnp.float32
    )
    return normalize(mixed).astype(jnp.bfloat16)


def fill(buffer, near_ref, across):
    total = near_ref.shape[0]
    cap = across[0].shape[0]
    buffer[:total] = near_ref[...]
    for d, ref in enumerate(across):
        buffer[total + d * cap : total + (d + 1) * cap] = ref[...]


def last_kernel(servers, x_ref, mask_ref, near_ref, *rest):
    across, out_ref, buffer = rest[:servers], rest[servers], rest[servers + 1]

    @pl.when(pl.program_id(0) == 0)
    def _():
        fill(buffer, near_ref, across)

    out_ref[...] = mix(x_ref, mask_ref, buffer)


def round_kernel(servers, x_ref, mask_ref, near_ref, *rest):
    across, rest = rest[:servers], rest[servers:]
    select_ref, out_ref, core_ref, own_ref = rest[:4]
    served, (buffer, whole) = rest[4 : 4 + servers], rest[4 + servers :]
    step = pl.program_id(0)

    @pl.when(step == 0)
    def _():
        fill(buffer, near_ref, across)

    block = mix(x_ref, mask_ref, buffer)
    out_ref[...] = block
    whole[pl.ds(pl.multiple_of(step * BLOCK, BLOCK), BLOCK), :] = block

    @pl.when(step == pl.num_programs(0) - 1)
    def _():
        serve(whole[...], select_ref[...], core_ref, own_ref, served)


def mix_call(x, mask, near, across, select):
    rows, width = x.shape
    total = near.shape[0]
    cap = across[0].shape[0]
    servers = len(across)
    again = select is not None

    def whole(shape):
        return pl.BlockSpec(shape, lambda i: (0, 0))

    in_specs = [
        pl.BlockSpec((BLOCK, width), lambda i: (i, 0)),
        pl.BlockSpec((BLOCK, 2 * total), lambda i: (i, 0)),
        whole(near.shape),
    ] + [whole((cap, width))] * servers
    out_specs = [pl.BlockSpec((BLOCK, width), lambda i: (i, 0))]
    out_shape = [jax.ShapeDtypeStruct((rows, width), jnp.bfloat16)]
    scratch = [pltpu.VMEM((2 * total, width), jnp.bfloat16)]
    args = [x, mask, near, *across]
    if again:
        in_specs.append(whole(select.shape))
        args.append(select)
        shapes = served_shapes(servers, cap, width)
        out_shape += shapes
        out_specs += [whole(s.shape) for s in shapes]
        scratch.append(pltpu.VMEM((rows, width), jnp.bfloat16))
    out = pl.pallas_call(
        functools.partial(round_kernel if again else last_kernel, servers),
        grid=(rows // BLOCK,),
        in_specs=in_specs,
        out_specs=out_specs,
        out_shape=out_shape,
        scratch_shapes=scratch,
        compiler_params=params(),
        cost_estimate=pl.CostEstimate(
            flops=8 * total * rows * width, bytes_accessed=6 * rows * width, transcendentals=rows
        ),
        name="mix_and_serve" if again else "mix",
    )(*args)
    return out[0], out[1:]


def local(descriptors, request, pick):
    width = descriptors.shape[3]
    wanted = request[0, 0]
    servers, cap = wanted.shape
    total = servers * cap
    groups = lax.axis_size("rep")
    column = lax.axis_index("clus")
    within = [g ^ 1 for g in range(groups)]
    beyond = [(g + 1) % groups if g % 2 else (g - 1) % groups for g in range(groups)]

    def swap(value, partner):
        return lax.ppermute(value, "rep", list(enumerate(partner)))

    def across(value, turn):
        pairs = [
            (c * groups + g, (c ^ turn) * groups + beyond[g])
            for g in range(groups)
            for c in range(servers)
        ]
        return lax.ppermute(value, ("clus", "rep"), pairs)

    core_wanted = swap(wanted, within)
    far_wanted = swap(wanted, beyond)
    x, mask = normalize_call(descriptors[0, 0], pick[0, 0], total, cap)

    place = lax.broadcasted_iota(jnp.int32, (servers, total), 1) // cap
    server = lax.broadcasted_iota(jnp.int32, (servers, total), 0)

    def placed(value, where):
        return jnp.where(place == where, jnp.tile(value, (1, servers)), 0)

    payload = jnp.stack(
        [
            placed(core_wanted, column),
            placed(wanted, column),
            placed(far_wanted, server ^ column),
        ],
        axis=1,
    )
    asked = lax.all_to_all(payload, "clus", split_axis=0, concat_axis=0, tiled=True)
    select, served = serve_call(x, asked, servers, cap)
    for step in range(ROUNDS):
        core, own, *far = served
        core = swap(core, within)
        far = [across(value, d) for d, value in enumerate(far)]
        near = lax.all_to_all(
            (core + own).reshape(servers, cap, width),
            "clus",
            split_axis=0,
            concat_axis=0,
            tiled=True,
        ).reshape(total, width)
        x, served = mix_call(x, mask, near, far, select if step < ROUNDS - 1 else None)
    return x[None, None]


def solution(mesh):
    return jax.shard_map(
        local,
        mesh=mesh,
        in_specs=(
            P("rep", "clus", None, None),
            P("rep", "clus", None, None),
            P("rep", "clus", None, None),
        ),
        out_specs=P("rep", "clus", None, None),
        check_vma=False,
    )
```

```python
import functools

import jax
import jax.numpy as jnp
from jax import lax
from jax.experimental import pallas as pl
from jax.experimental.pallas import tpu as pltpu
from jax.sharding import PartitionSpec as P

ROUNDS = 2
LANES = 128
BLOCK = 128


def params():
    return pltpu.CompilerParams(vmem_limit_bytes=32 * 1024 * 1024)


def bf16(*shape):
    return jax.ShapeDtypeStruct(shape, jnp.bfloat16)


def normalize(value):
    return value * lax.rsqrt(jnp.mean(value * value, axis=-1, keepdims=True) + 1e-06)


def normalize_kernel(slot_cap, x_ref, pick_ref, out_ref, mask_ref):
    out_ref[...] = normalize(x_ref[...].astype(jnp.float32)).astype(jnp.bfloat16)
    slot = lax.broadcasted_iota(jnp.int32, mask_ref.shape, 1)
    slot = slot ^ (lax.axis_index("clus") * slot_cap)
    chosen = jnp.zeros(mask_ref.shape, jnp.float32)
    for k in range(pick_ref.shape[1]):
        chosen = jnp.where(pick_ref[:, k : k + 1] == slot, 1.0, chosen)
    mask_ref[...] = chosen.astype(jnp.bfloat16)


def normalize_call(descriptors, slots, total, slot_cap):
    rows, width = descriptors.shape
    return pl.pallas_call(
        functools.partial(normalize_kernel, slot_cap),
        grid=(rows // BLOCK,),
        in_specs=[
            pl.BlockSpec((BLOCK, width), lambda i: (i, 0)),
            pl.BlockSpec((BLOCK, slots.shape[1]), lambda i: (i, 0)),
        ],
        out_specs=[
            pl.BlockSpec((BLOCK, width), lambda i: (i, 0)),
            pl.BlockSpec((BLOCK, total), lambda i: (i, 0)),
        ],
        out_shape=[bf16(rows, width), bf16(rows, total)],
        compiler_params=params(),
        cost_estimate=pl.CostEstimate(
            flops=6 * rows * width, bytes_accessed=4 * rows * width, transcendentals=rows
        ),
        name="normalize",
    )(descriptors, slots)


def serve(x, select_ref, core_ref, own_ref, far_ref):
    total, sent = own_ref.shape[0], far_ref.shape[0]
    fetched = jnp.dot(
        select_ref[: 2 * total + sent], x, preferred_element_type=jnp.float32
    ).astype(jnp.bfloat16)
    core_ref[...] = fetched[:total]
    own_ref[...] = fetched[total : 2 * total]
    far_ref[...] = fetched[2 * total :]


def one_hot(asked, third, rows):
    total = asked.shape[1]
    column = jnp.broadcast_to(asked, (LANES, total)).T - third * rows
    tiles = []
    for t in range(rows // LANES):
        lane = lax.broadcasted_iota(jnp.int32, (total, LANES), 1) + t * LANES
        tiles.append(jnp.where(column == lane, 1.0, 0.0))
    return jnp.concatenate(tiles, axis=1)


def index_kernel(groups, x_ref, asked_ref, select_ref, expand_ref, core_ref, own_ref, far_ref):
    rows = x_ref.shape[0]
    servers, cap = asked_ref.shape[1:]
    total = servers * cap
    group, column = lax.axis_index("rep"), lax.axis_index("clus")
    odd = group % 2
    beyond = (group + 2 * odd - 1 + groups) % groups

    def asked(requester):
        parts = [
            asked_ref[(column ^ d) * groups + requester, pl.ds(column, 1), :]
            for d in range(servers)
        ]
        return jnp.concatenate(parts, axis=1)

    own = asked(group)
    from_own = one_hot(own, 1, rows)
    from_core = one_hot(asked(group ^ 1), 2 * odd, rows)
    to_far = one_hot(asked(beyond), 2 - 2 * odd, rows)
    from_far = one_hot(own, 2 * odd, rows)
    needed = jnp.concatenate(
        [
            jnp.broadcast_to(jnp.max(to_far, axis=0, keepdims=True), (8, rows)),
            jnp.broadcast_to(jnp.max(from_far, axis=0, keepdims=True), (8, rows)),
        ],
        axis=0,
    )
    before = lax.broadcasted_iota(jnp.int32, (rows, rows), 0) < lax.broadcasted_iota(
        jnp.int32, (rows, rows), 1
    )
    rank = jnp.dot(
        needed.astype(jnp.bfloat16),
        jnp.where(before, 1.0, 0.0).astype(jnp.bfloat16),
        preferred_element_type=jnp.float32,
    )
    rank = jnp.where(needed > 0, rank, -1.0).astype(jnp.int32)
    place = lax.broadcasted_iota(jnp.int32, (total, rows), 0)
    pack = jnp.where(place == rank[0:1], 1.0, 0.0).astype(jnp.bfloat16)
    packed = jnp.where(place == rank[8:9], 1.0, 0.0).astype(jnp.bfloat16)
    expand_ref[...] = lax.dot_general(
        from_far.astype(jnp.bfloat16),
        packed,
        (((1,), (1,)), ((), ())),
        preferred_element_type=jnp.float32,
    ).astype(jnp.bfloat16)
    select_ref[:total] = from_core.astype(jnp.bfloat16)
    select_ref[total : 2 * total] = from_own.astype(jnp.bfloat16)
    select_ref[2 * total :] = pack
    serve(x_ref[...], select_ref, core_ref, own_ref, far_ref)


def index_call(x, asked, groups):
    rows, width = x.shape
    total = asked.shape[1] * asked.shape[2]
    return pl.pallas_call(
        functools.partial(index_kernel, groups),
        out_shape=[
            bf16(3 * total, rows),
            bf16(total, total),
            bf16(total, width),
            bf16(total, width),
            bf16(total, width),
        ],
        compiler_params=params(),
        cost_estimate=pl.CostEstimate(
            flops=6 * total * rows * width, bytes_accessed=4 * rows * width, transcendentals=0
        ),
        name="index_and_serve",
    )(x, asked)


def combine_kernel(expand_ref, far_ref, own_ref, core_ref, *out_refs):
    cap, sent = out_refs[0].shape[0], far_ref.shape[0]
    far = jnp.dot(expand_ref[:, :sent], far_ref[...], preferred_element_type=jnp.float32)
    rows = (far + own_ref[...].astype(jnp.float32) + core_ref[...].astype(jnp.float32)).astype(
        jnp.bfloat16
    )
    for d, out in enumerate(out_refs):
        out[...] = rows[d * cap : (d + 1) * cap]


def combine_call(expand, far, own, core, servers):
    total, width = own.shape
    return pl.pallas_call(
        combine_kernel,
        out_shape=[bf16(total // servers, width)] * servers,
        compiler_params=params(),
        cost_estimate=pl.CostEstimate(
            flops=2 * total * far.shape[0] * width,
            bytes_accessed=8 * total * width,
            transcendentals=0,
        ),
        name="combine",
    )(expand, far, own, core)


def fill(buffer, parts):
    cap = parts[0].shape[0]
    for d, ref in enumerate(parts):
        buffer[d * cap : (d + 1) * cap] = ref[...]


def weigh(x, buffer, mask):
    sims = lax.dot_general(x, buffer, (((1,), (1,)), ((), ())), preferred_element_type=jnp.float32)
    positive = jnp.maximum(sims * (1.0 / x.shape[1]), 0.0)
    return (positive * positive * positive).astype(jnp.bfloat16) * mask


def add_up(x, weights, buffer):
    mixed = x.astype(jnp.float32) + jnp.dot(weights, buffer, preferred_element_type=jnp.float32)
    return normalize(mixed).astype(jnp.bfloat16)


def last_kernel(servers, x_ref, mask_ref, *rest):
    parts, out_ref, buffer = rest[:servers], rest[servers], rest[servers + 1]

    @pl.when(pl.program_id(0) == 0)
    def _():
        fill(buffer, parts)

    x = x_ref[...]
    out_ref[...] = add_up(x, weigh(x, buffer[...], mask_ref[...]), buffer[...])


def last_call(x, mask, parts):
    rows, width = x.shape
    total, servers = mask.shape[1], len(parts)
    return pl.pallas_call(
        functools.partial(last_kernel, servers),
        grid=(rows // BLOCK,),
        in_specs=[
            pl.BlockSpec((BLOCK, width), lambda i: (i, 0)),
            pl.BlockSpec((BLOCK, total), lambda i: (i, 0)),
        ]
        + [pl.BlockSpec(part.shape, lambda i: (0, 0)) for part in parts],
        out_specs=pl.BlockSpec((BLOCK, width), lambda i: (i, 0)),
        out_shape=bf16(rows, width),
        scratch_shapes=[pltpu.VMEM((total, width), jnp.bfloat16)],
        compiler_params=params(),
        cost_estimate=pl.CostEstimate(
            flops=4 * total * rows * width, bytes_accessed=4 * rows * width, transcendentals=rows
        ),
        name="mix",
    )(x, mask, *parts)


def round_kernel(servers, x_ref, mask_ref, select_ref, *rest):
    parts, rest = rest[:servers], rest[servers:]
    out_ref, core_ref, own_ref, far_ref, buffer, weights = rest
    fill(buffer, parts)
    weights[...] = weigh(x_ref[...], buffer[...], mask_ref[...])
    for start in range(0, x_ref.shape[0], BLOCK):
        stop = start + BLOCK
        out_ref[start:stop] = add_up(x_ref[start:stop], weights[start:stop], buffer[...])
    serve(out_ref[...], select_ref, core_ref, own_ref, far_ref)


def round_call(x, mask, select, parts, sent):
    rows, width = x.shape
    total, servers = mask.shape[1], len(parts)
    return pl.pallas_call(
        functools.partial(round_kernel, servers),
        out_shape=[bf16(rows, width), bf16(total, width), bf16(total, width), bf16(sent, width)],
        scratch_shapes=[
            pltpu.VMEM((total, width), jnp.bfloat16),
            pltpu.VMEM((rows, total), jnp.bfloat16),
        ],
        compiler_params=params(),
        cost_estimate=pl.CostEstimate(
            flops=10 * total * rows * width, bytes_accessed=6 * rows * width, transcendentals=rows
        ),
        name="mix_and_serve",
    )(x, mask, select, *parts)


def local(descriptors, request, pick):
    wanted = request[0, 0]
    servers, cap = wanted.shape
    total = servers * cap
    groups = lax.axis_size("rep")
    within = [(g, g ^ 1) for g in range(groups)]
    beyond = [(g, (g + 2 * (g % 2) - 1 + groups) % groups) for g in range(groups)]

    everyone = servers * groups
    asked = lax.all_to_all(
        jnp.broadcast_to(wanted[None], (everyone, servers, cap)),
        ("clus", "rep"),
        split_axis=0,
        concat_axis=0,
        tiled=True,
    )
    x, mask = normalize_call(descriptors[0, 0], pick[0, 0], total, cap)
    select, expand, core, own, far = index_call(x, asked, groups)
    for step in range(ROUNDS):
        far = lax.ppermute(far, "rep", beyond)
        core = lax.ppermute(core, "rep", within)
        parts = combine_call(expand, far, own, core, servers)
        parts = [parts[0]] + [
            lax.ppermute(parts[d], "clus", [(c, c ^ d) for c in range(servers)])
            for d in range(1, servers)
        ]
        if step < ROUNDS - 1:
            x, core, own, far = round_call(x, mask, select, parts, far.shape[0])
        else:
            x = last_call(x, mask, parts)
    return x[None, None]


def solution(mesh):
    return jax.shard_map(
        local,
        mesh=mesh,
        in_specs=(
            P("rep", "clus", None, None),
            P("rep", "clus", None, None),
            P("rep", "clus", None, None),
        ),
        out_specs=P("rep", "clus", None, None),
        check_vma=False,
    )
```

```python
import functools

import jax
import jax.numpy as jnp
from jax import lax
from jax.experimental import pallas as pl
from jax.experimental.pallas import tpu as pltpu
from jax.sharding import PartitionSpec as P

ROUNDS = 2
LANES = 128
BLOCK = 128


def params():
    return pltpu.CompilerParams(vmem_limit_bytes=32 * 1024 * 1024)


def bf16(*shape):
    return jax.ShapeDtypeStruct(shape, jnp.bfloat16)


def normalize(value):
    return value * lax.rsqrt(jnp.mean(value * value, axis=-1, keepdims=True) + 1e-06)


def normalize_kernel(slot_cap, x_ref, pick_ref, out_ref, mask_ref):
    out_ref[...] = normalize(x_ref[...].astype(jnp.float32)).astype(jnp.bfloat16)
    slot = lax.broadcasted_iota(jnp.int32, mask_ref.shape, 1)
    slot = slot ^ (lax.axis_index("clus") * slot_cap)
    chosen = jnp.zeros(mask_ref.shape, jnp.float32)
    for k in range(pick_ref.shape[1]):
        chosen = jnp.where(pick_ref[:, k : k + 1] == slot, 1.0, chosen)
    mask_ref[...] = chosen.astype(jnp.bfloat16)


def normalize_call(descriptors, slots, total, slot_cap):
    rows, width = descriptors.shape
    return pl.pallas_call(
        functools.partial(normalize_kernel, slot_cap),
        grid=(rows // BLOCK,),
        in_specs=[
            pl.BlockSpec((BLOCK, width), lambda i: (i, 0)),
            pl.BlockSpec((BLOCK, slots.shape[1]), lambda i: (i, 0)),
        ],
        out_specs=[
            pl.BlockSpec((BLOCK, width), lambda i: (i, 0)),
            pl.BlockSpec((BLOCK, total), lambda i: (i, 0)),
        ],
        out_shape=[bf16(rows, width), bf16(rows, total)],
        compiler_params=params(),
        cost_estimate=pl.CostEstimate(
            flops=6 * rows * width, bytes_accessed=4 * rows * width, transcendentals=rows
        ),
        name="normalize",
    )(descriptors, slots)


def serve(x, select_ref, core_ref, own_ref, far_ref):
    total, sent = own_ref.shape[0], far_ref.shape[0]
    fetched = jnp.dot(
        select_ref[: 2 * total + sent], x, preferred_element_type=jnp.float32
    ).astype(jnp.bfloat16)
    core_ref[...] = fetched[:total]
    own_ref[...] = fetched[total : 2 * total]
    far_ref[...] = fetched[2 * total :]


def one_hot(asked, third, rows):
    total = asked.shape[1]
    column = jnp.broadcast_to(asked, (LANES, total)).T - third * rows
    tiles = []
    for t in range(rows // LANES):
        lane = lax.broadcasted_iota(jnp.int32, (total, LANES), 1) + t * LANES
        tiles.append(jnp.where(column == lane, 1.0, 0.0))
    return jnp.concatenate(tiles, axis=1)


def index_kernel(groups, x_ref, asked_ref, select_ref, expand_ref, core_ref, own_ref, far_ref):
    rows = x_ref.shape[0]
    servers, cap = asked_ref.shape[1:]
    total = servers * cap
    group, column = lax.axis_index("rep"), lax.axis_index("clus")
    odd = group % 2
    beyond = (group + 2 * odd - 1 + groups) % groups

    def asked(requester):
        parts = [
            asked_ref[(column ^ d) * groups + requester, pl.ds(column, 1), :]
            for d in range(servers)
        ]
        return jnp.concatenate(parts, axis=1)

    own = asked(group)
    from_own = one_hot(own, 1, rows)
    from_core = one_hot(asked(group ^ 1), 2 * odd, rows)
    to_far = one_hot(asked(beyond), 2 - 2 * odd, rows)
    from_far = one_hot(own, 2 * odd, rows)
    needed = jnp.concatenate(
        [
            jnp.broadcast_to(jnp.max(to_far, axis=0, keepdims=True), (8, rows)),
            jnp.broadcast_to(jnp.max(from_far, axis=0, keepdims=True), (8, rows)),
        ],
        axis=0,
    )
    before = lax.broadcasted_iota(jnp.int32, (rows, rows), 0) < lax.broadcasted_iota(
        jnp.int32, (rows, rows), 1
    )
    rank = jnp.dot(
        needed.astype(jnp.bfloat16),
        jnp.where(before, 1.0, 0.0).astype(jnp.bfloat16),
        preferred_element_type=jnp.float32,
    )
    rank = jnp.where(needed > 0, rank, -1.0).astype(jnp.int32)
    place = lax.broadcasted_iota(jnp.int32, (total, rows), 0)
    pack = jnp.where(place == rank[0:1], 1.0, 0.0).astype(jnp.bfloat16)
    packed = jnp.where(place == rank[8:9], 1.0, 0.0).astype(jnp.bfloat16)
    expand_ref[...] = lax.dot_general(
        from_far.astype(jnp.bfloat16),
        packed,
        (((1,), (1,)), ((), ())),
        preferred_element_type=jnp.float32,
    ).astype(jnp.bfloat16)
    select_ref[:total] = from_core.astype(jnp.bfloat16)
    select_ref[total : 2 * total] = from_own.astype(jnp.bfloat16)
    select_ref[2 * total :] = pack
    serve(x_ref[...], select_ref, core_ref, own_ref, far_ref)


def index_call(x, asked, groups):
    rows, width = x.shape
    total = asked.shape[1] * asked.shape[2]
    return pl.pallas_call(
        functools.partial(index_kernel, groups),
        out_shape=[
            bf16(3 * total, rows),
            bf16(total, total),
            bf16(total, width),
            bf16(total, width),
            bf16(total, width),
        ],
        compiler_params=params(),
        cost_estimate=pl.CostEstimate(
            flops=6 * total * rows * width, bytes_accessed=4 * rows * width, transcendentals=0
        ),
        name="index_and_serve",
    )(x, asked)


def combine_kernel(expand_ref, far_ref, own_ref, core_ref, *out_refs):
    cap, sent = out_refs[0].shape[0], far_ref.shape[0]
    far = jnp.dot(expand_ref[:, :sent], far_ref[...], preferred_element_type=jnp.float32)
    rows = (far + own_ref[...].astype(jnp.float32) + core_ref[...].astype(jnp.float32)).astype(
        jnp.bfloat16
    )
    for d, out in enumerate(out_refs):
        out[...] = rows[d * cap : (d + 1) * cap]


def combine_call(expand, far, own, core, servers):
    total, width = own.shape
    return pl.pallas_call(
        combine_kernel,
        out_shape=[bf16(total // servers, width)] * servers,
        compiler_params=params(),
        cost_estimate=pl.CostEstimate(
            flops=2 * total * far.shape[0] * width,
            bytes_accessed=8 * total * width,
            transcendentals=0,
        ),
        name="combine",
    )(expand, far, own, core)


def fill(buffer, parts):
    cap = parts[0].shape[0]
    for d, ref in enumerate(parts):
        buffer[d * cap : (d + 1) * cap] = ref[...]


def weigh(x, buffer, mask):
    sims = lax.dot_general(x, buffer, (((1,), (1,)), ((), ())), preferred_element_type=jnp.float32)
    positive = jnp.maximum(sims * (1.0 / x.shape[1]), 0.0)
    return (positive * positive * positive).astype(jnp.bfloat16) * mask


def add_up(x, weights, buffer):
    mixed = x.astype(jnp.float32) + jnp.dot(weights, buffer, preferred_element_type=jnp.float32)
    return normalize(mixed).astype(jnp.bfloat16)


def last_kernel(servers, x_ref, mask_ref, *rest):
    parts, rest = rest[:servers], rest[servers:]
    out_ref, buffer, weights, whole, sems = rest
    fill(buffer, parts)
    weights[...] = weigh(x_ref[...], buffer[...], mask_ref[...])
    copies = []
    for i, start in enumerate(range(0, x_ref.shape[0], BLOCK)):
        here = pl.ds(start, BLOCK)
        whole[here] = add_up(x_ref[here], weights[here], buffer[...])
        copies.append(pltpu.make_async_copy(whole.at[here], out_ref.at[here], sems.at[i]))
        copies[-1].start()
    for copy in copies:
        copy.wait()


def last_call(x, mask, parts):
    rows, width = x.shape
    total, servers = mask.shape[1], len(parts)
    return pl.pallas_call(
        functools.partial(last_kernel, servers),
        out_specs=pl.BlockSpec(memory_space=pl.ANY),
        out_shape=bf16(rows, width),
        scratch_shapes=[
            pltpu.VMEM((total, width), jnp.bfloat16),
            pltpu.VMEM((rows, total), jnp.bfloat16),
            pltpu.VMEM((rows, width), jnp.bfloat16),
            pltpu.SemaphoreType.DMA((rows // BLOCK,)),
        ],
        compiler_params=params(),
        cost_estimate=pl.CostEstimate(
            flops=4 * total * rows * width, bytes_accessed=4 * rows * width, transcendentals=rows
        ),
        name="mix",
    )(x, mask, *parts)


def round_kernel(servers, x_ref, mask_ref, select_ref, *rest):
    parts, rest = rest[:servers], rest[servers:]
    out_ref, core_ref, own_ref, far_ref, buffer, weights = rest
    fill(buffer, parts)
    weights[...] = weigh(x_ref[...], buffer[...], mask_ref[...])
    for start in range(0, x_ref.shape[0], BLOCK):
        stop = start + BLOCK
        out_ref[start:stop] = add_up(x_ref[start:stop], weights[start:stop], buffer[...])
    serve(out_ref[...], select_ref, core_ref, own_ref, far_ref)


def round_call(x, mask, select, parts, sent):
    rows, width = x.shape
    total, servers = mask.shape[1], len(parts)
    return pl.pallas_call(
        functools.partial(round_kernel, servers),
        out_shape=[bf16(rows, width), bf16(total, width), bf16(total, width), bf16(sent, width)],
        scratch_shapes=[
            pltpu.VMEM((total, width), jnp.bfloat16),
            pltpu.VMEM((rows, total), jnp.bfloat16),
        ],
        compiler_params=params(),
        cost_estimate=pl.CostEstimate(
            flops=10 * total * rows * width, bytes_accessed=6 * rows * width, transcendentals=rows
        ),
        name="mix_and_serve",
    )(x, mask, select, *parts)


def local(descriptors, request, pick):
    wanted = request[0, 0]
    servers, cap = wanted.shape
    total = servers * cap
    groups = lax.axis_size("rep")
    within = [(g, g ^ 1) for g in range(groups)]
    beyond = [(g, (g + 2 * (g % 2) - 1 + groups) % groups) for g in range(groups)]

    asked = lax.all_gather(wanted, ("clus", "rep"), axis=0, tiled=False)
    x, mask = normalize_call(descriptors[0, 0], pick[0, 0], total, cap)
    select, expand, core, own, far = index_call(x, asked, groups)
    for step in range(ROUNDS):
        far = lax.ppermute(far, "rep", beyond)
        core = lax.ppermute(core, "rep", within)
        parts = combine_call(expand, far, own, core, servers)
        parts = [parts[0]] + [
            lax.ppermute(parts[d], "clus", [(c, c ^ d) for c in range(servers)])
            for d in range(1, servers)
        ]
        if step < ROUNDS - 1:
            x, core, own, far = round_call(x, mask, select, parts, far.shape[0])
        else:
            x = last_call(x, mask, parts)
    return x[None, None]


def solution(mesh):
    return jax.shard_map(
        local,
        mesh=mesh,
        in_specs=(
            P("rep", "clus", None, None),
            P("rep", "clus", None, None),
            P("rep", "clus", None, None),
        ),
        out_specs=P("rep", "clus", None, None),
        check_vma=False,
    )
```

```python
import functools

import jax
import jax.numpy as jnp
from jax import lax
from jax.experimental import pallas as pl
from jax.experimental.pallas import tpu as pltpu
from jax.sharding import PartitionSpec as P

ROUNDS = 2
LANES = 128
BLOCK = 128


FAR_SHARE = 3, 8


def params(mib=32):
    return pltpu.CompilerParams(vmem_limit_bytes=mib * 1024 * 1024)


def bf16(*shape):
    return jax.ShapeDtypeStruct(shape, jnp.bfloat16)


def normalize(value):
    return value * lax.rsqrt(jnp.mean(value * value, axis=-1, keepdims=True) + 1e-06)


def normalize_kernel(slot_cap, x_ref, pick_ref, out_ref, mask_ref):
    out_ref[...] = normalize(x_ref[...].astype(jnp.float32)).astype(jnp.bfloat16)
    shape = mask_ref.shape[1], mask_ref.shape[0]
    slot = lax.broadcasted_iota(jnp.int32, shape, 0)
    slot = slot ^ (lax.axis_index("clus") * slot_cap)
    chosen = jnp.zeros(shape, jnp.float32)
    for k in range(pick_ref.shape[0]):
        chosen = jnp.where(pick_ref[k] == slot, 1.0, chosen)
    mask_ref[...] = chosen.T.astype(jnp.bfloat16)


def normalize_call(descriptors, slots, total, slot_cap):
    rows, width = descriptors.shape
    count = slots.shape[0]
    return pl.pallas_call(
        functools.partial(normalize_kernel, slot_cap),
        grid=(rows // BLOCK,),
        in_specs=[
            pl.BlockSpec((BLOCK, width), lambda i: (i, 0)),
            pl.BlockSpec((count, 1, BLOCK), lambda i: (0, 0, i)),
        ],
        out_specs=[
            pl.BlockSpec((BLOCK, width), lambda i: (i, 0)),
            pl.BlockSpec((BLOCK, total), lambda i: (i, 0)),
        ],
        out_shape=[bf16(rows, width), bf16(rows, total)],
        compiler_params=params(56),
        cost_estimate=pl.CostEstimate(
            flops=6 * rows * width, bytes_accessed=4 * rows * width, transcendentals=rows
        ),
        name="normalize",
    )(descriptors, slots)


def list_kernel(rows, *refs):
    parts, out_ref = refs[:-1], refs[-1]
    column = lax.axis_index("clus")
    third = lax.axis_index("rep") % 2 * 2
    total = out_ref.shape[1]
    mine = jnp.concatenate([ref[pl.ds(column, 1), :] for ref in parts], axis=1)
    most = jnp.zeros((1, 1), jnp.float32)
    lane = lax.broadcasted_iota(jnp.int32, (1, total), 1)
    earlier = lax.broadcasted_iota(jnp.int32, (total, total), 0) < lax.broadcasted_iota(
        jnp.int32, (total, total), 1
    )
    for server in range(len(parts)):
        asked = jnp.concatenate([ref[server : server + 1, :] for ref in parts], axis=1)
        far = (asked >= third * rows) & (asked < (third + 1) * rows)
        key = jnp.where(far, asked, -1 - lane).astype(jnp.float32)
        column_key = jnp.broadcast_to(key, (total, total)).T
        again = jnp.where((column_key == key) & earlier, 1.0, 0.0)
        again = jnp.max(again, axis=0, keepdims=True)
        first = jnp.where(far, 1.0 - again, 0.0)
        most = jnp.maximum(most, jnp.sum(first, axis=1, keepdims=True))
    place = lax.broadcasted_iota(jnp.int32, out_ref.shape, 0)
    out_ref[...] = jnp.where(
        place == 1, jnp.broadcast_to(most.astype(jnp.int32), out_ref.shape), mine
    )


def list_call(parts, rows):
    total = parts[0].size
    return pl.pallas_call(
        functools.partial(list_kernel, rows),
        out_shape=jax.ShapeDtypeStruct((8, total), jnp.int32),
        compiler_params=params(),
        cost_estimate=pl.CostEstimate(
            flops=6 * total * total, bytes_accessed=8 * total, transcendentals=0
        ),
        name="list",
    )(*parts)


def serve(x, select_ref, *out_refs):
    count = sum(out.shape[0] for out in out_refs)
    fetched = jnp.dot(select_ref[:count], x, preferred_element_type=jnp.float32)
    start = 0
    for out in out_refs:
        stop = start + out.shape[0]
        out[...] = fetched[start:stop].astype(jnp.bfloat16)
        start = stop


def one_hot(asked, third, rows):
    total = asked.shape[1]
    column = jnp.broadcast_to(asked, (LANES, total)).T - third * rows
    tiles = []
    for t in range(rows // LANES):
        lane = lax.broadcasted_iota(jnp.int32, (total, LANES), 1) + t * LANES
        tiles.append(jnp.where(column == lane, 1.0, 0.0))
    return jnp.concatenate(tiles, axis=1)


def index_kernel(x_ref, mine_ref, within_ref, beyond_ref, *out_refs):
    select_ref, expand_ref, most_ref, core_ref, own_ref, far_ref, rest_ref = out_refs
    rows, total = x_ref.shape[0], mine_ref.shape[1]
    odd = lax.axis_index("rep") % 2
    most = jnp.maximum(mine_ref[...], jnp.maximum(within_ref[...], beyond_ref[...]))
    most_ref[...] = jnp.broadcast_to(most[1:2, :LANES], most_ref.shape)
    own = mine_ref[0:1]
    from_own = one_hot(own, 1, rows)
    from_core = one_hot(within_ref[0:1], 2 * odd, rows)
    to_far = one_hot(beyond_ref[0:1], 2 - 2 * odd, rows)
    from_far = one_hot(own, 2 * odd, rows)
    needed = jnp.concatenate(
        [
            jnp.broadcast_to(jnp.max(to_far, axis=0, keepdims=True), (8, rows)),
            jnp.broadcast_to(jnp.max(from_far, axis=0, keepdims=True), (8, rows)),
        ],
        axis=0,
    )
    before = lax.broadcasted_iota(jnp.int32, (rows, rows), 0) < lax.broadcasted_iota(
        jnp.int32, (rows, rows), 1
    )
    rank = jnp.dot(
        needed.astype(jnp.bfloat16),
        jnp.where(before, 1.0, 0.0).astype(jnp.bfloat16),
        preferred_element_type=jnp.float32,
    )
    rank = jnp.where(needed > 0, rank, -1.0).astype(jnp.int32)
    place = lax.broadcasted_iota(jnp.int32, (total, rows), 0)
    pack = jnp.where(place == rank[0:1], 1.0, 0.0).astype(jnp.bfloat16)
    packed = jnp.where(place == rank[8:9], 1.0, 0.0).astype(jnp.bfloat16)
    expand_ref[...] = lax.dot_general(
        from_far.astype(jnp.bfloat16),
        packed,
        (((1,), (1,)), ((), ())),
        preferred_element_type=jnp.float32,
    ).astype(jnp.bfloat16)
    select_ref[:total] = from_core.astype(jnp.bfloat16)
    select_ref[total : 2 * total] = from_own.astype(jnp.bfloat16)
    select_ref[2 * total :] = pack
    serve(x_ref[...], select_ref, core_ref, own_ref, far_ref, rest_ref)


def index_call(x, mine, within, beyond, sent):
    rows, width = x.shape
    total = mine.shape[1]
    return pl.pallas_call(
        index_kernel,
        out_shape=[
            bf16(3 * total, rows),
            bf16(total, total),
            jax.ShapeDtypeStruct((8, LANES), jnp.int32),
            bf16(total, width),
            bf16(total, width),
            bf16(sent, width),
            bf16(total - sent, width),
        ],
        compiler_params=params(),
        cost_estimate=pl.CostEstimate(
            flops=6 * total * rows * width, bytes_accessed=4 * rows * width, transcendentals=0
        ),
        name="index_and_serve",
    )(x, mine, within, beyond)


def combine_kernel(expand_ref, far_ref, own_ref, core_ref, *out_refs):
    cap, sent = out_refs[0].shape[0], far_ref.shape[0]
    far = jnp.dot(expand_ref[:, :sent], far_ref[...], preferred_element_type=jnp.float32)
    rows = (far + own_ref[...].astype(jnp.float32) + core_ref[...].astype(jnp.float32)).astype(
        jnp.bfloat16
    )
    for d, out in enumerate(out_refs):
        out[...] = rows[d * cap : (d + 1) * cap]


def combine_call(expand, far, own, core, servers):
    total, width = own.shape
    return pl.pallas_call(
        combine_kernel,
        out_shape=[bf16(total // servers, width)] * servers,
        compiler_params=params(),
        cost_estimate=pl.CostEstimate(
            flops=2 * total * far.shape[0] * width,
            bytes_accessed=8 * total * width,
            transcendentals=0,
        ),
        name="combine",
    )(expand, far, own, core)


def fill(buffer, parts):
    cap = parts[0].shape[0]
    for d, ref in enumerate(parts):
        buffer[d * cap : (d + 1) * cap] = ref[...]


def weigh(x, buffer, mask):
    sims = lax.dot_general(x, buffer, (((1,), (1,)), ((), ())), preferred_element_type=jnp.float32)
    positive = jnp.maximum(sims * (1.0 / x.shape[1]), 0.0)
    return (positive * positive * positive).astype(jnp.bfloat16) * mask


def add_up(x, weights, buffer):
    mixed = x.astype(jnp.float32) + jnp.dot(weights, buffer, preferred_element_type=jnp.float32)
    return normalize(mixed).astype(jnp.bfloat16)


def last_kernel(servers, x_ref, mask_ref, *rest):
    parts, rest = rest[:servers], rest[servers:]
    out_ref, buffer, weights, whole, sems = rest
    fill(buffer, parts)
    weights[...] = weigh(x_ref[...], buffer[...], mask_ref[...])
    copies = []
    for i, start in enumerate(range(0, x_ref.shape[0], BLOCK)):
        here = pl.ds(start, BLOCK)
        whole[here] = add_up(x_ref[here], weights[here], buffer[...])
        copies.append(pltpu.make_async_copy(whole.at[here], out_ref.at[here], sems.at[i]))
        copies[-1].start()
    for copy in copies:
        copy.wait()


def last_call(x, mask, parts):
    rows, width = x.shape
    total, servers = mask.shape[1], len(parts)
    return pl.pallas_call(
        functools.partial(last_kernel, servers),
        out_specs=pl.BlockSpec(memory_space=pl.ANY),
        out_shape=bf16(rows, width),
        scratch_shapes=[
            pltpu.VMEM((total, width), jnp.bfloat16),
            pltpu.VMEM((rows, total), jnp.bfloat16),
            pltpu.VMEM((rows, width), jnp.bfloat16),
            pltpu.SemaphoreType.DMA((rows // BLOCK,)),
        ],
        compiler_params=params(),
        cost_estimate=pl.CostEstimate(
            flops=4 * total * rows * width, bytes_accessed=4 * rows * width, transcendentals=rows
        ),
        name="mix",
    )(x, mask, *parts)


def round_kernel(servers, x_ref, mask_ref, select_ref, *rest):
    parts, rest = rest[:servers], rest[servers:]
    out_ref, core_ref, own_ref, far_ref, buffer, weights = rest
    fill(buffer, parts)
    weights[...] = weigh(x_ref[...], buffer[...], mask_ref[...])
    for start in range(0, x_ref.shape[0], BLOCK):
        stop = start + BLOCK
        out_ref[start:stop] = add_up(x_ref[start:stop], weights[start:stop], buffer[...])
    serve(out_ref[...], select_ref, core_ref, own_ref, far_ref)


def round_call(x, mask, select, parts, sent):
    rows, width = x.shape
    total, servers = mask.shape[1], len(parts)
    return pl.pallas_call(
        functools.partial(round_kernel, servers),
        out_shape=[bf16(rows, width), bf16(total, width), bf16(total, width), bf16(sent, width)],
        scratch_shapes=[
            pltpu.VMEM((total, width), jnp.bfloat16),
            pltpu.VMEM((rows, total), jnp.bfloat16),
        ],
        compiler_params=params(),
        cost_estimate=pl.CostEstimate(
            flops=10 * total * rows * width, bytes_accessed=6 * rows * width, transcendentals=rows
        ),
        name="mix_and_serve",
    )(x, mask, select, *parts)


def local(descriptors, request, pick):
    wanted = request[0, 0]
    rows = descriptors.shape[2]
    servers, cap = wanted.shape
    total = servers * cap
    groups = lax.axis_size("rep")
    sent = total * FAR_SHARE[0] // FAR_SHARE[1]
    within = [(g, g ^ 1) for g in range(groups)]
    beyond = [(g, (g + 2 * (g % 2) - 1 + groups) % groups) for g in range(groups)]

    def turn(value, d):
        return lax.ppermute(value, "clus", [(c, c ^ d) for c in range(servers)])

    def shift(value, by):
        return lax.ppermute(value, "rep", [(g, (g + by) % groups) for g in range(groups)])

    def across(value):
        return lax.ppermute(value, "rep", beyond)

    def exchange(expand, far, own, core):
        parts = combine_call(expand, far, own, core, servers)
        return [parts[0]] + [turn(parts[d], d) for d in range(1, servers)]

    def rounds(x, mask, select, expand, far, own, core):
        for step in range(ROUNDS):
            if step:
                far, core = across(far), lax.ppermute(core, "rep", within)
            parts = exchange(expand, far, own, core)
            if step < ROUNDS - 1:
                x, core, own, far = round_call(x, mask, select, parts, far.shape[0])
        return last_call(x, mask, parts)

    def in_full(x, mask, select, expand, far, rest, own, core):
        far = jnp.concatenate([far, across(rest)], axis=0)
        return rounds(x, mask, select, expand, far, own, core)

    def as_sent(x, mask, select, expand, far, rest, own, core):
        return rounds(x, mask, select, expand, far, own, core)

    asked = [wanted] + [turn(wanted, d) for d in range(1, servers)]
    x, mask = normalize_call(descriptors[0, 0], pick.transpose(0, 3, 1, 2)[0], total, cap)
    mine = list_call(asked, rows)
    select, expand, most, core, own, far, rest = index_call(
        x, mine, lax.ppermute(mine, "rep", within), across(mine), sent
    )
    far, core = across(far), lax.ppermute(core, "rep", within)
    reach = 1
    while 2 * reach + 1 < groups:
        by = 2 * reach + 1
        most = jnp.maximum(most, jnp.maximum(shift(most, by), shift(most, -by)))
        reach += by
    x = lax.cond(
        most[0, 0] > sent, in_full, as_sent, x, mask, select, expand, far, rest, own, core
    )
    return x[None, None]


def solution(mesh):
    return jax.shard_map(
        local,
        mesh=mesh,
        in_specs=(
            P("rep", "clus", None, None),
            P("rep", "clus", None, None),
            P("rep", "clus", None, None),
        ),
        out_specs=P("rep", "clus", None, None),
        check_vma=False,
    )
```

```python
import functools

import jax
import jax.numpy as jnp
from jax import lax
from jax.experimental import pallas as pl
from jax.experimental.pallas import tpu as pltpu
from jax.sharding import PartitionSpec as P

ROUNDS = 2
LANES = 128
BLOCK = 128


FAR_SHARE = 3, 8


def params(mib=32):
    return pltpu.CompilerParams(vmem_limit_bytes=mib * 1024 * 1024)


def bf16(*shape):
    return jax.ShapeDtypeStruct(shape, jnp.bfloat16)


def normalize(value):
    return value * lax.rsqrt(jnp.mean(value * value, axis=-1, keepdims=True) + 1e-06)


def normalize_kernel(x_hbm, wanted_hbm, out_ref, wanted_ref, raw, sems):
    copies = [pltpu.make_async_copy(wanted_hbm, wanted_ref, sems.at[0])]
    starts = range(0, raw.shape[0], BLOCK)
    for i, start in enumerate(starts):
        here = pl.ds(start, BLOCK)
        copies.append(pltpu.make_async_copy(x_hbm.at[here], raw.at[here], sems.at[i + 1]))
    for copy in copies:
        copy.start()
    for copy, start in zip(copies[1:], starts):
        copy.wait()
        here = pl.ds(start, BLOCK)
        out_ref[here] = normalize(raw[here].astype(jnp.float32)).astype(jnp.bfloat16)
    copies[0].wait()


def normalize_call(descriptors, wanted):
    rows, width = descriptors.shape
    return pl.pallas_call(
        normalize_kernel,
        in_specs=[pl.BlockSpec(memory_space=pl.ANY)] * 2,
        out_shape=[bf16(rows, width), jax.ShapeDtypeStruct(wanted.shape, jnp.int32)],
        scratch_shapes=[
            pltpu.VMEM((rows, width), jnp.bfloat16),
            pltpu.SemaphoreType.DMA((rows // BLOCK + 1,)),
        ],
        compiler_params=params(56),
        cost_estimate=pl.CostEstimate(
            flops=6 * rows * width, bytes_accessed=4 * rows * width, transcendentals=rows
        ),
        name="normalize",
    )(descriptors, wanted)


def mask_kernel(slot_cap, pick_ref, mask_ref):
    shape = mask_ref.shape[1], mask_ref.shape[0]
    slot = lax.broadcasted_iota(jnp.int32, shape, 0)
    slot = slot ^ (lax.axis_index("clus") * slot_cap)
    chosen = jnp.zeros(shape, jnp.float32)
    for k in range(pick_ref.shape[0]):
        chosen = jnp.where(pick_ref[k] == slot, 1.0, chosen)
    mask_ref[...] = chosen.T.astype(jnp.bfloat16)


def mask_call(slots, total, slot_cap):
    count, _, rows = slots.shape
    return pl.pallas_call(
        functools.partial(mask_kernel, slot_cap),
        out_shape=bf16(rows, total),
        compiler_params=params(),
        cost_estimate=pl.CostEstimate(
            flops=2 * count * rows * total, bytes_accessed=2 * rows * total, transcendentals=0
        ),
        name="mask",
    )(slots)


def list_kernel(rows, *refs):
    parts, out_ref = refs[:-1], refs[-1]
    column = lax.axis_index("clus")
    third = lax.axis_index("rep") % 2 * 2
    total = out_ref.shape[1]
    mine = jnp.concatenate([ref[pl.ds(column, 1), :] for ref in parts], axis=1)
    most = jnp.zeros((1, 1), jnp.float32)
    lane = lax.broadcasted_iota(jnp.int32, (1, total), 1)
    earlier = lax.broadcasted_iota(jnp.int32, (total, total), 0) < lax.broadcasted_iota(
        jnp.int32, (total, total), 1
    )
    for server in range(len(parts)):
        asked = jnp.concatenate([ref[server : server + 1, :] for ref in parts], axis=1)
        far = (asked >= third * rows) & (asked < (third + 1) * rows)
        key = jnp.where(far, asked, -1 - lane).astype(jnp.float32)
        column_key = jnp.broadcast_to(key, (total, total)).T
        again = jnp.where((column_key == key) & earlier, 1.0, 0.0)
        again = jnp.max(again, axis=0, keepdims=True)
        first = jnp.where(far, 1.0 - again, 0.0)
        most = jnp.maximum(most, jnp.sum(first, axis=1, keepdims=True))
    place = lax.broadcasted_iota(jnp.int32, out_ref.shape, 0)
    out_ref[...] = jnp.where(
        place == 1, jnp.broadcast_to(most.astype(jnp.int32), out_ref.shape), mine
    )


def list_call(parts, rows):
    total = parts[0].size
    return pl.pallas_call(
        functools.partial(list_kernel, rows),
        out_shape=jax.ShapeDtypeStruct((8, total), jnp.int32),
        compiler_params=params(),
        cost_estimate=pl.CostEstimate(
            flops=6 * total * total, bytes_accessed=8 * total, transcendentals=0
        ),
        name="list",
    )(*parts)


def serve(x, select_ref, *out_refs):
    count = sum(out.shape[0] for out in out_refs)
    fetched = jnp.dot(select_ref[:count], x, preferred_element_type=jnp.float32)
    start = 0
    for out in out_refs:
        stop = start + out.shape[0]
        out[...] = fetched[start:stop].astype(jnp.bfloat16)
        start = stop


def one_hot(asked, third, rows):
    total = asked.shape[1]
    column = jnp.broadcast_to(asked, (LANES, total)).T - third * rows
    tiles = []
    for t in range(rows // LANES):
        lane = lax.broadcasted_iota(jnp.int32, (total, LANES), 1) + t * LANES
        tiles.append(jnp.where(column == lane, 1.0, 0.0))
    return jnp.concatenate(tiles, axis=1)


def packing(selected, rows):
    total = selected.shape[0]
    needed = jnp.broadcast_to(jnp.max(selected, axis=0, keepdims=True), (8, rows))
    before = lax.broadcasted_iota(jnp.int32, (rows, rows), 0) < lax.broadcasted_iota(
        jnp.int32, (rows, rows), 1
    )
    rank = jnp.dot(
        needed.astype(jnp.bfloat16),
        jnp.where(before, 1.0, 0.0).astype(jnp.bfloat16),
        preferred_element_type=jnp.float32,
    )
    rank = jnp.where(needed > 0, rank, -1.0).astype(jnp.int32)
    place = lax.broadcasted_iota(jnp.int32, (total, rows), 0)
    return jnp.where(place == rank[0:1], 1.0, 0.0).astype(jnp.bfloat16)


def far_kernel(x_ref, beyond_ref, pack_ref, far_ref):
    rows = x_ref.shape[0]
    third = 2 - lax.axis_index("rep") % 2 * 2
    pack_ref[...] = packing(one_hot(beyond_ref[0:1], third, rows), rows)
    serve(x_ref[...], pack_ref, far_ref)


def far_call(x, beyond, sent):
    rows, width = x.shape
    total = beyond.shape[1]
    return pl.pallas_call(
        far_kernel,
        out_shape=[bf16(total, rows), bf16(sent, width)],
        compiler_params=params(),
        cost_estimate=pl.CostEstimate(
            flops=2 * rows * rows * LANES, bytes_accessed=2 * rows * width, transcendentals=0
        ),
        name="pack_far",
    )(x, beyond)


def near_kernel(x_ref, pack_ref, mine_ref, within_ref, beyond_ref, *out_refs):
    select_ref, expand_ref, most_ref, core_ref, own_ref, rest_ref = out_refs
    rows, total = x_ref.shape[0], mine_ref.shape[1]
    third = lax.axis_index("rep") % 2 * 2
    most = jnp.maximum(mine_ref[...], jnp.maximum(within_ref[...], beyond_ref[...]))
    most_ref[...] = jnp.broadcast_to(most[1:2, :LANES], most_ref.shape)
    own = mine_ref[0:1]
    select_ref[:total] = one_hot(within_ref[0:1], third, rows).astype(jnp.bfloat16)
    select_ref[total:] = one_hot(own, 1, rows).astype(jnp.bfloat16)
    x = x_ref[...]
    serve(x, select_ref, core_ref, own_ref)
    rest = total - rest_ref.shape[0]
    serve(x, pack_ref.at[rest:], rest_ref)
    from_far = one_hot(own, third, rows)
    expand_ref[...] = lax.dot_general(
        from_far.astype(jnp.bfloat16),
        packing(from_far, rows),
        (((1,), (1,)), ((), ())),
        preferred_element_type=jnp.float32,
    ).astype(jnp.bfloat16)


def near_call(x, pack, mine, within, beyond, sent):
    rows, width = x.shape
    total = mine.shape[1]
    return pl.pallas_call(
        near_kernel,
        out_shape=[
            bf16(2 * total, rows),
            bf16(total, total),
            jax.ShapeDtypeStruct((8, LANES), jnp.int32),
            bf16(total, width),
            bf16(total, width),
            bf16(total - sent, width),
        ],
        compiler_params=params(),
        cost_estimate=pl.CostEstimate(
            flops=6 * total * rows * width, bytes_accessed=4 * rows * width, transcendentals=0
        ),
        name="serve_near",
    )(x, pack, mine, within, beyond)


def again_kernel(x_ref, select_ref, core_ref, own_ref):
    serve(x_ref[...], select_ref, core_ref, own_ref)


def again_call(x, select):
    rows, width = x.shape
    total = select.shape[0] // 2
    return pl.pallas_call(
        again_kernel,
        out_shape=[bf16(total, width)] * 2,
        compiler_params=params(),
        cost_estimate=pl.CostEstimate(
            flops=4 * total * rows * width, bytes_accessed=4 * rows * width, transcendentals=0
        ),
        name="serve_again",
    )(x, select)


def combine_kernel(expand_ref, far_ref, own_ref, core_ref, *out_refs):
    cap, sent = out_refs[0].shape[0], far_ref.shape[0]
    far = jnp.dot(expand_ref[:, :sent], far_ref[...], preferred_element_type=jnp.float32)
    rows = (far + own_ref[...].astype(jnp.float32) + core_ref[...].astype(jnp.float32)).astype(
        jnp.bfloat16
    )
    for d, out in enumerate(out_refs):
        out[...] = rows[d * cap : (d + 1) * cap]


def combine_call(expand, far, own, core, servers):
    total, width = own.shape
    return pl.pallas_call(
        combine_kernel,
        out_shape=[bf16(total // servers, width)] * servers,
        compiler_params=params(),
        cost_estimate=pl.CostEstimate(
            flops=2 * total * far.shape[0] * width,
            bytes_accessed=8 * total * width,
            transcendentals=0,
        ),
        name="combine",
    )(expand, far, own, core)


def fill(buffer, parts):
    cap = parts[0].shape[0]
    for d, ref in enumerate(parts):
        buffer[d * cap : (d + 1) * cap] = ref[...]


def weigh(x, buffer, mask):
    sims = lax.dot_general(x, buffer, (((1,), (1,)), ((), ())), preferred_element_type=jnp.float32)
    positive = jnp.maximum(sims * (1.0 / x.shape[1]), 0.0)
    return (positive * positive * positive).astype(jnp.bfloat16) * mask


def add_up(x, weights, buffer):
    mixed = x.astype(jnp.float32) + jnp.dot(weights, buffer, preferred_element_type=jnp.float32)
    return normalize(mixed).astype(jnp.bfloat16)


def last_kernel(servers, x_ref, mask_ref, *rest):
    parts, rest = rest[:servers], rest[servers:]
    out_ref, buffer, weights, whole, sems = rest
    fill(buffer, parts)
    weights[...] = weigh(x_ref[...], buffer[...], mask_ref[...])
    copies = []
    for i, start in enumerate(range(0, x_ref.shape[0], BLOCK)):
        here = pl.ds(start, BLOCK)
        whole[here] = add_up(x_ref[here], weights[here], buffer[...])
        copies.append(pltpu.make_async_copy(whole.at[here], out_ref.at[here], sems.at[i]))
        copies[-1].start()
    for copy in copies:
        copy.wait()


def last_call(x, mask, parts):
    rows, width = x.shape
    total, servers = mask.shape[1], len(parts)
    return pl.pallas_call(
        functools.partial(last_kernel, servers),
        out_specs=pl.BlockSpec(memory_space=pl.ANY),
        out_shape=bf16(rows, width),
        scratch_shapes=[
            pltpu.VMEM((total, width), jnp.bfloat16),
            pltpu.VMEM((rows, total), jnp.bfloat16),
            pltpu.VMEM((rows, width), jnp.bfloat16),
            pltpu.SemaphoreType.DMA((rows // BLOCK,)),
        ],
        compiler_params=params(),
        cost_estimate=pl.CostEstimate(
            flops=4 * total * rows * width, bytes_accessed=4 * rows * width, transcendentals=rows
        ),
        name="mix",
    )(x, mask, *parts)


def round_kernel(servers, x_ref, mask_ref, pack_ref, *rest):
    parts, rest = rest[:servers], rest[servers:]
    out_ref, far_ref, buffer, weights = rest
    fill(buffer, parts)
    weights[...] = weigh(x_ref[...], buffer[...], mask_ref[...])
    for start in range(0, x_ref.shape[0], BLOCK):
        stop = start + BLOCK
        out_ref[start:stop] = add_up(x_ref[start:stop], weights[start:stop], buffer[...])
    serve(out_ref[...], pack_ref, far_ref)


def round_call(x, mask, pack, parts, sent):
    rows, width = x.shape
    total, servers = mask.shape[1], len(parts)
    return pl.pallas_call(
        functools.partial(round_kernel, servers),
        out_shape=[bf16(rows, width), bf16(sent, width)],
        scratch_shapes=[
            pltpu.VMEM((total, width), jnp.bfloat16),
            pltpu.VMEM((rows, total), jnp.bfloat16),
        ],
        compiler_params=params(),
        cost_estimate=pl.CostEstimate(
            flops=5 * total * rows * width, bytes_accessed=6 * rows * width, transcendentals=rows
        ),
        name="mix_and_pack",
    )(x, mask, pack, *parts)


def local(descriptors, request, pick):
    wanted = request[0, 0]
    rows = descriptors.shape[2]
    servers, cap = wanted.shape
    total = servers * cap
    groups = lax.axis_size("rep")
    sent = total * FAR_SHARE[0] // FAR_SHARE[1]
    within = [(g, g ^ 1) for g in range(groups)]
    beyond = [(g, (g + 2 * (g % 2) - 1 + groups) % groups) for g in range(groups)]

    def turn(value, d):
        return lax.ppermute(value, "clus", [(c, c ^ d) for c in range(servers)])

    def shift(value, by):
        return lax.ppermute(value, "rep", [(g, (g + by) % groups) for g in range(groups)])

    def across(value):
        return lax.ppermute(value, "rep", beyond)

    def inside(value):
        return lax.ppermute(value, "rep", within)

    def exchange(expand, far, own, core):
        parts = combine_call(expand, far, own, core, servers)
        got = {d: turn(parts[d], d) for d in reversed(range(1, servers))}
        return [parts[0]] + [got[d] for d in range(1, servers)]

    def rounds(x, mask, pack, select, expand, far, own, core):
        parts = exchange(expand, far, own, core)
        for _ in range(ROUNDS - 1):
            x, far = round_call(x, mask, pack, parts, far.shape[0])
            far = across(far)
            core, own = again_call(x, select)
            parts = exchange(expand, far, own, inside(core))
        return x, *parts

    def in_full(x, mask, pack, select, expand, far, rest, own, core):
        far = jnp.concatenate([far, across(rest)], axis=0)
        return rounds(x, mask, pack, select, expand, far, own, core)

    def as_sent(x, mask, pack, select, expand, far, rest, own, core):
        return rounds(x, mask, pack, select, expand, far, own, core)

    asked = {d: turn(wanted, d) for d in reversed(range(1, servers))}
    x, held = normalize_call(descriptors[0, 0], wanted)
    mine = list_call([held] + [asked[d] for d in range(1, servers)], rows)
    beyond_list, within_list = across(mine), inside(mine)
    pack, far = far_call(x, beyond_list, sent)
    far = across(far)
    select, expand, most, core, own, rest = near_call(
        x, pack, mine, within_list, beyond_list, sent
    )
    core = inside(core)
    mask = mask_call(pick.transpose(0, 3, 1, 2)[0], total, cap)
    reach = 1
    while 2 * reach + 1 < groups:
        by = 2 * reach + 1
        most = jnp.maximum(most, jnp.maximum(shift(most, by), shift(most, -by)))
        reach += by
    x, *parts = lax.cond(
        most[0, 0] > sent, in_full, as_sent, x, mask, pack, select, expand, far, rest, own, core
    )
    return last_call(x, mask, parts)[None, None]


def solution(mesh):
    return jax.shard_map(
        local,
        mesh=mesh,
        in_specs=(
            P("rep", "clus", None, None),
            P("rep", "clus", None, None),
            P("rep", "clus", None, None),
        ),
        out_specs=P("rep", "clus", None, None),
        check_vma=False,
    )
```

```python
import functools

import jax
import jax.numpy as jnp
from jax import lax
from jax.experimental import pallas as pl
from jax.experimental.pallas import tpu as pltpu
from jax.sharding import PartitionSpec as P

ROUNDS = 2
LANES = 128
BLOCK = 128


FAR_SHARE = 3, 8


def params(mib=32):
    return pltpu.CompilerParams(vmem_limit_bytes=mib * 1024 * 1024)


def bf16(*shape):
    return jax.ShapeDtypeStruct(shape, jnp.bfloat16)


def normalize(value):
    return value * lax.rsqrt(jnp.mean(value * value, axis=-1, keepdims=True) + 1e-06)


def normalize_kernel(x_hbm, wanted_hbm, out_ref, wanted_ref, raw, sems):
    copies = [pltpu.make_async_copy(wanted_hbm, wanted_ref, sems.at[0])]
    starts = range(0, raw.shape[0], BLOCK)
    for i, start in enumerate(starts):
        here = pl.ds(start, BLOCK)
        copies.append(pltpu.make_async_copy(x_hbm.at[here], raw.at[here], sems.at[i + 1]))
    for copy in copies:
        copy.start()
    for copy, start in zip(copies[1:], starts):
        copy.wait()
        here = pl.ds(start, BLOCK)
        out_ref[here] = normalize(raw[here].astype(jnp.float32)).astype(jnp.bfloat16)
    copies[0].wait()


def normalize_call(descriptors, wanted):
    rows, width = descriptors.shape
    return pl.pallas_call(
        normalize_kernel,
        in_specs=[pl.BlockSpec(memory_space=pl.ANY)] * 2,
        out_shape=[bf16(rows, width), pltpu.VMEM(wanted.shape, jnp.int32)],
        scratch_shapes=[
            pltpu.VMEM((rows, width), jnp.bfloat16),
            pltpu.SemaphoreType.DMA((rows // BLOCK + 1,)),
        ],
        compiler_params=params(56),
        cost_estimate=pl.CostEstimate(
            flops=6 * rows * width, bytes_accessed=4 * rows * width, transcendentals=rows
        ),
        name="normalize",
    )(descriptors, wanted)


def mask_kernel(slot_cap, pick_ref, mask_ref):
    shape = mask_ref.shape[1], mask_ref.shape[0]
    slot = lax.broadcasted_iota(jnp.int32, shape, 0)
    slot = slot ^ (lax.axis_index("clus") * slot_cap)
    chosen = jnp.zeros(shape, jnp.float32)
    for k in range(pick_ref.shape[0]):
        chosen = jnp.where(pick_ref[k] == slot, 1.0, chosen)
    mask_ref[...] = chosen.T.astype(jnp.bfloat16)


def mask_call(slots, total, slot_cap):
    count, _, rows = slots.shape
    return pl.pallas_call(
        functools.partial(mask_kernel, slot_cap),
        out_shape=bf16(rows, total),
        compiler_params=params(),
        cost_estimate=pl.CostEstimate(
            flops=2 * count * rows * total, bytes_accessed=2 * rows * total, transcendentals=0
        ),
        name="mask",
    )(slots)


def list_kernel(rows, *refs):
    parts, out_ref = refs[:-1], refs[-1]
    column = lax.axis_index("clus")
    third = lax.axis_index("rep") % 2 * 2
    total = out_ref.shape[1]
    mine = jnp.concatenate([ref[pl.ds(column, 1), :] for ref in parts], axis=1)
    most = jnp.zeros((1, 1), jnp.float32)
    lane = lax.broadcasted_iota(jnp.int32, (1, total), 1)
    earlier = lax.broadcasted_iota(jnp.int32, (total, total), 0) < lax.broadcasted_iota(
        jnp.int32, (total, total), 1
    )
    for server in range(len(parts)):
        asked = jnp.concatenate([ref[server : server + 1, :] for ref in parts], axis=1)
        far = (asked >= third * rows) & (asked < (third + 1) * rows)
        key = jnp.where(far, asked, -1 - lane).astype(jnp.float32)
        column_key = jnp.broadcast_to(key, (total, total)).T
        again = jnp.where((column_key == key) & earlier, 1.0, 0.0)
        again = jnp.max(again, axis=0, keepdims=True)
        first = jnp.where(far, 1.0 - again, 0.0)
        most = jnp.maximum(most, jnp.sum(first, axis=1, keepdims=True))
    place = lax.broadcasted_iota(jnp.int32, out_ref.shape, 0)
    out_ref[...] = jnp.where(
        place == 1, jnp.broadcast_to(most.astype(jnp.int32), out_ref.shape), mine
    )


def list_call(parts, rows):
    total = parts[0].size
    return pl.pallas_call(
        functools.partial(list_kernel, rows),
        out_shape=jax.ShapeDtypeStruct((8, total), jnp.int32),
        compiler_params=params(),
        cost_estimate=pl.CostEstimate(
            flops=6 * total * total, bytes_accessed=8 * total, transcendentals=0
        ),
        name="list",
    )(*parts)


def serve(x, select_ref, *out_refs):
    count = sum(out.shape[0] for out in out_refs)
    fetched = jnp.dot(select_ref[:count], x, preferred_element_type=jnp.float32)
    start = 0
    for out in out_refs:
        stop = start + out.shape[0]
        out[...] = fetched[start:stop].astype(jnp.bfloat16)
        start = stop


def one_hot(asked, third, rows):
    total = asked.shape[1]
    column = jnp.broadcast_to(asked, (LANES, total)).T - third * rows
    tiles = []
    for t in range(rows // LANES):
        lane = lax.broadcasted_iota(jnp.int32, (total, LANES), 1) + t * LANES
        tiles.append(jnp.where(column == lane, 1.0, 0.0))
    return jnp.concatenate(tiles, axis=1)


def packing(selected, rows):
    total = selected.shape[0]
    needed = jnp.broadcast_to(jnp.max(selected, axis=0, keepdims=True), (8, rows))
    before = lax.broadcasted_iota(jnp.int32, (rows, rows), 0) < lax.broadcasted_iota(
        jnp.int32, (rows, rows), 1
    )
    rank = jnp.dot(
        needed.astype(jnp.bfloat16),
        jnp.where(before, 1.0, 0.0).astype(jnp.bfloat16),
        preferred_element_type=jnp.float32,
    )
    rank = jnp.where(needed > 0, rank, -1.0).astype(jnp.int32)
    place = lax.broadcasted_iota(jnp.int32, (total, rows), 0)
    return jnp.where(place == rank[0:1], 1.0, 0.0).astype(jnp.bfloat16)


def far_kernel(x_ref, beyond_ref, pack_ref, far_ref):
    rows = x_ref.shape[0]
    third = 2 - lax.axis_index("rep") % 2 * 2
    pack_ref[...] = packing(one_hot(beyond_ref[0:1], third, rows), rows)
    serve(x_ref[...], pack_ref, far_ref)


def far_call(x, beyond, sent):
    rows, width = x.shape
    total = beyond.shape[1]
    return pl.pallas_call(
        far_kernel,
        out_shape=[bf16(total, rows), bf16(sent, width)],
        compiler_params=params(),
        cost_estimate=pl.CostEstimate(
            flops=2 * rows * rows * LANES, bytes_accessed=2 * rows * width, transcendentals=0
        ),
        name="pack_far",
    )(x, beyond)


def near_kernel(x_ref, pack_ref, mine_ref, within_ref, beyond_ref, *out_refs):
    select_ref, expand_ref, most_ref, core_ref, own_ref, rest_ref = out_refs
    rows, total = x_ref.shape[0], mine_ref.shape[1]
    third = lax.axis_index("rep") % 2 * 2
    most = jnp.maximum(mine_ref[...], jnp.maximum(within_ref[...], beyond_ref[...]))
    most_ref[...] = jnp.broadcast_to(most[1:2, :LANES], most_ref.shape)
    own = mine_ref[0:1]
    select_ref[:total] = one_hot(within_ref[0:1], third, rows).astype(jnp.bfloat16)
    select_ref[total:] = one_hot(own, 1, rows).astype(jnp.bfloat16)
    x = x_ref[...]
    serve(x, select_ref, core_ref, own_ref)
    rest = total - rest_ref.shape[0]
    serve(x, pack_ref.at[rest:], rest_ref)
    from_far = one_hot(own, third, rows)
    expand_ref[...] = lax.dot_general(
        from_far.astype(jnp.bfloat16),
        packing(from_far, rows),
        (((1,), (1,)), ((), ())),
        preferred_element_type=jnp.float32,
    ).astype(jnp.bfloat16)


def near_call(x, pack, mine, within, beyond, sent):
    rows, width = x.shape
    total = mine.shape[1]
    return pl.pallas_call(
        near_kernel,
        out_shape=[
            bf16(2 * total, rows),
            bf16(total, total),
            jax.ShapeDtypeStruct((8, LANES), jnp.int32),
            bf16(total, width),
            bf16(total, width),
            bf16(total - sent, width),
        ],
        compiler_params=params(),
        cost_estimate=pl.CostEstimate(
            flops=6 * total * rows * width, bytes_accessed=4 * rows * width, transcendentals=0
        ),
        name="serve_near",
    )(x, pack, mine, within, beyond)


def again_kernel(x_ref, select_ref, core_ref, own_ref):
    serve(x_ref[...], select_ref, core_ref, own_ref)


def again_call(x, select):
    rows, width = x.shape
    total = select.shape[0] // 2
    return pl.pallas_call(
        again_kernel,
        out_shape=[bf16(total, width)] * 2,
        compiler_params=params(),
        cost_estimate=pl.CostEstimate(
            flops=4 * total * rows * width, bytes_accessed=4 * rows * width, transcendentals=0
        ),
        name="serve_again",
    )(x, select)


def unpack_kernel(first, expand_ref, far_ref, base_ref, out_ref):
    sent = far_ref.shape[0]
    far = jnp.dot(
        expand_ref[:, first : first + sent], far_ref[...], preferred_element_type=jnp.float32
    )
    out_ref[...] = (far + base_ref[...].astype(jnp.float32)).astype(jnp.bfloat16)


def unpack_call(expand, far, base, first=0):
    return pl.pallas_call(
        functools.partial(unpack_kernel, first),
        out_shape=bf16(*base.shape),
        compiler_params=params(),
        cost_estimate=pl.CostEstimate(flops=2**34, bytes_accessed=2**25, transcendentals=0),
        name="unpack",
    )(expand, far, base)


def combine_kernel(base_ref, core_ref, *out_refs):
    cap = out_refs[0].shape[0]
    for d, out in enumerate(out_refs):
        here = slice(d * cap, (d + 1) * cap)
        out[...] = base_ref[here] + core_ref[here]


def combine_call(base, core, servers):
    total, width = base.shape
    return pl.pallas_call(
        combine_kernel,
        out_shape=[bf16(total // servers, width)] * servers,
        compiler_params=params(),
        cost_estimate=pl.CostEstimate(
            flops=total * width, bytes_accessed=6 * total * width, transcendentals=0
        ),
        name="combine",
    )(base, core)


def fill(buffer, parts):
    cap = parts[0].shape[0]
    for d, ref in enumerate(parts):
        buffer[d * cap : (d + 1) * cap] = ref[...]


def weigh(x, buffer, mask):
    sims = lax.dot_general(x, buffer, (((1,), (1,)), ((), ())), preferred_element_type=jnp.float32)
    positive = jnp.maximum(sims * (1.0 / x.shape[1]), 0.0)
    return (positive * positive * positive).astype(jnp.bfloat16) * mask


def add_up(x, weights, buffer):
    mixed = x.astype(jnp.float32) + jnp.dot(weights, buffer, preferred_element_type=jnp.float32)
    return normalize(mixed).astype(jnp.bfloat16)


def last_kernel(servers, x_ref, mask_ref, *rest):
    parts, rest = rest[:servers], rest[servers:]
    out_ref, buffer, weights, whole, sems = rest
    fill(buffer, parts)
    weights[...] = weigh(x_ref[...], buffer[...], mask_ref[...])
    copies = []
    for i, start in enumerate(range(0, x_ref.shape[0], BLOCK)):
        here = pl.ds(start, BLOCK)
        whole[here] = add_up(x_ref[here], weights[here], buffer[...])
        copies.append(pltpu.make_async_copy(whole.at[here], out_ref.at[here], sems.at[i]))
        copies[-1].start()
    for copy in copies:
        copy.wait()


def last_call(x, mask, parts):
    rows, width = x.shape
    total, servers = mask.shape[1], len(parts)
    return pl.pallas_call(
        functools.partial(last_kernel, servers),
        out_specs=pl.BlockSpec(memory_space=pltpu.HBM),
        out_shape=pltpu.HBM((rows, width), jnp.bfloat16),
        scratch_shapes=[
            pltpu.VMEM((total, width), jnp.bfloat16),
            pltpu.VMEM((rows, total), jnp.bfloat16),
            pltpu.VMEM((rows, width), jnp.bfloat16),
            pltpu.SemaphoreType.DMA((rows // BLOCK,)),
        ],
        compiler_params=params(),
        cost_estimate=pl.CostEstimate(
            flops=4 * total * rows * width, bytes_accessed=4 * rows * width, transcendentals=rows
        ),
        name="mix",
    )(x, mask, *parts)


def round_kernel(servers, x_ref, mask_ref, pack_ref, *rest):
    parts, rest = rest[:servers], rest[servers:]
    out_ref, far_ref, buffer, weights = rest
    fill(buffer, parts)
    weights[...] = weigh(x_ref[...], buffer[...], mask_ref[...])
    for start in range(0, x_ref.shape[0], BLOCK):
        stop = start + BLOCK
        out_ref[start:stop] = add_up(x_ref[start:stop], weights[start:stop], buffer[...])
    serve(out_ref[...], pack_ref, far_ref)


def round_call(x, mask, pack, parts, sent):
    rows, width = x.shape
    total, servers = mask.shape[1], len(parts)
    return pl.pallas_call(
        functools.partial(round_kernel, servers),
        out_shape=[bf16(rows, width), bf16(sent, width)],
        scratch_shapes=[
            pltpu.VMEM((total, width), jnp.bfloat16),
            pltpu.VMEM((rows, total), jnp.bfloat16),
        ],
        compiler_params=params(),
        cost_estimate=pl.CostEstimate(
            flops=5 * total * rows * width, bytes_accessed=6 * rows * width, transcendentals=rows
        ),
        name="mix_and_pack",
    )(x, mask, pack, *parts)


def local(descriptors, request, pick):
    wanted = request[0, 0]
    rows = descriptors.shape[2]
    servers, cap = wanted.shape
    total = servers * cap
    groups = lax.axis_size("rep")
    sent = total * FAR_SHARE[0] // FAR_SHARE[1]
    within = [(g, g ^ 1) for g in range(groups)]
    beyond = [(g, (g + 2 * (g % 2) - 1 + groups) % groups) for g in range(groups)]

    def turn(value, d):
        return lax.ppermute(value, "clus", [(c, c ^ d) for c in range(servers)])

    def shift(value, by):
        return lax.ppermute(value, "rep", [(g, (g + by) % groups) for g in range(groups)])

    def across(value):
        return lax.ppermute(value, "rep", beyond)

    def inside(value):
        return lax.ppermute(value, "rep", within)

    def exchange(base, core):
        parts = combine_call(base, core, servers)
        got = {d: turn(parts[d], d) for d in reversed(range(1, servers))}
        return [parts[0]] + [got[d] for d in range(1, servers)]

    def rounds(x, mask, pack, select, expand, count, base, core):
        parts = exchange(base, core)
        for _ in range(ROUNDS - 1):
            x, far = round_call(x, mask, pack, parts, count)
            far = across(far)
            core, own = again_call(x, select)
            core = inside(core)
            parts = exchange(unpack_call(expand, far, own), core)
        return last_call(x, mask, parts)

    def in_full(x, mask, pack, select, expand, rest, base, core):
        base = unpack_call(expand, across(rest), base, sent)
        return rounds(x, mask, pack, select, expand, total, base, core)

    def as_sent(x, mask, pack, select, expand, rest, base, core):
        return rounds(x, mask, pack, select, expand, sent, base, core)

    asked = {d: turn(wanted, d) for d in reversed(range(1, servers))}
    x, held = normalize_call(descriptors[0, 0], wanted)
    mine = list_call([held] + [asked[d] for d in range(1, servers)], rows)
    beyond_list, within_list = across(mine), inside(mine)
    pack, far = far_call(x, beyond_list, sent)
    far = across(far)
    select, expand, most, core, own, rest = near_call(
        x, pack, mine, within_list, beyond_list, sent
    )
    core = inside(core)
    base = unpack_call(expand, far, own)
    mask = mask_call(pick.transpose(0, 3, 1, 2)[0], total, cap)
    reach = 1
    while 2 * reach + 1 < groups:
        by = 2 * reach + 1
        most = jnp.maximum(most, jnp.maximum(shift(most, by), shift(most, -by)))
        reach += by
    out = lax.cond(
        most[0, 0] > sent, in_full, as_sent, x, mask, pack, select, expand, rest, base, core
    )
    return out[None, None]


def solution(mesh):
    return jax.shard_map(
        local,
        mesh=mesh,
        in_specs=(
            P("rep", "clus", None, None),
            P("rep", "clus", None, None),
            P("rep", "clus", None, None),
        ),
        out_specs=P("rep", "clus", None, None),
        check_vma=False,
    )
```

```python
import functools

import jax
import jax.numpy as jnp
from jax import lax
from jax.experimental import pallas as pl
from jax.experimental.pallas import tpu as pltpu
from jax.sharding import PartitionSpec as P

ROUNDS = 2
LANES = 128
BLOCK = 128


FAR_SHARE = 3, 8


def params(mib=32):
    return pltpu.CompilerParams(vmem_limit_bytes=mib * 1024 * 1024)


def bf16(*shape):
    return jax.ShapeDtypeStruct(shape, jnp.bfloat16)


def normalize(value):
    return value * lax.rsqrt(jnp.mean(value * value, axis=-1, keepdims=True) + 1e-06)


def normalize_kernel(x_hbm, out_ref, raw, sems):
    copies = []
    starts = range(0, raw.shape[0], BLOCK)
    for i, start in enumerate(starts):
        here = pl.ds(start, BLOCK)
        copies.append(pltpu.make_async_copy(x_hbm.at[here], raw.at[here], sems.at[i]))
        copies[-1].start()
    for copy, start in zip(copies, starts):
        copy.wait()
        here = pl.ds(start, BLOCK)
        out_ref[here] = normalize(raw[here].astype(jnp.float32)).astype(jnp.bfloat16)


def normalize_call(descriptors):
    rows, width = descriptors.shape
    return pl.pallas_call(
        normalize_kernel,
        in_specs=[pl.BlockSpec(memory_space=pl.ANY)],
        out_shape=bf16(rows, width),
        scratch_shapes=[
            pltpu.VMEM((rows, width), jnp.bfloat16),
            pltpu.SemaphoreType.DMA((rows // BLOCK,)),
        ],
        compiler_params=params(56),
        cost_estimate=pl.CostEstimate(
            flops=6 * rows * width, bytes_accessed=4 * rows * width, transcendentals=rows
        ),
        name="normalize",
    )(descriptors)


def mask_kernel(slot_cap, pick_hbm, wanted_hbm, mask_ref, wanted_ref, pick, sems):
    copies = [
        pltpu.make_async_copy(pick_hbm, pick, sems.at[0]),
        pltpu.make_async_copy(wanted_hbm, wanted_ref, sems.at[1]),
    ]
    for copy in copies:
        copy.start()
    shape = mask_ref.shape[1], mask_ref.shape[0]
    slot = lax.broadcasted_iota(jnp.int32, shape, 0)
    slot = slot ^ (lax.axis_index("clus") * slot_cap)
    chosen = jnp.zeros(shape, jnp.float32)
    copies[0].wait()
    for k in range(pick.shape[0]):
        chosen = jnp.where(pick[k] == slot, 1.0, chosen)
    mask_ref[...] = chosen.T.astype(jnp.bfloat16)
    copies[1].wait()


def mask_call(slots, wanted):
    count, _, rows = slots.shape
    total = wanted.size
    return pl.pallas_call(
        functools.partial(mask_kernel, wanted.shape[1]),
        in_specs=[pl.BlockSpec(memory_space=pl.ANY)] * 2,
        out_shape=[bf16(rows, total), pltpu.VMEM(wanted.shape, jnp.int32)],
        scratch_shapes=[pltpu.VMEM(slots.shape, jnp.int32), pltpu.SemaphoreType.DMA((2,))],
        compiler_params=params(56),
        cost_estimate=pl.CostEstimate(
            flops=2 * count * rows * total, bytes_accessed=2 * rows * total, transcendentals=0
        ),
        name="mask",
    )(slots, wanted)


def list_kernel(rows, *refs):
    parts, out_ref = refs[:-1], refs[-1]
    column = lax.axis_index("clus")
    third = lax.axis_index("rep") % 2 * 2
    total = out_ref.shape[1]
    mine = jnp.concatenate([ref[pl.ds(column, 1), :] for ref in parts], axis=1)
    most = jnp.zeros((1, 1), jnp.float32)
    lane = lax.broadcasted_iota(jnp.int32, (1, total), 1)
    earlier = lax.broadcasted_iota(jnp.int32, (total, total), 0) < lax.broadcasted_iota(
        jnp.int32, (total, total), 1
    )
    for server in range(len(parts)):
        asked = jnp.concatenate([ref[server : server + 1, :] for ref in parts], axis=1)
        far = (asked >= third * rows) & (asked < (third + 1) * rows)
        key = jnp.where(far, asked, -1 - lane).astype(jnp.float32)
        column_key = jnp.broadcast_to(key, (total, total)).T
        again = jnp.where((column_key == key) & earlier, 1.0, 0.0)
        again = jnp.max(again, axis=0, keepdims=True)
        first = jnp.where(far, 1.0 - again, 0.0)
        most = jnp.maximum(most, jnp.sum(first, axis=1, keepdims=True))
    place = lax.broadcasted_iota(jnp.int32, out_ref.shape, 0)
    out_ref[...] = jnp.where(
        place == 1, jnp.broadcast_to(most.astype(jnp.int32), out_ref.shape), mine
    )


def list_call(parts, rows):
    total = parts[0].size
    return pl.pallas_call(
        functools.partial(list_kernel, rows),
        out_shape=jax.ShapeDtypeStruct((8, total), jnp.int32),
        compiler_params=params(),
        cost_estimate=pl.CostEstimate(
            flops=6 * total * total, bytes_accessed=8 * total, transcendentals=0
        ),
        name="list",
    )(*parts)


def serve(x, select_ref, *out_refs):
    count = sum(out.shape[0] for out in out_refs)
    fetched = jnp.dot(select_ref[:count], x, preferred_element_type=jnp.float32)
    start = 0
    for out in out_refs:
        stop = start + out.shape[0]
        out[...] = fetched[start:stop].astype(jnp.bfloat16)
        start = stop


def one_hot(asked, third, rows):
    total = asked.shape[1]
    column = jnp.broadcast_to(asked, (LANES, total)).T - third * rows
    tiles = []
    for t in range(rows // LANES):
        lane = lax.broadcasted_iota(jnp.int32, (total, LANES), 1) + t * LANES
        tiles.append(jnp.where(column == lane, 1.0, 0.0))
    return jnp.concatenate(tiles, axis=1)


def packing(selected, rows):
    total = selected.shape[0]
    needed = jnp.broadcast_to(jnp.max(selected, axis=0, keepdims=True), (8, rows))
    before = lax.broadcasted_iota(jnp.int32, (rows, rows), 0) < lax.broadcasted_iota(
        jnp.int32, (rows, rows), 1
    )
    rank = jnp.dot(
        needed.astype(jnp.bfloat16),
        jnp.where(before, 1.0, 0.0).astype(jnp.bfloat16),
        preferred_element_type=jnp.float32,
    )
    rank = jnp.where(needed > 0, rank, -1.0).astype(jnp.int32)
    place = lax.broadcasted_iota(jnp.int32, (total, rows), 0)
    return jnp.where(place == rank[0:1], 1.0, 0.0).astype(jnp.bfloat16)


def far_kernel(x_ref, mine_ref, within_ref, beyond_ref, pack_ref, most_ref, far_ref):
    rows = x_ref.shape[0]
    most = jnp.maximum(mine_ref[...], jnp.maximum(within_ref[...], beyond_ref[...]))
    most_ref[...] = jnp.broadcast_to(most[1:2, :LANES], most_ref.shape)
    third = 2 - lax.axis_index("rep") % 2 * 2
    pack_ref[...] = packing(one_hot(beyond_ref[0:1], third, rows), rows)
    serve(x_ref[...], pack_ref, far_ref)


def far_call(x, mine, within, beyond, sent):
    rows, width = x.shape
    total = mine.shape[1]
    return pl.pallas_call(
        far_kernel,
        out_shape=[
            bf16(total, rows),
            jax.ShapeDtypeStruct((8, LANES), jnp.int32),
            bf16(sent, width),
        ],
        compiler_params=params(),
        cost_estimate=pl.CostEstimate(
            flops=2 * rows * rows * LANES, bytes_accessed=2 * rows * width, transcendentals=0
        ),
        name="pack_far",
    )(x, mine, within, beyond)


def near_kernel(x_ref, pack_ref, mine_ref, within_ref, *out_refs):
    select_ref, expand_ref, core_ref, own_ref, rest_ref = out_refs
    rows, total = x_ref.shape[0], mine_ref.shape[1]
    third = lax.axis_index("rep") % 2 * 2
    own = mine_ref[0:1]
    select_ref[:total] = one_hot(within_ref[0:1], third, rows).astype(jnp.bfloat16)
    select_ref[total:] = one_hot(own, 1, rows).astype(jnp.bfloat16)
    x = x_ref[...]
    serve(x, select_ref, core_ref, own_ref)
    rest = total - rest_ref.shape[0]
    serve(x, pack_ref.at[rest:], rest_ref)
    from_far = one_hot(own, third, rows)
    expand_ref[...] = lax.dot_general(
        from_far.astype(jnp.bfloat16),
        packing(from_far, rows),
        (((1,), (1,)), ((), ())),
        preferred_element_type=jnp.float32,
    ).astype(jnp.bfloat16)


def near_call(x, pack, mine, within, sent):
    rows, width = x.shape
    total = mine.shape[1]
    return pl.pallas_call(
        near_kernel,
        out_shape=[
            bf16(2 * total, rows),
            bf16(total, total),
            bf16(total, width),
            bf16(total, width),
            bf16(total - sent, width),
        ],
        compiler_params=params(),
        cost_estimate=pl.CostEstimate(
            flops=6 * total * rows * width, bytes_accessed=4 * rows * width, transcendentals=0
        ),
        name="serve_near",
    )(x, pack, mine, within)


def again_kernel(x_ref, select_ref, core_ref, own_ref):
    serve(x_ref[...], select_ref, core_ref, own_ref)


def again_call(x, select):
    rows, width = x.shape
    total = select.shape[0] // 2
    return pl.pallas_call(
        again_kernel,
        out_shape=[bf16(total, width)] * 2,
        compiler_params=params(),
        cost_estimate=pl.CostEstimate(
            flops=4 * total * rows * width, bytes_accessed=4 * rows * width, transcendentals=0
        ),
        name="serve_again",
    )(x, select)


def unpack_kernel(first, expand_ref, far_ref, *refs):
    out_ref, sent = refs[-1], far_ref.shape[0]
    rows = jnp.dot(
        expand_ref[:, first : first + sent], far_ref[...], preferred_element_type=jnp.float32
    )
    for base_ref in refs[:-1]:
        rows += base_ref[...].astype(jnp.float32)
    out_ref[...] = rows.astype(jnp.bfloat16)


def unpack_call(expand, far, *base, first=0):
    return pl.pallas_call(
        functools.partial(unpack_kernel, first),
        out_shape=bf16(expand.shape[0], far.shape[1]),
        compiler_params=params(),
        cost_estimate=pl.CostEstimate(flops=2**34, bytes_accessed=2**25, transcendentals=0),
        name="unpack",
    )(expand, far, *base)


def combine_kernel(base_ref, core_ref, most_ref, out_most_ref, *out_refs):
    cap = out_refs[0].shape[0]
    out_most_ref[...] = most_ref[...]
    for d, out in enumerate(out_refs):
        here = slice(d * cap, (d + 1) * cap)
        out[...] = base_ref[here] + core_ref[here]


def combine_call(base, core, most, servers):
    total, width = base.shape
    most, *parts = pl.pallas_call(
        combine_kernel,
        out_shape=[jax.ShapeDtypeStruct(most.shape, most.dtype)]
        + [bf16(total // servers, width)] * servers,
        compiler_params=params(),
        cost_estimate=pl.CostEstimate(
            flops=total * width, bytes_accessed=6 * total * width, transcendentals=0
        ),
        name="combine",
    )(base, core, most)
    return most, parts


def fill(buffer, parts):
    cap = parts[0].shape[0]
    for d, ref in enumerate(reversed(parts)):
        buffer[d * cap : (d + 1) * cap] = ref[...]


def weigh(x, buffer, mask):
    sims = lax.dot_general(x, buffer, (((1,), (1,)), ((), ())), preferred_element_type=jnp.float32)
    positive = jnp.maximum(sims * (1.0 / x.shape[1]), 0.0)
    return (positive * positive * positive).astype(jnp.bfloat16) * mask


def add_up(x, weights, buffer):
    mixed = x.astype(jnp.float32) + jnp.dot(weights, buffer, preferred_element_type=jnp.float32)
    return normalize(mixed).astype(jnp.bfloat16)


def last_kernel(servers, x_ref, mask_ref, *rest):
    parts, rest = rest[:servers], rest[servers:]
    out_ref, buffer, weights, whole, sems = rest
    fill(buffer, parts)
    weights[...] = weigh(x_ref[...], buffer[...], mask_ref[...])
    copies = []
    for i, start in enumerate(range(0, x_ref.shape[0], BLOCK)):
        here = pl.ds(start, BLOCK)
        whole[here] = add_up(x_ref[here], weights[here], buffer[...])
        copies.append(pltpu.make_async_copy(whole.at[here], out_ref.at[here], sems.at[i]))
        copies[-1].start()
    for copy in copies:
        copy.wait()


def last_call(x, mask, parts):
    rows, width = x.shape
    total, servers = mask.shape[1], len(parts)
    return pl.pallas_call(
        functools.partial(last_kernel, servers),
        out_specs=pl.BlockSpec(memory_space=pltpu.HBM),
        out_shape=pltpu.HBM((rows, width), jnp.bfloat16),
        scratch_shapes=[
            pltpu.VMEM((total, width), jnp.bfloat16),
            pltpu.VMEM((rows, total), jnp.bfloat16),
            pltpu.VMEM((rows, width), jnp.bfloat16),
            pltpu.SemaphoreType.DMA((rows // BLOCK,)),
        ],
        compiler_params=params(),
        cost_estimate=pl.CostEstimate(
            flops=4 * total * rows * width, bytes_accessed=4 * rows * width, transcendentals=rows
        ),
        name="mix",
    )(x, mask, *reversed(parts))


def round_kernel(servers, x_ref, mask_ref, pack_ref, *rest):
    parts, rest = rest[:servers], rest[servers:]
    *most_refs, out_ref, far_ref, most_ref, buffer, weights = rest
    most_ref[...] = functools.reduce(jnp.maximum, [ref[...] for ref in most_refs])
    fill(buffer, parts)
    weights[...] = weigh(x_ref[...], buffer[...], mask_ref[...])
    for start in range(0, x_ref.shape[0], BLOCK):
        stop = start + BLOCK
        out_ref[start:stop] = add_up(x_ref[start:stop], weights[start:stop], buffer[...])
    serve(out_ref[...], pack_ref, far_ref)


def round_call(x, mask, pack, parts, mosts, sent):
    rows, width = x.shape
    total, servers = mask.shape[1], len(parts)
    return pl.pallas_call(
        functools.partial(round_kernel, servers),
        out_shape=[
            bf16(rows, width),
            bf16(sent, width),
            jax.ShapeDtypeStruct((8, LANES), jnp.int32),
        ],
        scratch_shapes=[
            pltpu.VMEM((total, width), jnp.bfloat16),
            pltpu.VMEM((rows, total), jnp.bfloat16),
        ],
        compiler_params=params(),
        cost_estimate=pl.CostEstimate(
            flops=5 * total * rows * width, bytes_accessed=6 * rows * width, transcendentals=rows
        ),
        name="mix_and_pack",
    )(x, mask, pack, *reversed(parts), *mosts)


def local(descriptors, request, pick):
    wanted = request[0, 0]
    rows = descriptors.shape[2]
    servers, cap = wanted.shape
    total = servers * cap
    groups = lax.axis_size("rep")
    sent = total * FAR_SHARE[0] // FAR_SHARE[1]
    within = [(g, g ^ 1) for g in range(groups)]
    beyond = [(g, (g + 2 * (g % 2) - 1 + groups) % groups) for g in range(groups)]

    def turn(value, d):
        return lax.ppermute(value, "clus", [(c, c ^ d) for c in range(servers)])

    def shift(value, by):
        return lax.ppermute(value, "rep", [(g, (g + by) % groups) for g in range(groups)])

    def across(value):
        return lax.ppermute(value, "rep", beyond)

    def inside(value):
        return lax.ppermute(value, "rep", within)

    def exchange(base, core, most):
        most, parts = combine_call(base, core, most, servers)
        return most, turned(parts)

    def turned(parts):
        got = {d: turn(parts[d], d) for d in reversed(range(1, servers))}
        return [parts[0]] + [got[d] for d in range(1, servers)]

    def next_parts(x, far, select, expand, most):
        far = across(far)
        core, own = again_call(x, select)
        core = inside(core)
        return exchange(unpack_call(expand, far, own), core, most)

    def in_full(raw, x, rest, mask, pack, select, expand, most, first, last):
        late = unpack_call(expand, across(rest), first=sent).reshape(servers, cap, -1)
        parts = [a + b for a, b in zip(first, turned(list(late)))]
        x = raw
        for _ in range(ROUNDS - 1):
            x, far, most = round_call(x, mask, pack, parts, [most], total)
            most, parts = next_parts(x, far, select, expand, most)
        return last_call(x, mask, parts)

    def as_sent(raw, x, rest, mask, pack, select, expand, most, first, last):
        return last_call(x, mask, last)

    asked = {d: turn(wanted, d) for d in reversed(range(1, servers))}
    mask, held = mask_call(pick.transpose(0, 3, 1, 2)[0], wanted)
    mine = list_call([held] + [asked[d] for d in range(1, servers)], rows)
    beyond_list, within_list = across(mine), inside(mine)
    x = normalize_call(descriptors[0, 0])
    pack, most, far = far_call(x, mine, within_list, beyond_list, sent)
    far = across(far)
    select, expand, core, own, rest = near_call(x, pack, mine, within_list, sent)
    core = inside(core)
    most, first = exchange(unpack_call(expand, far, own), core, most)
    mosts = [most]
    reach = 1
    while 2 * reach + 1 < groups:
        by = 2 * reach + 1
        most = functools.reduce(jnp.maximum, mosts)
        mosts = [most, shift(most, by), shift(most, -by)]
        reach += by
    mixed, parts = x, first
    for _ in range(ROUNDS - 1):
        mixed, far, most = round_call(mixed, mask, pack, parts, mosts, sent)
        most, parts = next_parts(mixed, far, select, expand, most)
        mosts = [most]
    state = x, mixed, rest, mask, pack, select, expand, most, first, parts
    return lax.cond(most[0, 0] > sent, in_full, as_sent, *state)[None, None]


def solution(mesh):
    return jax.shard_map(
        local,
        mesh=mesh,
        in_specs=(
            P("rep", "clus", None, None),
            P("rep", "clus", None, None),
            P("rep", "clus", None, None),
        ),
        out_specs=P("rep", "clus", None, None),
        check_vma=False,
    )
```

```python
import functools

import jax
import jax.numpy as jnp
from jax import lax
from jax.experimental import pallas as pl
from jax.experimental.pallas import tpu as pltpu
from jax.sharding import PartitionSpec as P

ROUNDS = 2
LANES = 128
BLOCK = 128
TILE = 256


FAR_SHARE = 3, 8


def params(mib=32):
    return pltpu.CompilerParams(vmem_limit_bytes=mib * 1024 * 1024)


def bf16(*shape):
    return jax.ShapeDtypeStruct(shape, jnp.bfloat16)


def normalize(value):
    return value * lax.rsqrt(jnp.mean(value * value, axis=-1, keepdims=True) + 1e-06)


def normalize_kernel(x_hbm, out_ref, raw, sems):
    copies = []
    starts = range(0, raw.shape[0], BLOCK)
    for i, start in enumerate(starts):
        here = pl.ds(start, BLOCK)
        copies.append(pltpu.make_async_copy(x_hbm.at[here], raw.at[here], sems.at[i]))
        copies[-1].start()
    for copy, start in zip(copies, starts):
        copy.wait()
        here = pl.ds(start, BLOCK)
        out_ref[here] = normalize(raw[here].astype(jnp.float32)).astype(jnp.bfloat16)


def normalize_call(descriptors):
    rows, width = descriptors.shape
    return pl.pallas_call(
        normalize_kernel,
        in_specs=[pl.BlockSpec(memory_space=pl.ANY)],
        out_shape=bf16(rows, width),
        scratch_shapes=[
            pltpu.VMEM((rows, width), jnp.bfloat16),
            pltpu.SemaphoreType.DMA((rows // BLOCK,)),
        ],
        compiler_params=params(56),
        cost_estimate=pl.CostEstimate(
            flops=6 * rows * width, bytes_accessed=4 * rows * width, transcendentals=rows
        ),
        name="normalize",
    )(descriptors)


def mask_kernel(slot_cap, pick_hbm, wanted_hbm, mask_ref, wanted_ref, pick, sems):
    copies = [
        pltpu.make_async_copy(pick_hbm, pick, sems.at[0]),
        pltpu.make_async_copy(wanted_hbm, wanted_ref, sems.at[1]),
    ]
    for copy in copies:
        copy.start()
    shape = mask_ref.shape[1], mask_ref.shape[0]
    slot = lax.broadcasted_iota(jnp.int32, shape, 0)
    slot = slot ^ (lax.axis_index("clus") * slot_cap)
    chosen = jnp.zeros(shape, jnp.float32)
    copies[0].wait()
    for k in range(pick.shape[0]):
        chosen = jnp.where(pick[k] == slot, 1.0, chosen)
    mask_ref[...] = chosen.T.astype(jnp.bfloat16)
    copies[1].wait()


def mask_call(slots, wanted):
    count, _, rows = slots.shape
    total = wanted.size
    return pl.pallas_call(
        functools.partial(mask_kernel, wanted.shape[1]),
        in_specs=[pl.BlockSpec(memory_space=pl.ANY)] * 2,
        out_shape=[bf16(rows, total), pltpu.VMEM(wanted.shape, jnp.int32)],
        scratch_shapes=[pltpu.VMEM(slots.shape, jnp.int32), pltpu.SemaphoreType.DMA((2,))],
        compiler_params=params(56),
        cost_estimate=pl.CostEstimate(
            flops=2 * count * rows * total, bytes_accessed=2 * rows * total, transcendentals=0
        ),
        name="mask",
    )(slots, wanted)


def list_kernel(rows, *refs):
    parts, out_ref = refs[:-1], refs[-1]
    column = lax.axis_index("clus")
    third = lax.axis_index("rep") % 2 * 2
    total = out_ref.shape[1]
    mine = jnp.concatenate([ref[pl.ds(column, 1), :] for ref in parts], axis=1)
    most = jnp.zeros((1, 1), jnp.float32)
    lane = lax.broadcasted_iota(jnp.int32, (1, total), 1)
    earlier = lax.broadcasted_iota(jnp.int32, (total, total), 0) < lax.broadcasted_iota(
        jnp.int32, (total, total), 1
    )
    for server in range(len(parts)):
        asked = jnp.concatenate([ref[server : server + 1, :] for ref in parts], axis=1)
        far = (asked >= third * rows) & (asked < (third + 1) * rows)
        key = jnp.where(far, asked, -1 - lane).astype(jnp.float32)
        column_key = jnp.broadcast_to(key, (total, total)).T
        again = jnp.where((column_key == key) & earlier, 1.0, 0.0)
        again = jnp.max(again, axis=0, keepdims=True)
        first = jnp.where(far, 1.0 - again, 0.0)
        most = jnp.maximum(most, jnp.sum(first, axis=1, keepdims=True))
    place = lax.broadcasted_iota(jnp.int32, out_ref.shape, 0)
    out_ref[...] = jnp.where(
        place == 1, jnp.broadcast_to(most.astype(jnp.int32), out_ref.shape), mine
    )


def list_call(parts, rows):
    total = parts[0].size
    return pl.pallas_call(
        functools.partial(list_kernel, rows),
        out_shape=jax.ShapeDtypeStruct((8, total), jnp.int32),
        compiler_params=params(),
        cost_estimate=pl.CostEstimate(
            flops=6 * total * total, bytes_accessed=8 * total, transcendentals=0
        ),
        name="list",
    )(*parts)


def serve(x, select_ref, *out_refs):
    count = sum(out.shape[0] for out in out_refs)
    fetched = jnp.dot(select_ref[:count], x, preferred_element_type=jnp.float32)
    start = 0
    for out in out_refs:
        stop = start + out.shape[0]
        out[...] = fetched[start:stop].astype(jnp.bfloat16)
        start = stop


def one_hot(asked, third, rows):
    total = asked.shape[1]
    column = jnp.broadcast_to(asked, (LANES, total)).T - third * rows
    tiles = []
    for t in range(rows // LANES):
        lane = lax.broadcasted_iota(jnp.int32, (total, LANES), 1) + t * LANES
        tiles.append(jnp.where(column == lane, 1.0, 0.0))
    return jnp.concatenate(tiles, axis=1)


def packing(selected, rows):
    total = selected.shape[0]
    needed = jnp.broadcast_to(jnp.max(selected, axis=0, keepdims=True), (8, rows))
    before = lax.broadcasted_iota(jnp.int32, (rows, rows), 0) < lax.broadcasted_iota(
        jnp.int32, (rows, rows), 1
    )
    rank = jnp.dot(
        needed.astype(jnp.bfloat16),
        jnp.where(before, 1.0, 0.0).astype(jnp.bfloat16),
        preferred_element_type=jnp.float32,
    )
    rank = jnp.where(needed > 0, rank, -1.0).astype(jnp.int32)
    place = lax.broadcasted_iota(jnp.int32, (total, rows), 0)
    return jnp.where(place == rank[0:1], 1.0, 0.0).astype(jnp.bfloat16)


def far_kernel(x_ref, mine_ref, within_ref, beyond_ref, pack_ref, most_ref, far_ref):
    rows = x_ref.shape[0]
    most = jnp.maximum(mine_ref[...], jnp.maximum(within_ref[...], beyond_ref[...]))
    most_ref[...] = jnp.broadcast_to(most[1:2, :LANES], most_ref.shape)
    third = 2 - lax.axis_index("rep") % 2 * 2
    pack_ref[...] = packing(one_hot(beyond_ref[0:1], third, rows), rows)
    serve(x_ref[...], pack_ref, far_ref)


def far_call(x, mine, within, beyond, sent):
    rows, width = x.shape
    total = mine.shape[1]
    return pl.pallas_call(
        far_kernel,
        out_shape=[
            bf16(total, rows),
            jax.ShapeDtypeStruct((8, LANES), jnp.int32),
            bf16(sent, width),
        ],
        compiler_params=params(),
        cost_estimate=pl.CostEstimate(
            flops=2 * rows * rows * LANES, bytes_accessed=2 * rows * width, transcendentals=0
        ),
        name="pack_far",
    )(x, mine, within, beyond)


def near_kernel(x_ref, pack_ref, mine_ref, within_ref, *out_refs):
    select_ref, expand_ref, core_ref, own_ref, rest_ref = out_refs
    rows, total = x_ref.shape[0], mine_ref.shape[1]
    third = lax.axis_index("rep") % 2 * 2
    own = mine_ref[0:1]
    select_ref[:total] = one_hot(within_ref[0:1], third, rows).astype(jnp.bfloat16)
    select_ref[total:] = one_hot(own, 1, rows).astype(jnp.bfloat16)
    x = x_ref[...]
    serve(x, select_ref, core_ref, own_ref)
    rest = total - rest_ref.shape[0]
    serve(x, pack_ref.at[rest:], rest_ref)
    from_far = one_hot(own, third, rows)
    expand_ref[...] = lax.dot_general(
        from_far.astype(jnp.bfloat16),
        packing(from_far, rows),
        (((1,), (1,)), ((), ())),
        preferred_element_type=jnp.float32,
    ).astype(jnp.bfloat16)


def near_call(x, pack, mine, within, sent):
    rows, width = x.shape
    total = mine.shape[1]
    return pl.pallas_call(
        near_kernel,
        out_shape=[
            bf16(2 * total, rows),
            bf16(total, total),
            bf16(total, width),
            bf16(total, width),
            bf16(total - sent, width),
        ],
        compiler_params=params(),
        cost_estimate=pl.CostEstimate(
            flops=6 * total * rows * width, bytes_accessed=4 * rows * width, transcendentals=0
        ),
        name="serve_near",
    )(x, pack, mine, within)


def again_kernel(x_ref, select_ref, core_ref, own_ref):
    serve(x_ref[...], select_ref, core_ref, own_ref)


def again_call(x, select):
    rows, width = x.shape
    total = select.shape[0] // 2
    return pl.pallas_call(
        again_kernel,
        out_shape=[bf16(total, width)] * 2,
        compiler_params=params(),
        cost_estimate=pl.CostEstimate(
            flops=4 * total * rows * width, bytes_accessed=4 * rows * width, transcendentals=0
        ),
        name="serve_again",
    )(x, select)


def unpack_kernel(first, expand_ref, far_ref, *refs):
    out_ref, sent = refs[-1], far_ref.shape[0]
    rows = jnp.dot(
        expand_ref[:, first : first + sent], far_ref[...], preferred_element_type=jnp.float32
    )
    for base_ref in refs[:-1]:
        rows += base_ref[...].astype(jnp.float32)
    out_ref[...] = rows.astype(jnp.bfloat16)


def unpack_call(expand, far, *base, first=0):
    return pl.pallas_call(
        functools.partial(unpack_kernel, first),
        out_shape=bf16(expand.shape[0], far.shape[1]),
        compiler_params=params(),
        cost_estimate=pl.CostEstimate(flops=2**34, bytes_accessed=2**25, transcendentals=0),
        name="unpack",
    )(expand, far, *base)


def combine_kernel(base_ref, core_ref, most_ref, out_most_ref, *out_refs):
    cap = out_refs[0].shape[0]
    out_most_ref[...] = most_ref[...]
    for d, out in enumerate(out_refs):
        here = slice(d * cap, (d + 1) * cap)
        out[...] = base_ref[here] + core_ref[here]


def combine_call(base, core, most, servers):
    total, width = base.shape
    most, *parts = pl.pallas_call(
        combine_kernel,
        out_shape=[jax.ShapeDtypeStruct(most.shape, most.dtype)]
        + [bf16(total // servers, width)] * servers,
        compiler_params=params(),
        cost_estimate=pl.CostEstimate(
            flops=total * width, bytes_accessed=6 * total * width, transcendentals=0
        ),
        name="combine",
    )(base, core, most)
    return most, parts


def fill(buffer, parts):
    cap = parts[0].shape[0]
    for d, ref in enumerate(reversed(parts)):
        buffer[d * cap : (d + 1) * cap] = ref[...]


def weigh(x_ref, buffer, mask):
    rows, width = x_ref.shape
    across = (((1,), (1,)), ((), ()))
    gram = lax.dot_general(buffer, buffer, across, preferred_element_type=jnp.float32)
    high = gram.astype(jnp.bfloat16)
    low = (gram - high.astype(jnp.float32)).astype(jnp.bfloat16)
    dots = lax.dot_general(x_ref[...], buffer, across, preferred_element_type=jnp.float32)
    positive = jnp.maximum(dots * (1.0 / width), 0.0)
    weights = (positive * positive * positive).astype(jnp.bfloat16) * mask
    crossed = jnp.dot(weights, high, preferred_element_type=jnp.float32)
    crossed += jnp.dot(weights, low, preferred_element_type=jnp.float32)
    squares = weights.astype(jnp.float32) * (2.0 * dots + crossed)
    own = jnp.zeros((rows, LANES), jnp.float32)
    for start in range(0, width, LANES):
        tile = x_ref[:, start : start + LANES].astype(jnp.float32)
        own += tile * tile
    if squares.shape[1] == LANES:
        total = jnp.sum(own + squares, axis=1, keepdims=True)
    else:
        total = jnp.sum(own, axis=1, keepdims=True) + jnp.sum(squares, axis=1, keepdims=True)
    return weights, lax.rsqrt(total * (1.0 / width) + 1e-06)


def add_up(x, weights, scale, buffer):
    mixed = x.astype(jnp.float32) + jnp.dot(weights, buffer, preferred_element_type=jnp.float32)
    return (mixed * scale).astype(jnp.bfloat16)


def last_kernel(servers, x_ref, mask_ref, *rest):
    parts, rest = rest[:servers], rest[servers:]
    out_ref, buffer, whole, sems = rest
    fill(buffer, parts)
    weights, scale = weigh(x_ref, buffer[...], mask_ref[...])
    copies = []
    for i, start in enumerate(range(0, x_ref.shape[1], TILE)):
        here = slice(start, start + TILE)
        whole[:, here] = add_up(x_ref[:, here], weights, scale, buffer[:, here])
        tile = pl.ds(start, TILE)
        copies.append(pltpu.make_async_copy(whole.at[:, tile], out_ref.at[:, tile], sems.at[i]))
        copies[-1].start()
    for copy in copies:
        copy.wait()


def last_call(x, mask, parts):
    rows, width = x.shape
    total, servers = mask.shape[1], len(parts)
    return pl.pallas_call(
        functools.partial(last_kernel, servers),
        out_specs=pl.BlockSpec(memory_space=pltpu.HBM),
        out_shape=pltpu.HBM((rows, width), jnp.bfloat16),
        scratch_shapes=[
            pltpu.VMEM((total, width), jnp.bfloat16),
            pltpu.VMEM((rows, width), jnp.bfloat16),
            pltpu.SemaphoreType.DMA((width // TILE,)),
        ],
        compiler_params=params(),
        cost_estimate=pl.CostEstimate(
            flops=4 * total * rows * width, bytes_accessed=4 * rows * width, transcendentals=rows
        ),
        name="mix",
    )(x, mask, *reversed(parts))


def round_kernel(servers, x_ref, mask_ref, pack_ref, *rest):
    parts, rest = rest[:servers], rest[servers:]
    *most_refs, out_ref, far_ref, most_ref, buffer = rest
    most_ref[...] = functools.reduce(jnp.maximum, [ref[...] for ref in most_refs])
    fill(buffer, parts)
    weights, scale = weigh(x_ref, buffer[...], mask_ref[...])
    pack = pack_ref[: far_ref.shape[0]]
    for start in range(0, x_ref.shape[1], TILE):
        here = slice(start, start + TILE)
        tile = add_up(x_ref[:, here], weights, scale, buffer[:, here])
        out_ref[:, here] = tile
        far_ref[:, here] = jnp.dot(pack, tile, preferred_element_type=jnp.float32).astype(
            jnp.bfloat16
        )


def round_call(x, mask, pack, parts, mosts, sent):
    rows, width = x.shape
    total, servers = mask.shape[1], len(parts)
    return pl.pallas_call(
        functools.partial(round_kernel, servers),
        out_shape=[
            bf16(rows, width),
            bf16(sent, width),
            jax.ShapeDtypeStruct((8, LANES), jnp.int32),
        ],
        scratch_shapes=[pltpu.VMEM((total, width), jnp.bfloat16)],
        compiler_params=params(),
        cost_estimate=pl.CostEstimate(
            flops=5 * total * rows * width, bytes_accessed=6 * rows * width, transcendentals=rows
        ),
        name="mix_and_pack",
    )(x, mask, pack, *reversed(parts), *mosts)


def local(descriptors, request, pick):
    wanted = request[0, 0]
    rows = descriptors.shape[2]
    servers, cap = wanted.shape
    total = servers * cap
    groups = lax.axis_size("rep")
    sent = total * FAR_SHARE[0] // FAR_SHARE[1]
    within = [(g, g ^ 1) for g in range(groups)]
    beyond = [(g, (g + 2 * (g % 2) - 1 + groups) % groups) for g in range(groups)]

    def turn(value, d):
        return lax.ppermute(value, "clus", [(c, c ^ d) for c in range(servers)])

    def shift(value, by):
        return lax.ppermute(value, "rep", [(g, (g + by) % groups) for g in range(groups)])

    def across(value):
        return lax.ppermute(value, "rep", beyond)

    def inside(value):
        return lax.ppermute(value, "rep", within)

    def exchange(base, core, most):
        most, parts = combine_call(base, core, most, servers)
        return most, turned(parts)

    def turned(parts):
        got = {d: turn(parts[d], d) for d in reversed(range(1, servers))}
        return [parts[0]] + [got[d] for d in range(1, servers)]

    def next_parts(x, far, select, expand, most):
        far = across(far)
        core, own = again_call(x, select)
        core = inside(core)
        return exchange(unpack_call(expand, far, own), core, most)

    def in_full(raw, x, rest, mask, pack, select, expand, most, first, last):
        late = unpack_call(expand, across(rest), first=sent).reshape(servers, cap, -1)
        parts = [a + b for a, b in zip(first, turned(list(late)))]
        x = raw
        for _ in range(ROUNDS - 1):
            x, far, most = round_call(x, mask, pack, parts, [most], total)
            most, parts = next_parts(x, far, select, expand, most)
        return last_call(x, mask, parts)

    def as_sent(raw, x, rest, mask, pack, select, expand, most, first, last):
        return last_call(x, mask, last)

    asked = {d: turn(wanted, d) for d in reversed(range(1, servers))}
    mask, held = mask_call(pick.transpose(0, 3, 1, 2)[0], wanted)
    mine = list_call([held] + [asked[d] for d in range(1, servers)], rows)
    beyond_list, within_list = across(mine), inside(mine)
    x = normalize_call(descriptors[0, 0])
    pack, most, far = far_call(x, mine, within_list, beyond_list, sent)
    far = across(far)
    select, expand, core, own, rest = near_call(x, pack, mine, within_list, sent)
    core = inside(core)
    most, first = exchange(unpack_call(expand, far, own), core, most)
    mosts = [most]
    reach = 1
    while 2 * reach + 1 < groups:
        by = 2 * reach + 1
        most = functools.reduce(jnp.maximum, mosts)
        mosts = [most, shift(most, by), shift(most, -by)]
        reach += by
    mixed, parts = x, first
    for _ in range(ROUNDS - 1):
        mixed, far, most = round_call(mixed, mask, pack, parts, mosts, sent)
        most, parts = next_parts(mixed, far, select, expand, most)
        mosts = [most]
    state = x, mixed, rest, mask, pack, select, expand, most, first, parts
    return lax.cond(most[0, 0] > sent, in_full, as_sent, *state)[None, None]


def solution(mesh):
    return jax.shard_map(
        local,
        mesh=mesh,
        in_specs=(
            P("rep", "clus", None, None),
            P("rep", "clus", None, None),
            P("rep", "clus", None, None),
        ),
        out_specs=P("rep", "clus", None, None),
        check_vma=False,
    )
```

```python
import functools

import jax
import jax.numpy as jnp
from jax import lax
from jax.experimental import pallas as pl
from jax.experimental.pallas import tpu as pltpu
from jax.sharding import PartitionSpec as P

ROUNDS = 2
LANES = 128
BLOCK = 128
TILE = 256
CHUNK = 32


FAR_SHARE = 3, 8


def params(mib=32):
    return pltpu.CompilerParams(vmem_limit_bytes=mib * 1024 * 1024)


def bf16(*shape):
    return jax.ShapeDtypeStruct(shape, jnp.bfloat16)


def normalize(value):
    return value * lax.rsqrt(jnp.mean(value * value, axis=-1, keepdims=True) + 1e-06)


def normalize_kernel(x_hbm, out_ref, raw, sems):
    copies = []
    starts = range(0, raw.shape[0], BLOCK)
    for i, start in enumerate(starts):
        here = pl.ds(start, BLOCK)
        copies.append(pltpu.make_async_copy(x_hbm.at[here], raw.at[here], sems.at[i]))
        copies[-1].start()
    for copy, start in zip(copies, starts):
        copy.wait()
        here = pl.ds(start, BLOCK)
        out_ref[here] = normalize(raw[here].astype(jnp.float32)).astype(jnp.bfloat16)


def normalize_call(descriptors):
    rows, width = descriptors.shape
    return pl.pallas_call(
        normalize_kernel,
        in_specs=[pl.BlockSpec(memory_space=pl.ANY)],
        out_shape=bf16(rows, width),
        scratch_shapes=[
            pltpu.VMEM((rows, width), jnp.bfloat16),
            pltpu.SemaphoreType.DMA((rows // BLOCK,)),
        ],
        compiler_params=params(56),
        cost_estimate=pl.CostEstimate(
            flops=6 * rows * width, bytes_accessed=4 * rows * width, transcendentals=rows
        ),
        name="normalize",
    )(descriptors)


def mask_kernel(slot_cap, pick_hbm, wanted_hbm, mask_ref, wanted_ref, pick, sems):
    copies = [
        pltpu.make_async_copy(pick_hbm, pick, sems.at[0]),
        pltpu.make_async_copy(wanted_hbm, wanted_ref, sems.at[1]),
    ]
    for copy in copies:
        copy.start()
    shape = mask_ref.shape[1], mask_ref.shape[0]
    slot = lax.broadcasted_iota(jnp.int32, shape, 0)
    slot = slot ^ (lax.axis_index("clus") * slot_cap)
    chosen = jnp.zeros(shape, jnp.float32)
    copies[0].wait()
    for k in range(pick.shape[0]):
        chosen = jnp.where(pick[k] == slot, 1.0, chosen)
    mask_ref[...] = chosen.T.astype(jnp.bfloat16)
    copies[1].wait()


def mask_call(slots, wanted):
    count, _, rows = slots.shape
    total = wanted.size
    return pl.pallas_call(
        functools.partial(mask_kernel, wanted.shape[1]),
        in_specs=[pl.BlockSpec(memory_space=pl.ANY)] * 2,
        out_shape=[bf16(rows, total), pltpu.VMEM(wanted.shape, jnp.int32)],
        scratch_shapes=[pltpu.VMEM(slots.shape, jnp.int32), pltpu.SemaphoreType.DMA((2,))],
        compiler_params=params(56),
        cost_estimate=pl.CostEstimate(
            flops=2 * count * rows * total, bytes_accessed=2 * rows * total, transcendentals=0
        ),
        name="mask",
    )(slots, wanted)


def list_kernel(rows, *refs):
    parts, out_ref = refs[:-1], refs[-1]
    column = lax.axis_index("clus")
    third = lax.axis_index("rep") % 2 * 2
    total = out_ref.shape[1]
    mine = jnp.concatenate([ref[pl.ds(column, 1), :] for ref in parts], axis=1)
    most = jnp.zeros((1, 1), jnp.float32)
    lane = lax.broadcasted_iota(jnp.int32, (1, total), 1)
    earlier = lax.broadcasted_iota(jnp.int32, (total, total), 0) < lax.broadcasted_iota(
        jnp.int32, (total, total), 1
    )
    for server in range(len(parts)):
        asked = jnp.concatenate([ref[server : server + 1, :] for ref in parts], axis=1)
        far = (asked >= third * rows) & (asked < (third + 1) * rows)
        key = jnp.where(far, asked, -1 - lane).astype(jnp.float32)
        column_key = jnp.broadcast_to(key, (total, total)).T
        again = jnp.where((column_key == key) & earlier, 1.0, 0.0)
        again = jnp.max(again, axis=0, keepdims=True)
        first = jnp.where(far, 1.0 - again, 0.0)
        most = jnp.maximum(most, jnp.sum(first, axis=1, keepdims=True))
    place = lax.broadcasted_iota(jnp.int32, out_ref.shape, 0)
    out_ref[...] = jnp.where(
        place == 1, jnp.broadcast_to(most.astype(jnp.int32), out_ref.shape), mine
    )


def list_call(parts, rows):
    total = parts[0].size
    return pl.pallas_call(
        functools.partial(list_kernel, rows),
        out_shape=jax.ShapeDtypeStruct((8, total), jnp.int32),
        compiler_params=params(),
        cost_estimate=pl.CostEstimate(
            flops=6 * total * total, bytes_accessed=8 * total, transcendentals=0
        ),
        name="list",
    )(*parts)


def serve(x, select_ref, *out_refs):
    count = sum(out.shape[0] for out in out_refs)
    fetched = jnp.dot(select_ref[:count], x, preferred_element_type=jnp.float32)
    start = 0
    for out in out_refs:
        stop = start + out.shape[0]
        out[...] = fetched[start:stop].astype(jnp.bfloat16)
        start = stop


def one_hot(asked, third, rows):
    total = asked.shape[1]
    column = jnp.broadcast_to(asked, (LANES, total)).T - third * rows
    tiles = []
    for t in range(rows // LANES):
        lane = lax.broadcasted_iota(jnp.int32, (total, LANES), 1) + t * LANES
        tiles.append(jnp.where(column == lane, 1.0, 0.0))
    return jnp.concatenate(tiles, axis=1)


def packing(selected, rows):
    total = selected.shape[0]
    needed = jnp.broadcast_to(jnp.max(selected, axis=0, keepdims=True), (8, rows))
    before = lax.broadcasted_iota(jnp.int32, (rows, rows), 0) < lax.broadcasted_iota(
        jnp.int32, (rows, rows), 1
    )
    rank = jnp.dot(
        needed.astype(jnp.bfloat16),
        jnp.where(before, 1.0, 0.0).astype(jnp.bfloat16),
        preferred_element_type=jnp.float32,
    )
    rank = jnp.where(needed > 0, rank, -1.0).astype(jnp.int32)
    place = lax.broadcasted_iota(jnp.int32, (total, rows), 0)
    return jnp.where(place == rank[0:1], 1.0, 0.0).astype(jnp.bfloat16)


def far_kernel(x_ref, mine_ref, within_ref, beyond_ref, pack_ref, most_ref, far_ref):
    rows = x_ref.shape[0]
    most = jnp.maximum(mine_ref[...], jnp.maximum(within_ref[...], beyond_ref[...]))
    most_ref[...] = jnp.broadcast_to(most[1:2, :LANES], most_ref.shape)
    third = 2 - lax.axis_index("rep") % 2 * 2
    pack_ref[...] = packing(one_hot(beyond_ref[0:1], third, rows), rows)
    serve(x_ref[...], pack_ref, far_ref)


def far_call(x, mine, within, beyond, sent):
    rows, width = x.shape
    total = mine.shape[1]
    return pl.pallas_call(
        far_kernel,
        out_shape=[
            bf16(total, rows),
            jax.ShapeDtypeStruct((8, LANES), jnp.int32),
            bf16(sent, width),
        ],
        compiler_params=params(),
        cost_estimate=pl.CostEstimate(
            flops=2 * rows * rows * LANES, bytes_accessed=2 * rows * width, transcendentals=0
        ),
        name="pack_far",
    )(x, mine, within, beyond)


def near_kernel(x_ref, pack_ref, mine_ref, within_ref, far_ref, *out_refs):
    select_ref, expand_ref, core_ref, own_ref, rest_ref, held_ref = out_refs
    held_ref[...] = far_ref[...]
    rows, total = x_ref.shape[0], mine_ref.shape[1]
    third = lax.axis_index("rep") % 2 * 2
    own = mine_ref[0:1]
    select_ref[:total] = one_hot(within_ref[0:1], third, rows).astype(jnp.bfloat16)
    select_ref[total:] = one_hot(own, 1, rows).astype(jnp.bfloat16)
    x = x_ref[...]
    serve(x, select_ref, core_ref, own_ref)
    rest = total - rest_ref.shape[0]
    serve(x, pack_ref.at[rest:], rest_ref)
    from_far = one_hot(own, third, rows)
    expand_ref[...] = lax.dot_general(
        from_far.astype(jnp.bfloat16),
        packing(from_far, rows),
        (((1,), (1,)), ((), ())),
        preferred_element_type=jnp.float32,
    ).astype(jnp.bfloat16)


def near_call(x, pack, mine, within, far):
    rows, width = x.shape
    total, sent = mine.shape[1], far.shape[0]
    return pl.pallas_call(
        near_kernel,
        out_shape=[
            bf16(2 * total, rows),
            bf16(total, total),
            bf16(total, width),
            bf16(total, width),
            bf16(total - sent, width),
            bf16(sent, width),
        ],
        compiler_params=params(),
        cost_estimate=pl.CostEstimate(
            flops=6 * total * rows * width, bytes_accessed=4 * rows * width, transcendentals=0
        ),
        name="serve_near",
    )(x, pack, mine, within, far)


def again_kernel(x_ref, select_ref, far_ref, core_ref, own_ref, held_ref):
    held_ref[...] = far_ref[...]
    serve(x_ref[...], select_ref, core_ref, own_ref)


def again_call(x, select, far):
    rows, width = x.shape
    total = select.shape[0] // 2
    return pl.pallas_call(
        again_kernel,
        out_shape=[bf16(total, width)] * 2 + [bf16(*far.shape)],
        compiler_params=params(),
        cost_estimate=pl.CostEstimate(
            flops=4 * total * rows * width, bytes_accessed=4 * rows * width, transcendentals=0
        ),
        name="serve_again",
    )(x, select, far)


def unpack_kernel(first, expand_ref, around_ref, beside_ref, *refs):
    out_ref, sent = refs[-1], around_ref.shape[0]
    far = around_ref[...] + beside_ref[...]
    rows = jnp.dot(
        expand_ref[:, first : first + sent], far, preferred_element_type=jnp.float32
    )
    for base_ref in refs[:-1]:
        rows += base_ref[...].astype(jnp.float32)
    out_ref[...] = rows.astype(jnp.bfloat16)


def unpack_call(expand, around, beside, *base, first=0):
    return pl.pallas_call(
        functools.partial(unpack_kernel, first),
        out_shape=bf16(expand.shape[0], around.shape[1]),
        compiler_params=params(),
        cost_estimate=pl.CostEstimate(flops=2**34, bytes_accessed=2**25, transcendentals=0),
        name="unpack",
    )(expand, around, beside, *base)


def combine_kernel(base_ref, core_ref, most_ref, out_most_ref, *out_refs):
    cap = out_refs[0].shape[0]
    out_most_ref[...] = most_ref[...]
    for d, out in enumerate(out_refs):
        here = slice(d * cap, (d + 1) * cap)
        out[...] = base_ref[here] + core_ref[here]


def combine_call(base, core, most, servers):
    total, width = base.shape
    most, *parts = pl.pallas_call(
        combine_kernel,
        out_shape=[jax.ShapeDtypeStruct(most.shape, most.dtype)]
        + [bf16(total // servers, width)] * servers,
        compiler_params=params(),
        cost_estimate=pl.CostEstimate(
            flops=total * width, bytes_accessed=6 * total * width, transcendentals=0
        ),
        name="combine",
    )(base, core, most)
    return most, parts


def fill(buffer, parts):
    cap = parts[0].shape[0]
    for d, ref in enumerate(reversed(parts)):
        buffer[d * cap : (d + 1) * cap] = ref[...]


def weigh(x_ref, buffer, mask):
    rows, width = x_ref.shape
    across = (((1,), (1,)), ((), ()))
    gram = lax.dot_general(buffer, buffer, across, preferred_element_type=jnp.float32)
    high = gram.astype(jnp.bfloat16)
    low = (gram - high.astype(jnp.float32)).astype(jnp.bfloat16)
    dots = lax.dot_general(x_ref[...], buffer, across, preferred_element_type=jnp.float32)
    positive = jnp.maximum(dots * (1.0 / width), 0.0)
    weights = (positive * positive * positive).astype(jnp.bfloat16) * mask
    crossed = jnp.dot(weights, high, preferred_element_type=jnp.float32)
    crossed += jnp.dot(weights, low, preferred_element_type=jnp.float32)
    squares = weights.astype(jnp.float32) * (2.0 * dots + crossed)
    own = []
    for first in range(0, rows, CHUNK):
        chunk = jnp.zeros((CHUNK, LANES), jnp.float32)
        for start in range(0, width, LANES):
            tile = x_ref[first : first + CHUNK, start : start + LANES].astype(jnp.float32)
            chunk += tile * tile
        own.append(jnp.sum(chunk, axis=1, keepdims=True))
    total = jnp.concatenate(own, axis=0) + jnp.sum(squares, axis=1, keepdims=True)
    return weights, lax.rsqrt(total * (1.0 / width) + 1e-06)


def add_up(x, weights, scale, buffer):
    mixed = x.astype(jnp.float32) + jnp.dot(weights, buffer, preferred_element_type=jnp.float32)
    return (mixed * scale).astype(jnp.bfloat16)


def last_kernel(servers, x_ref, mask_ref, *rest):
    parts, rest = rest[:servers], rest[servers:]
    out_ref, buffer, whole, sems = rest
    fill(buffer, parts)
    weights, scale = weigh(x_ref, buffer[...], mask_ref[...])
    copies = []
    for i, start in enumerate(range(0, x_ref.shape[1], TILE)):
        here = slice(start, start + TILE)
        whole[:, here] = add_up(x_ref[:, here], weights, scale, buffer[:, here])
        tile = pl.ds(start, TILE)
        copies.append(pltpu.make_async_copy(whole.at[:, tile], out_ref.at[:, tile], sems.at[i]))
        copies[-1].start()
    for copy in copies:
        copy.wait()


def last_call(x, mask, parts):
    rows, width = x.shape
    total, servers = mask.shape[1], len(parts)
    return pl.pallas_call(
        functools.partial(last_kernel, servers),
        out_specs=pl.BlockSpec(memory_space=pltpu.HBM),
        out_shape=pltpu.HBM((rows, width), jnp.bfloat16),
        scratch_shapes=[
            pltpu.VMEM((total, width), jnp.bfloat16),
            pltpu.VMEM((rows, width), jnp.bfloat16),
            pltpu.SemaphoreType.DMA((width // TILE,)),
        ],
        compiler_params=params(),
        cost_estimate=pl.CostEstimate(
            flops=4 * total * rows * width, bytes_accessed=4 * rows * width, transcendentals=rows
        ),
        name="mix",
    )(x, mask, *reversed(parts))


def round_kernel(servers, x_ref, mask_ref, pack_ref, *rest):
    parts, rest = rest[:servers], rest[servers:]
    *most_refs, out_ref, far_ref, most_ref, buffer = rest
    most_ref[...] = functools.reduce(jnp.maximum, [ref[...] for ref in most_refs])
    fill(buffer, parts)
    weights, scale = weigh(x_ref, buffer[...], mask_ref[...])
    for start in range(0, x_ref.shape[1], TILE):
        here = slice(start, start + TILE)
        out_ref[:, here] = add_up(x_ref[:, here], weights, scale, buffer[:, here])
    serve(out_ref[...], pack_ref, far_ref)


def round_call(x, mask, pack, parts, mosts, sent):
    rows, width = x.shape
    total, servers = mask.shape[1], len(parts)
    return pl.pallas_call(
        functools.partial(round_kernel, servers),
        out_shape=[
            bf16(rows, width),
            bf16(sent, width),
            jax.ShapeDtypeStruct((8, LANES), jnp.int32),
        ],
        scratch_shapes=[pltpu.VMEM((total, width), jnp.bfloat16)],
        compiler_params=params(),
        cost_estimate=pl.CostEstimate(
            flops=5 * total * rows * width, bytes_accessed=6 * rows * width, transcendentals=rows
        ),
        name="mix_and_pack",
    )(x, mask, pack, *reversed(parts), *mosts)


def local(descriptors, request, pick):
    wanted = request[0, 0]
    rows = descriptors.shape[2]
    servers, cap = wanted.shape
    total = servers * cap
    groups = lax.axis_size("rep")
    sent = total * FAR_SHARE[0] // FAR_SHARE[1]
    within = [(g, g ^ 1) for g in range(groups)]
    beyond = [(g, (g + 2 * (g % 2) - 1 + groups) % groups) for g in range(groups)]
    ends = [(g, to) for g, to in beyond if abs(g - to) > 1]
    beside = [(g, to) for g, to in beyond if abs(g - to) == 1]

    def turn(value, d):
        return lax.ppermute(value, "clus", [(c, c ^ d) for c in range(servers)])

    def shift(value, by):
        return lax.ppermute(value, "rep", [(g, (g + by) % groups) for g in range(groups)])

    def across(value):
        return lax.ppermute(value, "rep", beyond)

    def around_ends(value):
        return lax.ppermute(value, "rep", ends)

    def to_side(value):
        return lax.ppermute(value, "rep", beside)

    def inside(value):
        return lax.ppermute(value, "rep", within)

    def exchange(base, core, most):
        most, parts = combine_call(base, core, most, servers)
        return most, turned(parts)

    def turned(parts):
        got = {d: turn(parts[d], d) for d in reversed(range(1, servers))}
        return [parts[0]] + [got[d] for d in range(1, servers)]

    def next_parts(x, far, select, expand, most):
        around = around_ends(far)
        core, own, far = again_call(x, select, far)
        base = unpack_call(expand, around, to_side(far), own)
        return exchange(base, inside(core), most)

    def in_full(raw, x, rest, mask, pack, select, expand, most, first, last):
        late = unpack_call(expand, around_ends(rest), to_side(rest), first=sent).reshape(servers, cap, -1)
        parts = [a + b for a, b in zip(first, turned(list(late)))]
        x = raw
        for _ in range(ROUNDS - 1):
            x, far, most = round_call(x, mask, pack, parts, [most], total)
            most, parts = next_parts(x, far, select, expand, most)
        return last_call(x, mask, parts)

    def as_sent(raw, x, rest, mask, pack, select, expand, most, first, last):
        return last_call(x, mask, last)

    asked = {d: turn(wanted, d) for d in reversed(range(1, servers))}
    mask, held = mask_call(pick.transpose(0, 3, 1, 2)[0], wanted)
    mine = list_call([held] + [asked[d] for d in range(1, servers)], rows)
    beyond_list, within_list = across(mine), inside(mine)
    x = normalize_call(descriptors[0, 0])
    pack, most, far = far_call(x, mine, within_list, beyond_list, sent)
    around = around_ends(far)
    select, expand, core, own, rest, far = near_call(x, pack, mine, within_list, far)
    base = unpack_call(expand, around, to_side(far), own)
    most, first = exchange(base, inside(core), most)
    mosts = [most]
    reach = 1
    while 2 * reach + 1 < groups:
        by = 2 * reach + 1
        most = functools.reduce(jnp.maximum, mosts)
        mosts = [most, shift(most, by), shift(most, -by)]
        reach += by
    mixed, parts = x, first
    for _ in range(ROUNDS - 1):
        mixed, far, most = round_call(mixed, mask, pack, parts, mosts, sent)
        most, parts = next_parts(mixed, far, select, expand, most)
        mosts = [most]
    state = x, mixed, rest, mask, pack, select, expand, most, first, parts
    return lax.cond(most[0, 0] > sent, in_full, as_sent, *state)[None, None]


def solution(mesh):
    return jax.shard_map(
        local,
        mesh=mesh,
        in_specs=(
            P("rep", "clus", None, None),
            P("rep", "clus", None, None),
            P("rep", "clus", None, None),
        ),
        out_specs=P("rep", "clus", None, None),
        check_vma=False,
    )
```

```python
import functools

import jax
import jax.numpy as jnp
from jax import lax
from jax.experimental import pallas as pl
from jax.experimental.pallas import tpu as pltpu
from jax.sharding import PartitionSpec as P

LANES = 128
BLOCK = 128
LAST_BLOCK = 256
CHUNK = 32
BOTH_LAST = (((1,), (1,)), ((), ()))


FAR_SHARE = 3, 8


def params(mib=32):
    return pltpu.CompilerParams(vmem_limit_bytes=mib * 1024 * 1024)


def bf16(*shape):
    return jax.ShapeDtypeStruct(shape, jnp.bfloat16)


def normalize(value):
    return value * lax.rsqrt(jnp.mean(value * value, axis=-1, keepdims=True) + 1e-06)


def normalize_kernel(x_hbm, out_ref, raw, sems):
    copies = []
    starts = range(0, raw.shape[0], BLOCK)
    for i, start in enumerate(starts):
        here = pl.ds(start, BLOCK)
        copies.append(pltpu.make_async_copy(x_hbm.at[here], raw.at[here], sems.at[i]))
        copies[-1].start()
    for copy, start in zip(copies, starts):
        copy.wait()
        here = pl.ds(start, BLOCK)
        out_ref[here] = normalize(raw[here].astype(jnp.float32)).astype(jnp.bfloat16)


def normalize_call(descriptors):
    rows, width = descriptors.shape
    return pl.pallas_call(
        normalize_kernel,
        in_specs=[pl.BlockSpec(memory_space=pl.ANY)],
        out_shape=bf16(rows, width),
        scratch_shapes=[
            pltpu.VMEM((rows, width), jnp.bfloat16),
            pltpu.SemaphoreType.DMA((rows // BLOCK,)),
        ],
        compiler_params=params(56),
        cost_estimate=pl.CostEstimate(
            flops=6 * rows * width, bytes_accessed=4 * rows * width, transcendentals=rows
        ),
        name="normalize",
    )(descriptors)


def mask_kernel(slot_cap, pick_hbm, wanted_hbm, mask_ref, wanted_ref, pick, sems):
    copies = [
        pltpu.make_async_copy(pick_hbm, pick, sems.at[0]),
        pltpu.make_async_copy(wanted_hbm, wanted_ref, sems.at[1]),
    ]
    for copy in copies:
        copy.start()
    shape = mask_ref.shape[1], mask_ref.shape[0]
    slot = lax.broadcasted_iota(jnp.int32, shape, 0)
    slot = slot ^ (lax.axis_index("clus") * slot_cap)
    chosen = jnp.zeros(shape, jnp.float32)
    copies[0].wait()
    for k in range(pick.shape[0]):
        chosen = jnp.where(pick[k] == slot, 1.0, chosen)
    mask_ref[...] = chosen.T.astype(jnp.bfloat16)
    copies[1].wait()


def mask_call(slots, wanted):
    count, _, rows = slots.shape
    total = wanted.size
    return pl.pallas_call(
        functools.partial(mask_kernel, wanted.shape[1]),
        in_specs=[pl.BlockSpec(memory_space=pl.ANY)] * 2,
        out_shape=[bf16(rows, total), pltpu.VMEM(wanted.shape, jnp.int32)],
        scratch_shapes=[pltpu.VMEM(slots.shape, jnp.int32), pltpu.SemaphoreType.DMA((2,))],
        compiler_params=params(56),
        cost_estimate=pl.CostEstimate(
            flops=2 * count * rows * total, bytes_accessed=2 * rows * total, transcendentals=0
        ),
        name="mask",
    )(slots, wanted)


def list_kernel(rows, *refs):
    parts, out_ref = refs[:-1], refs[-1]
    column = lax.axis_index("clus")
    third = lax.axis_index("rep") % 2 * 2
    total = out_ref.shape[1]
    mine = jnp.concatenate([ref[pl.ds(column, 1), :] for ref in parts], axis=1)
    most = jnp.zeros((1, 1), jnp.float32)
    lane = lax.broadcasted_iota(jnp.int32, (1, total), 1)
    earlier = lax.broadcasted_iota(jnp.int32, (total, total), 0) < lax.broadcasted_iota(
        jnp.int32, (total, total), 1
    )
    for server in range(len(parts)):
        asked = jnp.concatenate([ref[server : server + 1, :] for ref in parts], axis=1)
        far = (asked >= third * rows) & (asked < (third + 1) * rows)
        key = jnp.where(far, asked, -1 - lane).astype(jnp.float32)
        column_key = jnp.broadcast_to(key, (total, total)).T
        again = jnp.where((column_key == key) & earlier, 1.0, 0.0)
        again = jnp.max(again, axis=0, keepdims=True)
        first = jnp.where(far, 1.0 - again, 0.0)
        most = jnp.maximum(most, jnp.sum(first, axis=1, keepdims=True))
    place = lax.broadcasted_iota(jnp.int32, out_ref.shape, 0)
    out_ref[...] = jnp.where(
        place == 1, jnp.broadcast_to(most.astype(jnp.int32), out_ref.shape), mine
    )


def list_call(parts, rows):
    total = parts[0].size
    return pl.pallas_call(
        functools.partial(list_kernel, rows),
        out_shape=jax.ShapeDtypeStruct((8, total), jnp.int32),
        compiler_params=params(),
        cost_estimate=pl.CostEstimate(
            flops=6 * total * total, bytes_accessed=8 * total, transcendentals=0
        ),
        name="list",
    )(*parts)


def serve(x, select_ref, *out_refs):
    count = sum(out.shape[0] for out in out_refs)
    fetched = jnp.dot(select_ref[:count], x, preferred_element_type=jnp.float32)
    start = 0
    for out in out_refs:
        stop = start + out.shape[0]
        out[...] = fetched[start:stop].astype(jnp.bfloat16)
        start = stop


def one_hot(asked, third, rows):
    total = asked.shape[1]
    column = jnp.broadcast_to(asked, (LANES, total)).T - third * rows
    tiles = []
    for t in range(rows // LANES):
        lane = lax.broadcasted_iota(jnp.int32, (total, LANES), 1) + t * LANES
        tiles.append(jnp.where(column == lane, 1.0, 0.0))
    return jnp.concatenate(tiles, axis=1)


def packing(selected, rows):
    total = selected.shape[0]
    needed = jnp.broadcast_to(jnp.max(selected, axis=0, keepdims=True), (8, rows))
    before = lax.broadcasted_iota(jnp.int32, (rows, rows), 0) < lax.broadcasted_iota(
        jnp.int32, (rows, rows), 1
    )
    rank = jnp.dot(
        needed.astype(jnp.bfloat16),
        jnp.where(before, 1.0, 0.0).astype(jnp.bfloat16),
        preferred_element_type=jnp.float32,
    )
    rank = jnp.where(needed > 0, rank, -1.0).astype(jnp.int32)
    place = lax.broadcasted_iota(jnp.int32, (total, rows), 0)
    return jnp.where(place == rank[0:1], 1.0, 0.0).astype(jnp.bfloat16)


def far_kernel(x_ref, mine_ref, within_ref, beyond_ref, pack_ref, most_ref, far_ref):
    rows = x_ref.shape[0]
    most = jnp.maximum(mine_ref[...], jnp.maximum(within_ref[...], beyond_ref[...]))
    most_ref[...] = jnp.broadcast_to(most[1:2, :LANES], most_ref.shape)
    third = 2 - lax.axis_index("rep") % 2 * 2
    pack_ref[...] = packing(one_hot(beyond_ref[0:1], third, rows), rows)
    serve(x_ref[...], pack_ref, far_ref)


def far_call(x, mine, within, beyond, sent):
    rows, width = x.shape
    total = mine.shape[1]
    return pl.pallas_call(
        far_kernel,
        out_shape=[
            bf16(total, rows),
            jax.ShapeDtypeStruct((8, LANES), jnp.int32),
            bf16(sent, width),
        ],
        compiler_params=params(),
        cost_estimate=pl.CostEstimate(
            flops=2 * rows * rows * LANES, bytes_accessed=2 * rows * width, transcendentals=0
        ),
        name="pack_far",
    )(x, mine, within, beyond)


def near_kernel(x_ref, pack_ref, mask_ref, mine_ref, within_ref, *out_refs):
    expand_ref, core_ref, own_ref, rest_ref, near_mask_ref, far_mask_ref, select_ref = out_refs
    rows, total = x_ref.shape[0], mine_ref.shape[1]
    third = lax.axis_index("rep") % 2 * 2
    own = mine_ref[0:1]
    select_ref[:total] = one_hot(within_ref[0:1], third, rows).astype(jnp.bfloat16)
    select_ref[total:] = one_hot(own, 1, rows).astype(jnp.bfloat16)
    x = x_ref[...]
    serve(x, select_ref, core_ref, own_ref)
    rest = total - rest_ref.shape[0]
    serve(x, pack_ref.at[rest:], rest_ref)
    from_far = one_hot(own, third, rows)
    mask = mask_ref[...]
    serve(mask, select_ref, near_mask_ref)
    serve(mask, pack_ref, far_mask_ref)
    expand_ref[...] = lax.dot_general(
        from_far.astype(jnp.bfloat16),
        packing(from_far, rows),
        (((1,), (1,)), ((), ())),
        preferred_element_type=jnp.float32,
    ).astype(jnp.bfloat16)


def near_call(x, pack, mask, mine, within, sent):
    rows, width = x.shape
    total = mine.shape[1]
    return pl.pallas_call(
        near_kernel,
        out_shape=[
            bf16(total, total),
            bf16(total, width),
            bf16(total, width),
            bf16(total - sent, width),
            bf16(2 * total, total),
            bf16(total, total),
        ],
        scratch_shapes=[pltpu.VMEM((2 * total, rows), jnp.bfloat16)],
        compiler_params=params(),
        cost_estimate=pl.CostEstimate(
            flops=6 * total * rows * width, bytes_accessed=4 * rows * width, transcendentals=0
        ),
        name="serve_near",
    )(x, pack, mask, mine, within)


def unpack_kernel(first, expand_ref, far_ref, *refs):
    out_ref, sent = refs[-1], far_ref.shape[0]
    rows = jnp.dot(
        expand_ref[:, first : first + sent], far_ref[...], preferred_element_type=jnp.float32
    )
    for base_ref in refs[:-1]:
        rows += base_ref[...].astype(jnp.float32)
    out_ref[...] = rows.astype(jnp.bfloat16)


def unpack_call(expand, far, *base, first=0):
    return pl.pallas_call(
        functools.partial(unpack_kernel, first),
        out_shape=bf16(expand.shape[0], far.shape[1]),
        compiler_params=params(),
        cost_estimate=pl.CostEstimate(flops=2**34, bytes_accessed=2**25, transcendentals=0),
        name="unpack",
    )(expand, far, *base)


def combine_kernel(base_ref, core_ref, most_ref, out_most_ref, *out_refs):
    cap = out_refs[0].shape[0]
    out_most_ref[...] = most_ref[...]
    for d, out in enumerate(out_refs):
        here = slice(d * cap, (d + 1) * cap)
        out[...] = base_ref[here] + core_ref[here]


def combine_call(base, core, most, servers):
    total, width = base.shape
    most, *parts = pl.pallas_call(
        combine_kernel,
        out_shape=[jax.ShapeDtypeStruct(most.shape, jnp.int32)]
        + [bf16(total // servers, width)] * servers,
        compiler_params=params(),
        cost_estimate=pl.CostEstimate(
            flops=total * width, bytes_accessed=6 * total * width, transcendentals=0
        ),
        name="combine",
    )(base, core, most)
    return most, parts


def fill(buffer, parts):
    cap = parts[0].shape[0]
    for d, ref in enumerate(reversed(parts)):
        buffer[d * cap : (d + 1) * cap] = ref[...]


def weigh(x, buffer, mask):
    dots = lax.dot_general(x, buffer, BOTH_LAST, preferred_element_type=jnp.float32)
    positive = jnp.maximum(dots * (1.0 / x.shape[1]), 0.0)
    return (positive * positive * positive).astype(jnp.bfloat16) * mask, dots


def mix(x, weights, buffer):
    mixed = x.astype(jnp.float32) + jnp.dot(weights, buffer, preferred_element_type=jnp.float32)
    return normalize(mixed).astype(jnp.bfloat16)


def far_mix_kernel(servers, x_ref, mask_ref, *rest):
    parts, rest = rest[:servers], rest[servers:]
    *most_refs, out_ref, most_ref, buffer = rest
    most_ref[...] = functools.reduce(jnp.maximum, [ref[...] for ref in most_refs])
    fill(buffer, parts)
    weights, _ = weigh(x_ref[...], buffer[...], mask_ref[: x_ref.shape[0]])
    out_ref[...] = mix(x_ref[...], weights, buffer[...])


def far_mix_call(x, mask, parts, mosts):
    rows, width = x.shape
    total, servers = mask.shape[1], len(parts)
    return pl.pallas_call(
        functools.partial(far_mix_kernel, servers),
        out_shape=[bf16(rows, width), jax.ShapeDtypeStruct(mosts[0].shape, jnp.int32)],
        scratch_shapes=[pltpu.VMEM((total, width), jnp.bfloat16)],
        compiler_params=params(),
        cost_estimate=pl.CostEstimate(
            flops=4 * total * rows * width, bytes_accessed=4 * rows * width, transcendentals=rows
        ),
        name="mix_far",
    )(x, mask, *reversed(parts), *mosts)


def near_mix_kernel(servers, core_ref, own_ref, mask_ref, *rest):
    parts, (new_core_ref, new_own_ref, buffer) = rest[:servers], rest[servers:]
    fill(buffer, parts)
    total = core_ref.shape[0]
    for i, (x_ref, out_ref) in enumerate([(core_ref, new_core_ref), (own_ref, new_own_ref)]):
        mask = mask_ref[i * total : (i + 1) * total]
        weights, _ = weigh(x_ref[...], buffer[...], mask)
        out_ref[...] = mix(x_ref[...], weights, buffer[...])


def near_mix_call(core, own, mask, parts):
    total, width = core.shape
    servers = len(parts)
    return pl.pallas_call(
        functools.partial(near_mix_kernel, servers),
        out_shape=[bf16(total, width)] * 2,
        scratch_shapes=[pltpu.VMEM((total, width), jnp.bfloat16)],
        compiler_params=params(),
        cost_estimate=pl.CostEstimate(
            flops=8 * total * total * width, bytes_accessed=8 * total * width, transcendentals=0
        ),
        name="mix_near",
    )(core, own, mask, *reversed(parts))


def squared(x):
    x = x.astype(jnp.float32)
    return sum(x[:, i : i + LANES] * x[:, i : i + LANES] for i in range(0, x.shape[1], LANES))


def whole_kernel(servers, x_ref, mask_ref, *rest):
    parts, (out_ref, squares_ref, buffer, weights) = rest[:servers], rest[servers:]
    fill(buffer, parts)
    weights[...], _ = weigh(x_ref[...], buffer[...], mask_ref[...])
    for start in range(0, x_ref.shape[0], BLOCK):
        here = slice(start, start + BLOCK)
        out_ref[here] = mix(x_ref[here], weights[here], buffer[...])
    for start in range(0, x_ref.shape[0], CHUNK):
        here = slice(start, start + CHUNK)
        squares_ref[here] = squared(out_ref[here])


def whole_call(x, mask, parts):
    rows, width = x.shape
    total, servers = mask.shape[1], len(parts)
    return pl.pallas_call(
        functools.partial(whole_kernel, servers),
        out_shape=[bf16(rows, width), jax.ShapeDtypeStruct((rows, LANES), jnp.float32)],
        scratch_shapes=[
            pltpu.VMEM((total, width), jnp.bfloat16),
            pltpu.VMEM((rows, total), jnp.bfloat16),
        ],
        compiler_params=params(),
        cost_estimate=pl.CostEstimate(
            flops=4 * total * rows * width, bytes_accessed=4 * rows * width, transcendentals=rows
        ),
        name="mix_whole",
    )(x, mask, *reversed(parts))


def last_kernel(servers, x_ref, mask_ref, squares_ref, *rest):
    parts, rest = rest[:servers], rest[servers:]
    out_ref, buffer, whole, sems = rest
    rows, width = x_ref.shape
    fill(buffer, parts)
    b = buffer[...]
    gram = lax.dot_general(b, b, BOTH_LAST, preferred_element_type=jnp.float32)
    high = gram.astype(jnp.bfloat16)
    low = (gram - high.astype(jnp.float32)).astype(jnp.bfloat16)
    weights, dots = weigh(x_ref[...], b, mask_ref[...])
    crossed = jnp.dot(weights, high, preferred_element_type=jnp.float32)
    crossed += jnp.dot(weights, low, preferred_element_type=jnp.float32)
    added = jnp.sum(weights.astype(jnp.float32) * (2.0 * dots + crossed), axis=1, keepdims=True)
    square = jnp.sum(squares_ref[...], axis=1, keepdims=True) + added
    scale = lax.rsqrt(square * (1.0 / width) + 1e-06)
    copies = []
    for i, start in enumerate(range(0, rows, LAST_BLOCK)):
        here = slice(start, start + LAST_BLOCK)
        mixed = jnp.dot(weights[here], b, preferred_element_type=jnp.float32)
        mixed += x_ref[here].astype(jnp.float32)
        whole[here] = (mixed * scale[here]).astype(jnp.bfloat16)
        block = pl.ds(start, LAST_BLOCK)
        copies.append(pltpu.make_async_copy(whole.at[block], out_ref.at[block], sems.at[i]))
        copies[-1].start()
    for copy in copies:
        copy.wait()


def last_call(x, mask, squares, parts):
    rows, width = x.shape
    total, servers = mask.shape[1], len(parts)
    return pl.pallas_call(
        functools.partial(last_kernel, servers),
        out_specs=pl.BlockSpec(memory_space=pltpu.HBM),
        out_shape=pltpu.HBM((rows, width), jnp.bfloat16),
        scratch_shapes=[
            pltpu.VMEM((total, width), jnp.bfloat16),
            pltpu.VMEM((rows, width), jnp.bfloat16),
            pltpu.SemaphoreType.DMA((rows // LAST_BLOCK,)),
        ],
        compiler_params=params(),
        cost_estimate=pl.CostEstimate(
            flops=4 * total * rows * width, bytes_accessed=4 * rows * width, transcendentals=rows
        ),
        name="mix",
    )(x, mask, squares, *reversed(parts))


def local(descriptors, request, pick):
    wanted = request[0, 0]
    rows = descriptors.shape[2]
    servers, cap = wanted.shape
    total = servers * cap
    groups = lax.axis_size("rep")
    sent = total * FAR_SHARE[0] // FAR_SHARE[1]
    within = [(g, g ^ 1) for g in range(groups)]
    beyond = [(g, (g + 2 * (g % 2) - 1 + groups) % groups) for g in range(groups)]

    def turn(value, d):
        return lax.ppermute(value, "clus", [(c, c ^ d) for c in range(servers)])

    def shift(value, by):
        return lax.ppermute(value, "rep", [(g, (g + by) % groups) for g in range(groups)])

    def across(value):
        return lax.ppermute(value, "rep", beyond)

    def inside(value):
        return lax.ppermute(value, "rep", within)

    def turned(parts):
        got = {d: turn(parts[d], d) for d in reversed(range(1, servers))}
        return [parts[0]] + [got[d] for d in range(1, servers)]

    def exchange(expand, far, core, own, most):
        base = unpack_call(expand, across(far), own)
        most, parts = combine_call(base, inside(core), most, servers)
        return most, turned(parts)

    def next_parts(served, masks, expand, parts, mosts):
        far, core, own = served
        far, most = far_mix_call(far, masks[1], parts, mosts)
        core, own = near_mix_call(core, own, masks[2], parts)
        return exchange(expand, far, core, own, most)

    def in_full(x, y, squares, masks, served, rest, expand, most, first, last):
        late = unpack_call(expand, across(rest), first=sent).reshape(servers, cap, -1)
        first = [a + b for a, b in zip(first, turned(list(late)))]
        served = jnp.concatenate([served[0], rest], axis=0), *served[1:]
        _, last = next_parts(served, masks, expand, first, [most])
        y, squares = whole_call(x, masks[0], first)
        return last_call(y, masks[0], squares, last)

    def as_sent(x, y, squares, masks, served, rest, expand, most, first, last):
        return last_call(y, masks[0], squares, last)

    asked = {d: turn(wanted, d) for d in reversed(range(1, servers))}
    mask, held = mask_call(pick.transpose(0, 3, 1, 2)[0], wanted)
    mine = list_call([held] + [asked[d] for d in range(1, servers)], rows)
    beyond_list, within_list = across(mine), inside(mine)
    x = normalize_call(descriptors[0, 0])
    pack, most, far = far_call(x, mine, within_list, beyond_list, sent)
    expand, core, own, rest, near_mask, far_mask = near_call(
        x, pack, mask, mine, within_list, sent
    )
    most, first = exchange(expand, far, core, own, most)
    mosts = [most]
    reach = 1
    while 2 * reach + 1 < groups:
        by = 2 * reach + 1
        most = functools.reduce(jnp.maximum, mosts)
        mosts = [most, shift(most, by), shift(most, -by)]
        reach += by
    masks, served = (mask, far_mask, near_mask), (far, core, own)
    most, last = next_parts(served, masks, expand, first, mosts)
    y, squares = whole_call(x, mask, first)
    state = x, y, squares, masks, served, rest, expand, most, first, last
    return lax.cond(most[0, 0] > sent, in_full, as_sent, *state)[None, None]


def solution(mesh):
    return jax.shard_map(
        local,
        mesh=mesh,
        in_specs=(
            P("rep", "clus", None, None),
            P("rep", "clus", None, None),
            P("rep", "clus", None, None),
        ),
        out_specs=P("rep", "clus", None, None),
        check_vma=False,
    )
```

```python
import functools

import jax
import jax.numpy as jnp
from jax import lax
from jax.experimental import pallas as pl
from jax.experimental.pallas import tpu as pltpu
from jax.sharding import PartitionSpec as P

LANES = 128
BLOCK = 128
FIRST_SHARE = 3, 8
BOTH_LAST = (((1,), (1,)), ((), ()))


def bf16(*shape):
    return jax.ShapeDtypeStruct(shape, jnp.bfloat16)


def int32(*shape):
    return jax.ShapeDtypeStruct(shape, jnp.int32)


def kernel_call(name, kernel, outs, *args, flops, moved=0, scratch=(), mib=32, **specs):
    return pl.pallas_call(
        kernel,
        out_shape=outs,
        scratch_shapes=scratch,
        compiler_params=pltpu.CompilerParams(vmem_limit_bytes=mib * 1024 * 1024),
        cost_estimate=pl.CostEstimate(flops=flops, bytes_accessed=moved, transcendentals=0),
        name=name,
        **specs,
    )(*args)


def normalize(value):
    return value * lax.rsqrt(jnp.mean(value * value, axis=-1, keepdims=True) + 1e-06)


def normalize_kernel(x_hbm, out_ref, raw, sems):
    copies = []
    starts = range(0, raw.shape[0], BLOCK)
    for i, start in enumerate(starts):
        here = pl.ds(start, BLOCK)
        copies.append(pltpu.make_async_copy(x_hbm.at[here], raw.at[here], sems.at[i]))
        copies[-1].start()
    for copy, start in zip(copies, starts):
        copy.wait()
        here = pl.ds(start, BLOCK)
        out_ref[here] = normalize(raw[here].astype(jnp.float32)).astype(jnp.bfloat16)


def normalize_call(descriptors):
    rows, width = descriptors.shape
    return kernel_call(
        "normalize",
        normalize_kernel,
        bf16(rows, width),
        descriptors,
        flops=6 * rows * width,
        moved=4 * rows * width,
        scratch=[
            pltpu.VMEM((rows, width), jnp.bfloat16),
            pltpu.SemaphoreType.DMA((rows // BLOCK,)),
        ],
        mib=56,
        in_specs=[pl.BlockSpec(memory_space=pl.ANY)],
    )


def mask_kernel(slot_cap, pick_hbm, wanted_hbm, mask_ref, wanted_ref, pick, sems):
    copies = [
        pltpu.make_async_copy(pick_hbm, pick, sems.at[0]),
        pltpu.make_async_copy(wanted_hbm, wanted_ref, sems.at[1]),
    ]
    for copy in copies:
        copy.start()
    shape = mask_ref.shape[1], mask_ref.shape[0]
    slot = lax.broadcasted_iota(jnp.int32, shape, 0)
    slot = slot ^ (lax.axis_index("clus") * slot_cap)
    chosen = jnp.zeros(shape, jnp.float32)
    copies[0].wait()
    for k in range(pick.shape[0]):
        chosen = jnp.where(pick[k] == slot, 1.0, chosen)
    mask_ref[...] = chosen.T.astype(jnp.bfloat16)
    copies[1].wait()


def mask_call(slots, wanted):
    count, _, rows = slots.shape
    total = wanted.size
    return kernel_call(
        "mask",
        functools.partial(mask_kernel, wanted.shape[1]),
        [bf16(rows, total), pltpu.VMEM(wanted.shape, jnp.int32)],
        slots,
        wanted,
        flops=2 * count * rows * total,
        moved=2 * rows * total,
        scratch=[pltpu.VMEM(slots.shape, jnp.int32), pltpu.SemaphoreType.DMA((2,))],
        mib=56,
        in_specs=[pl.BlockSpec(memory_space=pl.ANY)] * 2,
    )


def list_kernel(rows, *refs):
    parts, refs = refs[:-5], refs[-5:]
    own_ref, far_ref, core_ref, expand_far_ref, expand_core_ref = refs
    total = own_ref.shape[1]
    lane = lax.broadcasted_iota(jnp.int32, (total, total), 1)
    sublane = lax.broadcasted_iota(jnp.int32, (total, total), 0)
    odd = lax.axis_index("rep") % 2
    lows = [(2 * odd * rows).astype(jnp.float32), ((2 - 2 * odd) * rows).astype(jnp.float32)]

    def inside(value, low):
        return (value >= low) & (value < low + rows)

    def asked(server):
        row = jnp.concatenate([ref[server, :] for ref in parts], axis=1).astype(jnp.float32)
        column = jnp.broadcast_to(row, (total, total)).T
        again = jnp.where((column == row) & (sublane < lane), 1.0, 0.0)
        return row, column, 1.0 - jnp.max(again, axis=0, keepdims=True)

    most = jnp.zeros((1, 1), jnp.float32)
    for server in range(len(parts)):
        row, _, first = asked(slice(server, server + 1))
        for low in lows:
            count = jnp.sum(jnp.where(inside(row, low), first, 0.0), axis=1, keepdims=True)
            most = jnp.maximum(most, count)
    row, column, first = asked(pl.ds(lax.axis_index("clus"), 1))
    own_ref[...] = jnp.broadcast_to(row - rows, own_ref.shape).astype(jnp.int32)
    place = lax.broadcasted_iota(jnp.int32, own_ref.shape, 0)
    for low, out_ref, expand_ref in zip(lows, (far_ref, core_ref), (expand_far_ref, expand_core_ref)):
        counted = jnp.where(inside(row, low), first, 0.0)
        rank = jnp.sum(jnp.where(row < column, counted, 0.0), axis=1, keepdims=True)
        here = inside(column, low) & (rank.astype(jnp.int32) == lane)
        expand_ref[...] = jnp.where(here, 1.0, 0.0).astype(jnp.bfloat16)
        packed = jnp.max(jnp.where(here, column - low, -1.0), axis=0, keepdims=True)
        out_ref[...] = jnp.where(place == 1, most, packed).astype(jnp.int32)


def list_call(parts, rows):
    total = parts[0].size
    return kernel_call(
        "list",
        functools.partial(list_kernel, rows),
        [int32(8, total)] * 3 + [bf16(total, total)] * 2,
        *parts,
        flops=40 * total * total,
    )


def one_hot(numbers, rows):
    total = numbers.shape[1]
    column = jnp.broadcast_to(numbers.astype(jnp.float32), (LANES, total)).T.astype(jnp.int32)
    tiles = []
    for start in range(0, rows, LANES):
        lane = lax.broadcasted_iota(jnp.int32, (total, LANES), 1) + start
        tiles.append(jnp.where(column == lane, 1.0, 0.0).astype(jnp.bfloat16))
    return jnp.concatenate(tiles, axis=1)


def take(select, x):
    return jnp.dot(select, x, preferred_element_type=jnp.float32).astype(jnp.bfloat16)


def far_kernel(x_ref, beyond_ref, pack_ref, far_ref):
    pack_ref[...] = one_hot(beyond_ref[0:1], x_ref.shape[0])
    far_ref[...] = take(pack_ref[: far_ref.shape[0]], x_ref[...])


def far_call(x, beyond, sent):
    rows, width = x.shape
    total = beyond.shape[1]
    return kernel_call(
        "pack_far",
        far_kernel,
        [bf16(total, rows), bf16(sent, width)],
        x,
        beyond,
        flops=2 * rows * sent * width,
    )


def near_kernel(x_ref, mask_ref, pack_ref, own_list_ref, *refs):
    far_list_ref, beyond_ref, within_ref, *refs = refs
    core_ref, own_ref, near_ref, rest_far_ref, rest_core_ref, *refs = refs
    far_mask_ref, core_mask_ref, near_mask_ref, most_ref, select = refs
    total, sent = own_ref.shape[0], core_ref.shape[0]
    rows = x_ref.shape[0]
    select[:total] = one_hot(within_ref[0:1], rows)
    select[total:] = one_hot(own_list_ref[0:1], rows)
    fetched = take(select[...], x_ref[...])
    core_ref[...] = fetched[:sent]
    near_ref[:sent] = fetched[:sent]
    rest_core_ref[...] = fetched[sent:total]
    own_ref[...] = fetched[total:]
    near_ref[sent:] = fetched[total:]
    rest_far_ref[...] = take(pack_ref[sent:], x_ref[...])
    masks = take(select[...], mask_ref[...])
    core_mask_ref[...] = masks[:total]
    near_mask_ref[:sent] = masks[:sent]
    near_mask_ref[sent:] = masks[total:]
    far_mask_ref[...] = take(pack_ref[...], mask_ref[...])
    most = jnp.maximum(far_list_ref[...], jnp.maximum(beyond_ref[...], within_ref[...]))
    most_ref[...] = jnp.broadcast_to(most[1:2, :LANES], most_ref.shape)


def near_call(x, mask, pack, own_list, far_list, beyond, within, sent):
    rows, width = x.shape
    total = mask.shape[1]
    return kernel_call(
        "serve_near",
        near_kernel,
        [
            bf16(sent, width),
            bf16(total, width),
            bf16(sent + total, width),
            bf16(total - sent, width),
            bf16(total - sent, width),
            bf16(total, total),
            bf16(total, total),
            bf16(sent + total, total),
            int32(8, LANES),
        ],
        x,
        mask,
        pack,
        own_list,
        far_list,
        beyond,
        within,
        flops=6 * total * rows * width,
        scratch=[pltpu.VMEM((2 * total, rows), jnp.bfloat16)],
    )


def unpack_kernel(first, bases, expand_ref, far_ref, *refs):
    out_ref, sent = refs[-1], far_ref.shape[0]
    rows = jnp.dot(
        expand_ref[:, first : first + sent], far_ref[...], preferred_element_type=jnp.float32
    )
    for base_ref in refs[:bases]:
        rows += base_ref[...].astype(jnp.float32)
    out_ref[...] = rows.astype(jnp.bfloat16)


def unpack_call(expand, far, *base, first=0, after=()):
    in_vmem = [pl.BlockSpec(memory_space=pltpu.VMEM)] * (2 + len(base))
    return kernel_call(
        "unpack",
        functools.partial(unpack_kernel, first, len(base)),
        bf16(expand.shape[0], far.shape[1]),
        expand,
        far,
        *base,
        *after,
        flops=2**34,
        moved=2**25,
        in_specs=in_vmem + [pl.BlockSpec(memory_space=pl.ANY)] * len(after),
    )


def combine_kernel(expand_ref, core_ref, base_ref, most_ref, out_most_ref, *out_refs):
    out_most_ref[...] = most_ref[...]
    cap, sent = out_refs[0].shape[0], core_ref.shape[0]
    rows = jnp.dot(expand_ref[:, :sent], core_ref[...], preferred_element_type=jnp.float32)
    rows = (rows + base_ref[...].astype(jnp.float32)).astype(jnp.bfloat16)
    for d, out in enumerate(out_refs):
        out[...] = rows[d * cap : (d + 1) * cap]


def combine_call(expand, core, base, most, servers):
    total, width = base.shape
    most, *parts = kernel_call(
        "combine",
        combine_kernel,
        [int32(*most.shape)] + [bf16(total // servers, width)] * servers,
        expand,
        core,
        base,
        most,
        flops=2 * total * core.shape[0] * width,
    )
    return most, parts


def fill(buffer, parts):
    cap = parts[0].shape[0]
    for d, ref in enumerate(reversed(parts)):
        buffer[d * cap : (d + 1) * cap] = ref[...]


def weigh(x, buffer, mask):
    dots = lax.dot_general(x, buffer, BOTH_LAST, preferred_element_type=jnp.float32)
    positive = jnp.maximum(dots * (1.0 / x.shape[1]), 0.0)
    return (positive * positive * positive).astype(jnp.bfloat16) * mask


def mix(x, weights, buffer):
    mixed = x.astype(jnp.float32) + jnp.dot(weights, buffer, preferred_element_type=jnp.float32)
    return normalize(mixed).astype(jnp.bfloat16)


def far_mix_kernel(servers, x_ref, mask_ref, *rest):
    parts, rest = rest[:servers], rest[servers:]
    *most_refs, out_ref, most_ref, buffer = rest
    most_ref[...] = functools.reduce(jnp.maximum, [ref[...] for ref in most_refs])
    fill(buffer, parts)
    weights = weigh(x_ref[...], buffer[...], mask_ref[: x_ref.shape[0]])
    out_ref[...] = mix(x_ref[...], weights, buffer[...])


def far_mix_call(x, mask, parts, mosts):
    rows, width = x.shape
    total, servers = mask.shape[1], len(parts)
    return kernel_call(
        "mix_far",
        functools.partial(far_mix_kernel, servers),
        [bf16(rows, width), int32(*mosts[0].shape)],
        x,
        mask,
        *reversed(parts),
        *mosts,
        flops=4 * total * rows * width,
        scratch=[pltpu.VMEM((total, width), jnp.bfloat16)],
    )


def near_mix_kernel(servers, x_ref, mask_ref, *rest):
    parts, (core_ref, own_ref, buffer) = rest[:servers], rest[servers:]
    fill(buffer, parts)
    weights = weigh(x_ref[...], buffer[...], mask_ref[...])
    mixed = mix(x_ref[...], weights, buffer[...])
    core_ref[...] = mixed[: core_ref.shape[0]]
    own_ref[...] = mixed[core_ref.shape[0] :]


def near_mix_call(x, mask, parts):
    rows, width = x.shape
    total, servers = mask.shape[1], len(parts)
    return kernel_call(
        "mix_near",
        functools.partial(near_mix_kernel, servers),
        [bf16(rows - total, width), bf16(total, width)],
        x,
        mask,
        *reversed(parts),
        flops=4 * total * rows * width,
        scratch=[pltpu.VMEM((total, width), jnp.bfloat16)],
    )


def whole_kernel(servers, x_ref, mask_ref, *rest):
    parts, (out_ref, buffer, weights) = rest[:servers], rest[servers:]
    fill(buffer, parts)
    weights[...] = weigh(x_ref[...], buffer[...], mask_ref[...])
    for start in range(0, x_ref.shape[0], BLOCK):
        here = pl.ds(start, BLOCK)
        out_ref[here] = mix(x_ref[here], weights[here], buffer[...])


def whole_call(x, mask, parts):
    rows, width = x.shape
    total, servers = mask.shape[1], len(parts)
    return kernel_call(
        "mix_whole",
        functools.partial(whole_kernel, servers),
        bf16(rows, width),
        x,
        mask,
        *reversed(parts),
        flops=4 * total * rows * width,
        scratch=[
            pltpu.VMEM((total, width), jnp.bfloat16),
            pltpu.VMEM((rows, total), jnp.bfloat16),
        ],
    )


def last_kernel(servers, x_ref, mask_ref, *rest):
    parts, rest = rest[:servers], rest[servers:]
    out_ref, buffer, weights, whole, sems = rest
    fill(buffer, parts)
    weights[...] = weigh(x_ref[...], buffer[...], mask_ref[...])
    copies = []
    for i, start in enumerate(range(0, x_ref.shape[0], BLOCK)):
        here = pl.ds(start, BLOCK)
        whole[here] = mix(x_ref[here], weights[here], buffer[...])
        copies.append(pltpu.make_async_copy(whole.at[here], out_ref.at[here], sems.at[i]))
        copies[-1].start()
    for copy in copies:
        copy.wait()


def last_call(x, mask, parts):
    rows, width = x.shape
    total, servers = mask.shape[1], len(parts)
    return kernel_call(
        "mix",
        functools.partial(last_kernel, servers),
        pltpu.HBM((rows, width), jnp.bfloat16),
        x,
        mask,
        *reversed(parts),
        flops=4 * total * rows * width,
        moved=4 * rows * width,
        scratch=[
            pltpu.VMEM((total, width), jnp.bfloat16),
            pltpu.VMEM((rows, total), jnp.bfloat16),
            pltpu.VMEM((rows, width), jnp.bfloat16),
            pltpu.SemaphoreType.DMA((rows // BLOCK,)),
        ],
        out_specs=pl.BlockSpec(memory_space=pltpu.HBM),
    )


def local(descriptors, request, pick):
    wanted = request[0, 0]
    rows = descriptors.shape[2]
    servers, cap = wanted.shape
    total = servers * cap
    groups = lax.axis_size("rep")
    sent = total * FIRST_SHARE[0] // FIRST_SHARE[1]
    within = [(g, g ^ 1) for g in range(groups)]
    beyond = [(g, (g + 2 * (g % 2) - 1 + groups) % groups) for g in range(groups)]

    def turn(value, d):
        return lax.ppermute(value, "clus", [(c, c ^ d) for c in range(servers)])

    def shift(value, by):
        return lax.ppermute(value, "rep", [(g, (g + by) % groups) for g in range(groups)])

    def across(value):
        return lax.ppermute(value, "rep", beyond)

    def inside(value):
        return lax.ppermute(value, "rep", within)

    def turned(parts):
        got = {d: turn(parts[d], d) for d in reversed(range(1, servers))}
        return [parts[0]] + [got[d] for d in range(1, servers)]

    def exchange(expands, far, core, own, most, after=()):
        base = unpack_call(expands[0], across(far), own, after=after)
        most, parts = combine_call(expands[1], inside(core), base, most, servers)
        return most, turned(parts)

    def next_round(x, mask, far, near, far_mask, near_mask, expands, parts, mosts):
        far, most = far_mix_call(far, far_mask, parts, mosts)
        core, own = near_mix_call(near, near_mask, parts)
        x = whole_call(x, mask, parts)
        return x, *exchange(expands, far, core, own, most, after=[x])

    def in_full(x, y, mask, far, near, rest, masks, expands, most, first, last):
        late = unpack_call(expands[1], inside(rest[1]), first=sent)
        late = unpack_call(expands[0], across(rest[0]), late, first=sent)
        late = turned(list(late.reshape(servers, cap, -1)))
        first = [a + b for a, b in zip(first, late)]
        far = jnp.concatenate([far, rest[0]], axis=0)
        near = jnp.concatenate([near[:sent], rest[1], near[sent:]], axis=0)
        near_mask = jnp.concatenate([masks[1], masks[2][sent:]], axis=0)
        y, _, last = next_round(
            x, mask, far, near, masks[0], near_mask, expands, first, [most]
        )
        return last_call(y, mask, last)

    def as_sent(x, y, mask, far, near, rest, masks, expands, most, first, last):
        return last_call(y, mask, last)

    asked = {d: turn(wanted, d) for d in reversed(range(1, servers))}
    mask, held = mask_call(pick.transpose(0, 3, 1, 2)[0], wanted)
    own_list, far_list, core_list, *expands = list_call(
        [held] + [asked[d] for d in range(1, servers)], rows
    )
    beyond_list, within_list = across(far_list), inside(core_list)
    x = normalize_call(descriptors[0, 0])
    pack, far = far_call(x, beyond_list, sent)
    core, own, near, *others, most = near_call(
        x, mask, pack, own_list, far_list, beyond_list, within_list, sent
    )
    rest, masks = others[:2], others[2:]
    most, first = exchange(expands, far, core, own, most)
    mosts = [most]
    reach = 1
    while 2 * reach + 1 < groups:
        by = 2 * reach + 1
        most = functools.reduce(jnp.maximum, mosts)
        mosts = [most, shift(most, by), shift(most, -by)]
        reach += by
    y, most, last = next_round(
        x, mask, far, near, masks[0], masks[2], expands, first, mosts
    )
    state = x, y, mask, far, near, rest, masks, expands, most, first, last
    return lax.cond(most[0, 0] > sent, in_full, as_sent, *state)[None, None]


def solution(mesh):
    return jax.shard_map(
        local,
        mesh=mesh,
        in_specs=(
            P("rep", "clus", None, None),
            P("rep", "clus", None, None),
            P("rep", "clus", None, None),
        ),
        out_specs=P("rep", "clus", None, None),
        check_vma=False,
    )
```

```python
import functools

import jax
import jax.numpy as jnp
from jax import lax
from jax.experimental import pallas as pl
from jax.experimental.pallas import tpu as pltpu
from jax.sharding import PartitionSpec as P

LANES = 128
BLOCK = 128
FIRST_SHARE = 3, 8
BOTH_LAST = (((1,), (1,)), ((), ()))


def bf16(*shape):
    return jax.ShapeDtypeStruct(shape, jnp.bfloat16)


def int32(*shape):
    return jax.ShapeDtypeStruct(shape, jnp.int32)


def kernel_call(name, kernel, outs, *args, flops, moved=0, scratch=(), mib=32, **specs):
    return pl.pallas_call(
        kernel,
        out_shape=outs,
        scratch_shapes=scratch,
        compiler_params=pltpu.CompilerParams(vmem_limit_bytes=mib * 1024 * 1024),
        cost_estimate=pl.CostEstimate(flops=flops, bytes_accessed=moved, transcendentals=0),
        name=name,
        **specs,
    )(*args)


def normalize(value):
    return value * lax.rsqrt(jnp.mean(value * value, axis=-1, keepdims=True) + 1e-06)


def normalize_kernel(x_hbm, out_ref, raw, sems):
    copies = []
    starts = range(0, raw.shape[0], BLOCK)
    for i, start in enumerate(starts):
        here = pl.ds(start, BLOCK)
        copies.append(pltpu.make_async_copy(x_hbm.at[here], raw.at[here], sems.at[i]))
        copies[-1].start()
    for copy, start in zip(copies, starts):
        copy.wait()
        here = pl.ds(start, BLOCK)
        out_ref[here] = normalize(raw[here].astype(jnp.float32)).astype(jnp.bfloat16)


def normalize_call(descriptors):
    rows, width = descriptors.shape
    return kernel_call(
        "normalize",
        normalize_kernel,
        bf16(rows, width),
        descriptors,
        flops=6 * rows * width,
        moved=4 * rows * width,
        scratch=[
            pltpu.VMEM((rows, width), jnp.bfloat16),
            pltpu.SemaphoreType.DMA((rows // BLOCK,)),
        ],
        mib=56,
        in_specs=[pl.BlockSpec(memory_space=pl.ANY)],
    )


def mask_kernel(slot_cap, pick_hbm, wanted_hbm, mask_ref, wanted_ref, pick, sems):
    copies = [
        pltpu.make_async_copy(pick_hbm, pick, sems.at[0]),
        pltpu.make_async_copy(wanted_hbm, wanted_ref, sems.at[1]),
    ]
    for copy in copies:
        copy.start()
    shape = mask_ref.shape[1], mask_ref.shape[0]
    slot = lax.broadcasted_iota(jnp.int32, shape, 0)
    slot = slot ^ (lax.axis_index("clus") * slot_cap)
    chosen = jnp.zeros(shape, jnp.float32)
    copies[0].wait()
    for k in range(pick.shape[0]):
        chosen = jnp.where(pick[k] == slot, 1.0, chosen)
    mask_ref[...] = chosen.T.astype(jnp.bfloat16)
    copies[1].wait()


def mask_call(slots, wanted):
    count, _, rows = slots.shape
    total = wanted.size
    return kernel_call(
        "mask",
        functools.partial(mask_kernel, wanted.shape[1]),
        [bf16(rows, total), pltpu.VMEM(wanted.shape, jnp.int32)],
        slots,
        wanted,
        flops=2 * count * rows * total,
        moved=2 * rows * total,
        scratch=[pltpu.VMEM(slots.shape, jnp.int32), pltpu.SemaphoreType.DMA((2,))],
        mib=56,
        in_specs=[pl.BlockSpec(memory_space=pl.ANY)] * 2,
    )


def list_kernel(rows, *refs):
    parts, refs = refs[-6::-1], refs[-5:]
    own_ref, far_ref, core_ref, expand_far_ref, expand_core_ref = refs
    total = own_ref.shape[1]
    lane = lax.broadcasted_iota(jnp.int32, (total, total), 1)
    sublane = lax.broadcasted_iota(jnp.int32, (total, total), 0)
    odd = lax.axis_index("rep") % 2
    lows = [(2 * odd * rows).astype(jnp.float32), ((2 - 2 * odd) * rows).astype(jnp.float32)]

    def inside(value, low):
        return (value >= low) & (value < low + rows)

    def asked(server):
        row = jnp.concatenate([ref[server, :] for ref in parts], axis=1).astype(jnp.float32)
        column = jnp.broadcast_to(row, (total, total)).T
        again = jnp.where((column == row) & (sublane < lane), 1.0, 0.0)
        return row, column, 1.0 - jnp.max(again, axis=0, keepdims=True)

    most = jnp.zeros((1, 1), jnp.float32)
    for server in range(len(parts)):
        row, _, first = asked(slice(server, server + 1))
        for low in lows:
            count = jnp.sum(jnp.where(inside(row, low), first, 0.0), axis=1, keepdims=True)
            most = jnp.maximum(most, count)
    row, column, first = asked(pl.ds(lax.axis_index("clus"), 1))
    own_ref[...] = jnp.broadcast_to(row - rows, own_ref.shape).astype(jnp.int32)
    place = lax.broadcasted_iota(jnp.int32, own_ref.shape, 0)
    for low, out_ref, expand_ref in zip(lows, (far_ref, core_ref), (expand_far_ref, expand_core_ref)):
        counted = jnp.where(inside(row, low), first, 0.0)
        rank = jnp.sum(jnp.where(row < column, counted, 0.0), axis=1, keepdims=True)
        here = inside(column, low) & (rank.astype(jnp.int32) == lane)
        expand_ref[...] = jnp.where(here, 1.0, 0.0).astype(jnp.bfloat16)
        packed = jnp.max(jnp.where(here, column - low, -1.0), axis=0, keepdims=True)
        out_ref[...] = jnp.where(place == 1, most, packed).astype(jnp.int32)


def list_call(parts, rows):
    total = parts[0].size
    return kernel_call(
        "list",
        functools.partial(list_kernel, rows),
        [int32(8, total)] * 3 + [bf16(total, total)] * 2,
        *reversed(parts),
        flops=40 * total * total,
    )


def one_hot(numbers, rows):
    total = numbers.shape[1]
    column = jnp.broadcast_to(numbers.astype(jnp.float32), (LANES, total)).T.astype(jnp.int32)
    tiles = []
    for start in range(0, rows, LANES):
        lane = lax.broadcasted_iota(jnp.int32, (total, LANES), 1) + start
        tiles.append(jnp.where(column == lane, 1.0, 0.0).astype(jnp.bfloat16))
    return jnp.concatenate(tiles, axis=1)


def take(select, x):
    return jnp.dot(select, x, preferred_element_type=jnp.float32).astype(jnp.bfloat16)


def far_kernel(x_ref, beyond_ref, pack_ref, far_ref):
    pack_ref[...] = one_hot(beyond_ref[0:1], x_ref.shape[0])
    far_ref[...] = take(pack_ref[: far_ref.shape[0]], x_ref[...])


def far_call(x, beyond, sent):
    rows, width = x.shape
    total = beyond.shape[1]
    return kernel_call(
        "pack_far",
        far_kernel,
        [bf16(total, rows), bf16(sent, width)],
        x,
        beyond,
        flops=2 * rows * sent * width,
    )


def near_kernel(x_ref, mask_ref, pack_ref, own_list_ref, *refs):
    far_list_ref, beyond_ref, within_ref, *refs = refs
    core_ref, own_ref, near_ref, rest_far_ref, rest_core_ref, *refs = refs
    far_mask_ref, core_mask_ref, near_mask_ref, most_ref, select = refs
    total, sent = own_ref.shape[0], core_ref.shape[0]
    rows = x_ref.shape[0]
    select[:total] = one_hot(within_ref[0:1], rows)
    select[total:] = one_hot(own_list_ref[0:1], rows)
    fetched = take(select[...], x_ref[...])
    core_ref[...] = fetched[:sent]
    near_ref[:sent] = fetched[:sent]
    rest_core_ref[...] = fetched[sent:total]
    own_ref[...] = fetched[total:]
    near_ref[sent:] = fetched[total:]
    rest_far_ref[...] = take(pack_ref[sent:], x_ref[...])
    masks = take(select[...], mask_ref[...])
    core_mask_ref[...] = masks[:total]
    near_mask_ref[:sent] = masks[:sent]
    near_mask_ref[sent:] = masks[total:]
    far_mask_ref[...] = take(pack_ref[...], mask_ref[...])
    most = jnp.maximum(far_list_ref[...], jnp.maximum(beyond_ref[...], within_ref[...]))
    most_ref[...] = jnp.broadcast_to(most[1:2, :LANES], most_ref.shape)


def near_call(x, mask, pack, own_list, far_list, beyond, within, sent):
    rows, width = x.shape
    total = mask.shape[1]
    return kernel_call(
        "serve_near",
        near_kernel,
        [
            bf16(sent, width),
            bf16(total, width),
            bf16(sent + total, width),
            bf16(total - sent, width),
            bf16(total - sent, width),
            bf16(total, total),
            bf16(total, total),
            bf16(sent + total, total),
            int32(8, LANES),
        ],
        x,
        mask,
        pack,
        own_list,
        far_list,
        beyond,
        within,
        flops=6 * total * rows * width,
        scratch=[pltpu.VMEM((2 * total, rows), jnp.bfloat16)],
    )


def unpack_kernel(first, bases, expand_ref, far_ref, *refs):
    out_ref, sent = refs[-1], far_ref.shape[0]
    rows = jnp.dot(
        expand_ref[:, first : first + sent], far_ref[...], preferred_element_type=jnp.float32
    )
    for base_ref in refs[:bases]:
        rows += base_ref[...].astype(jnp.float32)
    out_ref[...] = rows.astype(jnp.bfloat16)


def unpack_call(expand, far, *base, first=0, after=()):
    in_vmem = [pl.BlockSpec(memory_space=pltpu.VMEM)] * (2 + len(base))
    return kernel_call(
        "unpack",
        functools.partial(unpack_kernel, first, len(base)),
        bf16(expand.shape[0], far.shape[1]),
        expand,
        far,
        *base,
        *after,
        flops=2**34,
        moved=2**25,
        in_specs=in_vmem + [pl.BlockSpec(memory_space=pl.ANY)] * len(after),
    )


def combine_kernel(expand_ref, core_ref, base_ref, most_ref, out_most_ref, *out_refs):
    out_most_ref[...] = most_ref[...]
    cap, sent = out_refs[0].shape[0], core_ref.shape[0]
    rows = jnp.dot(expand_ref[:, :sent], core_ref[...], preferred_element_type=jnp.float32)
    rows = (rows + base_ref[...].astype(jnp.float32)).astype(jnp.bfloat16)
    for d, out in enumerate(out_refs):
        out[...] = rows[d * cap : (d + 1) * cap]


def combine_call(expand, core, base, most, servers):
    total, width = base.shape
    most, *parts = kernel_call(
        "combine",
        combine_kernel,
        [int32(*most.shape)] + [bf16(total // servers, width)] * servers,
        expand,
        core,
        base,
        most,
        flops=2 * total * core.shape[0] * width,
    )
    return most, parts


def fill(buffer, parts):
    cap = parts[0].shape[0]
    for d, ref in enumerate(reversed(parts)):
        buffer[d * cap : (d + 1) * cap] = ref[...]


def weigh(x, buffer, mask):
    dots = lax.dot_general(x, buffer, BOTH_LAST, preferred_element_type=jnp.float32)
    positive = jnp.maximum(dots * (1.0 / x.shape[1]), 0.0)
    return (positive * positive * positive).astype(jnp.bfloat16) * mask


def mix(x, weights, buffer):
    mixed = x.astype(jnp.float32) + jnp.dot(weights, buffer, preferred_element_type=jnp.float32)
    return normalize(mixed).astype(jnp.bfloat16)


def at_end(groups):
    group = lax.axis_index("rep")
    return (group == 0) | (group == groups - 1)


def near_mix(x_ref, mask_ref, buffer, core_ref, own_ref):
    weights = weigh(x_ref[...], buffer[...], mask_ref[...])
    mixed = mix(x_ref[...], weights, buffer[...])
    core_ref[...] = mixed[: core_ref.shape[0]]
    own_ref[...] = mixed[core_ref.shape[0] :]


def far_mix_kernel(groups, servers, far_ref, far_mask_ref, near_ref, near_mask_ref, *rest):
    parts, rest = rest[:servers], rest[servers:]
    *most_refs, out_ref, core_ref, own_ref, most_ref, buffer = rest
    most_ref[...] = functools.reduce(jnp.maximum, [ref[...] for ref in most_refs])
    fill(buffer, parts)
    weights = weigh(far_ref[...], buffer[...], far_mask_ref[: far_ref.shape[0]])
    out_ref[...] = mix(far_ref[...], weights, buffer[...])

    @pl.when(jnp.logical_not(at_end(groups)))
    def _():
        near_mix(near_ref, near_mask_ref, buffer, core_ref, own_ref)


def far_mix_call(groups, far, far_mask, near, near_mask, parts, mosts):
    rows, width = far.shape
    total, servers = far_mask.shape[1], len(parts)
    return kernel_call(
        "mix_far",
        functools.partial(far_mix_kernel, groups, servers),
        [
            bf16(rows, width),
            bf16(near.shape[0] - total, width),
            bf16(total, width),
            int32(*mosts[0].shape),
        ],
        far,
        far_mask,
        near,
        near_mask,
        *reversed(parts),
        *mosts,
        flops=4 * total * rows * width,
        scratch=[pltpu.VMEM((total, width), jnp.bfloat16)],
    )


def end_mix_kernel(groups, servers, near_ref, mask_ref, core_in, own_in, *rest):
    parts, (core_ref, own_ref, buffer) = rest[:servers], rest[servers:]

    @pl.when(at_end(groups))
    def _():
        fill(buffer, parts)
        near_mix(near_ref, mask_ref, buffer, core_ref, own_ref)


def end_mix_call(groups, near, mask, core, own, parts):
    rows, width = near.shape
    total, servers = mask.shape[1], len(parts)
    return kernel_call(
        "mix_near_at_ends",
        functools.partial(end_mix_kernel, groups, servers),
        [bf16(*core.shape), bf16(*own.shape)],
        near,
        mask,
        core,
        own,
        *reversed(parts),
        flops=4 * total * rows * width,
        scratch=[pltpu.VMEM((total, width), jnp.bfloat16)],
        input_output_aliases={2: 0, 3: 1},
    )


def whole_kernel(servers, x_ref, mask_ref, *rest):
    parts, (out_ref, buffer, weights) = rest[:servers], rest[servers:]
    fill(buffer, parts)
    weights[...] = weigh(x_ref[...], buffer[...], mask_ref[...])
    for start in range(0, x_ref.shape[0], BLOCK):
        here = pl.ds(start, BLOCK)
        out_ref[here] = mix(x_ref[here], weights[here], buffer[...])


def whole_call(x, mask, parts):
    rows, width = x.shape
    total, servers = mask.shape[1], len(parts)
    return kernel_call(
        "mix_whole",
        functools.partial(whole_kernel, servers),
        bf16(rows, width),
        x,
        mask,
        *reversed(parts),
        flops=4 * total * rows * width,
        scratch=[
            pltpu.VMEM((total, width), jnp.bfloat16),
            pltpu.VMEM((rows, total), jnp.bfloat16),
        ],
    )


def last_kernel(servers, x_ref, mask_ref, *rest):
    parts, rest = rest[:servers], rest[servers:]
    out_ref, buffer, weights, whole, sems = rest
    fill(buffer, parts)
    weights[...] = weigh(x_ref[...], buffer[...], mask_ref[...])
    copies = []
    for i, start in enumerate(range(0, x_ref.shape[0], BLOCK)):
        here = pl.ds(start, BLOCK)
        whole[here] = mix(x_ref[here], weights[here], buffer[...])
        copies.append(pltpu.make_async_copy(whole.at[here], out_ref.at[here], sems.at[i]))
        copies[-1].start()
    for copy in copies:
        copy.wait()


def last_call(x, mask, parts):
    rows, width = x.shape
    total, servers = mask.shape[1], len(parts)
    return kernel_call(
        "mix",
        functools.partial(last_kernel, servers),
        pltpu.HBM((rows, width), jnp.bfloat16),
        x,
        mask,
        *reversed(parts),
        flops=4 * total * rows * width,
        moved=4 * rows * width,
        scratch=[
            pltpu.VMEM((total, width), jnp.bfloat16),
            pltpu.VMEM((rows, total), jnp.bfloat16),
            pltpu.VMEM((rows, width), jnp.bfloat16),
            pltpu.SemaphoreType.DMA((rows // BLOCK,)),
        ],
        out_specs=pl.BlockSpec(memory_space=pltpu.HBM),
    )


def local(descriptors, request, pick):
    wanted = request[0, 0]
    rows = descriptors.shape[2]
    servers, cap = wanted.shape
    total = servers * cap
    groups = lax.axis_size("rep")
    sent = total * FIRST_SHARE[0] // FIRST_SHARE[1]
    within = [(g, g ^ 1) for g in range(groups)]
    beyond = [(g, (g + 2 * (g % 2) - 1 + groups) % groups) for g in range(groups)]

    def turn(value, d):
        return lax.ppermute(value, "clus", [(c, c ^ d) for c in range(servers)])

    def shift(value, by):
        return lax.ppermute(value, "rep", [(g, (g + by) % groups) for g in range(groups)])

    def across(value):
        return lax.ppermute(value, "rep", beyond)

    def inside(value):
        return lax.ppermute(value, "rep", within)

    def turned(parts):
        got = {d: turn(parts[d], d) for d in reversed(range(1, servers))}
        return [parts[0]] + [got[d] for d in range(1, servers)]

    def exchange(expands, far, core, own, most, after=()):
        base = unpack_call(expands[0], across(far), own, after=after)
        most, parts = combine_call(expands[1], inside(core), base, most, servers)
        return most, turned(parts)

    def next_round(x, mask, far, near, far_mask, near_mask, expands, parts, mosts):
        far, core, own, most = far_mix_call(
            groups, far, far_mask, near, near_mask, parts, mosts
        )
        core, own = end_mix_call(groups, near, near_mask, core, own, parts)
        x = whole_call(x, mask, parts)
        return x, *exchange(expands, far, core, own, most, after=[x])

    def in_full(x, y, mask, far, near, rest, masks, expands, most, first, last):
        late = unpack_call(expands[1], inside(rest[1]), first=sent)
        late = unpack_call(expands[0], across(rest[0]), late, first=sent)
        late = turned(list(late.reshape(servers, cap, -1)))
        first = [a + b for a, b in zip(first, late)]
        far = jnp.concatenate([far, rest[0]], axis=0)
        near = jnp.concatenate([near[:sent], rest[1], near[sent:]], axis=0)
        near_mask = jnp.concatenate([masks[1], masks[2][sent:]], axis=0)
        y, _, last = next_round(
            x, mask, far, near, masks[0], near_mask, expands, first, [most]
        )
        return last_call(y, mask, last)

    def as_sent(x, y, mask, far, near, rest, masks, expands, most, first, last):
        return last_call(y, mask, last)

    asked = {d: turn(wanted, d) for d in reversed(range(1, servers))}
    mask, held = mask_call(pick.transpose(0, 3, 1, 2)[0], wanted)
    own_list, far_list, core_list, *expands = list_call(
        [held] + [asked[d] for d in range(1, servers)], rows
    )
    beyond_list, within_list = across(far_list), inside(core_list)
    x = normalize_call(descriptors[0, 0])
    pack, far = far_call(x, beyond_list, sent)
    core, own, near, *others, most = near_call(
        x, mask, pack, own_list, far_list, beyond_list, within_list, sent
    )
    rest, masks = others[:2], others[2:]
    most, first = exchange(expands, far, core, own, most)
    mosts = [most]
    reach = 1
    while 2 * reach + 1 < groups:
        by = 2 * reach + 1
        most = functools.reduce(jnp.maximum, mosts)
        mosts = [most, shift(most, by), shift(most, -by)]
        reach += by
    y, most, last = next_round(
        x, mask, far, near, masks[0], masks[2], expands, first, mosts
    )
    state = x, y, mask, far, near, rest, masks, expands, most, first, last
    return lax.cond(most[0, 0] > sent, in_full, as_sent, *state)[None, None]


def solution(mesh):
    return jax.shard_map(
        local,
        mesh=mesh,
        in_specs=(
            P("rep", "clus", None, None),
            P("rep", "clus", None, None),
            P("rep", "clus", None, None),
        ),
        out_specs=P("rep", "clus", None, None),
        check_vma=False,
    )
```

```python
import functools

import jax
import jax.numpy as jnp
from jax import lax
from jax.experimental import pallas as pl
from jax.experimental.pallas import tpu as pltpu
from jax.sharding import PartitionSpec as P

LANES = 128
BLOCK = 128
FIRST_SHARE = 3, 8
BOTH_LAST = (((1,), (1,)), ((), ()))


def bf16(*shape):
    return jax.ShapeDtypeStruct(shape, jnp.bfloat16)


def int32(*shape):
    return jax.ShapeDtypeStruct(shape, jnp.int32)


def kernel_call(name, kernel, outs, *args, flops, moved=0, scratch=(), mib=32, **specs):
    return pl.pallas_call(
        kernel,
        out_shape=outs,
        scratch_shapes=scratch,
        compiler_params=pltpu.CompilerParams(vmem_limit_bytes=mib * 1024 * 1024),
        cost_estimate=pl.CostEstimate(flops=flops, bytes_accessed=moved, transcendentals=0),
        name=name,
        **specs,
    )(*args)


def normalize(value):
    return value * lax.rsqrt(jnp.mean(value * value, axis=-1, keepdims=True) + 1e-06)


def normalize_kernel(x_hbm, out_ref, raw, sems):
    copies = []
    starts = range(0, raw.shape[0], BLOCK)
    for i, start in enumerate(starts):
        here = pl.ds(start, BLOCK)
        copies.append(pltpu.make_async_copy(x_hbm.at[here], raw.at[here], sems.at[i]))
        copies[-1].start()
    for copy, start in zip(copies, starts):
        copy.wait()
        here = pl.ds(start, BLOCK)
        out_ref[here] = normalize(raw[here].astype(jnp.float32)).astype(jnp.bfloat16)


def normalize_call(descriptors):
    rows, width = descriptors.shape
    return kernel_call(
        "normalize",
        normalize_kernel,
        bf16(rows, width),
        descriptors,
        flops=6 * rows * width,
        moved=4 * rows * width,
        scratch=[
            pltpu.VMEM((rows, width), jnp.bfloat16),
            pltpu.SemaphoreType.DMA((rows // BLOCK,)),
        ],
        mib=56,
        in_specs=[pl.BlockSpec(memory_space=pl.ANY)],
    )


def mask_kernel(slot_cap, pick_hbm, wanted_hbm, mask_ref, wanted_ref, pick, sems):
    copies = [
        pltpu.make_async_copy(pick_hbm, pick, sems.at[0]),
        pltpu.make_async_copy(wanted_hbm, wanted_ref, sems.at[1]),
    ]
    for copy in copies:
        copy.start()
    shape = mask_ref.shape[1], mask_ref.shape[0]
    slot = lax.broadcasted_iota(jnp.int32, shape, 0)
    slot = slot ^ (lax.axis_index("clus") * slot_cap)
    chosen = jnp.zeros(shape, jnp.float32)
    copies[0].wait()
    for k in range(pick.shape[0]):
        chosen = jnp.where(pick[k] == slot, 1.0, chosen)
    mask_ref[...] = chosen.T.astype(jnp.bfloat16)
    copies[1].wait()


def mask_call(slots, wanted):
    count, _, rows = slots.shape
    total = wanted.size
    return kernel_call(
        "mask",
        functools.partial(mask_kernel, wanted.shape[1]),
        [bf16(rows, total), pltpu.VMEM(wanted.shape, jnp.int32)],
        slots,
        wanted,
        flops=2 * count * rows * total,
        moved=2 * rows * total,
        scratch=[pltpu.VMEM(slots.shape, jnp.int32), pltpu.SemaphoreType.DMA((2,))],
        mib=56,
        in_specs=[pl.BlockSpec(memory_space=pl.ANY)] * 2,
    )


def list_kernel(rows, *refs):
    parts, refs = refs[-6::-1], refs[-5:]
    own_ref, far_ref, core_ref, expand_far_ref, expand_core_ref = refs
    total = own_ref.shape[1]
    lane = lax.broadcasted_iota(jnp.int32, (total, total), 1)
    sublane = lax.broadcasted_iota(jnp.int32, (total, total), 0)
    odd = lax.axis_index("rep") % 2
    lows = [(2 * odd * rows).astype(jnp.float32), ((2 - 2 * odd) * rows).astype(jnp.float32)]

    def inside(value, low):
        return (value >= low) & (value < low + rows)

    def asked(server):
        row = jnp.concatenate([ref[server, :] for ref in parts], axis=1).astype(jnp.float32)
        column = jnp.broadcast_to(row, (total, total)).T
        again = jnp.where((column == row) & (sublane < lane), 1.0, 0.0)
        return row, column, 1.0 - jnp.max(again, axis=0, keepdims=True)

    most = jnp.zeros((1, 1), jnp.float32)
    for server in range(len(parts)):
        row, _, first = asked(slice(server, server + 1))
        for low in lows:
            count = jnp.sum(jnp.where(inside(row, low), first, 0.0), axis=1, keepdims=True)
            most = jnp.maximum(most, count)
    row, column, first = asked(pl.ds(lax.axis_index("clus"), 1))
    own_ref[...] = jnp.broadcast_to(row - rows, own_ref.shape).astype(jnp.int32)
    place = lax.broadcasted_iota(jnp.int32, own_ref.shape, 0)
    for low, out_ref, expand_ref in zip(lows, (far_ref, core_ref), (expand_far_ref, expand_core_ref)):
        counted = jnp.where(inside(row, low), first, 0.0)
        rank = jnp.sum(jnp.where(row < column, counted, 0.0), axis=1, keepdims=True)
        here = inside(column, low) & (rank.astype(jnp.int32) == lane)
        expand_ref[...] = jnp.where(here, 1.0, 0.0).astype(jnp.bfloat16)
        packed = jnp.max(jnp.where(here, column - low, -1.0), axis=0, keepdims=True)
        out_ref[...] = jnp.where(place == 1, most, packed).astype(jnp.int32)


def list_call(parts, rows):
    total = parts[0].size
    return kernel_call(
        "list",
        functools.partial(list_kernel, rows),
        [int32(8, total)] * 3 + [bf16(total, total)] * 2,
        *reversed(parts),
        flops=40 * total * total,
    )


def one_hot(numbers, rows):
    total = numbers.shape[1]
    column = jnp.broadcast_to(numbers.astype(jnp.float32), (LANES, total)).T.astype(jnp.int32)
    tiles = []
    for start in range(0, rows, LANES):
        lane = lax.broadcasted_iota(jnp.int32, (total, LANES), 1) + start
        tiles.append(jnp.where(column == lane, 1.0, 0.0).astype(jnp.bfloat16))
    return jnp.concatenate(tiles, axis=1)


def take(select, x):
    return jnp.dot(select, x, preferred_element_type=jnp.float32).astype(jnp.bfloat16)


def far_kernel(x_ref, beyond_ref, pack_ref, far_ref):
    pack_ref[...] = one_hot(beyond_ref[0:1], x_ref.shape[0])
    far_ref[...] = take(pack_ref[: far_ref.shape[0]], x_ref[...])


def far_call(x, beyond, sent):
    rows, width = x.shape
    total = beyond.shape[1]
    return kernel_call(
        "pack_far",
        far_kernel,
        [bf16(total, rows), bf16(sent, width)],
        x,
        beyond,
        flops=2 * rows * sent * width,
    )


def near_kernel(x_ref, mask_ref, pack_ref, own_list_ref, *refs):
    far_list_ref, beyond_ref, within_ref, *refs = refs
    core_ref, own_ref, near_ref, rest_far_ref, rest_core_ref, *refs = refs
    far_mask_ref, core_mask_ref, near_mask_ref, most_ref, select = refs
    total, sent = own_ref.shape[0], core_ref.shape[0]
    rows = x_ref.shape[0]
    select[:total] = one_hot(within_ref[0:1], rows)
    select[total:] = one_hot(own_list_ref[0:1], rows)
    fetched = take(select[...], x_ref[...])
    core_ref[...] = fetched[:sent]
    near_ref[:sent] = fetched[:sent]
    rest_core_ref[...] = fetched[sent:total]
    own_ref[...] = fetched[total:]
    near_ref[sent:] = fetched[total:]
    rest_far_ref[...] = take(pack_ref[sent:], x_ref[...])
    masks = take(select[...], mask_ref[...])
    core_mask_ref[...] = masks[:total]
    near_mask_ref[:sent] = masks[:sent]
    near_mask_ref[sent:] = masks[total:]
    far_mask_ref[...] = take(pack_ref[...], mask_ref[...])
    most = jnp.maximum(far_list_ref[...], jnp.maximum(beyond_ref[...], within_ref[...]))
    most_ref[...] = jnp.broadcast_to(most[1:2, :LANES], most_ref.shape)


def near_call(x, mask, pack, own_list, far_list, beyond, within, sent):
    rows, width = x.shape
    total = mask.shape[1]
    return kernel_call(
        "serve_near",
        near_kernel,
        [
            bf16(sent, width),
            bf16(total, width),
            bf16(sent + total, width),
            bf16(total - sent, width),
            bf16(total - sent, width),
            bf16(total, total),
            bf16(total, total),
            bf16(sent + total, total),
            int32(8, LANES),
        ],
        x,
        mask,
        pack,
        own_list,
        far_list,
        beyond,
        within,
        flops=6 * total * rows * width,
        scratch=[pltpu.VMEM((2 * total, rows), jnp.bfloat16)],
    )


def unpack_kernel(first, bases, expand_ref, far_ref, *refs):
    out_ref, sent = refs[-1], far_ref.shape[0]
    rows = jnp.dot(
        expand_ref[:, first : first + sent], far_ref[...], preferred_element_type=jnp.float32
    )
    for base_ref in refs[:bases]:
        rows += base_ref[...].astype(jnp.float32)
    out_ref[...] = rows.astype(jnp.bfloat16)


def unpack_call(expand, far, *base, first=0, after=()):
    in_vmem = [pl.BlockSpec(memory_space=pltpu.VMEM)] * (2 + len(base))
    return kernel_call(
        "unpack",
        functools.partial(unpack_kernel, first, len(base)),
        bf16(expand.shape[0], far.shape[1]),
        expand,
        far,
        *base,
        *after,
        flops=2**34,
        moved=2**25,
        in_specs=in_vmem + [pl.BlockSpec(memory_space=pl.ANY)] * len(after),
    )


def combine_kernel(expand_ref, core_ref, base_ref, most_ref, out_most_ref, *out_refs):
    out_most_ref[...] = most_ref[...]
    cap, sent = out_refs[0].shape[0], core_ref.shape[0]
    rows = jnp.dot(expand_ref[:, :sent], core_ref[...], preferred_element_type=jnp.float32)
    rows = (rows + base_ref[...].astype(jnp.float32)).astype(jnp.bfloat16)
    for d, out in enumerate(out_refs):
        out[...] = rows[d * cap : (d + 1) * cap]


def combine_call(expand, core, base, most, servers):
    total, width = base.shape
    most, *parts = kernel_call(
        "combine",
        combine_kernel,
        [int32(*most.shape)] + [bf16(total // servers, width)] * servers,
        expand,
        core,
        base,
        most,
        flops=2 * total * core.shape[0] * width,
    )
    return most, parts


def fill(buffer, parts):
    cap = parts[0].shape[0]
    for d, ref in enumerate(reversed(parts)):
        buffer[d * cap : (d + 1) * cap] = ref[...]


def weigh(x, buffer, mask):
    dots = lax.dot_general(x, buffer, BOTH_LAST, preferred_element_type=jnp.float32)
    positive = jnp.maximum(dots * (1.0 / x.shape[1]), 0.0)
    return (positive * positive * positive).astype(jnp.bfloat16) * mask


def mix(x, weights, buffer):
    mixed = x.astype(jnp.float32) + jnp.dot(weights, buffer, preferred_element_type=jnp.float32)
    return normalize(mixed).astype(jnp.bfloat16)


def far_mix_kernel(servers, x_ref, mask_ref, *rest):
    parts, rest = rest[:servers], rest[servers:]
    *most_refs, out_ref, most_ref, buffer = rest
    most_ref[...] = functools.reduce(jnp.maximum, [ref[...] for ref in most_refs])
    fill(buffer, parts)
    weights = weigh(x_ref[...], buffer[...], mask_ref[: x_ref.shape[0]])
    out_ref[...] = mix(x_ref[...], weights, buffer[...])


def far_mix_call(x, mask, parts, mosts):
    rows, width = x.shape
    total, servers = mask.shape[1], len(parts)
    return kernel_call(
        "mix_far",
        functools.partial(far_mix_kernel, servers),
        [bf16(rows, width), int32(*mosts[0].shape)],
        x,
        mask,
        *reversed(parts),
        *mosts,
        flops=4 * total * rows * width,
        scratch=[pltpu.VMEM((total, width), jnp.bfloat16)],
    )


def near_mix_kernel(servers, x_ref, mask_ref, *rest):
    parts, (core_ref, own_ref, buffer) = rest[:servers], rest[servers:]
    fill(buffer, parts)
    weights = weigh(x_ref[...], buffer[...], mask_ref[...])
    mixed = mix(x_ref[...], weights, buffer[...])
    core_ref[...] = mixed[: core_ref.shape[0]]
    own_ref[...] = mixed[core_ref.shape[0] :]


def near_mix_call(x, mask, parts):
    rows, width = x.shape
    total, servers = mask.shape[1], len(parts)
    return kernel_call(
        "mix_near",
        functools.partial(near_mix_kernel, servers),
        [bf16(rows - total, width), bf16(total, width)],
        x,
        mask,
        *reversed(parts),
        flops=4 * total * rows * width,
        scratch=[pltpu.VMEM((total, width), jnp.bfloat16)],
    )


def whole_kernel(late, servers, x_ref, mask_ref, *rest):
    parts, (out_ref, buffer, weights, whole, sems) = rest[:servers], rest[-5:]

    @pl.when(((lax.axis_index("rep") + 1) % 4 < 2) == late)
    def _():
        fill(buffer, parts)
        weights[...] = weigh(x_ref[...], buffer[...], mask_ref[...])
        copies = []
        for i, start in enumerate(range(0, x_ref.shape[0], BLOCK)):
            here = pl.ds(start, BLOCK)
            whole[here] = mix(x_ref[here], weights[here], buffer[...])
            copies.append(pltpu.make_async_copy(whole.at[here], out_ref.at[here], sems.at[i]))
            copies[-1].start()
        for copy in copies:
            copy.wait()


def whole_call(late, x, mask, parts, out=()):
    rows, width = x.shape
    total, servers = mask.shape[1], len(parts)
    in_vmem = [pl.BlockSpec(memory_space=pltpu.VMEM)] * (2 + servers)
    return kernel_call(
        "mix_whole_late" if late else "mix_whole_early",
        functools.partial(whole_kernel, late, servers),
        bf16(rows, width),
        x,
        mask,
        *reversed(parts),
        *out,
        flops=4 * total * rows * width,
        scratch=[
            pltpu.VMEM((total, width), jnp.bfloat16),
            pltpu.VMEM((rows, total), jnp.bfloat16),
            pltpu.VMEM((rows, width), jnp.bfloat16),
            pltpu.SemaphoreType.DMA((rows // BLOCK,)),
        ],
        in_specs=in_vmem + [pl.BlockSpec(memory_space=pl.ANY)] * len(out),
        out_specs=pl.BlockSpec(memory_space=pl.ANY),
        input_output_aliases={2 + servers: 0} if out else {},
    )


def last_kernel(servers, x_ref, mask_ref, *rest):
    parts, rest = rest[:servers], rest[servers:]
    out_ref, buffer, weights, whole, sems = rest
    fill(buffer, parts)
    weights[...] = weigh(x_ref[...], buffer[...], mask_ref[...])
    copies = []
    for i, start in enumerate(range(0, x_ref.shape[0], BLOCK)):
        here = pl.ds(start, BLOCK)
        whole[here] = mix(x_ref[here], weights[here], buffer[...])
        copies.append(pltpu.make_async_copy(whole.at[here], out_ref.at[here], sems.at[i]))
        copies[-1].start()
    for copy in copies:
        copy.wait()


def last_call(x, mask, parts):
    rows, width = x.shape
    total, servers = mask.shape[1], len(parts)
    return kernel_call(
        "mix",
        functools.partial(last_kernel, servers),
        pltpu.HBM((rows, width), jnp.bfloat16),
        x,
        mask,
        *reversed(parts),
        flops=4 * total * rows * width,
        moved=4 * rows * width,
        scratch=[
            pltpu.VMEM((total, width), jnp.bfloat16),
            pltpu.VMEM((rows, total), jnp.bfloat16),
            pltpu.VMEM((rows, width), jnp.bfloat16),
            pltpu.SemaphoreType.DMA((rows // BLOCK,)),
        ],
        out_specs=pl.BlockSpec(memory_space=pltpu.HBM),
    )


def local(descriptors, request, pick):
    wanted = request[0, 0]
    rows = descriptors.shape[2]
    servers, cap = wanted.shape
    total = servers * cap
    groups = lax.axis_size("rep")
    sent = total * FIRST_SHARE[0] // FIRST_SHARE[1]
    within = [(g, g ^ 1) for g in range(groups)]
    beyond = [(g, (g + 2 * (g % 2) - 1 + groups) % groups) for g in range(groups)]

    def turn(value, d):
        return lax.ppermute(value, "clus", [(c, c ^ d) for c in range(servers)])

    def shift(value, by):
        return lax.ppermute(value, "rep", [(g, (g + by) % groups) for g in range(groups)])

    def across(value):
        return lax.ppermute(value, "rep", beyond)

    def inside(value):
        return lax.ppermute(value, "rep", within)

    def turned(parts):
        got = {d: turn(parts[d], d) for d in reversed(range(1, servers))}
        return [parts[0]] + [got[d] for d in range(1, servers)]

    def exchange(expands, far, core, own, most, after=()):
        base = unpack_call(expands[0], across(far), own, after=after)
        most, parts = combine_call(expands[1], inside(core), base, most, servers)
        return most, turned(parts)

    def next_round(x, mask, far, near, far_mask, near_mask, expands, parts, mosts):
        far, most = far_mix_call(far, far_mask, parts, mosts)
        core, own = near_mix_call(near, near_mask, parts)
        y = whole_call(True, x, mask, parts)
        most, last = exchange(expands, far, core, own, most, after=[y])
        return whole_call(False, x, mask, parts, out=[y]), most, last

    def in_full(x, y, mask, far, near, rest, masks, expands, most, first, last):
        late = unpack_call(expands[1], inside(rest[1]), first=sent)
        late = unpack_call(expands[0], across(rest[0]), late, first=sent)
        late = turned(list(late.reshape(servers, cap, -1)))
        first = [a + b for a, b in zip(first, late)]
        far = jnp.concatenate([far, rest[0]], axis=0)
        near = jnp.concatenate([near[:sent], rest[1], near[sent:]], axis=0)
        near_mask = jnp.concatenate([masks[1], masks[2][sent:]], axis=0)
        y, _, last = next_round(
            x, mask, far, near, masks[0], near_mask, expands, first, [most]
        )
        return last_call(y, mask, last)

    def as_sent(x, y, mask, far, near, rest, masks, expands, most, first, last):
        return last_call(y, mask, last)

    asked = {d: turn(wanted, d) for d in reversed(range(1, servers))}
    mask, held = mask_call(pick.transpose(0, 3, 1, 2)[0], wanted)
    own_list, far_list, core_list, *expands = list_call(
        [held] + [asked[d] for d in range(1, servers)], rows
    )
    beyond_list, within_list = across(far_list), inside(core_list)
    x = normalize_call(descriptors[0, 0])
    pack, far = far_call(x, beyond_list, sent)
    core, own, near, *others, most = near_call(
        x, mask, pack, own_list, far_list, beyond_list, within_list, sent
    )
    rest, masks = others[:2], others[2:]
    most, first = exchange(expands, far, core, own, most)
    mosts = [most]
    reach = 1
    while 2 * reach + 1 < groups:
        by = 2 * reach + 1
        most = functools.reduce(jnp.maximum, mosts)
        mosts = [most, shift(most, by), shift(most, -by)]
        reach += by
    y, most, last = next_round(
        x, mask, far, near, masks[0], masks[2], expands, first, mosts
    )
    state = x, y, mask, far, near, rest, masks, expands, most, first, last
    return lax.cond(most[0, 0] > sent, in_full, as_sent, *state)[None, None]


def solution(mesh):
    return jax.shard_map(
        local,
        mesh=mesh,
        in_specs=(
            P("rep", "clus", None, None),
            P("rep", "clus", None, None),
            P("rep", "clus", None, None),
        ),
        out_specs=P("rep", "clus", None, None),
        check_vma=False,
    )
```

```python
import functools

import jax
import jax.numpy as jnp
from jax import lax
from jax.experimental import pallas as pl
from jax.experimental.pallas import tpu as pltpu
from jax.sharding import PartitionSpec as P

LANES = 128
BLOCK = 128
FIRST_SHARE = 3, 8
BOTH_LAST = (((1,), (1,)), ((), ()))


def bf16(*shape):
    return jax.ShapeDtypeStruct(shape, jnp.bfloat16)


def int32(*shape):
    return jax.ShapeDtypeStruct(shape, jnp.int32)


def kernel_call(name, kernel, outs, *args, flops, moved=0, scratch=(), mib=32, **specs):
    return pl.pallas_call(
        kernel,
        out_shape=outs,
        scratch_shapes=scratch,
        compiler_params=pltpu.CompilerParams(vmem_limit_bytes=mib * 1024 * 1024),
        cost_estimate=pl.CostEstimate(flops=flops, bytes_accessed=moved, transcendentals=0),
        name=name,
        **specs,
    )(*args)


def normalize(value):
    return value * lax.rsqrt(jnp.mean(value * value, axis=-1, keepdims=True) + 1e-06)


def normalize_kernel(x_hbm, out_ref, raw, sems):
    copies = []
    starts = range(0, raw.shape[0], BLOCK)
    for i, start in enumerate(starts):
        here = pl.ds(start, BLOCK)
        copies.append(pltpu.make_async_copy(x_hbm.at[here], raw.at[here], sems.at[i]))
        copies[-1].start()
    for copy, start in zip(copies, starts):
        copy.wait()
        here = pl.ds(start, BLOCK)
        out_ref[here] = normalize(raw[here].astype(jnp.float32)).astype(jnp.bfloat16)


def normalize_call(descriptors):
    rows, width = descriptors.shape
    return kernel_call(
        "normalize",
        normalize_kernel,
        bf16(rows, width),
        descriptors,
        flops=6 * rows * width,
        moved=4 * rows * width,
        scratch=[
            pltpu.VMEM((rows, width), jnp.bfloat16),
            pltpu.SemaphoreType.DMA((rows // BLOCK,)),
        ],
        mib=56,
        in_specs=[pl.BlockSpec(memory_space=pl.ANY)],
    )


def mask_kernel(slot_cap, pick_hbm, wanted_hbm, mask_ref, wanted_ref, pick, sems):
    copies = [
        pltpu.make_async_copy(pick_hbm, pick, sems.at[0]),
        pltpu.make_async_copy(wanted_hbm, wanted_ref, sems.at[1]),
    ]
    for copy in copies:
        copy.start()
    shape = mask_ref.shape[1], mask_ref.shape[0]
    slot = lax.broadcasted_iota(jnp.int32, shape, 0)
    slot = slot ^ (lax.axis_index("clus") * slot_cap)
    chosen = jnp.zeros(shape, jnp.float32)
    copies[0].wait()
    for k in range(pick.shape[0]):
        chosen = jnp.where(pick[k] == slot, 1.0, chosen)
    mask_ref[...] = chosen.T.astype(jnp.bfloat16)
    copies[1].wait()


def mask_call(slots, wanted):
    count, _, rows = slots.shape
    total = wanted.size
    return kernel_call(
        "mask",
        functools.partial(mask_kernel, wanted.shape[1]),
        [bf16(rows, total), pltpu.VMEM(wanted.shape, jnp.int32)],
        slots,
        wanted,
        flops=2 * count * rows * total,
        moved=2 * rows * total,
        scratch=[pltpu.VMEM(slots.shape, jnp.int32), pltpu.SemaphoreType.DMA((2,))],
        mib=56,
        in_specs=[pl.BlockSpec(memory_space=pl.ANY)] * 2,
    )


def list_kernel(rows, *refs):
    parts, refs = refs[-6::-1], refs[-5:]
    own_ref, far_ref, core_ref, expand_far_ref, expand_core_ref = refs
    total = own_ref.shape[1]
    lane = lax.broadcasted_iota(jnp.int32, (total, total), 1)
    sublane = lax.broadcasted_iota(jnp.int32, (total, total), 0)
    odd = lax.axis_index("rep") % 2
    lows = [(2 * odd * rows).astype(jnp.float32), ((2 - 2 * odd) * rows).astype(jnp.float32)]

    def inside(value, low):
        return (value >= low) & (value < low + rows)

    def asked(server):
        row = jnp.concatenate([ref[server, :] for ref in parts], axis=1).astype(jnp.float32)
        column = jnp.broadcast_to(row, (total, total)).T
        again = jnp.where((column == row) & (sublane < lane), 1.0, 0.0)
        return row, column, 1.0 - jnp.max(again, axis=0, keepdims=True)

    most = jnp.zeros((1, 1), jnp.float32)
    for server in range(len(parts)):
        row, _, first = asked(slice(server, server + 1))
        for low in lows:
            count = jnp.sum(jnp.where(inside(row, low), first, 0.0), axis=1, keepdims=True)
            most = jnp.maximum(most, count)
    row, column, first = asked(pl.ds(lax.axis_index("clus"), 1))
    own_ref[...] = jnp.broadcast_to(row - rows, own_ref.shape).astype(jnp.int32)
    place = lax.broadcasted_iota(jnp.int32, own_ref.shape, 0)
    for low, out_ref, expand_ref in zip(lows, (far_ref, core_ref), (expand_far_ref, expand_core_ref)):
        counted = jnp.where(inside(row, low), first, 0.0)
        rank = jnp.sum(jnp.where(row < column, counted, 0.0), axis=1, keepdims=True)
        here = inside(column, low) & (rank.astype(jnp.int32) == lane)
        expand_ref[...] = jnp.where(here, 1.0, 0.0).astype(jnp.bfloat16)
        packed = jnp.max(jnp.where(here, column - low, -1.0), axis=0, keepdims=True)
        out_ref[...] = jnp.where(place == 1, most, packed).astype(jnp.int32)


def list_call(parts, rows):
    total = parts[0].size
    return kernel_call(
        "list",
        functools.partial(list_kernel, rows),
        [int32(8, total)] * 3 + [bf16(total, total)] * 2,
        *reversed(parts),
        flops=40 * total * total,
    )


def one_hot(numbers, rows):
    total = numbers.shape[1]
    column = jnp.broadcast_to(numbers.astype(jnp.float32), (LANES, total)).T.astype(jnp.int32)
    tiles = []
    for start in range(0, rows, LANES):
        lane = lax.broadcasted_iota(jnp.int32, (total, LANES), 1) + start
        tiles.append(jnp.where(column == lane, 1.0, 0.0).astype(jnp.bfloat16))
    return jnp.concatenate(tiles, axis=1)


def take(select, x):
    return jnp.dot(select, x, preferred_element_type=jnp.float32).astype(jnp.bfloat16)


def far_kernel(x_ref, beyond_ref, pack_ref, far_ref):
    pack_ref[...] = one_hot(beyond_ref[0:1], x_ref.shape[0])
    far_ref[...] = take(pack_ref[: far_ref.shape[0]], x_ref[...])


def far_call(x, beyond, sent):
    rows, width = x.shape
    total = beyond.shape[1]
    return kernel_call(
        "pack_far",
        far_kernel,
        [bf16(total, rows), bf16(sent, width)],
        x,
        beyond,
        flops=2 * rows * sent * width,
    )


def near_kernel(x_ref, mask_ref, pack_ref, own_list_ref, *refs):
    far_list_ref, beyond_ref, within_ref, *refs = refs
    core_ref, own_ref, near_ref, rest_far_ref, rest_core_ref, *refs = refs
    far_mask_ref, core_mask_ref, near_mask_ref, most_ref, select = refs
    total, sent = own_ref.shape[0], core_ref.shape[0]
    rows = x_ref.shape[0]
    select[:total] = one_hot(within_ref[0:1], rows)
    select[total:] = one_hot(own_list_ref[0:1], rows)
    fetched = take(select[...], x_ref[...])
    core_ref[...] = fetched[:sent]
    near_ref[:sent] = fetched[:sent]
    rest_core_ref[...] = fetched[sent:total]
    own_ref[...] = fetched[total:]
    near_ref[sent:] = fetched[total:]
    rest_far_ref[...] = take(pack_ref[sent:], x_ref[...])
    masks = take(select[...], mask_ref[...])
    core_mask_ref[...] = masks[:total]
    near_mask_ref[:sent] = masks[:sent]
    near_mask_ref[sent:] = masks[total:]
    far_mask_ref[...] = take(pack_ref[...], mask_ref[...])
    most = jnp.maximum(far_list_ref[...], jnp.maximum(beyond_ref[...], within_ref[...]))
    most_ref[...] = jnp.broadcast_to(most[1:2, :LANES], most_ref.shape)


def near_call(x, mask, pack, own_list, far_list, beyond, within, sent):
    rows, width = x.shape
    total = mask.shape[1]
    return kernel_call(
        "serve_near",
        near_kernel,
        [
            bf16(sent, width),
            bf16(total, width),
            bf16(sent + total, width),
            bf16(total - sent, width),
            bf16(total - sent, width),
            bf16(total, total),
            bf16(total, total),
            bf16(sent + total, total),
            int32(8, LANES),
        ],
        x,
        mask,
        pack,
        own_list,
        far_list,
        beyond,
        within,
        flops=6 * total * rows * width,
        scratch=[pltpu.VMEM((2 * total, rows), jnp.bfloat16)],
    )


def unpack_kernel(first, expand_ref, far_ref, own_ref, *refs):
    out_ref, sent = refs[-1], far_ref.shape[0]
    rows = jnp.dot(
        expand_ref[:, first : first + sent], far_ref[...], preferred_element_type=jnp.float32
    )
    out_ref[...] = (rows + own_ref[...].astype(jnp.float32)).astype(jnp.bfloat16)


def unpack_call(expand, far, own, first=0, after=()):
    return kernel_call(
        "unpack",
        functools.partial(unpack_kernel, first),
        bf16(*own.shape),
        expand,
        far,
        own,
        *after,
        flops=2**34,
        moved=2**25,
        in_specs=[pl.BlockSpec(memory_space=pltpu.VMEM)] * 3
        + [pl.BlockSpec(memory_space=pl.ANY)] * len(after),
    )


def combine_kernel(first, expand_ref, core_ref, base_ref, *out_refs):
    cap, sent = out_refs[0].shape[0], core_ref.shape[0]
    rows = jnp.dot(
        expand_ref[:, first : first + sent], core_ref[...], preferred_element_type=jnp.float32
    )
    rows = (rows + base_ref[...].astype(jnp.float32)).astype(jnp.bfloat16)
    for d, out in enumerate(out_refs):
        out[...] = rows[d * cap : (d + 1) * cap]


def combine_call(expand, core, base, servers, first=0):
    total, width = base.shape
    return kernel_call(
        "combine",
        functools.partial(combine_kernel, first),
        [bf16(total // servers, width)] * servers,
        expand,
        core,
        base,
        flops=2 * total * core.shape[0] * width,
    )


def gather_kernel(sent, servers, *refs):
    parts, most_refs, (buffer_ref, over_ref) = refs[:servers], refs[servers:-2], refs[-2:]
    fill(buffer_ref, parts)
    most = functools.reduce(jnp.maximum, [ref[...] for ref in most_refs])
    over_ref[0, 0] = (jnp.max(most) > sent).astype(jnp.int32)


def gather_call(parts, mosts, sent):
    cap, width = parts[0].shape
    return kernel_call(
        "gather",
        functools.partial(gather_kernel, sent, len(parts)),
        [bf16(cap * len(parts), width), int32(1, 1)],
        *reversed(parts),
        *mosts,
        flops=cap * width,
        out_specs=[
            pl.BlockSpec(memory_space=pltpu.VMEM),
            pl.BlockSpec(memory_space=pltpu.SMEM),
        ],
    )


def fill(buffer, parts):
    cap = parts[0].shape[0]
    for d, ref in enumerate(reversed(parts)):
        buffer[d * cap : (d + 1) * cap] = ref[...]


def weigh(x, buffer, mask):
    dots = lax.dot_general(x, buffer, BOTH_LAST, preferred_element_type=jnp.float32)
    positive = jnp.maximum(dots * (1.0 / x.shape[1]), 0.0)
    return (positive * positive * positive).astype(jnp.bfloat16) * mask


def mix(x, weights, buffer):
    mixed = x.astype(jnp.float32) + jnp.dot(weights, buffer, preferred_element_type=jnp.float32)
    return normalize(mixed).astype(jnp.bfloat16)


def far_mix_kernel(servers, x_ref, mask_ref, *rest):
    parts, (out_ref, buffer) = rest[:servers], rest[servers:]
    fill(buffer, parts)
    weights = weigh(x_ref[...], buffer[...], mask_ref[: x_ref.shape[0]])
    out_ref[...] = mix(x_ref[...], weights, buffer[...])


def far_mix_call(x, mask, parts):
    rows, width = x.shape
    total, servers = mask.shape[1], len(parts)
    return kernel_call(
        "mix_far",
        functools.partial(far_mix_kernel, servers),
        bf16(rows, width),
        x,
        mask,
        *reversed(parts),
        flops=4 * total * rows * width,
        scratch=[pltpu.VMEM((total, width), jnp.bfloat16)],
    )


def near_mix_kernel(servers, x_ref, mask_ref, *rest):
    parts, (core_ref, own_ref, buffer) = rest[:servers], rest[servers:]
    fill(buffer, parts)
    weights = weigh(x_ref[...], buffer[...], mask_ref[...])
    mixed = mix(x_ref[...], weights, buffer[...])
    core_ref[...] = mixed[: core_ref.shape[0]]
    own_ref[...] = mixed[core_ref.shape[0] :]


def near_mix_call(x, mask, parts):
    rows, width = x.shape
    total, servers = mask.shape[1], len(parts)
    return kernel_call(
        "mix_near",
        functools.partial(near_mix_kernel, servers),
        [bf16(rows - total, width), bf16(total, width)],
        x,
        mask,
        *reversed(parts),
        flops=4 * total * rows * width,
        scratch=[pltpu.VMEM((total, width), jnp.bfloat16)],
    )


def whole_kernel(late, servers, x_ref, mask_ref, *rest):
    parts, (out_ref, buffer, weights, whole, sems) = rest[:servers], rest[-5:]

    @pl.when(((lax.axis_index("rep") + 1) % 4 < 2) == late)
    def _():
        fill(buffer, parts)
        weights[...] = weigh(x_ref[...], buffer[...], mask_ref[...])
        copies = []
        for i, start in enumerate(range(0, x_ref.shape[0], BLOCK)):
            here = pl.ds(start, BLOCK)
            whole[here] = mix(x_ref[here], weights[here], buffer[...])
            copies.append(pltpu.make_async_copy(whole.at[here], out_ref.at[here], sems.at[i]))
            copies[-1].start()
        for copy in copies:
            copy.wait()


def whole_call(late, x, mask, parts, out=()):
    rows, width = x.shape
    total, servers = mask.shape[1], len(parts)
    in_vmem = [pl.BlockSpec(memory_space=pltpu.VMEM)] * (2 + servers)
    return kernel_call(
        "mix_whole_late" if late else "mix_whole_early",
        functools.partial(whole_kernel, late, servers),
        bf16(rows, width),
        x,
        mask,
        *reversed(parts),
        *out,
        flops=4 * total * rows * width,
        scratch=[
            pltpu.VMEM((total, width), jnp.bfloat16),
            pltpu.VMEM((rows, total), jnp.bfloat16),
            pltpu.VMEM((rows, width), jnp.bfloat16),
            pltpu.SemaphoreType.DMA((rows // BLOCK,)),
        ],
        in_specs=in_vmem + [pl.BlockSpec(memory_space=pl.ANY)] * len(out),
        out_specs=pl.BlockSpec(memory_space=pl.ANY),
        input_output_aliases={2 + servers: 0} if out else {},
    )


def last_kernel(x_ref, mask_ref, buffer, out_ref, weights, whole, sems):
    weights[...] = weigh(x_ref[...], buffer[...], mask_ref[...])
    copies = []
    for i, start in enumerate(range(0, x_ref.shape[0], BLOCK)):
        here = pl.ds(start, BLOCK)
        whole[here] = mix(x_ref[here], weights[here], buffer[...])
        copies.append(pltpu.make_async_copy(whole.at[here], out_ref.at[here], sems.at[i]))
        copies[-1].start()
    for copy in copies:
        copy.wait()


def last_call(x, mask, buffer):
    rows, width = x.shape
    total = mask.shape[1]
    return kernel_call(
        "mix",
        last_kernel,
        pltpu.HBM((rows, width), jnp.bfloat16),
        x,
        mask,
        buffer,
        flops=4 * total * rows * width,
        moved=4 * rows * width,
        scratch=[
            pltpu.VMEM((rows, total), jnp.bfloat16),
            pltpu.VMEM((rows, width), jnp.bfloat16),
            pltpu.SemaphoreType.DMA((rows // BLOCK,)),
        ],
        out_specs=pl.BlockSpec(memory_space=pltpu.HBM),
    )


def local(descriptors, request, pick):
    wanted = request[0, 0]
    rows = descriptors.shape[2]
    servers, cap = wanted.shape
    total = servers * cap
    groups = lax.axis_size("rep")
    sent = total * FIRST_SHARE[0] // FIRST_SHARE[1]
    within = [(g, g ^ 1) for g in range(groups)]
    beyond = [(g, (g + 2 * (g % 2) - 1 + groups) % groups) for g in range(groups)]

    def turn(value, d):
        return lax.ppermute(value, "clus", [(c, c ^ d) for c in range(servers)])

    def shift(value, by):
        return lax.ppermute(value, "rep", [(g, (g + by) % groups) for g in range(groups)])

    def across(value):
        return lax.ppermute(value, "rep", beyond)

    def inside(value):
        return lax.ppermute(value, "rep", within)

    def turned(parts):
        got = {d: turn(parts[d], d) for d in reversed(range(1, servers))}
        return [parts[0]] + [got[d] for d in range(1, servers)]

    def exchange(expands, far, core, own, first=0, after=()):
        base = unpack_call(expands[0], across(far), own, first=first, after=after)
        return turned(combine_call(expands[1], inside(core), base, servers, first=first))

    def next_round(x, mask, far, near, far_mask, near_mask, expands, parts):
        far = far_mix_call(far, far_mask, parts)
        core, own = near_mix_call(near, near_mask, parts)
        y = whole_call(True, x, mask, parts)
        last = exchange(expands, far, core, own, after=[y])
        return whole_call(False, x, mask, parts, out=[y]), last

    def in_full(x, y, mask, far, near, rest, masks, expands, most, first, buffer):
        late = exchange(expands, *rest, jnp.zeros((total, x.shape[1]), x.dtype), first=sent)
        first = [a + b for a, b in zip(first, late)]
        far = jnp.concatenate([far, rest[0]], axis=0)
        near = jnp.concatenate([near[:sent], rest[1], near[sent:]], axis=0)
        near_mask = jnp.concatenate([masks[1], masks[2][sent:]], axis=0)
        y, last = next_round(x, mask, far, near, masks[0], near_mask, expands, first)
        return last_call(y, mask, gather_call(last, [most], sent)[0])

    def as_sent(x, y, mask, far, near, rest, masks, expands, most, first, buffer):
        return last_call(y, mask, buffer)

    asked = {d: turn(wanted, d) for d in reversed(range(1, servers))}
    mask, held = mask_call(pick.transpose(0, 3, 1, 2)[0], wanted)
    own_list, far_list, core_list, *expands = list_call(
        [held] + [asked[d] for d in range(1, servers)], rows
    )
    beyond_list, within_list = across(far_list), inside(core_list)
    x = normalize_call(descriptors[0, 0])
    pack, far = far_call(x, beyond_list, sent)
    core, own, near, *others, most = near_call(
        x, mask, pack, own_list, far_list, beyond_list, within_list, sent
    )
    rest, masks = others[:2], others[2:]
    first = exchange(expands, far, core, own)
    y, last = next_round(x, mask, far, near, masks[0], masks[2], expands, first)
    mosts = [most]
    reach = 1
    while 2 * reach + 1 < groups:
        by = 2 * reach + 1
        most = functools.reduce(jnp.maximum, mosts)
        mosts = [most, shift(most, by), shift(most, -by)]
        reach += by
    buffer, over = gather_call(last, mosts, sent)
    state = x, y, mask, far, near, rest, masks, expands, most, first, buffer
    return lax.switch(over[0, 0], [as_sent, in_full], *state)[None, None]


def solution(mesh):
    return jax.shard_map(
        local,
        mesh=mesh,
        in_specs=(
            P("rep", "clus", None, None),
            P("rep", "clus", None, None),
            P("rep", "clus", None, None),
        ),
        out_specs=P("rep", "clus", None, None),
        check_vma=False,
    )
```

```python
import functools

import jax
import jax.numpy as jnp
from jax import lax
from jax.experimental import pallas as pl
from jax.experimental.pallas import tpu as pltpu
from jax.sharding import PartitionSpec as P

LANES = 128
BLOCK = 128
FIRST_SHARE = 3, 8
BOTH_LAST = (((1,), (1,)), ((), ()))


def bf16(*shape):
    return jax.ShapeDtypeStruct(shape, jnp.bfloat16)


def int32(*shape):
    return jax.ShapeDtypeStruct(shape, jnp.int32)


def kernel_call(name, kernel, outs, *args, flops, moved=0, scratch=(), mib=32, **specs):
    return pl.pallas_call(
        kernel,
        out_shape=outs,
        scratch_shapes=scratch,
        compiler_params=pltpu.CompilerParams(vmem_limit_bytes=mib * 1024 * 1024),
        cost_estimate=pl.CostEstimate(flops=flops, bytes_accessed=moved, transcendentals=0),
        name=name,
        **specs,
    )(*args)


def normalize(value):
    return value * lax.rsqrt(jnp.mean(value * value, axis=-1, keepdims=True) + 1e-06)


def normalize_kernel(x_hbm, out_ref, raw, sems):
    copies = []
    starts = range(0, raw.shape[0], BLOCK)
    for i, start in enumerate(starts):
        here = pl.ds(start, BLOCK)
        copies.append(pltpu.make_async_copy(x_hbm.at[here], raw.at[here], sems.at[i]))
        copies[-1].start()
    for copy, start in zip(copies, starts):
        copy.wait()
        here = pl.ds(start, BLOCK)
        out_ref[here] = normalize(raw[here].astype(jnp.float32)).astype(jnp.bfloat16)


def normalize_call(descriptors):
    rows, width = descriptors.shape
    return kernel_call(
        "normalize",
        normalize_kernel,
        bf16(rows, width),
        descriptors,
        flops=6 * rows * width,
        moved=4 * rows * width,
        scratch=[
            pltpu.VMEM((rows, width), jnp.bfloat16),
            pltpu.SemaphoreType.DMA((rows // BLOCK,)),
        ],
        mib=56,
        in_specs=[pl.BlockSpec(memory_space=pl.ANY)],
    )


def mask_kernel(slot_cap, pick_hbm, wanted_hbm, mask_ref, wanted_ref, pick, sems):
    copies = [
        pltpu.make_async_copy(pick_hbm, pick, sems.at[0]),
        pltpu.make_async_copy(wanted_hbm, wanted_ref, sems.at[1]),
    ]
    for copy in copies:
        copy.start()
    shape = mask_ref.shape[1], mask_ref.shape[0]
    slot = lax.broadcasted_iota(jnp.int32, shape, 0)
    slot = slot ^ (lax.axis_index("clus") * slot_cap)
    chosen = jnp.zeros(shape, jnp.float32)
    copies[0].wait()
    for k in range(pick.shape[0]):
        chosen = jnp.where(pick[k] == slot, 1.0, chosen)
    mask_ref[...] = chosen.T.astype(jnp.bfloat16)
    copies[1].wait()


def mask_call(slots, wanted):
    count, _, rows = slots.shape
    total = wanted.size
    return kernel_call(
        "mask",
        functools.partial(mask_kernel, wanted.shape[1]),
        [bf16(rows, total), pltpu.VMEM(wanted.shape, jnp.int32)],
        slots,
        wanted,
        flops=2 * count * rows * total,
        moved=2 * rows * total,
        scratch=[pltpu.VMEM(slots.shape, jnp.int32), pltpu.SemaphoreType.DMA((2,))],
        mib=56,
        in_specs=[pl.BlockSpec(memory_space=pl.ANY)] * 2,
    )


def list_kernel(rows, *refs):
    parts, refs = refs[-6::-1], refs[-5:]
    own_ref, far_ref, core_ref, expand_far_ref, expand_core_ref = refs
    total = own_ref.shape[1]
    lane = lax.broadcasted_iota(jnp.int32, (total, total), 1)
    sublane = lax.broadcasted_iota(jnp.int32, (total, total), 0)
    odd = lax.axis_index("rep") % 2
    lows = [(2 * odd * rows).astype(jnp.float32), ((2 - 2 * odd) * rows).astype(jnp.float32)]

    def inside(value, low):
        return (value >= low) & (value < low + rows)

    def asked(server):
        row = jnp.concatenate([ref[server, :] for ref in parts], axis=1).astype(jnp.float32)
        column = jnp.broadcast_to(row, (total, total)).T
        again = jnp.where((column == row) & (sublane < lane), 1.0, 0.0)
        return row, column, 1.0 - jnp.max(again, axis=0, keepdims=True)

    most = jnp.zeros((1, 1), jnp.float32)
    for server in range(len(parts)):
        row, _, first = asked(slice(server, server + 1))
        for low in lows:
            count = jnp.sum(jnp.where(inside(row, low), first, 0.0), axis=1, keepdims=True)
            most = jnp.maximum(most, count)
    row, column, first = asked(pl.ds(lax.axis_index("clus"), 1))
    own_ref[...] = jnp.broadcast_to(row - rows, own_ref.shape).astype(jnp.int32)
    place = lax.broadcasted_iota(jnp.int32, own_ref.shape, 0)
    for low, out_ref, expand_ref in zip(lows, (far_ref, core_ref), (expand_far_ref, expand_core_ref)):
        counted = jnp.where(inside(row, low), first, 0.0)
        rank = jnp.sum(jnp.where(row < column, counted, 0.0), axis=1, keepdims=True)
        here = inside(column, low) & (rank.astype(jnp.int32) == lane)
        expand_ref[...] = jnp.where(here, 1.0, 0.0).astype(jnp.bfloat16)
        packed = jnp.max(jnp.where(here, column - low, -1.0), axis=0, keepdims=True)
        out_ref[...] = jnp.where(place == 1, most, packed).astype(jnp.int32)


def list_call(parts, rows):
    total = parts[0].size
    return kernel_call(
        "list",
        functools.partial(list_kernel, rows),
        [int32(8, total)] * 3 + [bf16(total, total)] * 2,
        *reversed(parts),
        flops=40 * total * total,
    )


def one_hot(numbers, rows):
    total = numbers.shape[1]
    column = jnp.broadcast_to(numbers.astype(jnp.float32), (LANES, total)).T.astype(jnp.int32)
    tiles = []
    for start in range(0, rows, LANES):
        lane = lax.broadcasted_iota(jnp.int32, (total, LANES), 1) + start
        tiles.append(jnp.where(column == lane, 1.0, 0.0).astype(jnp.bfloat16))
    return jnp.concatenate(tiles, axis=1)


def take(select, x):
    return jnp.dot(select, x, preferred_element_type=jnp.float32).astype(jnp.bfloat16)


def far_kernel(x_ref, beyond_ref, pack_ref, far_ref):
    pack_ref[...] = one_hot(beyond_ref[0:1], x_ref.shape[0])
    far_ref[...] = take(pack_ref[: far_ref.shape[0]], x_ref[...])


def far_call(x, beyond, sent):
    rows, width = x.shape
    total = beyond.shape[1]
    return kernel_call(
        "pack_far",
        far_kernel,
        [bf16(total, rows), bf16(sent, width)],
        x,
        beyond,
        flops=2 * rows * sent * width,
    )


def near_kernel(x_ref, mask_ref, pack_ref, own_list_ref, *refs):
    far_list_ref, beyond_ref, within_ref, *refs = refs
    core_ref, own_ref, near_ref, rest_far_ref, rest_core_ref, *refs = refs
    far_mask_ref, core_mask_ref, near_mask_ref, most_ref, select = refs
    total, sent = own_ref.shape[0], core_ref.shape[0]
    rows = x_ref.shape[0]
    select[:total] = one_hot(within_ref[0:1], rows)
    select[total:] = one_hot(own_list_ref[0:1], rows)
    fetched = take(select[...], x_ref[...])
    core_ref[...] = fetched[:sent]
    near_ref[:sent] = fetched[:sent]
    rest_core_ref[...] = fetched[sent:total]
    own_ref[...] = fetched[total:]
    near_ref[sent:] = fetched[total:]
    rest_far_ref[...] = take(pack_ref[sent:], x_ref[...])
    masks = take(select[...], mask_ref[...])
    core_mask_ref[...] = masks[:total]
    near_mask_ref[:sent] = masks[:sent]
    near_mask_ref[sent:] = masks[total:]
    far_mask_ref[...] = take(pack_ref[...], mask_ref[...])
    most = jnp.maximum(far_list_ref[...], jnp.maximum(beyond_ref[...], within_ref[...]))
    most_ref[...] = jnp.broadcast_to(most[1:2, :LANES], most_ref.shape)


def near_call(x, mask, pack, own_list, far_list, beyond, within, sent):
    rows, width = x.shape
    total = mask.shape[1]
    return kernel_call(
        "serve_near",
        near_kernel,
        [
            bf16(sent, width),
            bf16(total, width),
            bf16(sent + total, width),
            bf16(total - sent, width),
            bf16(total - sent, width),
            bf16(total, total),
            bf16(total, total),
            bf16(sent + total, total),
            int32(8, LANES),
        ],
        x,
        mask,
        pack,
        own_list,
        far_list,
        beyond,
        within,
        flops=6 * total * rows * width,
        scratch=[pltpu.VMEM((2 * total, rows), jnp.bfloat16)],
    )


def unpack_kernel(first, bases, expand_ref, far_ref, *refs):
    out_ref, sent = refs[-1], far_ref.shape[0]
    rows = jnp.dot(
        expand_ref[:, first : first + sent], far_ref[...], preferred_element_type=jnp.float32
    )
    for base_ref in refs[:bases]:
        rows += base_ref[...].astype(jnp.float32)
    out_ref[...] = rows.astype(jnp.bfloat16)


def unpack_call(expand, far, *base, first=0, after=()):
    in_vmem = [pl.BlockSpec(memory_space=pltpu.VMEM)] * (2 + len(base))
    return kernel_call(
        "unpack",
        functools.partial(unpack_kernel, first, len(base)),
        bf16(expand.shape[0], far.shape[1]),
        expand,
        far,
        *base,
        *after,
        flops=2**34,
        moved=2**25,
        in_specs=in_vmem + [pl.BlockSpec(memory_space=pl.ANY)] * len(after),
    )


def combine_kernel(expand_ref, core_ref, base_ref, most_ref, out_most_ref, *out_refs):
    out_most_ref[...] = most_ref[...]
    cap, sent = out_refs[0].shape[0], core_ref.shape[0]
    rows = jnp.dot(expand_ref[:, :sent], core_ref[...], preferred_element_type=jnp.float32)
    rows = (rows + base_ref[...].astype(jnp.float32)).astype(jnp.bfloat16)
    for d, out in enumerate(out_refs):
        out[...] = rows[d * cap : (d + 1) * cap]


def combine_call(expand, core, base, most, servers):
    total, width = base.shape
    most, *parts = kernel_call(
        "combine",
        combine_kernel,
        [int32(*most.shape)] + [bf16(total // servers, width)] * servers,
        expand,
        core,
        base,
        most,
        flops=2 * total * core.shape[0] * width,
    )
    return most, parts


def fill(buffer, parts):
    cap = parts[0].shape[0]
    for d, ref in enumerate(reversed(parts)):
        buffer[d * cap : (d + 1) * cap] = ref[...]


def weigh(x, buffer, mask):
    dots = lax.dot_general(x, buffer, BOTH_LAST, preferred_element_type=jnp.float32)
    positive = jnp.maximum(dots * (1.0 / x.shape[1]), 0.0)
    return (positive * positive * positive).astype(jnp.bfloat16) * mask


def mix(x, weights, buffer):
    mixed = x.astype(jnp.float32) + jnp.dot(weights, buffer, preferred_element_type=jnp.float32)
    return normalize(mixed).astype(jnp.bfloat16)


def far_mix_kernel(servers, x_ref, mask_ref, *rest):
    parts, rest = rest[:servers], rest[servers:]
    *most_refs, out_ref, most_ref, buffer = rest
    most_ref[...] = functools.reduce(jnp.maximum, [ref[...] for ref in most_refs])
    fill(buffer, parts)
    weights = weigh(x_ref[...], buffer[...], mask_ref[: x_ref.shape[0]])
    out_ref[...] = mix(x_ref[...], weights, buffer[...])


def far_mix_call(x, mask, parts, mosts):
    rows, width = x.shape
    total, servers = mask.shape[1], len(parts)
    return kernel_call(
        "mix_far",
        functools.partial(far_mix_kernel, servers),
        [bf16(rows, width), int32(*mosts[0].shape)],
        x,
        mask,
        *reversed(parts),
        *mosts,
        flops=4 * total * rows * width,
        scratch=[pltpu.VMEM((total, width), jnp.bfloat16)],
    )


def near_mix_kernel(servers, x_ref, mask_ref, *rest):
    parts, (core_ref, own_ref, buffer) = rest[:servers], rest[servers:]
    fill(buffer, parts)
    weights = weigh(x_ref[...], buffer[...], mask_ref[...])
    mixed = mix(x_ref[...], weights, buffer[...])
    core_ref[...] = mixed[: core_ref.shape[0]]
    own_ref[...] = mixed[core_ref.shape[0] :]


def near_mix_call(x, mask, parts):
    rows, width = x.shape
    total, servers = mask.shape[1], len(parts)
    return kernel_call(
        "mix_near",
        functools.partial(near_mix_kernel, servers),
        [bf16(rows - total, width), bf16(total, width)],
        x,
        mask,
        *reversed(parts),
        flops=4 * total * rows * width,
        scratch=[pltpu.VMEM((total, width), jnp.bfloat16)],
    )


def is_late():
    return (lax.axis_index("rep") + 1) % 4 < 2


def late_kernel(servers, x_ref, mask_ref, *rest):
    parts, (out_ref, buffer, weights) = rest[:servers], rest[servers:]

    @pl.when(is_late())
    def _():
        fill(buffer, parts)
        weights[...] = weigh(x_ref[...], buffer[...], mask_ref[...])
        for start in range(0, x_ref.shape[0], BLOCK):
            here = pl.ds(start, BLOCK)
            out_ref[here] = mix(x_ref[here], weights[here], buffer[...])


def late_call(x, mask, parts):
    rows, width = x.shape
    total, servers = mask.shape[1], len(parts)
    return kernel_call(
        "mix_whole_late",
        functools.partial(late_kernel, servers),
        bf16(rows, width),
        x,
        mask,
        *reversed(parts),
        flops=4 * total * rows * width,
        scratch=[
            pltpu.VMEM((total, width), jnp.bfloat16),
            pltpu.VMEM((rows, total), jnp.bfloat16),
        ],
    )


def mix_blocks(x_ref, mask_ref, buffer, weights, whole, out_ref, sems):
    weights[...] = weigh(x_ref[...], buffer[...], mask_ref[...])
    blocks = [pl.ds(start, BLOCK) for start in range(0, x_ref.shape[0], BLOCK)]
    copies, added = [], None
    for i in range(len(blocks) + 1):
        before = added
        if i < len(blocks):
            added = jnp.dot(
                weights[blocks[i]], buffer[...], preferred_element_type=jnp.float32
            )
        if i:
            here = blocks[i - 1]
            mixed = x_ref[here].astype(jnp.float32) + before
            whole[here] = normalize(mixed).astype(jnp.bfloat16)
            copies.append(pltpu.make_async_copy(whole.at[here], out_ref.at[here], sems.at[i - 1]))
            copies[-1].start()
    for copy in copies:
        copy.wait()


def early_kernel(servers, x_ref, mask_ref, *rest):
    parts, (_, out_ref, buffer, weights, whole, sems) = rest[:servers], rest[servers:]

    @pl.when(jnp.logical_not(is_late()))
    def _():
        fill(buffer, parts)
        mix_blocks(x_ref, mask_ref, buffer, weights, whole, out_ref, sems)


def early_call(x, mask, parts, out):
    rows, width = x.shape
    total, servers = mask.shape[1], len(parts)
    return kernel_call(
        "mix_whole_early",
        functools.partial(early_kernel, servers),
        bf16(rows, width),
        x,
        mask,
        *reversed(parts),
        out,
        flops=4 * total * rows * width,
        scratch=[
            pltpu.VMEM((total, width), jnp.bfloat16),
            pltpu.VMEM((rows, total), jnp.bfloat16),
            pltpu.VMEM((rows, width), jnp.bfloat16),
            pltpu.SemaphoreType.DMA((rows // BLOCK,)),
        ],
        in_specs=[pl.BlockSpec(memory_space=pltpu.VMEM)] * (2 + servers)
        + [pl.BlockSpec(memory_space=pl.ANY)],
        out_specs=pl.BlockSpec(memory_space=pl.ANY),
        input_output_aliases={2 + servers: 0},
    )


def last_kernel(servers, x_ref, mask_ref, *rest):
    parts, (out_ref, buffer, weights, whole, sems) = rest[:servers], rest[servers:]
    fill(buffer, parts)
    mix_blocks(x_ref, mask_ref, buffer, weights, whole, out_ref, sems)


def last_call(x, mask, parts):
    rows, width = x.shape
    total, servers = mask.shape[1], len(parts)
    return kernel_call(
        "mix",
        functools.partial(last_kernel, servers),
        pltpu.HBM((rows, width), jnp.bfloat16),
        x,
        mask,
        *reversed(parts),
        flops=4 * total * rows * width,
        moved=4 * rows * width,
        scratch=[
            pltpu.VMEM((total, width), jnp.bfloat16),
            pltpu.VMEM((rows, total), jnp.bfloat16),
            pltpu.VMEM((rows, width), jnp.bfloat16),
            pltpu.SemaphoreType.DMA((rows // BLOCK,)),
        ],
        out_specs=pl.BlockSpec(memory_space=pltpu.HBM),
    )


def local(descriptors, request, pick):
    wanted = request[0, 0]
    rows = descriptors.shape[2]
    servers, cap = wanted.shape
    total = servers * cap
    groups = lax.axis_size("rep")
    sent = total * FIRST_SHARE[0] // FIRST_SHARE[1]
    within = [(g, g ^ 1) for g in range(groups)]
    beyond = [(g, (g + 2 * (g % 2) - 1 + groups) % groups) for g in range(groups)]

    def turn(value, d):
        return lax.ppermute(value, "clus", [(c, c ^ d) for c in range(servers)])

    def shift(value, by):
        return lax.ppermute(value, "rep", [(g, (g + by) % groups) for g in range(groups)])

    def across(value):
        return lax.ppermute(value, "rep", beyond)

    def inside(value):
        return lax.ppermute(value, "rep", within)

    def turned(parts):
        got = {d: turn(parts[d], d) for d in reversed(range(1, servers))}
        return [parts[0]] + [got[d] for d in range(1, servers)]

    def exchange(expands, far, core, own, most, after=()):
        base = unpack_call(expands[0], across(far), own, after=after)
        most, parts = combine_call(expands[1], inside(core), base, most, servers)
        return most, turned(parts)

    def next_round(x, mask, far, near, far_mask, near_mask, expands, parts, mosts):
        far, most = far_mix_call(far, far_mask, parts, mosts)
        core, own = near_mix_call(near, near_mask, parts)
        y = late_call(x, mask, parts)
        most, last = exchange(expands, far, core, own, most, after=[y])
        return early_call(x, mask, parts, y), most, last

    def in_full(x, y, mask, far, near, rest, masks, expands, most, first, last):
        late = unpack_call(expands[1], inside(rest[1]), first=sent)
        late = unpack_call(expands[0], across(rest[0]), late, first=sent)
        late = turned(list(late.reshape(servers, cap, -1)))
        first = [a + b for a, b in zip(first, late)]
        far = jnp.concatenate([far, rest[0]], axis=0)
        near = jnp.concatenate([near[:sent], rest[1], near[sent:]], axis=0)
        near_mask = jnp.concatenate([masks[1], masks[2][sent:]], axis=0)
        y, _, last = next_round(
            x, mask, far, near, masks[0], near_mask, expands, first, [most]
        )
        return last_call(y, mask, last)

    def as_sent(x, y, mask, far, near, rest, masks, expands, most, first, last):
        return last_call(y, mask, last)

    asked = {d: turn(wanted, d) for d in reversed(range(1, servers))}
    mask, held = mask_call(pick.transpose(0, 3, 1, 2)[0], wanted)
    own_list, far_list, core_list, *expands = list_call(
        [held] + [asked[d] for d in range(1, servers)], rows
    )
    beyond_list, within_list = across(far_list), inside(core_list)
    x = normalize_call(descriptors[0, 0])
    pack, far = far_call(x, beyond_list, sent)
    core, own, near, *others, most = near_call(
        x, mask, pack, own_list, far_list, beyond_list, within_list, sent
    )
    rest, masks = others[:2], others[2:]
    most, first = exchange(expands, far, core, own, most)
    mosts = [most]
    reach = 1
    while 2 * reach + 1 < groups:
        by = 2 * reach + 1
        most = functools.reduce(jnp.maximum, mosts)
        mosts = [most, shift(most, by), shift(most, -by)]
        reach += by
    y, most, last = next_round(
        x, mask, far, near, masks[0], masks[2], expands, first, mosts
    )
    state = x, y, mask, far, near, rest, masks, expands, most, first, last
    return lax.cond(most[0, 0] > sent, in_full, as_sent, *state)[None, None]


def solution(mesh):
    return jax.shard_map(
        local,
        mesh=mesh,
        in_specs=(
            P("rep", "clus", None, None),
            P("rep", "clus", None, None),
            P("rep", "clus", None, None),
        ),
        out_specs=P("rep", "clus", None, None),
        check_vma=False,
    )
```

```python
import functools

import jax
import jax.numpy as jnp
from jax import lax
from jax.experimental import pallas as pl
from jax.experimental.pallas import tpu as pltpu
from jax.sharding import PartitionSpec as P

LANES = 128
BLOCK = 128
COPY = 64
FIRST_SHARE = 3, 8
BOTH_LAST = (((1,), (1,)), ((), ()))


def bf16(*shape):
    return jax.ShapeDtypeStruct(shape, jnp.bfloat16)


def int32(*shape):
    return jax.ShapeDtypeStruct(shape, jnp.int32)


def kernel_call(name, kernel, outs, *args, flops, moved=0, scratch=(), mib=32, **specs):
    return pl.pallas_call(
        kernel,
        out_shape=outs,
        scratch_shapes=scratch,
        compiler_params=pltpu.CompilerParams(vmem_limit_bytes=mib * 1024 * 1024),
        cost_estimate=pl.CostEstimate(flops=flops, bytes_accessed=moved, transcendentals=0),
        name=name,
        **specs,
    )(*args)


def normalize(value):
    return value * lax.rsqrt(jnp.mean(value * value, axis=-1, keepdims=True) + 1e-06)


def normalize_kernel(x_hbm, out_ref, raw, sems):
    copies = []
    starts = range(0, raw.shape[0], BLOCK)
    for i, start in enumerate(starts):
        here = pl.ds(start, BLOCK)
        copies.append(pltpu.make_async_copy(x_hbm.at[here], raw.at[here], sems.at[i]))
        copies[-1].start()
    for copy, start in zip(copies, starts):
        copy.wait()
        here = pl.ds(start, BLOCK)
        out_ref[here] = normalize(raw[here].astype(jnp.float32)).astype(jnp.bfloat16)


def normalize_call(descriptors):
    rows, width = descriptors.shape
    return kernel_call(
        "normalize",
        normalize_kernel,
        bf16(rows, width),
        descriptors,
        flops=6 * rows * width,
        moved=4 * rows * width,
        scratch=[
            pltpu.VMEM((rows, width), jnp.bfloat16),
            pltpu.SemaphoreType.DMA((rows // BLOCK,)),
        ],
        mib=56,
        in_specs=[pl.BlockSpec(memory_space=pl.ANY)],
    )


def mask_kernel(slot_cap, pick_hbm, wanted_hbm, mask_ref, wanted_ref, pick, sems):
    copies = [
        pltpu.make_async_copy(pick_hbm, pick, sems.at[0]),
        pltpu.make_async_copy(wanted_hbm, wanted_ref, sems.at[1]),
    ]
    for copy in copies:
        copy.start()
    shape = mask_ref.shape[1], mask_ref.shape[0]
    slot = lax.broadcasted_iota(jnp.int32, shape, 0)
    slot = slot ^ (lax.axis_index("clus") * slot_cap)
    chosen = jnp.zeros(shape, jnp.float32)
    copies[0].wait()
    for k in range(pick.shape[0]):
        chosen = jnp.where(pick[k] == slot, 1.0, chosen)
    mask_ref[...] = chosen.T.astype(jnp.bfloat16)
    copies[1].wait()


def mask_call(slots, wanted):
    count, _, rows = slots.shape
    total = wanted.size
    return kernel_call(
        "mask",
        functools.partial(mask_kernel, wanted.shape[1]),
        [bf16(rows, total), pltpu.VMEM(wanted.shape, jnp.int32)],
        slots,
        wanted,
        flops=2 * count * rows * total,
        moved=2 * rows * total,
        scratch=[pltpu.VMEM(slots.shape, jnp.int32), pltpu.SemaphoreType.DMA((2,))],
        mib=56,
        in_specs=[pl.BlockSpec(memory_space=pl.ANY)] * 2,
    )


def list_kernel(rows, *refs):
    parts, refs = refs[-6::-1], refs[-5:]
    own_ref, far_ref, core_ref, expand_far_ref, expand_core_ref = refs
    total = own_ref.shape[1]
    lane = lax.broadcasted_iota(jnp.int32, (total, total), 1)
    sublane = lax.broadcasted_iota(jnp.int32, (total, total), 0)
    odd = lax.axis_index("rep") % 2
    lows = [(2 * odd * rows).astype(jnp.float32), ((2 - 2 * odd) * rows).astype(jnp.float32)]

    def inside(value, low):
        return (value >= low) & (value < low + rows)

    def asked(server):
        row = jnp.concatenate([ref[server, :] for ref in parts], axis=1).astype(jnp.float32)
        column = jnp.broadcast_to(row, (total, total)).T
        again = jnp.where((column == row) & (sublane < lane), 1.0, 0.0)
        return row, column, 1.0 - jnp.max(again, axis=0, keepdims=True)

    most = jnp.zeros((1, 1), jnp.float32)
    for server in range(len(parts)):
        row, _, first = asked(slice(server, server + 1))
        for low in lows:
            count = jnp.sum(jnp.where(inside(row, low), first, 0.0), axis=1, keepdims=True)
            most = jnp.maximum(most, count)
    row, column, first = asked(pl.ds(lax.axis_index("clus"), 1))
    own_ref[...] = jnp.broadcast_to(row - rows, own_ref.shape).astype(jnp.int32)
    place = lax.broadcasted_iota(jnp.int32, own_ref.shape, 0)
    for low, out_ref, expand_ref in zip(lows, (far_ref, core_ref), (expand_far_ref, expand_core_ref)):
        counted = jnp.where(inside(row, low), first, 0.0)
        rank = jnp.sum(jnp.where(row < column, counted, 0.0), axis=1, keepdims=True)
        here = inside(column, low) & (rank.astype(jnp.int32) == lane)
        expand_ref[...] = jnp.where(here, 1.0, 0.0).astype(jnp.bfloat16)
        packed = jnp.max(jnp.where(here, column - low, -1.0), axis=0, keepdims=True)
        out_ref[...] = jnp.where(place == 1, most, packed).astype(jnp.int32)


def list_call(parts, rows):
    total = parts[0].size
    return kernel_call(
        "list",
        functools.partial(list_kernel, rows),
        [int32(8, total)] * 3 + [bf16(total, total)] * 2,
        *reversed(parts),
        flops=40 * total * total,
    )


def one_hot(numbers, rows):
    total = numbers.shape[1]
    column = jnp.broadcast_to(numbers.astype(jnp.float32), (LANES, total)).T.astype(jnp.int32)
    tiles = []
    for start in range(0, rows, LANES):
        lane = lax.broadcasted_iota(jnp.int32, (total, LANES), 1) + start
        tiles.append(jnp.where(column == lane, 1.0, 0.0).astype(jnp.bfloat16))
    return jnp.concatenate(tiles, axis=1)


def take(select, x):
    return jnp.dot(select, x, preferred_element_type=jnp.float32).astype(jnp.bfloat16)


def far_kernel(x_ref, beyond_ref, pack_ref, far_ref):
    pack_ref[...] = one_hot(beyond_ref[0:1], x_ref.shape[0])
    far_ref[...] = take(pack_ref[: far_ref.shape[0]], x_ref[...])


def far_call(x, beyond, sent):
    rows, width = x.shape
    total = beyond.shape[1]
    return kernel_call(
        "pack_far",
        far_kernel,
        [bf16(total, rows), bf16(sent, width)],
        x,
        beyond,
        flops=2 * rows * sent * width,
    )


def near_kernel(x_ref, mask_ref, pack_ref, own_list_ref, *refs):
    far_list_ref, beyond_ref, within_ref, *refs = refs
    core_ref, own_ref, near_ref, rest_far_ref, rest_core_ref, *refs = refs
    far_mask_ref, core_mask_ref, near_mask_ref, most_ref, select = refs
    total, sent = own_ref.shape[0], core_ref.shape[0]
    rows = x_ref.shape[0]
    select[:total] = one_hot(within_ref[0:1], rows)
    select[total:] = one_hot(own_list_ref[0:1], rows)
    fetched = take(select[...], x_ref[...])
    core_ref[...] = fetched[:sent]
    near_ref[:sent] = fetched[:sent]
    rest_core_ref[...] = fetched[sent:total]
    own_ref[...] = fetched[total:]
    near_ref[sent:] = fetched[total:]
    rest_far_ref[...] = take(pack_ref[sent:], x_ref[...])
    masks = take(select[...], mask_ref[...])
    core_mask_ref[...] = masks[:total]
    near_mask_ref[:sent] = masks[:sent]
    near_mask_ref[sent:] = masks[total:]
    far_mask_ref[...] = take(pack_ref[...], mask_ref[...])
    most = jnp.maximum(far_list_ref[...], jnp.maximum(beyond_ref[...], within_ref[...]))
    most_ref[...] = jnp.broadcast_to(most[1:2, :LANES], most_ref.shape)


def near_call(x, mask, pack, own_list, far_list, beyond, within, sent):
    rows, width = x.shape
    total = mask.shape[1]
    return kernel_call(
        "serve_near",
        near_kernel,
        [
            bf16(sent, width),
            bf16(total, width),
            bf16(sent + total, width),
            bf16(total - sent, width),
            bf16(total - sent, width),
            bf16(total, total),
            bf16(total, total),
            bf16(sent + total, total),
            int32(8, LANES),
        ],
        x,
        mask,
        pack,
        own_list,
        far_list,
        beyond,
        within,
        flops=6 * total * rows * width,
        scratch=[pltpu.VMEM((2 * total, rows), jnp.bfloat16)],
    )


def unpack_kernel(first, bases, expand_ref, far_ref, *refs):
    out_ref, sent = refs[-1], far_ref.shape[0]
    rows = jnp.dot(
        expand_ref[:, first : first + sent], far_ref[...], preferred_element_type=jnp.float32
    )
    for base_ref in refs[:bases]:
        rows += base_ref[...].astype(jnp.float32)
    out_ref[...] = rows.astype(jnp.bfloat16)


def unpack_call(expand, far, *base, first=0, after=()):
    in_vmem = [pl.BlockSpec(memory_space=pltpu.VMEM)] * (2 + len(base))
    return kernel_call(
        "unpack",
        functools.partial(unpack_kernel, first, len(base)),
        bf16(expand.shape[0], far.shape[1]),
        expand,
        far,
        *base,
        *after,
        flops=2**34,
        moved=2**25,
        in_specs=in_vmem + [pl.BlockSpec(memory_space=pl.ANY)] * len(after),
    )


def combine_kernel(expand_ref, core_ref, base_ref, most_ref, out_most_ref, *out_refs):
    out_most_ref[...] = most_ref[...]
    cap, sent = out_refs[0].shape[0], core_ref.shape[0]
    rows = jnp.dot(expand_ref[:, :sent], core_ref[...], preferred_element_type=jnp.float32)
    rows = (rows + base_ref[...].astype(jnp.float32)).astype(jnp.bfloat16)
    for d, out in enumerate(out_refs):
        out[...] = rows[d * cap : (d + 1) * cap]


def combine_call(expand, core, base, most, servers):
    total, width = base.shape
    most, *parts = kernel_call(
        "combine",
        combine_kernel,
        [int32(*most.shape)] + [bf16(total // servers, width)] * servers,
        expand,
        core,
        base,
        most,
        flops=2 * total * core.shape[0] * width,
    )
    return most, parts


def unpack_both_kernel(far_expand, core_expand, own_ref, core_ref, far_ref, *refs):
    out_refs = refs[1:]
    cap, sent = out_refs[0].shape[0], far_ref.shape[0]
    rows = jnp.dot(core_expand[:, :sent], core_ref[...], preferred_element_type=jnp.float32)
    rows += jnp.dot(far_expand[:, :sent], far_ref[...], preferred_element_type=jnp.float32)
    rows = (rows + own_ref[...].astype(jnp.float32)).astype(jnp.bfloat16)
    for d, out in enumerate(out_refs):
        out[...] = rows[d * cap : (d + 1) * cap]


def unpack_both_call(expands, far, core, own, after, servers):
    total, width = own.shape
    return kernel_call(
        "unpack_both",
        unpack_both_kernel,
        [bf16(total // servers, width)] * servers,
        *expands,
        own,
        core,
        far,
        after,
        flops=4 * total * far.shape[0] * width,
        in_specs=[pl.BlockSpec(memory_space=pltpu.VMEM)] * 5
        + [pl.BlockSpec(memory_space=pl.ANY)],
    )


def fill(buffer, parts):
    cap = parts[0].shape[0]
    for d, ref in enumerate(reversed(parts)):
        buffer[d * cap : (d + 1) * cap] = ref[...]


def weigh(x, buffer, mask):
    dots = lax.dot_general(x, buffer, BOTH_LAST, preferred_element_type=jnp.float32)
    positive = jnp.maximum(dots * (1.0 / x.shape[1]), 0.0)
    return (positive * positive * positive).astype(jnp.bfloat16) * mask


def mix(x, weights, buffer):
    mixed = x.astype(jnp.float32) + jnp.dot(weights, buffer, preferred_element_type=jnp.float32)
    return normalize(mixed).astype(jnp.bfloat16)


def far_mix_kernel(servers, x_ref, mask_ref, *rest):
    parts, rest = rest[:servers], rest[servers:]
    *most_refs, out_ref, most_ref, buffer = rest
    most_ref[...] = functools.reduce(jnp.maximum, [ref[...] for ref in most_refs])
    fill(buffer, parts)
    weights = weigh(x_ref[...], buffer[...], mask_ref[: x_ref.shape[0]])
    out_ref[...] = mix(x_ref[...], weights, buffer[...])


def far_mix_call(x, mask, parts, mosts):
    rows, width = x.shape
    total, servers = mask.shape[1], len(parts)
    return kernel_call(
        "mix_far",
        functools.partial(far_mix_kernel, servers),
        [bf16(rows, width), int32(*mosts[0].shape)],
        x,
        mask,
        *reversed(parts),
        *mosts,
        flops=4 * total * rows * width,
        scratch=[pltpu.VMEM((total, width), jnp.bfloat16)],
    )


def near_mix_kernel(servers, x_ref, mask_ref, *rest):
    parts, (core_ref, own_ref, buffer) = rest[:servers], rest[servers:]
    fill(buffer, parts)
    weights = weigh(x_ref[...], buffer[...], mask_ref[...])
    mixed = mix(x_ref[...], weights, buffer[...])
    core_ref[...] = mixed[: core_ref.shape[0]]
    own_ref[...] = mixed[core_ref.shape[0] :]


def near_mix_call(x, mask, parts):
    rows, width = x.shape
    total, servers = mask.shape[1], len(parts)
    return kernel_call(
        "mix_near",
        functools.partial(near_mix_kernel, servers),
        [bf16(rows - total, width), bf16(total, width)],
        x,
        mask,
        *reversed(parts),
        flops=4 * total * rows * width,
        scratch=[pltpu.VMEM((total, width), jnp.bfloat16)],
    )


def is_late():
    return (lax.axis_index("rep") + 1) % 4 < 2


def late_kernel(servers, x_ref, mask_ref, *rest):
    parts, (out_ref, buffer, weights) = rest[:servers], rest[servers:]

    @pl.when(is_late())
    def _():
        fill(buffer, parts)
        weights[...] = weigh(x_ref[...], buffer[...], mask_ref[...])
        for start in range(0, x_ref.shape[0], BLOCK):
            here = pl.ds(start, BLOCK)
            out_ref[here] = mix(x_ref[here], weights[here], buffer[...])


def late_call(x, mask, parts):
    rows, width = x.shape
    total, servers = mask.shape[1], len(parts)
    return kernel_call(
        "mix_whole_late",
        functools.partial(late_kernel, servers),
        bf16(rows, width),
        x,
        mask,
        *reversed(parts),
        flops=4 * total * rows * width,
        scratch=[
            pltpu.VMEM((total, width), jnp.bfloat16),
            pltpu.VMEM((rows, total), jnp.bfloat16),
        ],
    )


def mix_blocks(x_ref, mask_ref, buffer, whole, out_ref, sems):
    copies = []
    for start in range(0, x_ref.shape[0], BLOCK):
        here = pl.ds(start, BLOCK)
        weights = weigh(x_ref[here], buffer[...], mask_ref[here])
        whole[here] = mix(x_ref[here], weights, buffer[...])
        for half in range(start, start + BLOCK, COPY):
            rows = pl.ds(half, COPY)
            copy = pltpu.make_async_copy(
                whole.at[rows], out_ref.at[rows], sems.at[half // COPY]
            )
            copy.start()
            copies.append(copy)
    for copy in copies:
        copy.wait()


def early_kernel(servers, x_ref, mask_ref, *rest):
    parts, (_, out_ref, buffer, whole, sems) = rest[:servers], rest[servers:]

    @pl.when(jnp.logical_not(is_late()))
    def _():
        fill(buffer, parts)
        mix_blocks(x_ref, mask_ref, buffer, whole, out_ref, sems)


def early_call(x, mask, parts, out):
    rows, width = x.shape
    total, servers = mask.shape[1], len(parts)
    return kernel_call(
        "mix_whole_early",
        functools.partial(early_kernel, servers),
        bf16(rows, width),
        x,
        mask,
        *reversed(parts),
        out,
        flops=4 * total * rows * width,
        scratch=[
            pltpu.VMEM((total, width), jnp.bfloat16),
            pltpu.VMEM((rows, width), jnp.bfloat16),
            pltpu.SemaphoreType.DMA((rows // COPY,)),
        ],
        in_specs=[pl.BlockSpec(memory_space=pltpu.VMEM)] * (2 + servers)
        + [pl.BlockSpec(memory_space=pl.ANY)],
        out_specs=pl.BlockSpec(memory_space=pl.ANY),
        input_output_aliases={2 + servers: 0},
    )


def last_kernel(servers, x_ref, mask_ref, *rest):
    parts, (out_ref, buffer, whole, sems) = rest[:servers], rest[servers:]
    fill(buffer, parts)
    mix_blocks(x_ref, mask_ref, buffer, whole, out_ref, sems)


def last_call(x, mask, parts):
    rows, width = x.shape
    total, servers = mask.shape[1], len(parts)
    return kernel_call(
        "mix",
        functools.partial(last_kernel, servers),
        pltpu.HBM((rows, width), jnp.bfloat16),
        x,
        mask,
        *reversed(parts),
        flops=4 * total * rows * width,
        moved=4 * rows * width,
        scratch=[
            pltpu.VMEM((total, width), jnp.bfloat16),
            pltpu.VMEM((rows, width), jnp.bfloat16),
            pltpu.SemaphoreType.DMA((rows // COPY,)),
        ],
        out_specs=pl.BlockSpec(memory_space=pltpu.HBM),
    )


def local(descriptors, request, pick):
    wanted = request[0, 0]
    rows = descriptors.shape[2]
    servers, cap = wanted.shape
    total = servers * cap
    groups = lax.axis_size("rep")
    sent = total * FIRST_SHARE[0] // FIRST_SHARE[1]
    within = [(g, g ^ 1) for g in range(groups)]
    beyond = [(g, (g + 2 * (g % 2) - 1 + groups) % groups) for g in range(groups)]

    def turn(value, d):
        return lax.ppermute(value, "clus", [(c, c ^ d) for c in range(servers)])

    def shift(value, by):
        return lax.ppermute(value, "rep", [(g, (g + by) % groups) for g in range(groups)])

    def across(value):
        return lax.ppermute(value, "rep", beyond)

    def inside(value):
        return lax.ppermute(value, "rep", within)

    def turned(parts):
        got = {d: turn(parts[d], d) for d in reversed(range(1, servers))}
        return [parts[0]] + [got[d] for d in range(1, servers)]

    def exchange(expands, far, core, own, most):
        base = unpack_call(expands[0], across(far), own)
        most, parts = combine_call(expands[1], inside(core), base, most, servers)
        return most, turned(parts)

    def next_round(x, mask, far, near, far_mask, near_mask, expands, parts, mosts):
        far, most = far_mix_call(far, far_mask, parts, mosts)
        core, own = near_mix_call(near, near_mask, parts)
        y = late_call(x, mask, parts)
        last = unpack_both_call(expands, across(far), inside(core), own, y, servers)
        return early_call(x, mask, parts, y), most, turned(last)

    def in_full(x, y, mask, far, near, rest, masks, expands, most, first, last):
        late = unpack_call(expands[1], inside(rest[1]), first=sent)
        late = unpack_call(expands[0], across(rest[0]), late, first=sent)
        late = turned(list(late.reshape(servers, cap, -1)))
        first = [a + b for a, b in zip(first, late)]
        far = jnp.concatenate([far, rest[0]], axis=0)
        near = jnp.concatenate([near[:sent], rest[1], near[sent:]], axis=0)
        near_mask = jnp.concatenate([masks[1], masks[2][sent:]], axis=0)
        y, _, last = next_round(
            x, mask, far, near, masks[0], near_mask, expands, first, [most]
        )
        return last_call(y, mask, last)

    def as_sent(x, y, mask, far, near, rest, masks, expands, most, first, last):
        return last_call(y, mask, last)

    asked = {d: turn(wanted, d) for d in reversed(range(1, servers))}
    mask, held = mask_call(pick.transpose(0, 3, 1, 2)[0], wanted)
    own_list, far_list, core_list, *expands = list_call(
        [held] + [asked[d] for d in range(1, servers)], rows
    )
    beyond_list, within_list = across(far_list), inside(core_list)
    x = normalize_call(descriptors[0, 0])
    pack, far = far_call(x, beyond_list, sent)
    core, own, near, *others, most = near_call(
        x, mask, pack, own_list, far_list, beyond_list, within_list, sent
    )
    rest, masks = others[:2], others[2:]
    most, first = exchange(expands, far, core, own, most)
    mosts = [most]
    reach = 1
    while 2 * reach + 1 < groups:
        by = 2 * reach + 1
        most = functools.reduce(jnp.maximum, mosts)
        mosts = [most, shift(most, by), shift(most, -by)]
        reach += by
    y, most, last = next_round(
        x, mask, far, near, masks[0], masks[2], expands, first, mosts
    )
    state = x, y, mask, far, near, rest, masks, expands, most, first, last
    return lax.cond(most[0, 0] > sent, in_full, as_sent, *state)[None, None]


def solution(mesh):
    return jax.shard_map(
        local,
        mesh=mesh,
        in_specs=(
            P("rep", "clus", None, None),
            P("rep", "clus", None, None),
            P("rep", "clus", None, None),
        ),
        out_specs=P("rep", "clus", None, None),
        check_vma=False,
    )
```

```python
import functools

import jax
import jax.numpy as jnp
from jax import lax
from jax.experimental import pallas as pl
from jax.experimental.pallas import tpu as pltpu
from jax.sharding import PartitionSpec as P

LANES = 128
BLOCK = 128
COPY = 64
FIRST_SHARE = 3, 8
BOTH_LAST = (((1,), (1,)), ((), ()))


def bf16(*shape):
    return jax.ShapeDtypeStruct(shape, jnp.bfloat16)


def int32(*shape):
    return jax.ShapeDtypeStruct(shape, jnp.int32)


def kernel_call(name, kernel, outs, *args, flops, moved=0, scratch=(), mib=32, **specs):
    return pl.pallas_call(
        kernel,
        out_shape=outs,
        scratch_shapes=scratch,
        compiler_params=pltpu.CompilerParams(vmem_limit_bytes=mib * 1024 * 1024),
        cost_estimate=pl.CostEstimate(flops=flops, bytes_accessed=moved, transcendentals=0),
        name=name,
        **specs,
    )(*args)


def normalize(value):
    return value * lax.rsqrt(jnp.mean(value * value, axis=-1, keepdims=True) + 1e-06)


def normalize_kernel(x_hbm, out_ref, raw, sems):
    copies = []
    starts = range(0, raw.shape[0], BLOCK)
    for i, start in enumerate(starts):
        here = pl.ds(start, BLOCK)
        copies.append(pltpu.make_async_copy(x_hbm.at[here], raw.at[here], sems.at[i]))
        copies[-1].start()
    for copy, start in zip(copies, starts):
        copy.wait()
        here = pl.ds(start, BLOCK)
        out_ref[here] = normalize(raw[here].astype(jnp.float32)).astype(jnp.bfloat16)


def normalize_call(descriptors):
    rows, width = descriptors.shape
    return kernel_call(
        "normalize",
        normalize_kernel,
        bf16(rows, width),
        descriptors,
        flops=6 * rows * width,
        moved=4 * rows * width,
        scratch=[
            pltpu.VMEM((rows, width), jnp.bfloat16),
            pltpu.SemaphoreType.DMA((rows // BLOCK,)),
        ],
        mib=56,
        in_specs=[pl.BlockSpec(memory_space=pl.ANY)],
    )


def mask_kernel(slot_cap, pick_hbm, wanted_hbm, mask_ref, wanted_ref, pick, sems):
    copies = [
        pltpu.make_async_copy(pick_hbm, pick, sems.at[0]),
        pltpu.make_async_copy(wanted_hbm, wanted_ref, sems.at[1]),
    ]
    for copy in copies:
        copy.start()
    shape = mask_ref.shape[1], mask_ref.shape[0]
    slot = lax.broadcasted_iota(jnp.int32, shape, 0)
    slot = slot ^ (lax.axis_index("clus") * slot_cap)
    chosen = jnp.zeros(shape, jnp.float32)
    copies[0].wait()
    for k in range(pick.shape[0]):
        chosen = jnp.where(pick[k] == slot, 1.0, chosen)
    mask_ref[...] = chosen.T.astype(jnp.bfloat16)
    copies[1].wait()


def mask_call(slots, wanted):
    count, _, rows = slots.shape
    total = wanted.size
    return kernel_call(
        "mask",
        functools.partial(mask_kernel, wanted.shape[1]),
        [bf16(rows, total), pltpu.VMEM(wanted.shape, jnp.int32)],
        slots,
        wanted,
        flops=2 * count * rows * total,
        moved=2 * rows * total,
        scratch=[pltpu.VMEM(slots.shape, jnp.int32), pltpu.SemaphoreType.DMA((2,))],
        mib=56,
        in_specs=[pl.BlockSpec(memory_space=pl.ANY)] * 2,
    )


def list_kernel(rows, *refs):
    parts, refs = refs[-6::-1], refs[-5:]
    own_ref, far_ref, core_ref, expand_far_ref, expand_core_ref = refs
    total = own_ref.shape[1]
    lane = lax.broadcasted_iota(jnp.int32, (total, total), 1)
    sublane = lax.broadcasted_iota(jnp.int32, (total, total), 0)
    odd = lax.axis_index("rep") % 2
    lows = [(2 * odd * rows).astype(jnp.float32), ((2 - 2 * odd) * rows).astype(jnp.float32)]

    def inside(value, low):
        return (value >= low) & (value < low + rows)

    def asked(server):
        row = jnp.concatenate([ref[server, :] for ref in parts], axis=1).astype(jnp.float32)
        column = jnp.broadcast_to(row, (total, total)).T
        again = jnp.where((column == row) & (sublane < lane), 1.0, 0.0)
        return row, column, 1.0 - jnp.max(again, axis=0, keepdims=True)

    most = jnp.zeros((1, 1), jnp.float32)
    for server in range(len(parts)):
        row, _, first = asked(slice(server, server + 1))
        for low in lows:
            count = jnp.sum(jnp.where(inside(row, low), first, 0.0), axis=1, keepdims=True)
            most = jnp.maximum(most, count)
    row, column, first = asked(pl.ds(lax.axis_index("clus"), 1))
    own_ref[...] = jnp.broadcast_to(row - rows, own_ref.shape).astype(jnp.int32)
    place = lax.broadcasted_iota(jnp.int32, own_ref.shape, 0)
    for low, out_ref, expand_ref in zip(lows, (far_ref, core_ref), (expand_far_ref, expand_core_ref)):
        counted = jnp.where(inside(row, low), first, 0.0)
        rank = jnp.sum(jnp.where(row < column, counted, 0.0), axis=1, keepdims=True)
        here = inside(column, low) & (rank.astype(jnp.int32) == lane)
        expand_ref[...] = jnp.where(here, 1.0, 0.0).astype(jnp.bfloat16)
        packed = jnp.max(jnp.where(here, column - low, -1.0), axis=0, keepdims=True)
        out_ref[...] = jnp.where(place == 1, most, packed).astype(jnp.int32)


def list_call(parts, rows):
    total = parts[0].size
    return kernel_call(
        "list",
        functools.partial(list_kernel, rows),
        [int32(8, total)] * 3 + [bf16(total, total)] * 2,
        *reversed(parts),
        flops=40 * total * total,
    )


def one_hot(numbers, rows):
    total = numbers.shape[1]
    column = jnp.broadcast_to(numbers.astype(jnp.float32), (LANES, total)).T.astype(jnp.int32)
    tiles = []
    for start in range(0, rows, LANES):
        lane = lax.broadcasted_iota(jnp.int32, (total, LANES), 1) + start
        tiles.append(jnp.where(column == lane, 1.0, 0.0).astype(jnp.bfloat16))
    return jnp.concatenate(tiles, axis=1)


def take(select, x):
    return jnp.dot(select, x, preferred_element_type=jnp.float32).astype(jnp.bfloat16)


def far_kernel(x_ref, beyond_ref, pack_ref, far_ref):
    pack_ref[...] = one_hot(beyond_ref[0:1], x_ref.shape[0])
    far_ref[...] = take(pack_ref[: far_ref.shape[0]], x_ref[...])


def far_call(x, beyond, sent):
    rows, width = x.shape
    total = beyond.shape[1]
    return kernel_call(
        "pack_far",
        far_kernel,
        [bf16(total, rows), bf16(sent, width)],
        x,
        beyond,
        flops=2 * rows * sent * width,
    )


def near_kernel(x_ref, mask_ref, pack_ref, own_list_ref, *refs):
    far_list_ref, beyond_ref, within_ref, *refs = refs
    core_ref, own_ref, near_ref, rest_far_ref, rest_core_ref, *refs = refs
    far_mask_ref, core_mask_ref, near_mask_ref, most_ref, select = refs
    total, sent = own_ref.shape[0], core_ref.shape[0]
    rows = x_ref.shape[0]
    select[:total] = one_hot(within_ref[0:1], rows)
    select[total:] = one_hot(own_list_ref[0:1], rows)
    fetched = take(select[...], x_ref[...])
    core_ref[...] = fetched[:sent]
    near_ref[:sent] = fetched[:sent]
    rest_core_ref[...] = fetched[sent:total]
    own_ref[...] = fetched[total:]
    near_ref[sent:] = fetched[total:]
    rest_far_ref[...] = take(pack_ref[sent:], x_ref[...])
    masks = take(select[...], mask_ref[...])
    core_mask_ref[...] = masks[:total]
    near_mask_ref[:sent] = masks[:sent]
    near_mask_ref[sent:] = masks[total:]
    far_mask_ref[...] = take(pack_ref[...], mask_ref[...])
    most = jnp.maximum(far_list_ref[...], jnp.maximum(beyond_ref[...], within_ref[...]))
    most_ref[...] = jnp.broadcast_to(most[1:2, :LANES], most_ref.shape)


def near_call(x, mask, pack, own_list, far_list, beyond, within, sent):
    rows, width = x.shape
    total = mask.shape[1]
    return kernel_call(
        "serve_near",
        near_kernel,
        [
            bf16(sent, width),
            bf16(total, width),
            bf16(sent + total, width),
            bf16(total - sent, width),
            bf16(total - sent, width),
            bf16(total, total),
            bf16(total, total),
            bf16(sent + total, total),
            int32(8, LANES),
        ],
        x,
        mask,
        pack,
        own_list,
        far_list,
        beyond,
        within,
        flops=6 * total * rows * width,
        scratch=[pltpu.VMEM((2 * total, rows), jnp.bfloat16)],
    )


def unpack_kernel(first, bases, expand_ref, far_ref, *refs):
    out_ref, sent = refs[-1], far_ref.shape[0]
    rows = jnp.dot(
        expand_ref[:, first : first + sent], far_ref[...], preferred_element_type=jnp.float32
    )
    for base_ref in refs[:bases]:
        rows += base_ref[...].astype(jnp.float32)
    out_ref[...] = rows.astype(jnp.bfloat16)


def unpack_call(expand, far, *base, first=0, after=()):
    in_vmem = [pl.BlockSpec(memory_space=pltpu.VMEM)] * (2 + len(base))
    return kernel_call(
        "unpack",
        functools.partial(unpack_kernel, first, len(base)),
        bf16(expand.shape[0], far.shape[1]),
        expand,
        far,
        *base,
        *after,
        flops=2**34,
        moved=2**25,
        in_specs=in_vmem + [pl.BlockSpec(memory_space=pl.ANY)] * len(after),
    )


def combine_kernel(expand_ref, core_ref, base_ref, most_ref, out_most_ref, *out_refs):
    out_most_ref[...] = most_ref[...]
    cap, sent = out_refs[0].shape[0], core_ref.shape[0]
    rows = jnp.dot(expand_ref[:, :sent], core_ref[...], preferred_element_type=jnp.float32)
    rows = (rows + base_ref[...].astype(jnp.float32)).astype(jnp.bfloat16)
    for d, out in enumerate(out_refs):
        out[...] = rows[d * cap : (d + 1) * cap]


def combine_call(expand, core, base, most, servers):
    total, width = base.shape
    most, *parts = kernel_call(
        "combine",
        combine_kernel,
        [int32(*most.shape)] + [bf16(total // servers, width)] * servers,
        expand,
        core,
        base,
        most,
        flops=2 * total * core.shape[0] * width,
    )
    return most, parts


def unpack_both_kernel(far_expand, core_expand, own_ref, core_ref, far_ref, *refs):
    out_refs = refs[1:]
    cap, sent = out_refs[0].shape[0], far_ref.shape[0]
    rows = jnp.dot(core_expand[:, :sent], core_ref[...], preferred_element_type=jnp.float32)
    rows += jnp.dot(far_expand[:, :sent], far_ref[...], preferred_element_type=jnp.float32)
    rows = (rows + own_ref[...].astype(jnp.float32)).astype(jnp.bfloat16)
    for d, out in enumerate(out_refs):
        out[...] = rows[d * cap : (d + 1) * cap]


def unpack_both_call(expands, far, core, own, after, servers):
    total, width = own.shape
    return kernel_call(
        "unpack_both",
        unpack_both_kernel,
        [bf16(total // servers, width)] * servers,
        *expands,
        own,
        core,
        far,
        after,
        flops=4 * total * far.shape[0] * width,
        in_specs=[pl.BlockSpec(memory_space=pltpu.VMEM)] * 5
        + [pl.BlockSpec(memory_space=pl.ANY)],
    )


def fill(buffer, parts):
    cap = parts[0].shape[0]
    for d, ref in enumerate(reversed(parts)):
        buffer[d * cap : (d + 1) * cap] = ref[...]


def weigh(x, buffer, mask):
    dots = lax.dot_general(x, buffer, BOTH_LAST, preferred_element_type=jnp.float32)
    positive = jnp.maximum(dots * (1.0 / x.shape[1]), 0.0)
    return (positive * positive * positive).astype(jnp.bfloat16) * mask


def mix(x, weights, buffer):
    mixed = x.astype(jnp.float32) + jnp.dot(weights, buffer, preferred_element_type=jnp.float32)
    return normalize(mixed).astype(jnp.bfloat16)


def far_mix_kernel(servers, x_ref, mask_ref, *rest):
    parts, rest = rest[:servers], rest[servers:]
    *most_refs, out_ref, most_ref, buffer = rest
    most_ref[...] = functools.reduce(jnp.maximum, [ref[...] for ref in most_refs])
    fill(buffer, parts)
    weights = weigh(x_ref[...], buffer[...], mask_ref[: x_ref.shape[0]])
    out_ref[...] = mix(x_ref[...], weights, buffer[...])


def far_mix_call(x, mask, parts, mosts):
    rows, width = x.shape
    total, servers = mask.shape[1], len(parts)
    return kernel_call(
        "mix_far",
        functools.partial(far_mix_kernel, servers),
        [bf16(rows, width), int32(*mosts[0].shape)],
        x,
        mask,
        *reversed(parts),
        *mosts,
        flops=4 * total * rows * width,
        scratch=[pltpu.VMEM((total, width), jnp.bfloat16)],
    )


def near_mix_kernel(servers, x_ref, mask_ref, *rest):
    parts, (core_ref, own_ref, buffer) = rest[:servers], rest[servers:]
    fill(buffer, parts)
    weights = weigh(x_ref[...], buffer[...], mask_ref[...])
    mixed = mix(x_ref[...], weights, buffer[...])
    core_ref[...] = mixed[: core_ref.shape[0]]
    own_ref[...] = mixed[core_ref.shape[0] :]


def near_mix_call(x, mask, parts):
    rows, width = x.shape
    total, servers = mask.shape[1], len(parts)
    return kernel_call(
        "mix_near",
        functools.partial(near_mix_kernel, servers),
        [bf16(rows - total, width), bf16(total, width)],
        x,
        mask,
        *reversed(parts),
        flops=4 * total * rows * width,
        scratch=[pltpu.VMEM((total, width), jnp.bfloat16)],
    )


def is_late():
    return (lax.axis_index("rep") + 1) % 4 < 2


def late_kernel(servers, x_ref, mask_ref, *rest):
    parts, (out_ref, buffer, weights) = rest[:servers], rest[servers:]

    @pl.when(is_late())
    def _():
        fill(buffer, parts)
        weights[...] = weigh(x_ref[...], buffer[...], mask_ref[...])
        for start in range(0, x_ref.shape[0], BLOCK):
            here = pl.ds(start, BLOCK)
            out_ref[here] = mix(x_ref[here], weights[here], buffer[...])


def late_call(x, mask, parts):
    rows, width = x.shape
    total, servers = mask.shape[1], len(parts)
    return kernel_call(
        "mix_whole_late",
        functools.partial(late_kernel, servers),
        bf16(rows, width),
        x,
        mask,
        *reversed(parts),
        flops=4 * total * rows * width,
        scratch=[
            pltpu.VMEM((total, width), jnp.bfloat16),
            pltpu.VMEM((rows, total), jnp.bfloat16),
        ],
    )


def mix_blocks(x_ref, mask_ref, buffer, whole, out_ref, sems):
    copies = []
    for start in range(0, x_ref.shape[0], BLOCK):
        here = pl.ds(start, BLOCK)
        weights = weigh(x_ref[here], buffer[...], mask_ref[here])
        whole[here] = mix(x_ref[here], weights, buffer[...])
        for half in range(start, start + BLOCK, COPY):
            rows = pl.ds(half, COPY)
            copy = pltpu.make_async_copy(
                whole.at[rows], out_ref.at[rows], sems.at[half // COPY]
            )
            copy.start()
            copies.append(copy)
    for copy in copies:
        copy.wait()


def early_kernel(servers, x_ref, mask_ref, *rest):
    parts, (_, out_ref, buffer, whole, sems) = rest[:servers], rest[servers:]

    @pl.when(jnp.logical_not(is_late()))
    def _():
        fill(buffer, parts)
        mix_blocks(x_ref, mask_ref, buffer, whole, out_ref, sems)


def early_call(x, mask, parts, out):
    rows, width = x.shape
    total, servers = mask.shape[1], len(parts)
    return kernel_call(
        "mix_whole_early",
        functools.partial(early_kernel, servers),
        bf16(rows, width),
        x,
        mask,
        *reversed(parts),
        out,
        flops=4 * total * rows * width,
        scratch=[
            pltpu.VMEM((total, width), jnp.bfloat16),
            pltpu.VMEM((rows, width), jnp.bfloat16),
            pltpu.SemaphoreType.DMA((rows // COPY,)),
        ],
        in_specs=[pl.BlockSpec(memory_space=pltpu.VMEM)] * (2 + servers)
        + [pl.BlockSpec(memory_space=pl.ANY)],
        out_specs=pl.BlockSpec(memory_space=pl.ANY),
        input_output_aliases={2 + servers: 0},
    )


def last_kernel(servers, x_ref, mask_ref, *rest):
    parts, (out_ref, buffer, whole, sems) = rest[:servers], rest[servers:]
    fill(buffer, parts)
    mix_blocks(x_ref, mask_ref, buffer, whole, out_ref, sems)


def last_call(x, mask, parts):
    rows, width = x.shape
    total, servers = mask.shape[1], len(parts)
    return kernel_call(
        "mix",
        functools.partial(last_kernel, servers),
        pltpu.HBM((rows, width), jnp.bfloat16),
        x,
        mask,
        *reversed(parts),
        flops=4 * total * rows * width,
        moved=4 * rows * width,
        scratch=[
            pltpu.VMEM((total, width), jnp.bfloat16),
            pltpu.VMEM((rows, width), jnp.bfloat16),
            pltpu.SemaphoreType.DMA((rows // COPY,)),
        ],
        out_specs=pl.BlockSpec(memory_space=pltpu.HBM),
    )


def local(descriptors, request, pick):
    wanted = request[0, 0]
    rows = descriptors.shape[2]
    servers, cap = wanted.shape
    total = servers * cap
    groups = lax.axis_size("rep")
    sent = total * FIRST_SHARE[0] // FIRST_SHARE[1]
    within = [(g, g ^ 1) for g in range(groups)]
    beyond = [(g, (g + 2 * (g % 2) - 1 + groups) % groups) for g in range(groups)]

    def turn(value, d):
        return lax.ppermute(value, "clus", [(c, c ^ d) for c in range(servers)])

    def shift(value, by):
        return lax.ppermute(value, "rep", [(g, (g + by) % groups) for g in range(groups)])

    def across(value):
        return lax.ppermute(value, "rep", beyond)

    def inside(value):
        return lax.ppermute(value, "rep", within)

    def turned(parts):
        got = {d: turn(parts[d], d) for d in reversed(range(1, servers))}
        return [parts[0]] + [got[d] for d in range(1, servers)]

    def exchange(expands, far, core, own, most):
        base = unpack_call(expands[0], across(far), own)
        most, parts = combine_call(expands[1], inside(core), base, most, servers)
        return most, turned(parts)

    def next_round(x, mask, far, near, far_mask, near_mask, expands, parts, mosts):
        far, most = far_mix_call(far, far_mask, parts, mosts)
        core, own = near_mix_call(near, near_mask, parts)
        y = late_call(x, mask, parts)
        last = unpack_both_call(expands, across(far), inside(core), own, y, servers)
        return early_call(x, mask, parts, y), most, turned(last)

    def in_full(x, y, mask, far, near, rest, masks, expands, most, first, last):
        late = unpack_call(expands[1], inside(rest[1]), first=sent)
        late = unpack_call(expands[0], across(rest[0]), late, first=sent)
        late = turned(list(late.reshape(servers, cap, -1)))
        first = [a + b for a, b in zip(first, late)]
        far = jnp.concatenate([far, rest[0]], axis=0)
        near = jnp.concatenate([near[:sent], rest[1], near[sent:]], axis=0)
        near_mask = jnp.concatenate([masks[1], masks[2][sent:]], axis=0)
        y, _, last = next_round(
            x, mask, far, near, masks[0], near_mask, expands, first, [most]
        )
        return last_call(y, mask, last)

    def as_sent(x, y, mask, far, near, rest, masks, expands, most, first, last):
        return last_call(y, mask, last)

    asked = {d: turn(wanted, d) for d in reversed(range(1, servers))}
    mask, held = mask_call(pick.transpose(0, 3, 1, 2)[0], wanted)
    own_list, far_list, core_list, *expands = list_call(
        [held] + [asked[d] for d in range(1, servers)], rows
    )
    beyond_list, within_list = across(far_list), inside(core_list)
    x = normalize_call(descriptors[0, 0])
    pack, far = far_call(x, beyond_list, sent)
    core, own, near, *others, most = near_call(
        x, mask, pack, own_list, far_list, beyond_list, within_list, sent
    )
    rest, masks = others[:2], others[2:]
    most, first = exchange(expands, far, core, own, most)
    mosts = [most]
    reach = 1
    while 2 * reach + 1 < groups:
        by = 2 * reach + 1
        most = functools.reduce(jnp.maximum, mosts)
        mosts = [most, shift(most, -by), shift(most, by)]
        reach += by
    y, most, last = next_round(
        x, mask, far, near, masks[0], masks[2], expands, first, mosts
    )
    state = x, y, mask, far, near, rest, masks, expands, most, first, last
    return lax.cond(most[0, 0] > sent, in_full, as_sent, *state)[None, None]


def solution(mesh):
    return jax.shard_map(
        local,
        mesh=mesh,
        in_specs=(
            P("rep", "clus", None, None),
            P("rep", "clus", None, None),
            P("rep", "clus", None, None),
        ),
        out_specs=P("rep", "clus", None, None),
        check_vma=False,
    )
```

```python
import functools

import jax
import jax.numpy as jnp
from jax import lax
from jax.experimental import pallas as pl
from jax.experimental.pallas import tpu as pltpu
from jax.sharding import PartitionSpec as P

LANES = 128
BLOCK = 128
COPY = 64
FIRST_SHARE = 3, 8
BOTH_LAST = (((1,), (1,)), ((), ()))


def bf16(*shape):
    return jax.ShapeDtypeStruct(shape, jnp.bfloat16)


def int32(*shape):
    return jax.ShapeDtypeStruct(shape, jnp.int32)


def kernel_call(name, kernel, outs, *args, flops, moved=0, scratch=(), mib=32, **specs):
    return pl.pallas_call(
        kernel,
        out_shape=outs,
        scratch_shapes=scratch,
        compiler_params=pltpu.CompilerParams(vmem_limit_bytes=mib * 1024 * 1024),
        cost_estimate=pl.CostEstimate(flops=flops, bytes_accessed=moved, transcendentals=0),
        name=name,
        **specs,
    )(*args)


def normalize(value):
    return value * lax.rsqrt(jnp.mean(value * value, axis=-1, keepdims=True) + 1e-06)


def normalize_kernel(x_hbm, out_ref, raw, sems):
    copies = []
    starts = range(0, raw.shape[0], BLOCK)
    for i, start in enumerate(starts):
        here = pl.ds(start, BLOCK)
        copies.append(pltpu.make_async_copy(x_hbm.at[here], raw.at[here], sems.at[i]))
        copies[-1].start()
    for copy, start in zip(copies, starts):
        copy.wait()
        here = pl.ds(start, BLOCK)
        out_ref[here] = normalize(raw[here].astype(jnp.float32)).astype(jnp.bfloat16)


def normalize_call(descriptors):
    rows, width = descriptors.shape
    return kernel_call(
        "normalize",
        normalize_kernel,
        bf16(rows, width),
        descriptors,
        flops=6 * rows * width,
        moved=4 * rows * width,
        scratch=[
            pltpu.VMEM((rows, width), jnp.bfloat16),
            pltpu.SemaphoreType.DMA((rows // BLOCK,)),
        ],
        mib=56,
        in_specs=[pl.BlockSpec(memory_space=pl.ANY)],
    )


def mask_kernel(slot_cap, pick_hbm, wanted_hbm, mask_ref, wanted_ref, pick, sems):
    copies = [
        pltpu.make_async_copy(pick_hbm, pick, sems.at[0]),
        pltpu.make_async_copy(wanted_hbm, wanted_ref, sems.at[1]),
    ]
    for copy in copies:
        copy.start()
    shape = mask_ref.shape[1], mask_ref.shape[0]
    slot = lax.broadcasted_iota(jnp.int32, shape, 0)
    slot = slot ^ (lax.axis_index("clus") * slot_cap)
    chosen = jnp.zeros(shape, jnp.float32)
    copies[0].wait()
    for k in range(pick.shape[0]):
        chosen = jnp.where(pick[k] == slot, 1.0, chosen)
    mask_ref[...] = chosen.T.astype(jnp.bfloat16)
    copies[1].wait()


def mask_call(slots, wanted):
    count, _, rows = slots.shape
    total = wanted.size
    return kernel_call(
        "mask",
        functools.partial(mask_kernel, wanted.shape[1]),
        [bf16(rows, total), pltpu.VMEM(wanted.shape, jnp.int32)],
        slots,
        wanted,
        flops=2 * count * rows * total,
        moved=2 * rows * total,
        scratch=[pltpu.VMEM(slots.shape, jnp.int32), pltpu.SemaphoreType.DMA((2,))],
        mib=56,
        in_specs=[pl.BlockSpec(memory_space=pl.ANY)] * 2,
    )


def list_kernel(rows, *refs):
    parts, refs = refs[:-5], refs[-5:]
    own_ref, far_ref, core_ref, expand_far_ref, expand_core_ref = refs
    total = own_ref.shape[1]
    lane = lax.broadcasted_iota(jnp.int32, (total, total), 1)
    sublane = lax.broadcasted_iota(jnp.int32, (total, total), 0)
    odd = lax.axis_index("rep") % 2
    lows = [(2 * odd * rows).astype(jnp.float32), ((2 - 2 * odd) * rows).astype(jnp.float32)]

    def inside(value, low):
        return (value >= low) & (value < low + rows)

    def asked(server):
        row = jnp.concatenate([ref[server, :] for ref in parts], axis=1).astype(jnp.float32)
        column = jnp.broadcast_to(row, (total, total)).T
        again = jnp.where((column == row) & (sublane < lane), 1.0, 0.0)
        return row, column, 1.0 - jnp.max(again, axis=0, keepdims=True)

    most = jnp.zeros((1, 1), jnp.float32)
    for server in range(len(parts)):
        row, _, first = asked(slice(server, server + 1))
        for low in lows:
            count = jnp.sum(jnp.where(inside(row, low), first, 0.0), axis=1, keepdims=True)
            most = jnp.maximum(most, count)
    row, column, first = asked(pl.ds(lax.axis_index("clus"), 1))
    own_ref[...] = jnp.broadcast_to(row - rows, own_ref.shape).astype(jnp.int32)
    place = lax.broadcasted_iota(jnp.int32, own_ref.shape, 0)
    for low, out_ref, expand_ref in zip(lows, (far_ref, core_ref), (expand_far_ref, expand_core_ref)):
        counted = jnp.where(inside(row, low), first, 0.0)
        rank = jnp.sum(jnp.where(row < column, counted, 0.0), axis=1, keepdims=True)
        here = inside(column, low) & (rank.astype(jnp.int32) == lane)
        expand_ref[...] = jnp.where(here, 1.0, 0.0).astype(jnp.bfloat16)
        packed = jnp.max(jnp.where(here, column - low, -1.0), axis=0, keepdims=True)
        out_ref[...] = jnp.where(place == 1, most, packed).astype(jnp.int32)


def list_call(parts, rows):
    total = parts[0].size
    return kernel_call(
        "list",
        functools.partial(list_kernel, rows),
        [int32(8, total)] * 3 + [bf16(total, total)] * 2,
        *parts,
        flops=40 * total * total,
    )


def one_hot(numbers, rows):
    total = numbers.shape[1]
    column = jnp.broadcast_to(numbers.astype(jnp.float32), (LANES, total)).T.astype(jnp.int32)
    tiles = []
    for start in range(0, rows, LANES):
        lane = lax.broadcasted_iota(jnp.int32, (total, LANES), 1) + start
        tiles.append(jnp.where(column == lane, 1.0, 0.0).astype(jnp.bfloat16))
    return jnp.concatenate(tiles, axis=1)


def take(select, x):
    return jnp.dot(select, x, preferred_element_type=jnp.float32).astype(jnp.bfloat16)


def far_kernel(x_ref, beyond_ref, pack_ref, far_ref):
    pack_ref[...] = one_hot(beyond_ref[0:1], x_ref.shape[0])
    far_ref[...] = take(pack_ref[: far_ref.shape[0]], x_ref[...])


def far_call(x, beyond, sent):
    rows, width = x.shape
    total = beyond.shape[1]
    return kernel_call(
        "pack_far",
        far_kernel,
        [bf16(total, rows), bf16(sent, width)],
        x,
        beyond,
        flops=2 * rows * sent * width,
    )


def near_kernel(x_ref, mask_ref, pack_ref, own_list_ref, *refs):
    far_list_ref, beyond_ref, within_ref, *refs = refs
    core_ref, own_ref, near_ref, rest_far_ref, rest_core_ref, *refs = refs
    far_mask_ref, core_mask_ref, near_mask_ref, most_ref, select = refs
    total, sent = own_ref.shape[0], core_ref.shape[0]
    rows = x_ref.shape[0]
    select[:total] = one_hot(within_ref[0:1], rows)
    select[total:] = one_hot(own_list_ref[0:1], rows)
    fetched = take(select[...], x_ref[...])
    core_ref[...] = fetched[:sent]
    near_ref[:sent] = fetched[:sent]
    rest_core_ref[...] = fetched[sent:total]
    own_ref[...] = fetched[total:]
    near_ref[sent:] = fetched[total:]
    rest_far_ref[...] = take(pack_ref[sent:], x_ref[...])
    masks = take(select[...], mask_ref[...])
    core_mask_ref[...] = masks[:total]
    near_mask_ref[:sent] = masks[:sent]
    near_mask_ref[sent:] = masks[total:]
    far_mask_ref[...] = take(pack_ref[...], mask_ref[...])
    most = jnp.maximum(far_list_ref[...], jnp.maximum(beyond_ref[...], within_ref[...]))
    most_ref[...] = jnp.broadcast_to(most[1:2, :LANES], most_ref.shape)


def near_call(x, mask, pack, own_list, far_list, beyond, within, sent):
    rows, width = x.shape
    total = mask.shape[1]
    return kernel_call(
        "serve_near",
        near_kernel,
        [
            bf16(sent, width),
            bf16(total, width),
            bf16(sent + total, width),
            bf16(total - sent, width),
            bf16(total - sent, width),
            bf16(total, total),
            bf16(total, total),
            bf16(sent + total, total),
            int32(8, LANES),
        ],
        x,
        mask,
        pack,
        own_list,
        far_list,
        beyond,
        within,
        flops=6 * total * rows * width,
        scratch=[pltpu.VMEM((2 * total, rows), jnp.bfloat16)],
    )


def unpack_kernel(first, bases, expand_ref, far_ref, *refs):
    out_ref, sent = refs[-1], far_ref.shape[0]
    rows = jnp.dot(
        expand_ref[:, first : first + sent], far_ref[...], preferred_element_type=jnp.float32
    )
    for base_ref in refs[:bases]:
        rows += base_ref[...].astype(jnp.float32)
    out_ref[...] = rows.astype(jnp.bfloat16)


def unpack_call(expand, far, *base, first=0, after=()):
    in_vmem = [pl.BlockSpec(memory_space=pltpu.VMEM)] * (2 + len(base))
    return kernel_call(
        "unpack",
        functools.partial(unpack_kernel, first, len(base)),
        bf16(expand.shape[0], far.shape[1]),
        expand,
        far,
        *base,
        *after,
        flops=2**34,
        moved=2**25,
        in_specs=in_vmem + [pl.BlockSpec(memory_space=pl.ANY)] * len(after),
    )


def combine_kernel(expand_ref, core_ref, base_ref, most_ref, out_most_ref, *out_refs):
    out_most_ref[...] = most_ref[...]
    cap, sent = out_refs[0].shape[0], core_ref.shape[0]
    rows = jnp.dot(expand_ref[:, :sent], core_ref[...], preferred_element_type=jnp.float32)
    rows = (rows + base_ref[...].astype(jnp.float32)).astype(jnp.bfloat16)
    for d, out in enumerate(out_refs):
        out[...] = rows[d * cap : (d + 1) * cap]


def combine_call(expand, core, base, most, servers):
    total, width = base.shape
    most, *parts = kernel_call(
        "combine",
        combine_kernel,
        [int32(*most.shape)] + [bf16(total // servers, width)] * servers,
        expand,
        core,
        base,
        most,
        flops=2 * total * core.shape[0] * width,
    )
    return most, parts


def unpack_both_kernel(far_expand, core_expand, own_ref, core_ref, far_ref, *refs):
    out_refs = refs[1:]
    cap, sent = out_refs[0].shape[0], far_ref.shape[0]
    rows = jnp.dot(core_expand[:, :sent], core_ref[...], preferred_element_type=jnp.float32)
    rows += jnp.dot(far_expand[:, :sent], far_ref[...], preferred_element_type=jnp.float32)
    rows = (rows + own_ref[...].astype(jnp.float32)).astype(jnp.bfloat16)
    for d, out in enumerate(out_refs):
        out[...] = rows[d * cap : (d + 1) * cap]


def unpack_both_call(expands, far, core, own, after, servers):
    total, width = own.shape
    return kernel_call(
        "unpack_both",
        unpack_both_kernel,
        [bf16(total // servers, width)] * servers,
        *expands,
        own,
        core,
        far,
        after,
        flops=4 * total * far.shape[0] * width,
        in_specs=[pl.BlockSpec(memory_space=pltpu.VMEM)] * 5
        + [pl.BlockSpec(memory_space=pl.ANY)],
    )


def fill(buffer, parts):
    cap = parts[0].shape[0]
    for d, ref in enumerate(reversed(parts)):
        buffer[d * cap : (d + 1) * cap] = ref[...]


def weigh(x, buffer, mask):
    dots = lax.dot_general(x, buffer, BOTH_LAST, preferred_element_type=jnp.float32)
    positive = jnp.maximum(dots * (1.0 / x.shape[1]), 0.0)
    return (positive * positive * positive).astype(jnp.bfloat16) * mask


def mix(x, weights, buffer):
    mixed = x.astype(jnp.float32) + jnp.dot(weights, buffer, preferred_element_type=jnp.float32)
    return normalize(mixed).astype(jnp.bfloat16)


def far_mix_kernel(servers, x_ref, mask_ref, *rest):
    parts, rest = rest[:servers], rest[servers:]
    *most_refs, out_ref, most_ref, buffer = rest
    most_ref[...] = functools.reduce(jnp.maximum, [ref[...] for ref in most_refs])
    fill(buffer, parts)
    weights = weigh(x_ref[...], buffer[...], mask_ref[: x_ref.shape[0]])
    out_ref[...] = mix(x_ref[...], weights, buffer[...])


def far_mix_call(x, mask, parts, mosts):
    rows, width = x.shape
    total, servers = mask.shape[1], len(parts)
    return kernel_call(
        "mix_far",
        functools.partial(far_mix_kernel, servers),
        [bf16(rows, width), int32(*mosts[0].shape)],
        x,
        mask,
        *reversed(parts),
        *mosts,
        flops=4 * total * rows * width,
        scratch=[pltpu.VMEM((total, width), jnp.bfloat16)],
    )


def near_mix_kernel(servers, x_ref, mask_ref, *rest):
    parts, (core_ref, own_ref, buffer) = rest[:servers], rest[servers:]
    fill(buffer, parts)
    weights = weigh(x_ref[...], buffer[...], mask_ref[...])
    mixed = mix(x_ref[...], weights, buffer[...])
    core_ref[...] = mixed[: core_ref.shape[0]]
    own_ref[...] = mixed[core_ref.shape[0] :]


def near_mix_call(x, mask, parts):
    rows, width = x.shape
    total, servers = mask.shape[1], len(parts)
    return kernel_call(
        "mix_near",
        functools.partial(near_mix_kernel, servers),
        [bf16(rows - total, width), bf16(total, width)],
        x,
        mask,
        *reversed(parts),
        flops=4 * total * rows * width,
        scratch=[pltpu.VMEM((total, width), jnp.bfloat16)],
    )


def is_late():
    return (lax.axis_index("rep") + 1) % 4 < 2


def late_kernel(servers, x_ref, mask_ref, *rest):
    parts, (out_ref, buffer, weights) = rest[:servers], rest[servers:]

    @pl.when(is_late())
    def _():
        fill(buffer, parts)
        weights[...] = weigh(x_ref[...], buffer[...], mask_ref[...])
        for start in range(0, x_ref.shape[0], BLOCK):
            here = pl.ds(start, BLOCK)
            out_ref[here] = mix(x_ref[here], weights[here], buffer[...])


def late_call(x, mask, parts):
    rows, width = x.shape
    total, servers = mask.shape[1], len(parts)
    return kernel_call(
        "mix_whole_late",
        functools.partial(late_kernel, servers),
        bf16(rows, width),
        x,
        mask,
        *reversed(parts),
        flops=4 * total * rows * width,
        scratch=[
            pltpu.VMEM((total, width), jnp.bfloat16),
            pltpu.VMEM((rows, total), jnp.bfloat16),
        ],
    )


def mix_blocks(x_ref, mask_ref, buffer, whole, out_ref, sems):
    copies = []
    for start in range(0, x_ref.shape[0], BLOCK):
        here = pl.ds(start, BLOCK)
        weights = weigh(x_ref[here], buffer[...], mask_ref[here])
        whole[here] = mix(x_ref[here], weights, buffer[...])
        for half in range(start, start + BLOCK, COPY):
            rows = pl.ds(half, COPY)
            copy = pltpu.make_async_copy(
                whole.at[rows], out_ref.at[rows], sems.at[half // COPY]
            )
            copy.start()
            copies.append(copy)
    for copy in copies:
        copy.wait()


def early_kernel(servers, x_ref, mask_ref, *rest):
    parts, (_, out_ref, buffer, whole, sems) = rest[:servers], rest[servers:]

    @pl.when(jnp.logical_not(is_late()))
    def _():
        fill(buffer, parts)
        mix_blocks(x_ref, mask_ref, buffer, whole, out_ref, sems)


def early_call(x, mask, parts, out):
    rows, width = x.shape
    total, servers = mask.shape[1], len(parts)
    return kernel_call(
        "mix_whole_early",
        functools.partial(early_kernel, servers),
        bf16(rows, width),
        x,
        mask,
        *reversed(parts),
        out,
        flops=4 * total * rows * width,
        scratch=[
            pltpu.VMEM((total, width), jnp.bfloat16),
            pltpu.VMEM((rows, width), jnp.bfloat16),
            pltpu.SemaphoreType.DMA((rows // COPY,)),
        ],
        in_specs=[pl.BlockSpec(memory_space=pltpu.VMEM)] * (2 + servers)
        + [pl.BlockSpec(memory_space=pl.ANY)],
        out_specs=pl.BlockSpec(memory_space=pl.ANY),
        input_output_aliases={2 + servers: 0},
    )


def last_kernel(servers, x_ref, mask_ref, *rest):
    parts, (out_ref, buffer, whole, sems) = rest[:servers], rest[servers:]
    fill(buffer, parts)
    mix_blocks(x_ref, mask_ref, buffer, whole, out_ref, sems)


def last_call(x, mask, parts):
    rows, width = x.shape
    total, servers = mask.shape[1], len(parts)
    return kernel_call(
        "mix",
        functools.partial(last_kernel, servers),
        pltpu.HBM((rows, width), jnp.bfloat16),
        x,
        mask,
        *reversed(parts),
        flops=4 * total * rows * width,
        moved=4 * rows * width,
        scratch=[
            pltpu.VMEM((total, width), jnp.bfloat16),
            pltpu.VMEM((rows, width), jnp.bfloat16),
            pltpu.SemaphoreType.DMA((rows // COPY,)),
        ],
        out_specs=pl.BlockSpec(memory_space=pltpu.HBM),
    )


def local(descriptors, request, pick):
    wanted = request[0, 0]
    rows = descriptors.shape[2]
    servers, cap = wanted.shape
    total = servers * cap
    groups = lax.axis_size("rep")
    sent = total * FIRST_SHARE[0] // FIRST_SHARE[1]
    within = [(g, g ^ 1) for g in range(groups)]
    beyond = [(g, (g + 2 * (g % 2) - 1 + groups) % groups) for g in range(groups)]

    def turn(value, d):
        return lax.ppermute(value, "clus", [(c, c ^ d) for c in range(servers)])

    def shift(value, by):
        return lax.ppermute(value, "rep", [(g, (g + by) % groups) for g in range(groups)])

    def across(value):
        return lax.ppermute(value, "rep", beyond)

    def inside(value):
        return lax.ppermute(value, "rep", within)

    def turned(parts):
        got = {d: turn(parts[d], d) for d in reversed(range(1, servers))}
        return [parts[0]] + [got[d] for d in range(1, servers)]

    def exchange(expands, far, core, own, most):
        base = unpack_call(expands[0], across(far), own)
        most, parts = combine_call(expands[1], inside(core), base, most, servers)
        return most, turned(parts)

    def next_round(x, mask, far, near, far_mask, near_mask, expands, parts, mosts):
        far, most = far_mix_call(far, far_mask, parts, mosts)
        core, own = near_mix_call(near, near_mask, parts)
        y = late_call(x, mask, parts)
        last = unpack_both_call(expands, across(far), inside(core), own, y, servers)
        return early_call(x, mask, parts, y), most, turned(last)

    def in_full(x, y, mask, far, near, rest, masks, expands, most, first, last):
        late = unpack_call(expands[1], inside(rest[1]), first=sent)
        late = unpack_call(expands[0], across(rest[0]), late, first=sent)
        late = turned(list(late.reshape(servers, cap, -1)))
        first = [a + b for a, b in zip(first, late)]
        far = jnp.concatenate([far, rest[0]], axis=0)
        near = jnp.concatenate([near[:sent], rest[1], near[sent:]], axis=0)
        near_mask = jnp.concatenate([masks[1], masks[2][sent:]], axis=0)
        y, _, last = next_round(
            x, mask, far, near, masks[0], near_mask, expands, first, [most]
        )
        return last_call(y, mask, last)

    def as_sent(x, y, mask, far, near, rest, masks, expands, most, first, last):
        return last_call(y, mask, last)

    asked = {d: turn(wanted, d) for d in reversed(range(1, servers))}
    mask, held = mask_call(pick.transpose(0, 3, 1, 2)[0], wanted)
    own_list, far_list, core_list, *expands = list_call(
        [held] + [asked[d] for d in range(1, servers)], rows
    )
    beyond_list, within_list = across(far_list), inside(core_list)
    x = normalize_call(descriptors[0, 0])
    pack, far = far_call(x, beyond_list, sent)
    core, own, near, *others, most = near_call(
        x, mask, pack, own_list, far_list, beyond_list, within_list, sent
    )
    rest, masks = others[:2], others[2:]
    most, first = exchange(expands, far, core, own, most)
    mosts = [most]
    reach = 1
    while 2 * reach + 1 < groups:
        by = 2 * reach + 1
        most = functools.reduce(jnp.maximum, mosts)
        mosts = [most, shift(most, -by), shift(most, by)]
        reach += by
    y, most, last = next_round(
        x, mask, far, near, masks[0], masks[2], expands, first, mosts
    )
    state = x, y, mask, far, near, rest, masks, expands, most, first, last
    return lax.cond(most[0, 0] > sent, in_full, as_sent, *state)[None, None]


def solution(mesh):
    return jax.shard_map(
        local,
        mesh=mesh,
        in_specs=(
            P("rep", "clus", None, None),
            P("rep", "clus", None, None),
            P("rep", "clus", None, None),
        ),
        out_specs=P("rep", "clus", None, None),
        check_vma=False,
    )
```

```python
import functools

import jax
import jax.numpy as jnp
from jax import lax
from jax.experimental import pallas as pl
from jax.experimental.pallas import tpu as pltpu
from jax.sharding import PartitionSpec as P

LANES = 128
BLOCK = 128
COPY = 64
FIRST_SHARE = 3, 8
BOTH_LAST = (((1,), (1,)), ((), ()))


def bf16(*shape):
    return jax.ShapeDtypeStruct(shape, jnp.bfloat16)


def int32(*shape):
    return jax.ShapeDtypeStruct(shape, jnp.int32)


def kernel_call(name, kernel, outs, *args, flops, moved=0, scratch=(), mib=32, **specs):
    return pl.pallas_call(
        kernel,
        out_shape=outs,
        scratch_shapes=scratch,
        compiler_params=pltpu.CompilerParams(vmem_limit_bytes=mib * 1024 * 1024),
        cost_estimate=pl.CostEstimate(flops=flops, bytes_accessed=moved, transcendentals=0),
        name=name,
        **specs,
    )(*args)


def normalize(value):
    return value * lax.rsqrt(jnp.mean(value * value, axis=-1, keepdims=True) + 1e-06)


def normalize_kernel(x_hbm, out_ref, raw, sems):
    copies = []
    starts = range(0, raw.shape[0], BLOCK)
    for i, start in enumerate(starts):
        here = pl.ds(start, BLOCK)
        copies.append(pltpu.make_async_copy(x_hbm.at[here], raw.at[here], sems.at[i]))
        copies[-1].start()
    for copy, start in zip(copies, starts):
        copy.wait()
        here = pl.ds(start, BLOCK)
        out_ref[here] = normalize(raw[here].astype(jnp.float32)).astype(jnp.bfloat16)


def normalize_call(descriptors):
    rows, width = descriptors.shape
    return kernel_call(
        "normalize",
        normalize_kernel,
        bf16(rows, width),
        descriptors,
        flops=6 * rows * width,
        moved=4 * rows * width,
        scratch=[
            pltpu.VMEM((rows, width), jnp.bfloat16),
            pltpu.SemaphoreType.DMA((rows // BLOCK,)),
        ],
        mib=56,
        in_specs=[pl.BlockSpec(memory_space=pl.ANY)],
    )


def mask_kernel(slot_cap, pick_hbm, wanted_hbm, mask_ref, wanted_ref, pick, sems):
    copies = [
        pltpu.make_async_copy(pick_hbm, pick, sems.at[0]),
        pltpu.make_async_copy(wanted_hbm, wanted_ref, sems.at[1]),
    ]
    for copy in copies:
        copy.start()
    shape = mask_ref.shape[1], mask_ref.shape[0]
    slot = lax.broadcasted_iota(jnp.int32, shape, 0)
    slot = slot ^ (lax.axis_index("clus") * slot_cap)
    chosen = jnp.zeros(shape, jnp.float32)
    copies[0].wait()
    for k in range(pick.shape[0]):
        chosen = jnp.where(pick[k] == slot, 1.0, chosen)
    mask_ref[...] = chosen.T.astype(jnp.bfloat16)
    copies[1].wait()


def mask_call(slots, wanted):
    count, _, rows = slots.shape
    total = wanted.size
    return kernel_call(
        "mask",
        functools.partial(mask_kernel, wanted.shape[1]),
        [bf16(rows, total), pltpu.VMEM(wanted.shape, jnp.int32)],
        slots,
        wanted,
        flops=2 * count * rows * total,
        moved=2 * rows * total,
        scratch=[pltpu.VMEM(slots.shape, jnp.int32), pltpu.SemaphoreType.DMA((2,))],
        mib=56,
        in_specs=[pl.BlockSpec(memory_space=pl.ANY)] * 2,
    )


def list_kernel(rows, *refs):
    parts, refs = refs[:-5], refs[-5:]
    own_ref, far_ref, core_ref, expand_far_ref, expand_core_ref = refs
    total = own_ref.shape[1]
    lane = lax.broadcasted_iota(jnp.int32, (total, total), 1)
    sublane = lax.broadcasted_iota(jnp.int32, (total, total), 0)
    odd = lax.axis_index("rep") % 2
    lows = [(2 * odd * rows).astype(jnp.float32), ((2 - 2 * odd) * rows).astype(jnp.float32)]

    def inside(value, low):
        return (value >= low) & (value < low + rows)

    def asked(server):
        row = jnp.concatenate([ref[server, :] for ref in parts], axis=1).astype(jnp.float32)
        column = jnp.broadcast_to(row, (total, total)).T
        again = jnp.where((column == row) & (sublane < lane), 1.0, 0.0)
        return row, column, 1.0 - jnp.max(again, axis=0, keepdims=True)

    most = jnp.zeros((1, 1), jnp.float32)
    for server in range(len(parts)):
        row, _, first = asked(slice(server, server + 1))
        for low in lows:
            count = jnp.sum(jnp.where(inside(row, low), first, 0.0), axis=1, keepdims=True)
            most = jnp.maximum(most, count)
    row, column, first = asked(pl.ds(lax.axis_index("clus"), 1))
    own_ref[...] = jnp.broadcast_to(row - rows, own_ref.shape).astype(jnp.int32)
    place = lax.broadcasted_iota(jnp.int32, own_ref.shape, 0)
    for low, out_ref, expand_ref in zip(lows, (far_ref, core_ref), (expand_far_ref, expand_core_ref)):
        counted = jnp.where(inside(row, low), first, 0.0)
        rank = jnp.sum(jnp.where(row < column, counted, 0.0), axis=1, keepdims=True)
        here = inside(column, low) & (rank.astype(jnp.int32) == lane)
        expand_ref[...] = jnp.where(here, 1.0, 0.0).astype(jnp.bfloat16)
        packed = jnp.max(jnp.where(here, column - low, -1.0), axis=0, keepdims=True)
        out_ref[...] = jnp.where(place == 1, most, packed).astype(jnp.int32)


def list_call(parts, rows):
    total = parts[0].size
    return kernel_call(
        "list",
        functools.partial(list_kernel, rows),
        [int32(8, total)] * 3 + [bf16(total, total)] * 2,
        *parts,
        flops=40 * total * total,
    )


def one_hot(numbers, rows):
    total = numbers.shape[1]
    column = jnp.broadcast_to(numbers.astype(jnp.float32), (LANES, total)).T.astype(jnp.int32)
    tiles = []
    for start in range(0, rows, LANES):
        lane = lax.broadcasted_iota(jnp.int32, (total, LANES), 1) + start
        tiles.append(jnp.where(column == lane, 1.0, 0.0).astype(jnp.bfloat16))
    return jnp.concatenate(tiles, axis=1)


def take(select, x):
    return jnp.dot(select, x, preferred_element_type=jnp.float32).astype(jnp.bfloat16)


def far_kernel(x_ref, beyond_ref, core_list_ref, pack_ref, told_ref, far_ref):
    place = lax.broadcasted_iota(jnp.int32, told_ref.shape, 0)
    most = jnp.maximum(core_list_ref[...], beyond_ref[...])
    told_ref[...] = jnp.where(place == 1, most, core_list_ref[...])
    pack_ref[...] = one_hot(beyond_ref[0:1], x_ref.shape[0])
    far_ref[...] = take(pack_ref[: far_ref.shape[0]], x_ref[...])


def far_call(x, beyond, core_list, sent):
    rows, width = x.shape
    total = beyond.shape[1]
    return kernel_call(
        "pack_far",
        far_kernel,
        [bf16(total, rows), int32(*core_list.shape), bf16(sent, width)],
        x,
        beyond,
        core_list,
        flops=2 * rows * sent * width,
    )


def near_kernel(x_ref, mask_ref, pack_ref, own_list_ref, *refs):
    told_ref, within_ref, *refs = refs
    core_ref, own_ref, near_ref, rest_far_ref, rest_core_ref, *refs = refs
    far_mask_ref, core_mask_ref, near_mask_ref, most_ref, select = refs
    total, sent = own_ref.shape[0], core_ref.shape[0]
    rows = x_ref.shape[0]
    select[:total] = one_hot(within_ref[0:1], rows)
    select[total:] = one_hot(own_list_ref[0:1], rows)
    fetched = take(select[...], x_ref[...])
    core_ref[...] = fetched[:sent]
    near_ref[:sent] = fetched[:sent]
    rest_core_ref[...] = fetched[sent:total]
    own_ref[...] = fetched[total:]
    near_ref[sent:] = fetched[total:]
    rest_far_ref[...] = take(pack_ref[sent:], x_ref[...])
    masks = take(select[...], mask_ref[...])
    core_mask_ref[...] = masks[:total]
    near_mask_ref[:sent] = masks[:sent]
    near_mask_ref[sent:] = masks[total:]
    far_mask_ref[...] = take(pack_ref[...], mask_ref[...])
    most = jnp.maximum(told_ref[...], within_ref[...])
    most_ref[...] = jnp.broadcast_to(most[1:2, :LANES], most_ref.shape)


def near_call(x, mask, pack, own_list, told, within, sent):
    rows, width = x.shape
    total = mask.shape[1]
    return kernel_call(
        "serve_near",
        near_kernel,
        [
            bf16(sent, width),
            bf16(total, width),
            bf16(sent + total, width),
            bf16(total - sent, width),
            bf16(total - sent, width),
            bf16(total, total),
            bf16(total, total),
            bf16(sent + total, total),
            int32(8, LANES),
        ],
        x,
        mask,
        pack,
        own_list,
        told,
        within,
        flops=6 * total * rows * width,
        scratch=[pltpu.VMEM((2 * total, rows), jnp.bfloat16)],
    )


def unpack_kernel(first, bases, expand_ref, far_ref, *refs):
    out_ref, sent = refs[-1], far_ref.shape[0]
    rows = jnp.dot(
        expand_ref[:, first : first + sent], far_ref[...], preferred_element_type=jnp.float32
    )
    for base_ref in refs[:bases]:
        rows += base_ref[...].astype(jnp.float32)
    out_ref[...] = rows.astype(jnp.bfloat16)


def unpack_call(expand, far, *base, first=0, after=()):
    in_vmem = [pl.BlockSpec(memory_space=pltpu.VMEM)] * (2 + len(base))
    return kernel_call(
        "unpack",
        functools.partial(unpack_kernel, first, len(base)),
        bf16(expand.shape[0], far.shape[1]),
        expand,
        far,
        *base,
        *after,
        flops=2**34,
        moved=2**25,
        in_specs=in_vmem + [pl.BlockSpec(memory_space=pl.ANY)] * len(after),
    )


def combine_kernel(expand_ref, core_ref, base_ref, most_ref, out_most_ref, *out_refs):
    out_most_ref[...] = most_ref[...]
    cap, sent = out_refs[0].shape[0], core_ref.shape[0]
    rows = jnp.dot(expand_ref[:, :sent], core_ref[...], preferred_element_type=jnp.float32)
    rows = (rows + base_ref[...].astype(jnp.float32)).astype(jnp.bfloat16)
    for d, out in enumerate(out_refs):
        out[...] = rows[d * cap : (d + 1) * cap]


def combine_call(expand, core, base, most, servers):
    total, width = base.shape
    most, *parts = kernel_call(
        "combine",
        combine_kernel,
        [int32(*most.shape)] + [bf16(total // servers, width)] * servers,
        expand,
        core,
        base,
        most,
        flops=2 * total * core.shape[0] * width,
    )
    return most, parts


def unpack_both_kernel(far_expand, core_expand, own_ref, core_ref, far_ref, *refs):
    out_refs = refs[1:]
    cap, sent = out_refs[0].shape[0], far_ref.shape[0]
    rows = jnp.dot(core_expand[:, :sent], core_ref[...], preferred_element_type=jnp.float32)
    rows += jnp.dot(far_expand[:, :sent], far_ref[...], preferred_element_type=jnp.float32)
    rows = (rows + own_ref[...].astype(jnp.float32)).astype(jnp.bfloat16)
    for d, out in enumerate(out_refs):
        out[...] = rows[d * cap : (d + 1) * cap]


def unpack_both_call(expands, far, core, own, after, servers):
    total, width = own.shape
    return kernel_call(
        "unpack_both",
        unpack_both_kernel,
        [bf16(total // servers, width)] * servers,
        *expands,
        own,
        core,
        far,
        after,
        flops=4 * total * far.shape[0] * width,
        in_specs=[pl.BlockSpec(memory_space=pltpu.VMEM)] * 5
        + [pl.BlockSpec(memory_space=pl.ANY)],
    )


def fill(buffer, parts):
    cap = parts[0].shape[0]
    for d, ref in enumerate(reversed(parts)):
        buffer[d * cap : (d + 1) * cap] = ref[...]


def weigh(x, buffer, mask):
    dots = lax.dot_general(x, buffer, BOTH_LAST, preferred_element_type=jnp.float32)
    positive = jnp.maximum(dots * (1.0 / x.shape[1]), 0.0)
    return (positive * positive * positive).astype(jnp.bfloat16) * mask


def mix(x, weights, buffer):
    mixed = x.astype(jnp.float32) + jnp.dot(weights, buffer, preferred_element_type=jnp.float32)
    return normalize(mixed).astype(jnp.bfloat16)


def far_mix_kernel(servers, x_ref, mask_ref, *rest):
    parts, rest = rest[:servers], rest[servers:]
    *most_refs, out_ref, most_ref, buffer = rest
    most_ref[...] = functools.reduce(jnp.maximum, [ref[...] for ref in most_refs])
    fill(buffer, parts)
    weights = weigh(x_ref[...], buffer[...], mask_ref[: x_ref.shape[0]])
    out_ref[...] = mix(x_ref[...], weights, buffer[...])


def far_mix_call(x, mask, parts, mosts):
    rows, width = x.shape
    total, servers = mask.shape[1], len(parts)
    return kernel_call(
        "mix_far",
        functools.partial(far_mix_kernel, servers),
        [bf16(rows, width), int32(*mosts[0].shape)],
        x,
        mask,
        *reversed(parts),
        *mosts,
        flops=4 * total * rows * width,
        scratch=[pltpu.VMEM((total, width), jnp.bfloat16)],
    )


def near_mix_kernel(servers, x_ref, mask_ref, *rest):
    parts, (core_ref, own_ref, buffer) = rest[:servers], rest[servers:]
    fill(buffer, parts)
    weights = weigh(x_ref[...], buffer[...], mask_ref[...])
    mixed = mix(x_ref[...], weights, buffer[...])
    core_ref[...] = mixed[: core_ref.shape[0]]
    own_ref[...] = mixed[core_ref.shape[0] :]


def near_mix_call(x, mask, parts):
    rows, width = x.shape
    total, servers = mask.shape[1], len(parts)
    return kernel_call(
        "mix_near",
        functools.partial(near_mix_kernel, servers),
        [bf16(rows - total, width), bf16(total, width)],
        x,
        mask,
        *reversed(parts),
        flops=4 * total * rows * width,
        scratch=[pltpu.VMEM((total, width), jnp.bfloat16)],
    )


def is_late():
    return (lax.axis_index("rep") + 1) % 4 < 2


def late_kernel(servers, x_ref, mask_ref, *rest):
    parts, (out_ref, buffer, weights) = rest[:servers], rest[servers:]

    @pl.when(is_late())
    def _():
        fill(buffer, parts)
        weights[...] = weigh(x_ref[...], buffer[...], mask_ref[...])
        for start in range(0, x_ref.shape[0], BLOCK):
            here = pl.ds(start, BLOCK)
            out_ref[here] = mix(x_ref[here], weights[here], buffer[...])


def late_call(x, mask, parts):
    rows, width = x.shape
    total, servers = mask.shape[1], len(parts)
    return kernel_call(
        "mix_whole_late",
        functools.partial(late_kernel, servers),
        bf16(rows, width),
        x,
        mask,
        *reversed(parts),
        flops=4 * total * rows * width,
        scratch=[
            pltpu.VMEM((total, width), jnp.bfloat16),
            pltpu.VMEM((rows, total), jnp.bfloat16),
        ],
    )


def mix_blocks(x_ref, mask_ref, buffer, whole, out_ref, sems):
    copies = []
    for start in range(0, x_ref.shape[0], BLOCK):
        here = pl.ds(start, BLOCK)
        weights = weigh(x_ref[here], buffer[...], mask_ref[here])
        whole[here] = mix(x_ref[here], weights, buffer[...])
        for half in range(start, start + BLOCK, COPY):
            rows = pl.ds(half, COPY)
            copy = pltpu.make_async_copy(
                whole.at[rows], out_ref.at[rows], sems.at[half // COPY]
            )
            copy.start()
            copies.append(copy)
    for copy in copies:
        copy.wait()


def early_kernel(servers, x_ref, mask_ref, *rest):
    parts, (_, out_ref, buffer, whole, sems) = rest[:servers], rest[servers:]

    @pl.when(jnp.logical_not(is_late()))
    def _():
        fill(buffer, parts)
        mix_blocks(x_ref, mask_ref, buffer, whole, out_ref, sems)


def early_call(x, mask, parts, out):
    rows, width = x.shape
    total, servers = mask.shape[1], len(parts)
    return kernel_call(
        "mix_whole_early",
        functools.partial(early_kernel, servers),
        bf16(rows, width),
        x,
        mask,
        *reversed(parts),
        out,
        flops=4 * total * rows * width,
        scratch=[
            pltpu.VMEM((total, width), jnp.bfloat16),
            pltpu.VMEM((rows, width), jnp.bfloat16),
            pltpu.SemaphoreType.DMA((rows // COPY,)),
        ],
        in_specs=[pl.BlockSpec(memory_space=pltpu.VMEM)] * (2 + servers)
        + [pl.BlockSpec(memory_space=pl.ANY)],
        out_specs=pl.BlockSpec(memory_space=pl.ANY),
        input_output_aliases={2 + servers: 0},
    )


def last_kernel(servers, x_ref, mask_ref, *rest):
    parts, (out_ref, buffer, whole, sems) = rest[:servers], rest[servers:]
    fill(buffer, parts)
    mix_blocks(x_ref, mask_ref, buffer, whole, out_ref, sems)


def last_call(x, mask, parts):
    rows, width = x.shape
    total, servers = mask.shape[1], len(parts)
    return kernel_call(
        "mix",
        functools.partial(last_kernel, servers),
        pltpu.HBM((rows, width), jnp.bfloat16),
        x,
        mask,
        *reversed(parts),
        flops=4 * total * rows * width,
        moved=4 * rows * width,
        scratch=[
            pltpu.VMEM((total, width), jnp.bfloat16),
            pltpu.VMEM((rows, width), jnp.bfloat16),
            pltpu.SemaphoreType.DMA((rows // COPY,)),
        ],
        out_specs=pl.BlockSpec(memory_space=pltpu.HBM),
    )


def local(descriptors, request, pick):
    wanted = request[0, 0]
    rows = descriptors.shape[2]
    servers, cap = wanted.shape
    total = servers * cap
    groups = lax.axis_size("rep")
    sent = total * FIRST_SHARE[0] // FIRST_SHARE[1]
    within = [(g, g ^ 1) for g in range(groups)]
    beyond = [(g, (g + 2 * (g % 2) - 1 + groups) % groups) for g in range(groups)]

    def turn(value, d):
        return lax.ppermute(value, "clus", [(c, c ^ d) for c in range(servers)])

    def shift(value, by):
        return lax.ppermute(value, "rep", [(g, (g + by) % groups) for g in range(groups)])

    def across(value):
        return lax.ppermute(value, "rep", beyond)

    def inside(value):
        return lax.ppermute(value, "rep", within)

    def turned(parts):
        got = {d: turn(parts[d], d) for d in reversed(range(1, servers))}
        return [parts[0]] + [got[d] for d in range(1, servers)]

    def exchange(expands, far, core, own, most):
        base = unpack_call(expands[0], across(far), own)
        most, parts = combine_call(expands[1], inside(core), base, most, servers)
        return most, turned(parts)

    def next_round(x, mask, far, near, far_mask, near_mask, expands, parts, mosts):
        far, most = far_mix_call(far, far_mask, parts, mosts)
        core, own = near_mix_call(near, near_mask, parts)
        y = late_call(x, mask, parts)
        last = unpack_both_call(expands, across(far), inside(core), own, y, servers)
        return early_call(x, mask, parts, y), most, turned(last)

    def in_full(x, y, mask, far, near, rest, masks, expands, most, first, last):
        late = unpack_call(expands[1], inside(rest[1]), first=sent)
        late = unpack_call(expands[0], across(rest[0]), late, first=sent)
        late = turned(list(late.reshape(servers, cap, -1)))
        first = [a + b for a, b in zip(first, late)]
        far = jnp.concatenate([far, rest[0]], axis=0)
        near = jnp.concatenate([near[:sent], rest[1], near[sent:]], axis=0)
        near_mask = jnp.concatenate([masks[1], masks[2][sent:]], axis=0)
        y, _, last = next_round(
            x, mask, far, near, masks[0], near_mask, expands, first, [most]
        )
        return last_call(y, mask, last)

    def as_sent(x, y, mask, far, near, rest, masks, expands, most, first, last):
        return last_call(y, mask, last)

    asked = {d: turn(wanted, d) for d in reversed(range(1, servers))}
    mask, held = mask_call(pick.transpose(0, 3, 1, 2)[0], wanted)
    own_list, far_list, core_list, *expands = list_call(
        [held] + [asked[d] for d in range(1, servers)], rows
    )
    beyond_list = across(far_list)
    x = normalize_call(descriptors[0, 0])
    pack, told, far = far_call(x, beyond_list, core_list, sent)
    core, own, near, *others, most = near_call(
        x, mask, pack, own_list, told, inside(told), sent
    )
    rest, masks = others[:2], others[2:]
    most, first = exchange(expands, far, core, own, most)
    mosts, known = [most], 4
    while known < groups:
        most = functools.reduce(jnp.maximum, mosts)
        mosts = [most, shift(most, known)]
        known *= 2
    y, most, last = next_round(
        x, mask, far, near, masks[0], masks[2], expands, first, mosts
    )
    state = x, y, mask, far, near, rest, masks, expands, most, first, last
    return lax.cond(most[0, 0] > sent, in_full, as_sent, *state)[None, None]


def solution(mesh):
    return jax.shard_map(
        local,
        mesh=mesh,
        in_specs=(
            P("rep", "clus", None, None),
            P("rep", "clus", None, None),
            P("rep", "clus", None, None),
        ),
        out_specs=P("rep", "clus", None, None),
        check_vma=False,
    )
```

```python
import functools

import jax
import jax.numpy as jnp
from jax import lax
from jax.experimental import pallas as pl
from jax.experimental.pallas import tpu as pltpu
from jax.sharding import PartitionSpec as P

LANES = 128
BLOCK = 128
COPY = 64
FIRST_SHARE = 3, 8
BOTH_LAST = (((1,), (1,)), ((), ()))


def bf16(*shape):
    return jax.ShapeDtypeStruct(shape, jnp.bfloat16)


def int32(*shape):
    return jax.ShapeDtypeStruct(shape, jnp.int32)


def kernel_call(name, kernel, outs, *args, flops, moved=0, scratch=(), mib=32, **specs):
    return pl.pallas_call(
        kernel,
        out_shape=outs,
        scratch_shapes=scratch,
        compiler_params=pltpu.CompilerParams(vmem_limit_bytes=mib * 1024 * 1024),
        cost_estimate=pl.CostEstimate(flops=flops, bytes_accessed=moved, transcendentals=0),
        name=name,
        **specs,
    )(*args)


def normalize(value):
    return value * lax.rsqrt(jnp.mean(value * value, axis=-1, keepdims=True) + 1e-06)


def normalize_kernel(x_hbm, out_ref, raw, sems):
    copies = []
    starts = range(0, raw.shape[0], BLOCK)
    for i, start in enumerate(starts):
        here = pl.ds(start, BLOCK)
        copies.append(pltpu.make_async_copy(x_hbm.at[here], raw.at[here], sems.at[i]))
        copies[-1].start()
    for copy, start in zip(copies, starts):
        copy.wait()
        here = pl.ds(start, BLOCK)
        out_ref[here] = normalize(raw[here].astype(jnp.float32)).astype(jnp.bfloat16)


def normalize_call(descriptors):
    rows, width = descriptors.shape
    return kernel_call(
        "normalize",
        normalize_kernel,
        bf16(rows, width),
        descriptors,
        flops=6 * rows * width,
        moved=4 * rows * width,
        scratch=[
            pltpu.VMEM((rows, width), jnp.bfloat16),
            pltpu.SemaphoreType.DMA((rows // BLOCK,)),
        ],
        mib=56,
        in_specs=[pl.BlockSpec(memory_space=pl.ANY)],
    )


def mask_kernel(slot_cap, pick_hbm, wanted_hbm, mask_ref, wanted_ref, pick, sems):
    copies = [
        pltpu.make_async_copy(pick_hbm, pick, sems.at[0]),
        pltpu.make_async_copy(wanted_hbm, wanted_ref, sems.at[1]),
    ]
    for copy in copies:
        copy.start()
    shape = mask_ref.shape[1], mask_ref.shape[0]
    slot = lax.broadcasted_iota(jnp.int32, shape, 0)
    slot = slot ^ (lax.axis_index("clus") * slot_cap)
    chosen = jnp.zeros(shape, jnp.float32)
    copies[0].wait()
    for k in range(pick.shape[0]):
        chosen = jnp.where(pick[k] == slot, 1.0, chosen)
    mask_ref[...] = chosen.T.astype(jnp.bfloat16)
    copies[1].wait()


def mask_call(slots, wanted):
    count, _, rows = slots.shape
    total = wanted.size
    return kernel_call(
        "mask",
        functools.partial(mask_kernel, wanted.shape[1]),
        [bf16(rows, total), pltpu.VMEM(wanted.shape, jnp.int32)],
        slots,
        wanted,
        flops=2 * count * rows * total,
        moved=2 * rows * total,
        scratch=[pltpu.VMEM(slots.shape, jnp.int32), pltpu.SemaphoreType.DMA((2,))],
        mib=56,
        in_specs=[pl.BlockSpec(memory_space=pl.ANY)] * 2,
    )


def list_kernel(rows, *refs):
    parts, refs = refs[:-5], refs[-5:]
    own_ref, far_ref, core_ref, expand_far_ref, expand_core_ref = refs
    total = own_ref.shape[1]
    lane = lax.broadcasted_iota(jnp.int32, (total, total), 1)
    sublane = lax.broadcasted_iota(jnp.int32, (total, total), 0)
    odd = lax.axis_index("rep") % 2
    lows = [(2 * odd * rows).astype(jnp.float32), ((2 - 2 * odd) * rows).astype(jnp.float32)]

    def inside(value, low):
        return (value >= low) & (value < low + rows)

    def asked(server):
        row = jnp.concatenate([ref[server, :] for ref in parts], axis=1).astype(jnp.float32)
        column = jnp.broadcast_to(row, (total, total)).T
        again = jnp.where((column == row) & (sublane < lane), 1.0, 0.0)
        return row, column, 1.0 - jnp.max(again, axis=0, keepdims=True)

    most = jnp.zeros((1, 1), jnp.float32)
    for server in range(len(parts)):
        row, _, first = asked(slice(server, server + 1))
        for low in lows:
            count = jnp.sum(jnp.where(inside(row, low), first, 0.0), axis=1, keepdims=True)
            most = jnp.maximum(most, count)
    row, column, first = asked(pl.ds(lax.axis_index("clus"), 1))
    own_ref[...] = jnp.broadcast_to(row - rows, own_ref.shape).astype(jnp.int32)
    place = lax.broadcasted_iota(jnp.int32, own_ref.shape, 0)
    for low, out_ref, expand_ref in zip(lows, (far_ref, core_ref), (expand_far_ref, expand_core_ref)):
        counted = jnp.where(inside(row, low), first, 0.0)
        rank = jnp.sum(jnp.where(row < column, counted, 0.0), axis=1, keepdims=True)
        here = inside(column, low) & (rank.astype(jnp.int32) == lane)
        expand_ref[...] = jnp.where(here, 1.0, 0.0).astype(jnp.bfloat16)
        packed = jnp.max(jnp.where(here, column - low, -1.0), axis=0, keepdims=True)
        out_ref[...] = jnp.where(place == 1, most, packed).astype(jnp.int32)


def list_call(parts, rows):
    total = parts[0].size
    return kernel_call(
        "list",
        functools.partial(list_kernel, rows),
        [int32(8, total)] * 3 + [bf16(total, total)] * 2,
        *parts,
        flops=40 * total * total,
    )


def one_hot(numbers, rows, count=None):
    total = numbers.shape[1]
    column = jnp.broadcast_to(numbers.astype(jnp.float32), (LANES, total)).T.astype(jnp.int32)
    column = column[:count]
    tiles = []
    for start in range(0, rows, LANES):
        lane = lax.broadcasted_iota(jnp.int32, column.shape, 1) + start
        tiles.append(jnp.where(column == lane, 1.0, 0.0).astype(jnp.bfloat16))
    return jnp.concatenate(tiles, axis=1)


def take(select, x):
    return jnp.dot(select, x, preferred_element_type=jnp.float32).astype(jnp.bfloat16)


def far_kernel(x_ref, beyond_ref, core_list_ref, told_ref, far_ref):
    far_ref[...] = take(one_hot(beyond_ref[0:1], *x_ref.shape[:1], far_ref.shape[0]), x_ref[...])
    place = lax.broadcasted_iota(jnp.int32, told_ref.shape, 0)
    most = jnp.maximum(core_list_ref[...], beyond_ref[...])
    told_ref[...] = jnp.where(place == 1, most, core_list_ref[...])


def far_call(x, beyond, core_list, sent):
    rows, width = x.shape
    return kernel_call(
        "pack_far",
        far_kernel,
        [int32(*core_list.shape), bf16(sent, width)],
        x,
        beyond,
        core_list,
        flops=2 * rows * sent * width,
    )


def near_kernel(x_ref, mask_ref, beyond_ref, own_list_ref, *refs):
    told_ref, within_ref, *refs = refs
    core_ref, own_ref, near_ref, rest_far_ref, rest_core_ref, *refs = refs
    far_mask_ref, core_mask_ref, near_mask_ref, most_ref, select = refs
    total, sent = own_ref.shape[0], core_ref.shape[0]
    rows = x_ref.shape[0]
    select[:total] = one_hot(within_ref[0:1], rows)
    select[total:] = one_hot(own_list_ref[0:1], rows)
    fetched = take(select[...], x_ref[...])
    core_ref[...] = fetched[:sent]
    near_ref[:sent] = fetched[:sent]
    rest_core_ref[...] = fetched[sent:total]
    own_ref[...] = fetched[total:]
    near_ref[sent:] = fetched[total:]
    pack = one_hot(beyond_ref[0:1], rows)
    rest_far_ref[...] = take(pack[sent:], x_ref[...])
    masks = take(select[...], mask_ref[...])
    core_mask_ref[...] = masks[:total]
    near_mask_ref[:sent] = masks[:sent]
    near_mask_ref[sent:] = masks[total:]
    far_mask_ref[...] = take(pack, mask_ref[...])
    most = jnp.maximum(told_ref[...], within_ref[...])
    most_ref[...] = jnp.broadcast_to(most[1:2, :LANES], most_ref.shape)


def near_call(x, mask, beyond, own_list, told, within, sent):
    rows, width = x.shape
    total = mask.shape[1]
    return kernel_call(
        "serve_near",
        near_kernel,
        [
            bf16(sent, width),
            bf16(total, width),
            bf16(sent + total, width),
            bf16(total - sent, width),
            bf16(total - sent, width),
            bf16(total, total),
            bf16(total, total),
            bf16(sent + total, total),
            int32(8, LANES),
        ],
        x,
        mask,
        beyond,
        own_list,
        told,
        within,
        flops=6 * total * rows * width,
        scratch=[pltpu.VMEM((2 * total, rows), jnp.bfloat16)],
    )


def unpack_kernel(first, bases, expand_ref, far_ref, *refs):
    out_ref, sent = refs[-1], far_ref.shape[0]
    rows = jnp.dot(
        expand_ref[:, first : first + sent], far_ref[...], preferred_element_type=jnp.float32
    )
    for base_ref in refs[:bases]:
        rows += base_ref[...].astype(jnp.float32)
    out_ref[...] = rows.astype(jnp.bfloat16)


def unpack_call(expand, far, *base, first=0, after=()):
    in_vmem = [pl.BlockSpec(memory_space=pltpu.VMEM)] * (2 + len(base))
    return kernel_call(
        "unpack",
        functools.partial(unpack_kernel, first, len(base)),
        bf16(expand.shape[0], far.shape[1]),
        expand,
        far,
        *base,
        *after,
        flops=2**34,
        moved=2**25,
        in_specs=in_vmem + [pl.BlockSpec(memory_space=pl.ANY)] * len(after),
    )


def combine_kernel(expand_ref, core_ref, base_ref, most_ref, out_most_ref, *out_refs):
    out_most_ref[...] = most_ref[...]
    cap, sent = out_refs[0].shape[0], core_ref.shape[0]
    rows = jnp.dot(expand_ref[:, :sent], core_ref[...], preferred_element_type=jnp.float32)
    rows = (rows + base_ref[...].astype(jnp.float32)).astype(jnp.bfloat16)
    for d, out in enumerate(out_refs):
        out[...] = rows[d * cap : (d + 1) * cap]


def combine_call(expand, core, base, most, servers):
    total, width = base.shape
    most, *parts = kernel_call(
        "combine",
        combine_kernel,
        [int32(*most.shape)] + [bf16(total // servers, width)] * servers,
        expand,
        core,
        base,
        most,
        flops=2 * total * core.shape[0] * width,
    )
    return most, parts


def unpack_both_kernel(far_expand, core_expand, own_ref, core_ref, far_ref, *refs):
    out_refs = refs[1:]
    cap, sent = out_refs[0].shape[0], far_ref.shape[0]
    rows = jnp.dot(core_expand[:, :sent], core_ref[...], preferred_element_type=jnp.float32)
    rows += jnp.dot(far_expand[:, :sent], far_ref[...], preferred_element_type=jnp.float32)
    rows = (rows + own_ref[...].astype(jnp.float32)).astype(jnp.bfloat16)
    for d, out in enumerate(out_refs):
        out[...] = rows[d * cap : (d + 1) * cap]


def unpack_both_call(expands, far, core, own, after, servers):
    total, width = own.shape
    return kernel_call(
        "unpack_both",
        unpack_both_kernel,
        [bf16(total // servers, width)] * servers,
        *expands,
        own,
        core,
        far,
        after,
        flops=4 * total * far.shape[0] * width,
        in_specs=[pl.BlockSpec(memory_space=pltpu.VMEM)] * 5
        + [pl.BlockSpec(memory_space=pl.ANY)],
    )


def fill(buffer, parts):
    cap = parts[0].shape[0]
    for d, ref in enumerate(reversed(parts)):
        buffer[d * cap : (d + 1) * cap] = ref[...]


def cube(dots, width):
    positive = jnp.maximum(dots * (1.0 / width), 0.0)
    return (positive * positive * positive).astype(jnp.bfloat16)


def weigh(x, buffer, mask):
    dots = lax.dot_general(x, buffer, BOTH_LAST, preferred_element_type=jnp.float32)
    return cube(dots, x.shape[1]) * mask


def mix(x, weights, buffer):
    mixed = x.astype(jnp.float32) + jnp.dot(weights, buffer, preferred_element_type=jnp.float32)
    return normalize(mixed).astype(jnp.bfloat16)


def far_mix_kernel(servers, x_ref, mask_ref, *rest):
    parts, rest = rest[:servers], rest[servers:]
    *most_refs, out_ref, most_ref, buffer = rest
    most_ref[...] = functools.reduce(jnp.maximum, [ref[...] for ref in most_refs])
    fill(buffer, parts)
    weights = weigh(x_ref[...], buffer[...], mask_ref[: x_ref.shape[0]])
    out_ref[...] = mix(x_ref[...], weights, buffer[...])


def far_mix_call(x, mask, parts, mosts):
    rows, width = x.shape
    total, servers = mask.shape[1], len(parts)
    return kernel_call(
        "mix_far",
        functools.partial(far_mix_kernel, servers),
        [bf16(rows, width), int32(*mosts[0].shape)],
        x,
        mask,
        *reversed(parts),
        *mosts,
        flops=4 * total * rows * width,
        scratch=[pltpu.VMEM((total, width), jnp.bfloat16)],
    )


def near_mix_kernel(servers, x_ref, mask_ref, *rest):
    parts, (core_ref, own_ref, buffer) = rest[:servers], rest[servers:]
    fill(buffer, parts)
    weights = weigh(x_ref[...], buffer[...], mask_ref[...])
    mixed = mix(x_ref[...], weights, buffer[...])
    core_ref[...] = mixed[: core_ref.shape[0]]
    own_ref[...] = mixed[core_ref.shape[0] :]


def near_mix_call(x, mask, parts):
    rows, width = x.shape
    total, servers = mask.shape[1], len(parts)
    return kernel_call(
        "mix_near",
        functools.partial(near_mix_kernel, servers),
        [bf16(rows - total, width), bf16(total, width)],
        x,
        mask,
        *reversed(parts),
        flops=4 * total * rows * width,
        scratch=[pltpu.VMEM((total, width), jnp.bfloat16)],
    )


def is_late():
    return (lax.axis_index("rep") + 1) % 4 < 2


def late_kernel(servers, x_ref, mask_ref, *rest):
    parts, (out_ref, buffer, weights) = rest[:servers], rest[servers:]

    @pl.when(is_late())
    def _():
        fill(buffer, parts)
        weights[...] = weigh(x_ref[...], buffer[...], mask_ref[...])
        for start in range(0, x_ref.shape[0], BLOCK):
            here = pl.ds(start, BLOCK)
            out_ref[here] = mix(x_ref[here], weights[here], buffer[...])


def late_call(x, mask, parts):
    rows, width = x.shape
    total, servers = mask.shape[1], len(parts)
    return kernel_call(
        "mix_whole_late",
        functools.partial(late_kernel, servers),
        bf16(rows, width),
        x,
        mask,
        *reversed(parts),
        flops=4 * total * rows * width,
        scratch=[
            pltpu.VMEM((total, width), jnp.bfloat16),
            pltpu.VMEM((rows, total), jnp.bfloat16),
        ],
    )


def mix_blocks(x_ref, mask_ref, buffer, turned, whole, out_ref, sems):
    copies = []
    turned[...] = buffer[...].T
    for start in range(0, x_ref.shape[0], BLOCK):
        here = pl.ds(start, BLOCK)
        dots = jnp.dot(x_ref[here], turned[...], preferred_element_type=jnp.float32)
        weights = cube(dots, x_ref.shape[1]) * mask_ref[here]
        whole[here] = mix(x_ref[here], weights, buffer[...])
        for half in range(start, start + BLOCK, COPY):
            rows = pl.ds(half, COPY)
            copy = pltpu.make_async_copy(
                whole.at[rows], out_ref.at[rows], sems.at[half // COPY]
            )
            copy.start()
            copies.append(copy)
    for copy in copies:
        copy.wait()


def early_kernel(servers, x_ref, mask_ref, *rest):
    parts, (_, out_ref, buffer, turned, whole, sems) = rest[:servers], rest[servers:]

    @pl.when(jnp.logical_not(is_late()))
    def _():
        fill(buffer, parts)
        mix_blocks(x_ref, mask_ref, buffer, turned, whole, out_ref, sems)


def early_call(x, mask, parts, out):
    rows, width = x.shape
    total, servers = mask.shape[1], len(parts)
    return kernel_call(
        "mix_whole_early",
        functools.partial(early_kernel, servers),
        bf16(rows, width),
        x,
        mask,
        *reversed(parts),
        out,
        flops=4 * total * rows * width,
        scratch=[
            pltpu.VMEM((total, width), jnp.bfloat16),
            pltpu.VMEM((width, total), jnp.bfloat16),
            pltpu.VMEM((rows, width), jnp.bfloat16),
            pltpu.SemaphoreType.DMA((rows // COPY,)),
        ],
        in_specs=[pl.BlockSpec(memory_space=pltpu.VMEM)] * (2 + servers)
        + [pl.BlockSpec(memory_space=pl.ANY)],
        out_specs=pl.BlockSpec(memory_space=pl.ANY),
        input_output_aliases={2 + servers: 0},
    )


def last_kernel(servers, x_ref, mask_ref, *rest):
    parts, (out_ref, buffer, turned, whole, sems) = rest[:servers], rest[servers:]
    fill(buffer, parts)
    mix_blocks(x_ref, mask_ref, buffer, turned, whole, out_ref, sems)


def last_call(x, mask, parts):
    rows, width = x.shape
    total, servers = mask.shape[1], len(parts)
    return kernel_call(
        "mix",
        functools.partial(last_kernel, servers),
        pltpu.HBM((rows, width), jnp.bfloat16),
        x,
        mask,
        *reversed(parts),
        flops=4 * total * rows * width,
        moved=4 * rows * width,
        scratch=[
            pltpu.VMEM((total, width), jnp.bfloat16),
            pltpu.VMEM((width, total), jnp.bfloat16),
            pltpu.VMEM((rows, width), jnp.bfloat16),
            pltpu.SemaphoreType.DMA((rows // COPY,)),
        ],
        out_specs=pl.BlockSpec(memory_space=pltpu.HBM),
    )


def local(descriptors, request, pick):
    wanted = request[0, 0]
    rows = descriptors.shape[2]
    servers, cap = wanted.shape
    total = servers * cap
    groups = lax.axis_size("rep")
    sent = total * FIRST_SHARE[0] // FIRST_SHARE[1]
    within = [(g, g ^ 1) for g in range(groups)]
    beyond = [(g, (g + 2 * (g % 2) - 1 + groups) % groups) for g in range(groups)]

    def turn(value, d):
        return lax.ppermute(value, "clus", [(c, c ^ d) for c in range(servers)])

    def shift(value, by):
        return lax.ppermute(value, "rep", [(g, (g + by) % groups) for g in range(groups)])

    def across(value):
        return lax.ppermute(value, "rep", beyond)

    def inside(value):
        return lax.ppermute(value, "rep", within)

    def turned(parts):
        got = {d: turn(parts[d], d) for d in reversed(range(1, servers))}
        return [parts[0]] + [got[d] for d in range(1, servers)]

    def exchange(expands, far, core, own, most):
        base = unpack_call(expands[0], across(far), own)
        most, parts = combine_call(expands[1], inside(core), base, most, servers)
        return most, turned(parts)

    def next_round(x, mask, far, near, far_mask, near_mask, expands, parts, mosts):
        far, most = far_mix_call(far, far_mask, parts, mosts)
        core, own = near_mix_call(near, near_mask, parts)
        y = late_call(x, mask, parts)
        last = unpack_both_call(expands, across(far), inside(core), own, y, servers)
        return early_call(x, mask, parts, y), most, turned(last)

    def in_full(x, y, mask, far, near, rest, masks, expands, most, first, last):
        late = unpack_call(expands[1], inside(rest[1]), first=sent)
        late = unpack_call(expands[0], across(rest[0]), late, first=sent)
        late = turned(list(late.reshape(servers, cap, -1)))
        first = [a + b for a, b in zip(first, late)]
        far = jnp.concatenate([far, rest[0]], axis=0)
        near = jnp.concatenate([near[:sent], rest[1], near[sent:]], axis=0)
        near_mask = jnp.concatenate([masks[1], masks[2][sent:]], axis=0)
        y, _, last = next_round(
            x, mask, far, near, masks[0], near_mask, expands, first, [most]
        )
        return last_call(y, mask, last)

    def as_sent(x, y, mask, far, near, rest, masks, expands, most, first, last):
        return last_call(y, mask, last)

    asked = {d: turn(wanted, d) for d in reversed(range(1, servers))}
    mask, held = mask_call(pick.transpose(0, 3, 1, 2)[0], wanted)
    own_list, far_list, core_list, *expands = list_call(
        [held] + [asked[d] for d in range(1, servers)], rows
    )
    beyond_list = across(far_list)
    x = normalize_call(descriptors[0, 0])
    told, far = far_call(x, beyond_list, core_list, sent)
    core, own, near, *others, most = near_call(
        x, mask, beyond_list, own_list, told, inside(told), sent
    )
    rest, masks = others[:2], others[2:]
    most, first = exchange(expands, far, core, own, most)
    mosts, known = [most], 4
    while known < groups:
        most = functools.reduce(jnp.maximum, mosts)
        mosts = [most, shift(most, known)]
        known *= 2
    y, most, last = next_round(
        x, mask, far, near, masks[0], masks[2], expands, first, mosts
    )
    state = x, y, mask, far, near, rest, masks, expands, most, first, last
    return lax.cond(most[0, 0] > sent, in_full, as_sent, *state)[None, None]


def solution(mesh):
    return jax.shard_map(
        local,
        mesh=mesh,
        in_specs=(
            P("rep", "clus", None, None),
            P("rep", "clus", None, None),
            P("rep", "clus", None, None),
        ),
        out_specs=P("rep", "clus", None, None),
        check_vma=False,
    )
```

```python
import functools

import jax
import jax.numpy as jnp
from jax import lax
from jax.experimental import pallas as pl
from jax.experimental.pallas import tpu as pltpu
from jax.sharding import PartitionSpec as P

LANES = 128
BLOCK = 128
COPY = 64
FIRST_SHARE = 3, 8
BOTH_LAST = (((1,), (1,)), ((), ()))


def bf16(*shape):
    return jax.ShapeDtypeStruct(shape, jnp.bfloat16)


def int32(*shape):
    return jax.ShapeDtypeStruct(shape, jnp.int32)


def kernel_call(name, kernel, outs, *args, flops, moved=0, scratch=(), mib=32, **specs):
    return pl.pallas_call(
        kernel,
        out_shape=outs,
        scratch_shapes=scratch,
        compiler_params=pltpu.CompilerParams(vmem_limit_bytes=mib * 1024 * 1024),
        cost_estimate=pl.CostEstimate(flops=flops, bytes_accessed=moved, transcendentals=0),
        name=name,
        **specs,
    )(*args)


def normalize(value):
    return value * lax.rsqrt(jnp.mean(value * value, axis=-1, keepdims=True) + 1e-06)


def normalize_kernel(x_hbm, out_ref, raw, sems):
    copies = []
    starts = range(0, raw.shape[0], BLOCK)
    for i, start in enumerate(starts):
        here = pl.ds(start, BLOCK)
        copies.append(pltpu.make_async_copy(x_hbm.at[here], raw.at[here], sems.at[i]))
        copies[-1].start()
    for copy, start in zip(copies, starts):
        copy.wait()
        here = pl.ds(start, BLOCK)
        out_ref[here] = normalize(raw[here].astype(jnp.float32)).astype(jnp.bfloat16)


def normalize_call(descriptors):
    rows, width = descriptors.shape
    return kernel_call(
        "normalize",
        normalize_kernel,
        bf16(rows, width),
        descriptors,
        flops=6 * rows * width,
        moved=4 * rows * width,
        scratch=[
            pltpu.VMEM((rows, width), jnp.bfloat16),
            pltpu.SemaphoreType.DMA((rows // BLOCK,)),
        ],
        mib=56,
        in_specs=[pl.BlockSpec(memory_space=pl.ANY)],
    )


def mask_kernel(slot_cap, pick_hbm, wanted_hbm, mask_ref, wanted_ref, pick, sems):
    copies = [
        pltpu.make_async_copy(pick_hbm, pick, sems.at[0]),
        pltpu.make_async_copy(wanted_hbm, wanted_ref, sems.at[1]),
    ]
    for copy in copies:
        copy.start()
    shape = mask_ref.shape[1], mask_ref.shape[0]
    slot = lax.broadcasted_iota(jnp.int32, shape, 0)
    slot = slot ^ (lax.axis_index("clus") * slot_cap)
    chosen = jnp.zeros(shape, jnp.float32)
    copies[0].wait()
    for k in range(pick.shape[0]):
        chosen = jnp.where(pick[k] == slot, 1.0, chosen)
    mask_ref[...] = chosen.T.astype(jnp.bfloat16)
    copies[1].wait()


def mask_call(slots, wanted):
    count, _, rows = slots.shape
    total = wanted.size
    return kernel_call(
        "mask",
        functools.partial(mask_kernel, wanted.shape[1]),
        [bf16(rows, total), pltpu.VMEM(wanted.shape, jnp.int32)],
        slots,
        wanted,
        flops=2 * count * rows * total,
        moved=2 * rows * total,
        scratch=[pltpu.VMEM(slots.shape, jnp.int32), pltpu.SemaphoreType.DMA((2,))],
        mib=56,
        in_specs=[pl.BlockSpec(memory_space=pl.ANY)] * 2,
    )


def list_kernel(rows, *refs):
    parts, refs = refs[:-5], refs[-5:]
    own_ref, far_ref, core_ref, expand_far_ref, expand_core_ref = refs
    total = own_ref.shape[1]
    lane = lax.broadcasted_iota(jnp.int32, (total, total), 1)
    sublane = lax.broadcasted_iota(jnp.int32, (total, total), 0)
    odd = lax.axis_index("rep") % 2
    lows = [(2 * odd * rows).astype(jnp.float32), ((2 - 2 * odd) * rows).astype(jnp.float32)]

    def inside(value, low):
        return (value >= low) & (value < low + rows)

    def asked(server):
        row = jnp.concatenate([ref[server, :] for ref in parts], axis=1).astype(jnp.float32)
        column = jnp.broadcast_to(row, (total, total)).T
        again = jnp.where((column == row) & (sublane < lane), 1.0, 0.0)
        return row, column, 1.0 - jnp.max(again, axis=0, keepdims=True)

    most = jnp.zeros((1, 1), jnp.float32)
    for server in range(len(parts)):
        row, _, first = asked(slice(server, server + 1))
        for low in lows:
            count = jnp.sum(jnp.where(inside(row, low), first, 0.0), axis=1, keepdims=True)
            most = jnp.maximum(most, count)
    row, column, first = asked(pl.ds(lax.axis_index("clus"), 1))
    own_ref[...] = jnp.broadcast_to(row - rows, own_ref.shape).astype(jnp.int32)
    place = lax.broadcasted_iota(jnp.int32, own_ref.shape, 0)
    for low, out_ref, expand_ref in zip(lows, (far_ref, core_ref), (expand_far_ref, expand_core_ref)):
        counted = jnp.where(inside(row, low), first, 0.0)
        rank = jnp.sum(jnp.where(row < column, counted, 0.0), axis=1, keepdims=True)
        here = inside(column, low) & (rank.astype(jnp.int32) == lane)
        expand_ref[...] = jnp.where(here, 1.0, 0.0).astype(jnp.bfloat16)
        packed = jnp.max(jnp.where(here, column - low, -1.0), axis=0, keepdims=True)
        out_ref[...] = jnp.where(place == 1, most, packed).astype(jnp.int32)


def list_call(parts, rows):
    total = parts[0].size
    return kernel_call(
        "list",
        functools.partial(list_kernel, rows),
        [int32(8, total)] * 3 + [bf16(total, total)] * 2,
        *parts,
        flops=40 * total * total,
    )


def one_hot(numbers, rows, count=None):
    total = numbers.shape[1]
    column = jnp.broadcast_to(numbers.astype(jnp.float32), (LANES, total)).T.astype(jnp.int32)
    column = column[:count]
    tiles = []
    for start in range(0, rows, LANES):
        lane = lax.broadcasted_iota(jnp.int32, column.shape, 1) + start
        tiles.append(jnp.where(column == lane, 1.0, 0.0).astype(jnp.bfloat16))
    return jnp.concatenate(tiles, axis=1)


def take(select, x):
    return jnp.dot(select, x, preferred_element_type=jnp.float32).astype(jnp.bfloat16)


def far_kernel(x_ref, beyond_ref, core_list_ref, told_ref, far_ref):
    far_ref[...] = take(one_hot(beyond_ref[0:1], *x_ref.shape[:1], far_ref.shape[0]), x_ref[...])
    place = lax.broadcasted_iota(jnp.int32, told_ref.shape, 0)
    most = jnp.maximum(core_list_ref[...], beyond_ref[...])
    told_ref[...] = jnp.where(place == 1, most, core_list_ref[...])


def far_call(x, beyond, core_list, sent):
    rows, width = x.shape
    return kernel_call(
        "pack_far",
        far_kernel,
        [int32(*core_list.shape), bf16(sent, width)],
        x,
        beyond,
        core_list,
        flops=2 * rows * sent * width,
    )


def near_kernel(x_ref, mask_ref, beyond_ref, own_list_ref, *refs):
    told_ref, within_ref, *refs = refs
    core_ref, own_ref, near_ref, rest_far_ref, rest_core_ref, *refs = refs
    far_mask_ref, core_mask_ref, near_mask_ref, far_turned_ref, most_ref, select = refs
    total, sent = own_ref.shape[0], core_ref.shape[0]
    rows = x_ref.shape[0]
    select[:total] = one_hot(within_ref[0:1], rows)
    select[total:] = one_hot(own_list_ref[0:1], rows)
    fetched = take(select[...], x_ref[...])
    core_ref[...] = fetched[:sent]
    near_ref[:sent] = fetched[:sent]
    rest_core_ref[...] = fetched[sent:total]
    own_ref[...] = fetched[total:]
    near_ref[sent:] = fetched[total:]
    pack = one_hot(beyond_ref[0:1], rows)
    far = jnp.dot(pack, x_ref[...], preferred_element_type=jnp.float32)
    rest_far_ref[...] = far[sent:].astype(jnp.bfloat16)
    far_turned_ref[...] = far.T.astype(jnp.bfloat16)
    masks = take(select[...], mask_ref[...])
    core_mask_ref[...] = masks[:total]
    near_mask_ref[:sent] = masks[:sent]
    near_mask_ref[sent:] = masks[total:]
    far_mask_ref[...] = take(pack, mask_ref[...])
    most = jnp.maximum(told_ref[...], within_ref[...])
    most_ref[...] = jnp.broadcast_to(most[1:2, :LANES], most_ref.shape)


def near_call(x, mask, beyond, own_list, told, within, sent):
    rows, width = x.shape
    total = mask.shape[1]
    return kernel_call(
        "serve_near",
        near_kernel,
        [
            bf16(sent, width),
            bf16(total, width),
            bf16(sent + total, width),
            bf16(total - sent, width),
            bf16(total - sent, width),
            bf16(total, total),
            bf16(total, total),
            bf16(sent + total, total),
            bf16(width, total),
            int32(8, LANES),
        ],
        x,
        mask,
        beyond,
        own_list,
        told,
        within,
        flops=6 * total * rows * width,
        scratch=[pltpu.VMEM((2 * total, rows), jnp.bfloat16)],
    )


def unpack_kernel(first, bases, expand_ref, far_ref, *refs):
    out_ref, sent = refs[-1], far_ref.shape[0]
    rows = jnp.dot(
        expand_ref[:, first : first + sent], far_ref[...], preferred_element_type=jnp.float32
    )
    for base_ref in refs[:bases]:
        rows += base_ref[...].astype(jnp.float32)
    out_ref[...] = rows.astype(jnp.bfloat16)


def unpack_call(expand, far, *base, first=0, after=()):
    in_vmem = [pl.BlockSpec(memory_space=pltpu.VMEM)] * (2 + len(base))
    return kernel_call(
        "unpack",
        functools.partial(unpack_kernel, first, len(base)),
        bf16(expand.shape[0], far.shape[1]),
        expand,
        far,
        *base,
        *after,
        flops=2**34,
        moved=2**25,
        in_specs=in_vmem + [pl.BlockSpec(memory_space=pl.ANY)] * len(after),
    )


def combine_kernel(expand_ref, core_ref, base_ref, most_ref, out_most_ref, *out_refs):
    out_most_ref[...] = most_ref[...]
    cap, sent = out_refs[0].shape[0], core_ref.shape[0]
    rows = jnp.dot(expand_ref[:, :sent], core_ref[...], preferred_element_type=jnp.float32)
    rows = (rows + base_ref[...].astype(jnp.float32)).astype(jnp.bfloat16)
    for d, out in enumerate(out_refs):
        out[...] = rows[d * cap : (d + 1) * cap]


def combine_call(expand, core, base, most, servers):
    total, width = base.shape
    most, *parts = kernel_call(
        "combine",
        combine_kernel,
        [int32(*most.shape)] + [bf16(total // servers, width)] * servers,
        expand,
        core,
        base,
        most,
        flops=2 * total * core.shape[0] * width,
    )
    return most, parts


def unpack_both_kernel(far_expand, core_expand, own_ref, core_ref, far_ref, *refs):
    out_refs = refs[1:]
    cap, sent = out_refs[0].shape[0], far_ref.shape[0]
    rows = jnp.dot(core_expand[:, :sent], core_ref[...], preferred_element_type=jnp.float32)
    rows += jnp.dot(far_expand[:, :sent], far_ref[...], preferred_element_type=jnp.float32)
    rows = (rows + own_ref[...].astype(jnp.float32)).astype(jnp.bfloat16)
    for d, out in enumerate(out_refs):
        out[...] = rows[d * cap : (d + 1) * cap]


def unpack_both_call(expands, far, core, own, after, servers):
    total, width = own.shape
    return kernel_call(
        "unpack_both",
        unpack_both_kernel,
        [bf16(total // servers, width)] * servers,
        *expands,
        own,
        core,
        far,
        after,
        flops=4 * total * far.shape[0] * width,
        in_specs=[pl.BlockSpec(memory_space=pltpu.VMEM)] * 5
        + [pl.BlockSpec(memory_space=pl.ANY)],
    )


def fill(buffer, parts):
    cap = parts[0].shape[0]
    for d, ref in enumerate(reversed(parts)):
        buffer[d * cap : (d + 1) * cap] = ref[...]


def cube(dots, width):
    positive = jnp.maximum(dots * (1.0 / width), 0.0)
    return (positive * positive * positive).astype(jnp.bfloat16)


def weigh(x, buffer, mask):
    dots = lax.dot_general(x, buffer, BOTH_LAST, preferred_element_type=jnp.float32)
    return cube(dots, x.shape[1]) * mask


def mix(x, weights, buffer):
    mixed = x.astype(jnp.float32) + jnp.dot(weights, buffer, preferred_element_type=jnp.float32)
    return normalize(mixed).astype(jnp.bfloat16)


def far_mix_kernel(servers, x_ref, turned_ref, mask_ref, *rest):
    parts, rest = rest[:servers], rest[servers:]
    *most_refs, out_ref, most_ref, buffer = rest
    most_ref[...] = functools.reduce(jnp.maximum, [ref[...] for ref in most_refs])
    fill(buffer, parts)
    rows, width = x_ref.shape
    dots = jnp.dot(buffer[...], turned_ref[...], preferred_element_type=jnp.float32).T[:rows]
    weights = cube(dots, width) * mask_ref[:rows]
    out_ref[...] = mix(x_ref[...], weights, buffer[...])


def far_mix_call(x, turned, mask, parts, mosts):
    rows, width = x.shape
    total, servers = mask.shape[1], len(parts)
    return kernel_call(
        "mix_far",
        functools.partial(far_mix_kernel, servers),
        [bf16(rows, width), int32(*mosts[0].shape)],
        x,
        turned,
        mask,
        *reversed(parts),
        *mosts,
        flops=4 * total * rows * width,
        scratch=[pltpu.VMEM((total, width), jnp.bfloat16)],
    )


def near_mix_kernel(servers, x_ref, mask_ref, *rest):
    parts, (core_ref, own_ref, buffer) = rest[:servers], rest[servers:]
    fill(buffer, parts)
    weights = weigh(x_ref[...], buffer[...], mask_ref[...])
    mixed = mix(x_ref[...], weights, buffer[...])
    core_ref[...] = mixed[: core_ref.shape[0]]
    own_ref[...] = mixed[core_ref.shape[0] :]


def near_mix_call(x, mask, parts):
    rows, width = x.shape
    total, servers = mask.shape[1], len(parts)
    return kernel_call(
        "mix_near",
        functools.partial(near_mix_kernel, servers),
        [bf16(rows - total, width), bf16(total, width)],
        x,
        mask,
        *reversed(parts),
        flops=4 * total * rows * width,
        scratch=[pltpu.VMEM((total, width), jnp.bfloat16)],
    )


def is_late():
    return (lax.axis_index("rep") + 1) % 4 < 2


def late_kernel(servers, x_ref, mask_ref, *rest):
    parts, (out_ref, buffer, weights) = rest[:servers], rest[servers:]

    @pl.when(is_late())
    def _():
        fill(buffer, parts)
        weights[...] = weigh(x_ref[...], buffer[...], mask_ref[...])
        for start in range(0, x_ref.shape[0], BLOCK):
            here = pl.ds(start, BLOCK)
            out_ref[here] = mix(x_ref[here], weights[here], buffer[...])


def late_call(x, mask, parts):
    rows, width = x.shape
    total, servers = mask.shape[1], len(parts)
    return kernel_call(
        "mix_whole_late",
        functools.partial(late_kernel, servers),
        bf16(rows, width),
        x,
        mask,
        *reversed(parts),
        flops=4 * total * rows * width,
        scratch=[
            pltpu.VMEM((total, width), jnp.bfloat16),
            pltpu.VMEM((rows, total), jnp.bfloat16),
        ],
    )


def mix_blocks(x_ref, mask_ref, buffer, turned, whole, out_ref, sems):
    copies = []
    turned[...] = buffer[...].T
    for start in range(0, x_ref.shape[0], BLOCK):
        here = pl.ds(start, BLOCK)
        if start % (2 * BLOCK) == 0:
            two = pl.ds(start, 2 * BLOCK)
            dots = jnp.dot(x_ref[two], turned[...], preferred_element_type=jnp.float32)
            weights = cube(dots, x_ref.shape[1]) * mask_ref[two]
        half = start % (2 * BLOCK)
        whole[here] = mix(x_ref[here], weights[half : half + BLOCK], buffer[...])
        for first in range(start, start + BLOCK, COPY):
            rows = pl.ds(first, COPY)
            copy = pltpu.make_async_copy(
                whole.at[rows], out_ref.at[rows], sems.at[first // COPY]
            )
            copy.start()
            copies.append(copy)
    for copy in copies:
        copy.wait()


def early_kernel(servers, x_ref, mask_ref, *rest):
    parts, (_, out_ref, buffer, turned, whole, sems) = rest[:servers], rest[servers:]

    @pl.when(jnp.logical_not(is_late()))
    def _():
        fill(buffer, parts)
        mix_blocks(x_ref, mask_ref, buffer, turned, whole, out_ref, sems)


def early_call(x, mask, parts, out):
    rows, width = x.shape
    total, servers = mask.shape[1], len(parts)
    return kernel_call(
        "mix_whole_early",
        functools.partial(early_kernel, servers),
        bf16(rows, width),
        x,
        mask,
        *reversed(parts),
        out,
        flops=4 * total * rows * width,
        scratch=[
            pltpu.VMEM((total, width), jnp.bfloat16),
            pltpu.VMEM((width, total), jnp.bfloat16),
            pltpu.VMEM((rows, width), jnp.bfloat16),
            pltpu.SemaphoreType.DMA((rows // COPY,)),
        ],
        in_specs=[pl.BlockSpec(memory_space=pltpu.VMEM)] * (2 + servers)
        + [pl.BlockSpec(memory_space=pl.ANY)],
        out_specs=pl.BlockSpec(memory_space=pl.ANY),
        input_output_aliases={2 + servers: 0},
    )


def last_kernel(servers, x_ref, mask_ref, *rest):
    parts, (out_ref, buffer, turned, whole, sems) = rest[:servers], rest[servers:]
    fill(buffer, parts)
    mix_blocks(x_ref, mask_ref, buffer, turned, whole, out_ref, sems)


def last_call(x, mask, parts):
    rows, width = x.shape
    total, servers = mask.shape[1], len(parts)
    return kernel_call(
        "mix",
        functools.partial(last_kernel, servers),
        pltpu.HBM((rows, width), jnp.bfloat16),
        x,
        mask,
        *reversed(parts),
        flops=4 * total * rows * width,
        moved=4 * rows * width,
        scratch=[
            pltpu.VMEM((total, width), jnp.bfloat16),
            pltpu.VMEM((width, total), jnp.bfloat16),
            pltpu.VMEM((rows, width), jnp.bfloat16),
            pltpu.SemaphoreType.DMA((rows // COPY,)),
        ],
        out_specs=pl.BlockSpec(memory_space=pltpu.HBM),
    )


def local(descriptors, request, pick):
    wanted = request[0, 0]
    rows = descriptors.shape[2]
    servers, cap = wanted.shape
    total = servers * cap
    groups = lax.axis_size("rep")
    sent = total * FIRST_SHARE[0] // FIRST_SHARE[1]
    within = [(g, g ^ 1) for g in range(groups)]
    beyond = [(g, (g + 2 * (g % 2) - 1 + groups) % groups) for g in range(groups)]

    def turn(value, d):
        return lax.ppermute(value, "clus", [(c, c ^ d) for c in range(servers)])

    def shift(value, by):
        return lax.ppermute(value, "rep", [(g, (g + by) % groups) for g in range(groups)])

    def across(value):
        return lax.ppermute(value, "rep", beyond)

    def inside(value):
        return lax.ppermute(value, "rep", within)

    def turned(parts):
        got = {d: turn(parts[d], d) for d in reversed(range(1, servers))}
        return [parts[0]] + [got[d] for d in range(1, servers)]

    def exchange(expands, far, core, own, most):
        base = unpack_call(expands[0], across(far), own)
        most, parts = combine_call(expands[1], inside(core), base, most, servers)
        return most, turned(parts)

    def next_round(x, mask, far, near, far_turned, far_mask, near_mask, expands, parts, mosts):
        far, most = far_mix_call(far, far_turned, far_mask, parts, mosts)
        core, own = near_mix_call(near, near_mask, parts)
        y = late_call(x, mask, parts)
        last = unpack_both_call(expands, across(far), inside(core), own, y, servers)
        return early_call(x, mask, parts, y), most, turned(last)

    def in_full(x, y, mask, far, near, rest, masks, expands, most, first, last):
        late = unpack_call(expands[1], inside(rest[1]), first=sent)
        late = unpack_call(expands[0], across(rest[0]), late, first=sent)
        late = turned(list(late.reshape(servers, cap, -1)))
        first = [a + b for a, b in zip(first, late)]
        far = jnp.concatenate([far, rest[0]], axis=0)
        near = jnp.concatenate([near[:sent], rest[1], near[sent:]], axis=0)
        near_mask = jnp.concatenate([masks[1], masks[2][sent:]], axis=0)
        y, _, last = next_round(
            x, mask, far, near, masks[3], masks[0], near_mask, expands, first, [most]
        )
        return last_call(y, mask, last)

    def as_sent(x, y, mask, far, near, rest, masks, expands, most, first, last):
        return last_call(y, mask, last)

    asked = {d: turn(wanted, d) for d in reversed(range(1, servers))}
    mask, held = mask_call(pick.transpose(0, 3, 1, 2)[0], wanted)
    own_list, far_list, core_list, *expands = list_call(
        [held] + [asked[d] for d in range(1, servers)], rows
    )
    beyond_list = across(far_list)
    x = normalize_call(descriptors[0, 0])
    told, far = far_call(x, beyond_list, core_list, sent)
    core, own, near, *others, most = near_call(
        x, mask, beyond_list, own_list, told, inside(told), sent
    )
    rest, masks = others[:2], others[2:]
    most, first = exchange(expands, far, core, own, most)
    mosts, known = [most], 4
    while known < groups:
        most = functools.reduce(jnp.maximum, mosts)
        mosts = [most, shift(most, known)]
        known *= 2
    y, most, last = next_round(
        x, mask, far, near, masks[3], masks[0], masks[2], expands, first, mosts
    )
    state = x, y, mask, far, near, rest, masks, expands, most, first, last
    return lax.cond(most[0, 0] > sent, in_full, as_sent, *state)[None, None]


def solution(mesh):
    return jax.shard_map(
        local,
        mesh=mesh,
        in_specs=(
            P("rep", "clus", None, None),
            P("rep", "clus", None, None),
            P("rep", "clus", None, None),
        ),
        out_specs=P("rep", "clus", None, None),
        check_vma=False,
    )
```

```python
import functools

import jax
import jax.numpy as jnp
from jax import lax
from jax.experimental import pallas as pl
from jax.experimental.pallas import tpu as pltpu
from jax.sharding import PartitionSpec as P

LANES = 128
BLOCK = 128
COPY = 64
FIRST_SHARE = 3, 8
BOTH_LAST = (((1,), (1,)), ((), ()))


def bf16(*shape):
    return jax.ShapeDtypeStruct(shape, jnp.bfloat16)


def int32(*shape):
    return jax.ShapeDtypeStruct(shape, jnp.int32)


def kernel_call(name, kernel, outs, *args, flops, moved=0, scratch=(), mib=32, **specs):
    return pl.pallas_call(
        kernel,
        out_shape=outs,
        scratch_shapes=scratch,
        compiler_params=pltpu.CompilerParams(vmem_limit_bytes=mib * 1024 * 1024),
        cost_estimate=pl.CostEstimate(flops=flops, bytes_accessed=moved, transcendentals=0),
        name=name,
        **specs,
    )(*args)


def normalize(value):
    return value * lax.rsqrt(jnp.mean(value * value, axis=-1, keepdims=True) + 1e-06)


def normalize_kernel(x_hbm, out_ref, raw, sems):
    copies = []
    starts = range(0, raw.shape[0], BLOCK)
    for i, start in enumerate(starts):
        here = pl.ds(start, BLOCK)
        copies.append(pltpu.make_async_copy(x_hbm.at[here], raw.at[here], sems.at[i]))
        copies[-1].start()
    for copy, start in zip(copies, starts):
        copy.wait()
        here = pl.ds(start, BLOCK)
        out_ref[here] = normalize(raw[here].astype(jnp.float32)).astype(jnp.bfloat16)


def normalize_call(descriptors):
    rows, width = descriptors.shape
    return kernel_call(
        "normalize",
        normalize_kernel,
        bf16(rows, width),
        descriptors,
        flops=6 * rows * width,
        moved=4 * rows * width,
        scratch=[
            pltpu.VMEM((rows, width), jnp.bfloat16),
            pltpu.SemaphoreType.DMA((rows // BLOCK,)),
        ],
        mib=56,
        in_specs=[pl.BlockSpec(memory_space=pl.ANY)],
    )


def mask_kernel(slot_cap, pick_hbm, wanted_hbm, mask_ref, wanted_ref, pick, sems):
    copies = [
        pltpu.make_async_copy(pick_hbm, pick, sems.at[0]),
        pltpu.make_async_copy(wanted_hbm, wanted_ref, sems.at[1]),
    ]
    for copy in copies:
        copy.start()
    shape = mask_ref.shape[1], mask_ref.shape[0]
    slot = lax.broadcasted_iota(jnp.int32, shape, 0)
    slot = slot ^ (lax.axis_index("clus") * slot_cap)
    chosen = jnp.zeros(shape, jnp.float32)
    copies[0].wait()
    for k in range(pick.shape[0]):
        chosen = jnp.where(pick[k] == slot, 1.0, chosen)
    mask_ref[...] = chosen.T.astype(jnp.bfloat16)
    copies[1].wait()


def mask_call(slots, wanted):
    count, _, rows = slots.shape
    total = wanted.size
    return kernel_call(
        "mask",
        functools.partial(mask_kernel, wanted.shape[1]),
        [bf16(rows, total), pltpu.VMEM(wanted.shape, jnp.int32)],
        slots,
        wanted,
        flops=2 * count * rows * total,
        moved=2 * rows * total,
        scratch=[pltpu.VMEM(slots.shape, jnp.int32), pltpu.SemaphoreType.DMA((2,))],
        mib=56,
        in_specs=[pl.BlockSpec(memory_space=pl.ANY)] * 2,
    )


def list_kernel(rows, *refs):
    parts, refs = refs[:-5], refs[-5:]
    own_ref, far_ref, core_ref, expand_far_ref, expand_core_ref = refs
    total = own_ref.shape[1]
    lane = lax.broadcasted_iota(jnp.int32, (total, total), 1)
    sublane = lax.broadcasted_iota(jnp.int32, (total, total), 0)
    odd = lax.axis_index("rep") % 2
    lows = [(2 * odd * rows).astype(jnp.float32), ((2 - 2 * odd) * rows).astype(jnp.float32)]

    def inside(value, low):
        return (value >= low) & (value < low + rows)

    def asked(server):
        row = jnp.concatenate([ref[server, :] for ref in parts], axis=1).astype(jnp.float32)
        column = jnp.broadcast_to(row, (total, total)).T
        again = jnp.where((column == row) & (sublane < lane), 1.0, 0.0)
        return row, column, 1.0 - jnp.max(again, axis=0, keepdims=True)

    most = jnp.zeros((1, 1), jnp.float32)
    for server in range(len(parts)):
        row, _, first = asked(slice(server, server + 1))
        for low in lows:
            count = jnp.sum(jnp.where(inside(row, low), first, 0.0), axis=1, keepdims=True)
            most = jnp.maximum(most, count)
    row, column, first = asked(pl.ds(lax.axis_index("clus"), 1))
    own_ref[...] = jnp.broadcast_to(row - rows, own_ref.shape).astype(jnp.int32)
    place = lax.broadcasted_iota(jnp.int32, own_ref.shape, 0)
    for low, out_ref, expand_ref in zip(lows, (far_ref, core_ref), (expand_far_ref, expand_core_ref)):
        counted = jnp.where(inside(row, low), first, 0.0)
        rank = jnp.sum(jnp.where(row < column, counted, 0.0), axis=1, keepdims=True)
        here = inside(column, low) & (rank.astype(jnp.int32) == lane)
        expand_ref[...] = jnp.where(here, 1.0, 0.0).astype(jnp.bfloat16)
        packed = jnp.max(jnp.where(here, column - low, -1.0), axis=0, keepdims=True)
        out_ref[...] = jnp.where(place == 1, most, packed).astype(jnp.int32)


def list_call(parts, rows):
    total = parts[0].size
    return kernel_call(
        "list",
        functools.partial(list_kernel, rows),
        [int32(8, total)] * 3 + [bf16(total, total)] * 2,
        *parts,
        flops=40 * total * total,
    )


def one_hot(numbers, rows, count=None):
    total = numbers.shape[1]
    column = jnp.broadcast_to(numbers.astype(jnp.float32), (LANES, total)).T.astype(jnp.int32)
    column = column[:count]
    tiles = []
    for start in range(0, rows, LANES):
        lane = lax.broadcasted_iota(jnp.int32, column.shape, 1) + start
        tiles.append(jnp.where(column == lane, 1.0, 0.0).astype(jnp.bfloat16))
    return jnp.concatenate(tiles, axis=1)


def take(select, x):
    return jnp.dot(select, x, preferred_element_type=jnp.float32).astype(jnp.bfloat16)


def far_kernel(x_ref, beyond_ref, core_list_ref, told_ref, far_ref):
    far_ref[...] = take(one_hot(beyond_ref[0:1], *x_ref.shape[:1], far_ref.shape[0]), x_ref[...])
    place = lax.broadcasted_iota(jnp.int32, told_ref.shape, 0)
    most = jnp.maximum(core_list_ref[...], beyond_ref[...])
    told_ref[...] = jnp.where(place == 1, most, core_list_ref[...])


def far_call(x, beyond, core_list, sent):
    rows, width = x.shape
    return kernel_call(
        "pack_far",
        far_kernel,
        [int32(*core_list.shape), bf16(sent, width)],
        x,
        beyond,
        core_list,
        flops=2 * rows * sent * width,
    )


def near_kernel(x_ref, mask_ref, beyond_ref, own_list_ref, *refs):
    told_ref, within_ref, *refs = refs
    core_ref, own_ref, near_ref, rest_far_ref, rest_core_ref, *refs = refs
    far_mask_ref, core_mask_ref, near_mask_ref, far_turned_ref, most_ref, select = refs
    total, sent = own_ref.shape[0], core_ref.shape[0]
    rows = x_ref.shape[0]
    select[:total] = one_hot(within_ref[0:1], rows)
    select[total:] = one_hot(own_list_ref[0:1], rows)
    fetched = take(select[...], x_ref[...])
    core_ref[...] = fetched[:sent]
    near_ref[:sent] = fetched[:sent]
    rest_core_ref[...] = fetched[sent:total]
    own_ref[...] = fetched[total:]
    near_ref[sent:] = fetched[total:]
    pack = one_hot(beyond_ref[0:1], rows)
    far = jnp.dot(pack, x_ref[...], preferred_element_type=jnp.float32)
    rest_far_ref[...] = far[sent:].astype(jnp.bfloat16)
    far_turned_ref[...] = far.T.astype(jnp.bfloat16)
    masks = take(select[...], mask_ref[...])
    core_mask_ref[...] = masks[:total]
    near_mask_ref[:sent] = masks[:sent]
    near_mask_ref[sent:] = masks[total:]
    far_mask_ref[...] = take(pack, mask_ref[...])
    most = jnp.maximum(told_ref[...], within_ref[...])
    most_ref[...] = jnp.broadcast_to(most[1:2, :LANES], most_ref.shape)


def near_call(x, mask, beyond, own_list, told, within, sent):
    rows, width = x.shape
    total = mask.shape[1]
    return kernel_call(
        "serve_near",
        near_kernel,
        [
            bf16(sent, width),
            bf16(total, width),
            bf16(sent + total, width),
            bf16(total - sent, width),
            bf16(total - sent, width),
            bf16(total, total),
            bf16(total, total),
            bf16(sent + total, total),
            bf16(width, total),
            int32(8, LANES),
        ],
        x,
        mask,
        beyond,
        own_list,
        told,
        within,
        flops=6 * total * rows * width,
        scratch=[pltpu.VMEM((2 * total, rows), jnp.bfloat16)],
    )


def unpack_kernel(first, bases, expand_ref, far_ref, *refs):
    out_ref, sent = refs[-1], far_ref.shape[0]
    rows = jnp.dot(
        expand_ref[:, first : first + sent], far_ref[...], preferred_element_type=jnp.float32
    )
    for base_ref in refs[:bases]:
        rows += base_ref[...].astype(jnp.float32)
    out_ref[...] = rows.astype(jnp.bfloat16)


def unpack_call(expand, far, *base, first=0, after=()):
    in_vmem = [pl.BlockSpec(memory_space=pltpu.VMEM)] * (2 + len(base))
    return kernel_call(
        "unpack",
        functools.partial(unpack_kernel, first, len(base)),
        bf16(expand.shape[0], far.shape[1]),
        expand,
        far,
        *base,
        *after,
        flops=2**34,
        moved=2**25,
        in_specs=in_vmem + [pl.BlockSpec(memory_space=pl.ANY)] * len(after),
    )


def combine_kernel(expand_ref, core_ref, base_ref, most_ref, out_most_ref, *out_refs):
    out_most_ref[...] = most_ref[...]
    cap, sent = out_refs[0].shape[0], core_ref.shape[0]
    rows = jnp.dot(expand_ref[:, :sent], core_ref[...], preferred_element_type=jnp.float32)
    rows = (rows + base_ref[...].astype(jnp.float32)).astype(jnp.bfloat16)
    for d, out in enumerate(out_refs):
        out[...] = rows[d * cap : (d + 1) * cap]


def combine_call(expand, core, base, most, servers):
    total, width = base.shape
    most, *parts = kernel_call(
        "combine",
        combine_kernel,
        [int32(*most.shape)] + [bf16(total // servers, width)] * servers,
        expand,
        core,
        base,
        most,
        flops=2 * total * core.shape[0] * width,
    )
    return most, parts


def unpack_both_kernel(far_expand, core_expand, own_ref, core_ref, far_ref, *refs):
    out_refs = refs[1:]
    cap, sent = out_refs[0].shape[0], far_ref.shape[0]
    rows = jnp.dot(core_expand[:, :sent], core_ref[...], preferred_element_type=jnp.float32)
    rows += jnp.dot(far_expand[:, :sent], far_ref[...], preferred_element_type=jnp.float32)
    rows = (rows + own_ref[...].astype(jnp.float32)).astype(jnp.bfloat16)
    for d, out in enumerate(out_refs):
        out[...] = rows[d * cap : (d + 1) * cap]


def unpack_both_call(expands, far, core, own, after, servers):
    total, width = own.shape
    return kernel_call(
        "unpack_both",
        unpack_both_kernel,
        [bf16(total // servers, width)] * servers,
        *expands,
        own,
        core,
        far,
        after,
        flops=4 * total * far.shape[0] * width,
        in_specs=[pl.BlockSpec(memory_space=pltpu.VMEM)] * 5
        + [pl.BlockSpec(memory_space=pl.ANY)],
    )


def fill(buffer, parts):
    cap = parts[0].shape[0]
    for d, ref in enumerate(reversed(parts)):
        buffer[d * cap : (d + 1) * cap] = ref[...]


def cube(dots, width):
    positive = jnp.maximum(dots * (1.0 / width), 0.0)
    return (positive * positive * positive).astype(jnp.bfloat16)


def weigh(x, buffer, mask):
    dots = lax.dot_general(x, buffer, BOTH_LAST, preferred_element_type=jnp.float32)
    return cube(dots, x.shape[1]) * mask


def mix(x, weights, buffer):
    mixed = x.astype(jnp.float32) + jnp.dot(weights, buffer, preferred_element_type=jnp.float32)
    return normalize(mixed).astype(jnp.bfloat16)


def far_mix_kernel(servers, x_ref, turned_ref, mask_ref, *rest):
    parts, (out_ref, buffer) = rest[:servers], rest[servers:]
    fill(buffer, parts)
    rows, width = x_ref.shape
    dots = jnp.dot(buffer[...], turned_ref[...], preferred_element_type=jnp.float32).T[:rows]
    weights = cube(dots, width) * mask_ref[:rows]
    out_ref[...] = mix(x_ref[...], weights, buffer[...])


def far_mix_call(x, turned, mask, parts):
    rows, width = x.shape
    total, servers = mask.shape[1], len(parts)
    return kernel_call(
        "mix_far",
        functools.partial(far_mix_kernel, servers),
        bf16(rows, width),
        x,
        turned,
        mask,
        *reversed(parts),
        flops=4 * total * rows * width,
        scratch=[pltpu.VMEM((total, width), jnp.bfloat16)],
    )


def near_mix_kernel(servers, x_ref, mask_ref, *rest):
    parts, rest = rest[:servers], rest[servers:]
    *most_refs, core_ref, own_ref, most_ref, buffer = rest
    most_ref[...] = functools.reduce(jnp.maximum, [ref[...] for ref in most_refs])
    fill(buffer, parts)
    weights = weigh(x_ref[...], buffer[...], mask_ref[...])
    mixed = mix(x_ref[...], weights, buffer[...])
    core_ref[...] = mixed[: core_ref.shape[0]]
    own_ref[...] = mixed[core_ref.shape[0] :]


def near_mix_call(x, mask, parts, mosts):
    rows, width = x.shape
    total, servers = mask.shape[1], len(parts)
    return kernel_call(
        "mix_near",
        functools.partial(near_mix_kernel, servers),
        [bf16(rows - total, width), bf16(total, width), int32(*mosts[0].shape)],
        x,
        mask,
        *reversed(parts),
        *mosts,
        flops=4 * total * rows * width,
        scratch=[pltpu.VMEM((total, width), jnp.bfloat16)],
    )


def is_late():
    return (lax.axis_index("rep") + 1) % 4 < 2


def late_kernel(servers, x_ref, mask_ref, *rest):
    parts, (out_ref, buffer, weights) = rest[:servers], rest[servers:]

    @pl.when(is_late())
    def _():
        fill(buffer, parts)
        weights[...] = weigh(x_ref[...], buffer[...], mask_ref[...])
        for start in range(0, x_ref.shape[0], BLOCK):
            here = pl.ds(start, BLOCK)
            out_ref[here] = mix(x_ref[here], weights[here], buffer[...])


def late_call(x, mask, parts):
    rows, width = x.shape
    total, servers = mask.shape[1], len(parts)
    return kernel_call(
        "mix_whole_late",
        functools.partial(late_kernel, servers),
        bf16(rows, width),
        x,
        mask,
        *reversed(parts),
        flops=4 * total * rows * width,
        scratch=[
            pltpu.VMEM((total, width), jnp.bfloat16),
            pltpu.VMEM((rows, total), jnp.bfloat16),
        ],
    )


def mix_blocks(x_ref, mask_ref, buffer, turned, whole, out_ref, sems):
    copies = []
    turned[...] = buffer[...].T
    for start in range(0, x_ref.shape[0], BLOCK):
        here = pl.ds(start, BLOCK)
        if start % (2 * BLOCK) == 0:
            two = pl.ds(start, 2 * BLOCK)
            dots = jnp.dot(x_ref[two], turned[...], preferred_element_type=jnp.float32)
            weights = cube(dots, x_ref.shape[1]) * mask_ref[two]
        half = start % (2 * BLOCK)
        whole[here] = mix(x_ref[here], weights[half : half + BLOCK], buffer[...])
        for first in range(start, start + BLOCK, COPY):
            rows = pl.ds(first, COPY)
            copy = pltpu.make_async_copy(
                whole.at[rows], out_ref.at[rows], sems.at[first // COPY]
            )
            copy.start()
            copies.append(copy)
    for copy in copies:
        copy.wait()


def early_kernel(servers, x_ref, mask_ref, *rest):
    parts, (_, out_ref, buffer, turned, whole, sems) = rest[:servers], rest[servers:]

    @pl.when(jnp.logical_not(is_late()))
    def _():
        fill(buffer, parts)
        mix_blocks(x_ref, mask_ref, buffer, turned, whole, out_ref, sems)


def early_call(x, mask, parts, out):
    rows, width = x.shape
    total, servers = mask.shape[1], len(parts)
    return kernel_call(
        "mix_whole_early",
        functools.partial(early_kernel, servers),
        bf16(rows, width),
        x,
        mask,
        *reversed(parts),
        out,
        flops=4 * total * rows * width,
        scratch=[
            pltpu.VMEM((total, width), jnp.bfloat16),
            pltpu.VMEM((width, total), jnp.bfloat16),
            pltpu.VMEM((rows, width), jnp.bfloat16),
            pltpu.SemaphoreType.DMA((rows // COPY,)),
        ],
        in_specs=[pl.BlockSpec(memory_space=pltpu.VMEM)] * (2 + servers)
        + [pl.BlockSpec(memory_space=pl.ANY)],
        out_specs=pl.BlockSpec(memory_space=pl.ANY),
        input_output_aliases={2 + servers: 0},
    )


def last_kernel(servers, x_ref, mask_ref, *rest):
    parts, (out_ref, buffer, turned, whole, sems) = rest[:servers], rest[servers:]
    fill(buffer, parts)
    mix_blocks(x_ref, mask_ref, buffer, turned, whole, out_ref, sems)


def last_call(x, mask, parts):
    rows, width = x.shape
    total, servers = mask.shape[1], len(parts)
    return kernel_call(
        "mix",
        functools.partial(last_kernel, servers),
        pltpu.HBM((rows, width), jnp.bfloat16),
        x,
        mask,
        *reversed(parts),
        flops=4 * total * rows * width,
        moved=4 * rows * width,
        scratch=[
            pltpu.VMEM((total, width), jnp.bfloat16),
            pltpu.VMEM((width, total), jnp.bfloat16),
            pltpu.VMEM((rows, width), jnp.bfloat16),
            pltpu.SemaphoreType.DMA((rows // COPY,)),
        ],
        out_specs=pl.BlockSpec(memory_space=pltpu.HBM),
    )


def local(descriptors, request, pick):
    wanted = request[0, 0]
    rows = descriptors.shape[2]
    servers, cap = wanted.shape
    total = servers * cap
    groups = lax.axis_size("rep")
    sent = total * FIRST_SHARE[0] // FIRST_SHARE[1]
    within = [(g, g ^ 1) for g in range(groups)]
    beyond = [(g, (g + 2 * (g % 2) - 1 + groups) % groups) for g in range(groups)]

    def turn(value, d):
        return lax.ppermute(value, "clus", [(c, c ^ d) for c in range(servers)])

    def shift(value, by):
        return lax.ppermute(value, "rep", [(g, (g + by) % groups) for g in range(groups)])

    def across(value):
        return lax.ppermute(value, "rep", beyond)

    def inside(value):
        return lax.ppermute(value, "rep", within)

    def turned(parts):
        got = {d: turn(parts[d], d) for d in reversed(range(1, servers))}
        return [parts[0]] + [got[d] for d in range(1, servers)]

    def exchange(expands, far, core, own, most):
        base = unpack_call(expands[0], across(far), own)
        most, parts = combine_call(expands[1], inside(core), base, most, servers)
        return most, turned(parts)

    def next_round(x, mask, far, near, far_turned, far_mask, near_mask, expands, parts, mosts):
        far = far_mix_call(far, far_turned, far_mask, parts)
        core, own, most = near_mix_call(near, near_mask, parts, mosts)
        y = late_call(x, mask, parts)
        last = unpack_both_call(expands, across(far), inside(core), own, y, servers)
        return early_call(x, mask, parts, y), most, turned(last)

    def in_full(x, y, mask, far, near, rest, masks, expands, most, first, last):
        late = unpack_call(expands[1], inside(rest[1]), first=sent)
        late = unpack_call(expands[0], across(rest[0]), late, first=sent)
        late = turned(list(late.reshape(servers, cap, -1)))
        first = [a + b for a, b in zip(first, late)]
        far = jnp.concatenate([far, rest[0]], axis=0)
        near = jnp.concatenate([near[:sent], rest[1], near[sent:]], axis=0)
        near_mask = jnp.concatenate([masks[1], masks[2][sent:]], axis=0)
        y, _, last = next_round(
            x, mask, far, near, masks[3], masks[0], near_mask, expands, first, [most]
        )
        return last_call(y, mask, last)

    def as_sent(x, y, mask, far, near, rest, masks, expands, most, first, last):
        return last_call(y, mask, last)

    asked = {d: turn(wanted, d) for d in reversed(range(1, servers))}
    mask, held = mask_call(pick.transpose(0, 3, 1, 2)[0], wanted)
    own_list, far_list, core_list, *expands = list_call(
        [held] + [asked[d] for d in range(1, servers)], rows
    )
    beyond_list = across(far_list)
    x = normalize_call(descriptors[0, 0])
    told, far = far_call(x, beyond_list, core_list, sent)
    core, own, near, *others, most = near_call(
        x, mask, beyond_list, own_list, told, inside(told), sent
    )
    rest, masks = others[:2], others[2:]
    most, first = exchange(expands, far, core, own, most)
    mosts, known = [most], 4
    while known < groups:
        most = functools.reduce(jnp.maximum, mosts)
        mosts = [most, shift(most, known)]
        known *= 2
    y, most, last = next_round(
        x, mask, far, near, masks[3], masks[0], masks[2], expands, first, mosts
    )
    state = x, y, mask, far, near, rest, masks, expands, most, first, last
    return lax.cond(most[0, 0] > sent, in_full, as_sent, *state)[None, None]


def solution(mesh):
    return jax.shard_map(
        local,
        mesh=mesh,
        in_specs=(
            P("rep", "clus", None, None),
            P("rep", "clus", None, None),
            P("rep", "clus", None, None),
        ),
        out_specs=P("rep", "clus", None, None),
        check_vma=False,
    )
```

```python
import functools

import jax
import jax.numpy as jnp
from jax import lax
from jax.experimental import pallas as pl
from jax.experimental.pallas import tpu as pltpu
from jax.sharding import PartitionSpec as P

LANES = 128
BLOCK = 128
COPY = 64
FIRST_SHARE = 3, 8
BOTH_LAST = (((1,), (1,)), ((), ()))


def bf16(*shape):
    return jax.ShapeDtypeStruct(shape, jnp.bfloat16)


def int32(*shape):
    return jax.ShapeDtypeStruct(shape, jnp.int32)


def kernel_call(name, kernel, outs, *args, flops, moved=0, scratch=(), mib=32, **specs):
    return pl.pallas_call(
        kernel,
        out_shape=outs,
        scratch_shapes=scratch,
        compiler_params=pltpu.CompilerParams(vmem_limit_bytes=mib * 1024 * 1024),
        cost_estimate=pl.CostEstimate(flops=flops, bytes_accessed=moved, transcendentals=0),
        name=name,
        **specs,
    )(*args)


def normalize(value):
    return value * lax.rsqrt(jnp.mean(value * value, axis=-1, keepdims=True) + 1e-06)


def normalize_kernel(x_hbm, out_ref, raw, sems):
    copies = []
    starts = range(0, raw.shape[0], BLOCK)
    for i, start in enumerate(starts):
        here = pl.ds(start, BLOCK)
        copies.append(pltpu.make_async_copy(x_hbm.at[here], raw.at[here], sems.at[i]))
        copies[-1].start()
    for copy, start in zip(copies, starts):
        copy.wait()
        here = pl.ds(start, BLOCK)
        out_ref[here] = normalize(raw[here].astype(jnp.float32)).astype(jnp.bfloat16)


def normalize_call(descriptors):
    rows, width = descriptors.shape
    return kernel_call(
        "normalize",
        normalize_kernel,
        bf16(rows, width),
        descriptors,
        flops=6 * rows * width,
        moved=4 * rows * width,
        scratch=[
            pltpu.VMEM((rows, width), jnp.bfloat16),
            pltpu.SemaphoreType.DMA((rows // BLOCK,)),
        ],
        mib=56,
        in_specs=[pl.BlockSpec(memory_space=pl.ANY)],
    )


def keeps_back(groups):
    return lax.axis_index("rep") == groups - 2


def make_mask(slot_cap, pick):
    total = lax.axis_size("clus") * slot_cap
    shape = total, pick.shape[2]
    slot = lax.broadcasted_iota(jnp.int32, shape, 0)
    slot = slot ^ (lax.axis_index("clus") * slot_cap)
    chosen = jnp.zeros(shape, jnp.float32)
    for k in range(pick.shape[0]):
        chosen = jnp.where(pick[k] == slot, 1.0, chosen)
    return chosen.T.astype(jnp.bfloat16)


def mask_kernel(groups, slot_cap, pick_hbm, wanted_hbm, mask_ref, wanted_ref, pick, sems):
    copies = [
        pltpu.make_async_copy(pick_hbm, pick, sems.at[0]),
        pltpu.make_async_copy(wanted_hbm, wanted_ref, sems.at[1]),
    ]
    for copy in copies:
        copy.start()
    copies[0].wait()

    @pl.when(jnp.logical_not(keeps_back(groups)))
    def _():
        mask_ref[...] = make_mask(slot_cap, pick)

    copies[1].wait()


def mask_call(groups, slots, wanted):
    count, _, rows = slots.shape
    total = wanted.size
    return kernel_call(
        "mask",
        functools.partial(mask_kernel, groups, wanted.shape[1]),
        [bf16(rows, total), pltpu.VMEM(wanted.shape, jnp.int32)],
        slots,
        wanted,
        flops=2 * count * rows * total,
        moved=2 * rows * total,
        scratch=[pltpu.VMEM(slots.shape, jnp.int32), pltpu.SemaphoreType.DMA((2,))],
        mib=56,
        in_specs=[pl.BlockSpec(memory_space=pl.ANY)] * 2,
    )


def late_mask_kernel(groups, slot_cap, pick_hbm, _, base_ref, out_ref, pick, mask, sem):
    @pl.when(keeps_back(groups))
    def _():
        copy = pltpu.make_async_copy(pick_hbm, pick, sem)
        copy.start()
        copy.wait()
        mask[...] = make_mask(slot_cap, pick)
        copy = pltpu.make_async_copy(mask, out_ref, sem)
        copy.start()
        copy.wait()


def late_mask_call(groups, slot_cap, slots, mask, base):
    any_space = pl.BlockSpec(memory_space=pl.ANY)
    return kernel_call(
        "mask_late",
        functools.partial(late_mask_kernel, groups, slot_cap),
        bf16(*mask.shape),
        slots,
        mask,
        base,
        flops=2 * mask.size,
        scratch=[
            pltpu.VMEM(slots.shape, jnp.int32),
            pltpu.VMEM(mask.shape, jnp.bfloat16),
            pltpu.SemaphoreType.DMA,
        ],
        in_specs=[any_space] * 3,
        out_specs=any_space,
        input_output_aliases={1: 0},
    )


def served_masks_kernel(mask_ref, beyond_ref, own_list_ref, within_ref, *out_refs):
    far_ref, core_ref, near_ref = out_refs
    rows, total = mask_ref.shape
    sent = near_ref.shape[0] - total
    mask = mask_ref[...]
    far_ref[...] = take(one_hot(beyond_ref[0:1], rows), mask)
    core = take(one_hot(within_ref[0:1], rows), mask)
    core_ref[...] = core
    near_ref[:sent] = core[:sent]
    near_ref[sent:] = take(one_hot(own_list_ref[0:1], rows), mask)


def served_masks_call(mask, beyond, own_list, within, sent):
    rows, total = mask.shape
    return kernel_call(
        "served_masks",
        served_masks_kernel,
        [bf16(total, total), bf16(total, total), bf16(sent + total, total)],
        mask,
        beyond,
        own_list,
        within,
        flops=6 * total * rows * total,
    )


def list_kernel(rows, *refs):
    parts, refs = refs[:-5], refs[-5:]
    own_ref, far_ref, core_ref, expand_far_ref, expand_core_ref = refs
    total = own_ref.shape[1]
    lane = lax.broadcasted_iota(jnp.int32, (total, total), 1)
    sublane = lax.broadcasted_iota(jnp.int32, (total, total), 0)
    odd = lax.axis_index("rep") % 2
    lows = [(2 * odd * rows).astype(jnp.float32), ((2 - 2 * odd) * rows).astype(jnp.float32)]

    def inside(value, low):
        return (value >= low) & (value < low + rows)

    def asked(server):
        row = jnp.concatenate([ref[server, :] for ref in parts], axis=1).astype(jnp.float32)
        column = jnp.broadcast_to(row, (total, total)).T
        again = jnp.where((column == row) & (sublane < lane), 1.0, 0.0)
        return row, column, 1.0 - jnp.max(again, axis=0, keepdims=True)

    most = jnp.zeros((1, 1), jnp.float32)
    for server in range(len(parts)):
        row, _, first = asked(slice(server, server + 1))
        for low in lows:
            count = jnp.sum(jnp.where(inside(row, low), first, 0.0), axis=1, keepdims=True)
            most = jnp.maximum(most, count)
    row, column, first = asked(pl.ds(lax.axis_index("clus"), 1))
    own_ref[...] = jnp.broadcast_to(row - rows, own_ref.shape).astype(jnp.int32)
    place = lax.broadcasted_iota(jnp.int32, own_ref.shape, 0)
    for low, out_ref, expand_ref in zip(lows, (far_ref, core_ref), (expand_far_ref, expand_core_ref)):
        counted = jnp.where(inside(row, low), first, 0.0)
        rank = jnp.sum(jnp.where(row < column, counted, 0.0), axis=1, keepdims=True)
        here = inside(column, low) & (rank.astype(jnp.int32) == lane)
        expand_ref[...] = jnp.where(here, 1.0, 0.0).astype(jnp.bfloat16)
        packed = jnp.max(jnp.where(here, column - low, -1.0), axis=0, keepdims=True)
        out_ref[...] = jnp.where(place == 1, most, packed).astype(jnp.int32)


def list_call(parts, rows):
    total = parts[0].size
    return kernel_call(
        "list",
        functools.partial(list_kernel, rows),
        [int32(8, total)] * 3 + [bf16(total, total)] * 2,
        *parts,
        flops=40 * total * total,
    )


def one_hot(numbers, rows, count=None):
    total = numbers.shape[1]
    column = jnp.broadcast_to(numbers.astype(jnp.float32), (LANES, total)).T.astype(jnp.int32)
    column = column[:count]
    tiles = []
    for start in range(0, rows, LANES):
        lane = lax.broadcasted_iota(jnp.int32, column.shape, 1) + start
        tiles.append(jnp.where(column == lane, 1.0, 0.0).astype(jnp.bfloat16))
    return jnp.concatenate(tiles, axis=1)


def take(select, x):
    return jnp.dot(select, x, preferred_element_type=jnp.float32).astype(jnp.bfloat16)


def far_kernel(x_ref, beyond_ref, core_list_ref, told_ref, far_ref):
    far_ref[...] = take(one_hot(beyond_ref[0:1], *x_ref.shape[:1], far_ref.shape[0]), x_ref[...])
    place = lax.broadcasted_iota(jnp.int32, told_ref.shape, 0)
    most = jnp.maximum(core_list_ref[...], beyond_ref[...])
    told_ref[...] = jnp.where(place == 1, most, core_list_ref[...])


def far_call(x, beyond, core_list, sent):
    rows, width = x.shape
    return kernel_call(
        "pack_far",
        far_kernel,
        [int32(*core_list.shape), bf16(sent, width)],
        x,
        beyond,
        core_list,
        flops=2 * rows * sent * width,
    )


def near_kernel(x_ref, beyond_ref, own_list_ref, *refs):
    told_ref, within_ref, *refs = refs
    core_ref, own_ref, near_ref, rest_far_ref, rest_core_ref, *refs = refs
    far_turned_ref, most_ref, select = refs
    total, sent = own_ref.shape[0], core_ref.shape[0]
    rows = x_ref.shape[0]
    select[:total] = one_hot(within_ref[0:1], rows)
    select[total:] = one_hot(own_list_ref[0:1], rows)
    fetched = take(select[...], x_ref[...])
    core_ref[...] = fetched[:sent]
    near_ref[:sent] = fetched[:sent]
    rest_core_ref[...] = fetched[sent:total]
    own_ref[...] = fetched[total:]
    near_ref[sent:] = fetched[total:]
    pack = one_hot(beyond_ref[0:1], rows)
    far = jnp.dot(pack, x_ref[...], preferred_element_type=jnp.float32)
    rest_far_ref[...] = far[sent:].astype(jnp.bfloat16)
    far_turned_ref[...] = far.T.astype(jnp.bfloat16)
    most = jnp.maximum(told_ref[...], within_ref[...])
    most_ref[...] = jnp.broadcast_to(most[1:2, :LANES], most_ref.shape)


def near_call(x, beyond, own_list, told, within, sent):
    rows, width = x.shape
    total = beyond.shape[1]
    return kernel_call(
        "serve_near",
        near_kernel,
        [
            bf16(sent, width),
            bf16(total, width),
            bf16(sent + total, width),
            bf16(total - sent, width),
            bf16(total - sent, width),
            bf16(width, total),
            int32(8, LANES),
        ],
        x,
        beyond,
        own_list,
        told,
        within,
        flops=6 * total * rows * width,
        scratch=[pltpu.VMEM((2 * total, rows), jnp.bfloat16)],
    )


def unpack_kernel(first, bases, expand_ref, far_ref, *refs):
    out_ref, sent = refs[-1], far_ref.shape[0]
    rows = jnp.dot(
        expand_ref[:, first : first + sent], far_ref[...], preferred_element_type=jnp.float32
    )
    for base_ref in refs[:bases]:
        rows += base_ref[...].astype(jnp.float32)
    out_ref[...] = rows.astype(jnp.bfloat16)


def unpack_call(expand, far, *base, first=0, after=()):
    in_vmem = [pl.BlockSpec(memory_space=pltpu.VMEM)] * (2 + len(base))
    return kernel_call(
        "unpack",
        functools.partial(unpack_kernel, first, len(base)),
        bf16(expand.shape[0], far.shape[1]),
        expand,
        far,
        *base,
        *after,
        flops=2**34,
        moved=2**25,
        in_specs=in_vmem + [pl.BlockSpec(memory_space=pl.ANY)] * len(after),
    )


def combine_kernel(expand_ref, core_ref, base_ref, most_ref, _, out_most_ref, *out_refs):
    out_most_ref[...] = most_ref[...]
    cap, sent = out_refs[0].shape[0], core_ref.shape[0]
    rows = jnp.dot(expand_ref[:, :sent], core_ref[...], preferred_element_type=jnp.float32)
    rows = (rows + base_ref[...].astype(jnp.float32)).astype(jnp.bfloat16)
    for d, out in enumerate(out_refs):
        out[...] = rows[d * cap : (d + 1) * cap]


def combine_call(expand, core, base, most, after, servers):
    total, width = base.shape
    most, *parts = kernel_call(
        "combine",
        combine_kernel,
        [int32(*most.shape)] + [bf16(total // servers, width)] * servers,
        expand,
        core,
        base,
        most,
        after,
        flops=2 * total * core.shape[0] * width,
        in_specs=[pl.BlockSpec(memory_space=pltpu.VMEM)] * 4
        + [pl.BlockSpec(memory_space=pl.ANY)],
    )
    return most, parts


def unpack_both_kernel(far_expand, core_expand, own_ref, core_ref, far_ref, *refs):
    out_refs = refs[1:]
    cap, sent = out_refs[0].shape[0], far_ref.shape[0]
    rows = jnp.dot(core_expand[:, :sent], core_ref[...], preferred_element_type=jnp.float32)
    rows += jnp.dot(far_expand[:, :sent], far_ref[...], preferred_element_type=jnp.float32)
    rows = (rows + own_ref[...].astype(jnp.float32)).astype(jnp.bfloat16)
    for d, out in enumerate(out_refs):
        out[...] = rows[d * cap : (d + 1) * cap]


def unpack_both_call(expands, far, core, own, after, servers):
    total, width = own.shape
    return kernel_call(
        "unpack_both",
        unpack_both_kernel,
        [bf16(total // servers, width)] * servers,
        *expands,
        own,
        core,
        far,
        after,
        flops=4 * total * far.shape[0] * width,
        in_specs=[pl.BlockSpec(memory_space=pltpu.VMEM)] * 5
        + [pl.BlockSpec(memory_space=pl.ANY)],
    )


def fill(buffer, parts):
    cap = parts[0].shape[0]
    for d, ref in enumerate(reversed(parts)):
        buffer[d * cap : (d + 1) * cap] = ref[...]


def cube(dots, width):
    positive = jnp.maximum(dots * (1.0 / width), 0.0)
    return (positive * positive * positive).astype(jnp.bfloat16)


def weigh(x, buffer, mask):
    dots = lax.dot_general(x, buffer, BOTH_LAST, preferred_element_type=jnp.float32)
    return cube(dots, x.shape[1]) * mask


def mix(x, weights, buffer):
    mixed = x.astype(jnp.float32) + jnp.dot(weights, buffer, preferred_element_type=jnp.float32)
    return normalize(mixed).astype(jnp.bfloat16)


def far_mix_kernel(servers, x_ref, turned_ref, mask_ref, *rest):
    parts, (out_ref, buffer) = rest[:servers], rest[servers:]
    fill(buffer, parts)
    rows, width = x_ref.shape
    dots = jnp.dot(buffer[...], turned_ref[...], preferred_element_type=jnp.float32).T[:rows]
    weights = cube(dots, width) * mask_ref[:rows]
    out_ref[...] = mix(x_ref[...], weights, buffer[...])


def far_mix_call(x, turned, mask, parts):
    rows, width = x.shape
    total, servers = mask.shape[1], len(parts)
    return kernel_call(
        "mix_far",
        functools.partial(far_mix_kernel, servers),
        bf16(rows, width),
        x,
        turned,
        mask,
        *reversed(parts),
        flops=4 * total * rows * width,
        scratch=[pltpu.VMEM((total, width), jnp.bfloat16)],
    )


def near_mix_kernel(servers, x_ref, mask_ref, *rest):
    parts, rest = rest[:servers], rest[servers:]
    *most_refs, core_ref, own_ref, most_ref, buffer = rest
    most_ref[...] = functools.reduce(jnp.maximum, [ref[...] for ref in most_refs])
    fill(buffer, parts)
    weights = weigh(x_ref[...], buffer[...], mask_ref[...])
    mixed = mix(x_ref[...], weights, buffer[...])
    core_ref[...] = mixed[: core_ref.shape[0]]
    own_ref[...] = mixed[core_ref.shape[0] :]


def near_mix_call(x, mask, parts, mosts):
    rows, width = x.shape
    total, servers = mask.shape[1], len(parts)
    return kernel_call(
        "mix_near",
        functools.partial(near_mix_kernel, servers),
        [bf16(rows - total, width), bf16(total, width), int32(*mosts[0].shape)],
        x,
        mask,
        *reversed(parts),
        *mosts,
        flops=4 * total * rows * width,
        scratch=[pltpu.VMEM((total, width), jnp.bfloat16)],
    )


def is_late():
    return (lax.axis_index("rep") + 1) % 4 < 2


def late_kernel(servers, x_ref, mask_ref, *rest):
    parts, (out_ref, buffer, weights) = rest[:servers], rest[servers:]

    @pl.when(is_late())
    def _():
        fill(buffer, parts)
        weights[...] = weigh(x_ref[...], buffer[...], mask_ref[...])
        for start in range(0, x_ref.shape[0], BLOCK):
            here = pl.ds(start, BLOCK)
            out_ref[here] = mix(x_ref[here], weights[here], buffer[...])


def late_call(x, mask, parts):
    rows, width = x.shape
    total, servers = mask.shape[1], len(parts)
    return kernel_call(
        "mix_whole_late",
        functools.partial(late_kernel, servers),
        bf16(rows, width),
        x,
        mask,
        *reversed(parts),
        flops=4 * total * rows * width,
        scratch=[
            pltpu.VMEM((total, width), jnp.bfloat16),
            pltpu.VMEM((rows, total), jnp.bfloat16),
        ],
    )


def mix_blocks(x_ref, mask_ref, buffer, turned, whole, out_ref, sems):
    copies = []
    turned[...] = buffer[...].T
    for start in range(0, x_ref.shape[0], BLOCK):
        here = pl.ds(start, BLOCK)
        if start % (2 * BLOCK) == 0:
            two = pl.ds(start, 2 * BLOCK)
            dots = jnp.dot(x_ref[two], turned[...], preferred_element_type=jnp.float32)
            weights = cube(dots, x_ref.shape[1]) * mask_ref[two]
        half = start % (2 * BLOCK)
        whole[here] = mix(x_ref[here], weights[half : half + BLOCK], buffer[...])
        for first in range(start, start + BLOCK, COPY):
            rows = pl.ds(first, COPY)
            copy = pltpu.make_async_copy(
                whole.at[rows], out_ref.at[rows], sems.at[first // COPY]
            )
            copy.start()
            copies.append(copy)
    for copy in copies:
        copy.wait()


def early_kernel(servers, x_ref, mask_ref, *rest):
    parts, (_, out_ref, buffer, turned, whole, sems) = rest[:servers], rest[servers:]

    @pl.when(jnp.logical_not(is_late()))
    def _():
        fill(buffer, parts)
        mix_blocks(x_ref, mask_ref, buffer, turned, whole, out_ref, sems)


def early_call(x, mask, parts, out):
    rows, width = x.shape
    total, servers = mask.shape[1], len(parts)
    return kernel_call(
        "mix_whole_early",
        functools.partial(early_kernel, servers),
        bf16(rows, width),
        x,
        mask,
        *reversed(parts),
        out,
        flops=4 * total * rows * width,
        scratch=[
            pltpu.VMEM((total, width), jnp.bfloat16),
            pltpu.VMEM((width, total), jnp.bfloat16),
            pltpu.VMEM((rows, width), jnp.bfloat16),
            pltpu.SemaphoreType.DMA((rows // COPY,)),
        ],
        in_specs=[pl.BlockSpec(memory_space=pltpu.VMEM)] * (2 + servers)
        + [pl.BlockSpec(memory_space=pl.ANY)],
        out_specs=pl.BlockSpec(memory_space=pl.ANY),
        input_output_aliases={2 + servers: 0},
    )


def last_kernel(servers, x_ref, mask_ref, *rest):
    parts, (out_ref, buffer, turned, whole, sems) = rest[:servers], rest[servers:]
    fill(buffer, parts)
    mix_blocks(x_ref, mask_ref, buffer, turned, whole, out_ref, sems)


def last_call(x, mask, parts):
    rows, width = x.shape
    total, servers = mask.shape[1], len(parts)
    return kernel_call(
        "mix",
        functools.partial(last_kernel, servers),
        pltpu.HBM((rows, width), jnp.bfloat16),
        x,
        mask,
        *reversed(parts),
        flops=4 * total * rows * width,
        moved=4 * rows * width,
        scratch=[
            pltpu.VMEM((total, width), jnp.bfloat16),
            pltpu.VMEM((width, total), jnp.bfloat16),
            pltpu.VMEM((rows, width), jnp.bfloat16),
            pltpu.SemaphoreType.DMA((rows // COPY,)),
        ],
        out_specs=pl.BlockSpec(memory_space=pltpu.HBM),
    )


def local(descriptors, request, pick):
    wanted = request[0, 0]
    rows = descriptors.shape[2]
    servers, cap = wanted.shape
    total = servers * cap
    groups = lax.axis_size("rep")
    sent = total * FIRST_SHARE[0] // FIRST_SHARE[1]
    within = [(g, g ^ 1) for g in range(groups)]
    beyond = [(g, (g + 2 * (g % 2) - 1 + groups) % groups) for g in range(groups)]

    def turn(value, d):
        return lax.ppermute(value, "clus", [(c, c ^ d) for c in range(servers)])

    def shift(value, by):
        return lax.ppermute(value, "rep", [(g, (g + by) % groups) for g in range(groups)])

    def across(value):
        return lax.ppermute(value, "rep", beyond)

    def inside(value):
        return lax.ppermute(value, "rep", within)

    def turned(parts):
        got = {d: turn(parts[d], d) for d in reversed(range(1, servers))}
        return [parts[0]] + [got[d] for d in range(1, servers)]

    def next_round(x, mask, far, near, far_turned, far_mask, near_mask, expands, parts, mosts):
        far = far_mix_call(far, far_turned, far_mask, parts)
        core, own, most = near_mix_call(near, near_mask, parts, mosts)
        y = late_call(x, mask, parts)
        last = unpack_both_call(expands, across(far), inside(core), own, y, servers)
        return early_call(x, mask, parts, y), most, turned(last)

    def in_full(x, y, mask, far, near, rest, masks, expands, most, first, last):
        late = unpack_call(expands[1], inside(rest[1]), first=sent)
        late = unpack_call(expands[0], across(rest[0]), late, first=sent)
        late = turned(list(late.reshape(servers, cap, -1)))
        first = [a + b for a, b in zip(first, late)]
        far = jnp.concatenate([far, rest[0]], axis=0)
        near = jnp.concatenate([near[:sent], rest[1], near[sent:]], axis=0)
        near_mask = jnp.concatenate([masks[1], masks[2][sent:]], axis=0)
        y, _, last = next_round(
            x, mask, far, near, masks[3], masks[0], near_mask, expands, first, [most]
        )
        return last_call(y, mask, last)

    def as_sent(x, y, mask, far, near, rest, masks, expands, most, first, last):
        return last_call(y, mask, last)

    asked = {d: turn(wanted, d) for d in reversed(range(1, servers))}
    slots = pick.transpose(0, 3, 1, 2)[0]
    mask, held = mask_call(groups, slots, wanted)
    own_list, far_list, core_list, *expands = list_call(
        [held] + [asked[d] for d in range(1, servers)], rows
    )
    beyond_list = across(far_list)
    x = normalize_call(descriptors[0, 0])
    told, far = far_call(x, beyond_list, core_list, sent)
    within_list = inside(told)
    core, own, near, *rest, far_turned, most = near_call(
        x, beyond_list, own_list, told, within_list, sent
    )
    base = unpack_call(expands[0], across(far), own)
    mask = late_mask_call(groups, cap, slots, mask, base)
    most, first = combine_call(expands[1], inside(core), base, most, mask, servers)
    first = turned(first)
    masks = *served_masks_call(mask, beyond_list, own_list, within_list, sent), far_turned
    mosts, known = [most], 4
    while known < groups:
        most = functools.reduce(jnp.maximum, mosts)
        mosts = [most, shift(most, known)]
        known *= 2
    y, most, last = next_round(
        x, mask, far, near, masks[3], masks[0], masks[2], expands, first, mosts
    )
    state = x, y, mask, far, near, rest, masks, expands, most, first, last
    return lax.cond(most[0, 0] > sent, in_full, as_sent, *state)[None, None]


def solution(mesh):
    return jax.shard_map(
        local,
        mesh=mesh,
        in_specs=(
            P("rep", "clus", None, None),
            P("rep", "clus", None, None),
            P("rep", "clus", None, None),
        ),
        out_specs=P("rep", "clus", None, None),
        check_vma=False,
    )
```

```python
import functools

import jax
import jax.numpy as jnp
from jax import lax
from jax.experimental import pallas as pl
from jax.experimental.pallas import tpu as pltpu
from jax.sharding import PartitionSpec as P

LANES = 128
BLOCK = 128
COPY = 64
FIRST_SHARE = 3, 8
BOTH_LAST = (((1,), (1,)), ((), ()))


def bf16(*shape):
    return jax.ShapeDtypeStruct(shape, jnp.bfloat16)


def int32(*shape):
    return jax.ShapeDtypeStruct(shape, jnp.int32)


def kernel_call(name, kernel, outs, *args, flops, moved=0, scratch=(), mib=32, **specs):
    return pl.pallas_call(
        kernel,
        out_shape=outs,
        scratch_shapes=scratch,
        compiler_params=pltpu.CompilerParams(vmem_limit_bytes=mib * 1024 * 1024),
        cost_estimate=pl.CostEstimate(flops=flops, bytes_accessed=moved, transcendentals=0),
        name=name,
        **specs,
    )(*args)


def normalize(value):
    return value * lax.rsqrt(jnp.mean(value * value, axis=-1, keepdims=True) + 1e-06)


def normalize_kernel(x_hbm, out_ref, raw, sems):
    copies = []
    starts = range(0, raw.shape[0], BLOCK)
    for i, start in enumerate(starts):
        here = pl.ds(start, BLOCK)
        copies.append(pltpu.make_async_copy(x_hbm.at[here], raw.at[here], sems.at[i]))
        copies[-1].start()
    for copy, start in zip(copies, starts):
        copy.wait()
        here = pl.ds(start, BLOCK)
        out_ref[here] = normalize(raw[here].astype(jnp.float32)).astype(jnp.bfloat16)


def normalize_call(descriptors):
    rows, width = descriptors.shape
    return kernel_call(
        "normalize",
        normalize_kernel,
        bf16(rows, width),
        descriptors,
        flops=6 * rows * width,
        moved=4 * rows * width,
        scratch=[
            pltpu.VMEM((rows, width), jnp.bfloat16),
            pltpu.SemaphoreType.DMA((rows // BLOCK,)),
        ],
        mib=56,
        in_specs=[pl.BlockSpec(memory_space=pl.ANY)],
    )


def mask_kernel(slot_cap, pick_hbm, wanted_hbm, mask_ref, wanted_ref, pick, sems):
    copies = [
        pltpu.make_async_copy(pick_hbm, pick, sems.at[0]),
        pltpu.make_async_copy(wanted_hbm, wanted_ref, sems.at[1]),
    ]
    for copy in copies:
        copy.start()
    shape = mask_ref.shape[1], mask_ref.shape[0]
    slot = lax.broadcasted_iota(jnp.int32, shape, 0)
    slot = slot ^ (lax.axis_index("clus") * slot_cap)
    chosen = jnp.zeros(shape, jnp.float32)
    copies[0].wait()
    for k in range(pick.shape[0]):
        chosen = jnp.where(pick[k] == slot, 1.0, chosen)
    mask_ref[...] = chosen.T.astype(jnp.bfloat16)
    copies[1].wait()


def mask_call(slots, wanted):
    count, _, rows = slots.shape
    total = wanted.size
    return kernel_call(
        "mask",
        functools.partial(mask_kernel, wanted.shape[1]),
        [bf16(rows, total), pltpu.VMEM(wanted.shape, jnp.int32)],
        slots,
        wanted,
        flops=2 * count * rows * total,
        moved=2 * rows * total,
        scratch=[pltpu.VMEM(slots.shape, jnp.int32), pltpu.SemaphoreType.DMA((2,))],
        mib=56,
        in_specs=[pl.BlockSpec(memory_space=pl.ANY)] * 2,
    )


def list_kernel(rows, *refs):
    parts, refs = refs[:-5], refs[-5:]
    own_ref, far_ref, core_ref, expand_far_ref, expand_core_ref = refs
    total = own_ref.shape[1]
    lane = lax.broadcasted_iota(jnp.int32, (total, total), 1)
    sublane = lax.broadcasted_iota(jnp.int32, (total, total), 0)
    odd = lax.axis_index("rep") % 2
    lows = [(2 * odd * rows).astype(jnp.float32), ((2 - 2 * odd) * rows).astype(jnp.float32)]

    def inside(value, low):
        return (value >= low) & (value < low + rows)

    def asked(server):
        row = jnp.concatenate([ref[server, :] for ref in parts], axis=1).astype(jnp.float32)
        column = jnp.broadcast_to(row, (total, total)).T
        again = jnp.where((column == row) & (sublane < lane), 1.0, 0.0)
        return row, column, 1.0 - jnp.max(again, axis=0, keepdims=True)

    most = jnp.zeros((1, 1), jnp.float32)
    for server in range(len(parts)):
        row, _, first = asked(slice(server, server + 1))
        for low in lows:
            count = jnp.sum(jnp.where(inside(row, low), first, 0.0), axis=1, keepdims=True)
            most = jnp.maximum(most, count)
    row, column, first = asked(pl.ds(lax.axis_index("clus"), 1))
    own_ref[...] = jnp.broadcast_to(row - rows, own_ref.shape).astype(jnp.int32)
    place = lax.broadcasted_iota(jnp.int32, own_ref.shape, 0)
    for low, out_ref, expand_ref in zip(lows, (far_ref, core_ref), (expand_far_ref, expand_core_ref)):
        counted = jnp.where(inside(row, low), first, 0.0)
        rank = jnp.sum(jnp.where(row < column, counted, 0.0), axis=1, keepdims=True)
        here = inside(column, low) & (rank.astype(jnp.int32) == lane)
        expand_ref[...] = jnp.where(here, 1.0, 0.0).astype(jnp.bfloat16)
        packed = jnp.max(jnp.where(here, column - low, -1.0), axis=0, keepdims=True)
        out_ref[...] = jnp.where(place == 1, most, packed).astype(jnp.int32)


def list_call(parts, rows):
    total = parts[0].size
    return kernel_call(
        "list",
        functools.partial(list_kernel, rows),
        [int32(8, total)] * 3 + [bf16(total, total)] * 2,
        *parts,
        flops=40 * total * total,
    )


def one_hot(numbers, rows, count=None):
    total = numbers.shape[1]
    column = jnp.broadcast_to(numbers.astype(jnp.float32), (LANES, total)).T.astype(jnp.int32)
    column = column[:count]
    tiles = []
    for start in range(0, rows, LANES):
        lane = lax.broadcasted_iota(jnp.int32, column.shape, 1) + start
        tiles.append(jnp.where(column == lane, 1.0, 0.0).astype(jnp.bfloat16))
    return jnp.concatenate(tiles, axis=1)


def take(select, x):
    return jnp.dot(select, x, preferred_element_type=jnp.float32).astype(jnp.bfloat16)


def far_kernel(x_ref, beyond_ref, core_list_ref, told_ref, far_ref):
    far_ref[...] = take(one_hot(beyond_ref[0:1], *x_ref.shape[:1], far_ref.shape[0]), x_ref[...])
    place = lax.broadcasted_iota(jnp.int32, told_ref.shape, 0)
    most = jnp.maximum(core_list_ref[...], beyond_ref[...])
    told_ref[...] = jnp.where(place == 1, most, core_list_ref[...])


def far_call(x, beyond, core_list, sent):
    rows, width = x.shape
    return kernel_call(
        "pack_far",
        far_kernel,
        [int32(*core_list.shape), bf16(sent, width)],
        x,
        beyond,
        core_list,
        flops=2 * rows * sent * width,
    )


def near_kernel(x_ref, mask_ref, beyond_ref, own_list_ref, *refs):
    told_ref, within_ref, *refs = refs
    core_ref, own_ref, near_ref, rest_far_ref, rest_core_ref, *refs = refs
    far_mask_ref, core_mask_ref, near_mask_ref, far_turned_ref, most_ref, select = refs
    total, sent = own_ref.shape[0], core_ref.shape[0]
    rows = x_ref.shape[0]
    select[:total] = one_hot(within_ref[0:1], rows)
    select[total:] = one_hot(own_list_ref[0:1], rows)
    fetched = take(select[...], x_ref[...])
    core_ref[...] = fetched[:sent]
    near_ref[:sent] = fetched[:sent]
    rest_core_ref[...] = fetched[sent:total]
    own_ref[...] = fetched[total:]
    near_ref[sent:] = fetched[total:]
    pack = one_hot(beyond_ref[0:1], rows)
    far = jnp.dot(pack, x_ref[...], preferred_element_type=jnp.float32)
    rest_far_ref[...] = far[sent:].astype(jnp.bfloat16)
    far_turned_ref[...] = far.T.astype(jnp.bfloat16)
    masks = take(select[...], mask_ref[...])
    core_mask_ref[...] = masks[:total]
    near_mask_ref[:sent] = masks[:sent]
    near_mask_ref[sent:] = masks[total:]
    far_mask_ref[...] = take(pack, mask_ref[...])
    most = jnp.maximum(told_ref[...], within_ref[...])
    most_ref[...] = jnp.broadcast_to(most[1:2, :LANES], most_ref.shape)


def near_call(x, mask, beyond, own_list, told, within, sent):
    rows, width = x.shape
    total = mask.shape[1]
    return kernel_call(
        "serve_near",
        near_kernel,
        [
            bf16(sent, width),
            bf16(total, width),
            bf16(sent + total, width),
            bf16(total - sent, width),
            bf16(total - sent, width),
            bf16(total, total),
            bf16(total, total),
            bf16(sent + total, total),
            bf16(width, total),
            int32(8, LANES),
        ],
        x,
        mask,
        beyond,
        own_list,
        told,
        within,
        flops=6 * total * rows * width,
        scratch=[pltpu.VMEM((2 * total, rows), jnp.bfloat16)],
    )


def unpack_kernel(first, bases, expand_ref, far_ref, *refs):
    out_ref, sent = refs[-1], far_ref.shape[0]
    rows = jnp.dot(
        expand_ref[:, first : first + sent], far_ref[...], preferred_element_type=jnp.float32
    )
    for base_ref in refs[:bases]:
        rows += base_ref[...].astype(jnp.float32)
    out_ref[...] = rows.astype(jnp.bfloat16)


def unpack_call(expand, far, *base, first=0, after=()):
    in_vmem = [pl.BlockSpec(memory_space=pltpu.VMEM)] * (2 + len(base))
    return kernel_call(
        "unpack",
        functools.partial(unpack_kernel, first, len(base)),
        bf16(expand.shape[0], far.shape[1]),
        expand,
        far,
        *base,
        *after,
        flops=2**34,
        moved=2**25,
        in_specs=in_vmem + [pl.BlockSpec(memory_space=pl.ANY)] * len(after),
    )


def unpack_both_kernel(far_first, far_expand, core_expand, own_ref, a_ref, b_ref, _, *out_refs):
    far_ref, core_ref = (a_ref, b_ref) if far_first else (b_ref, a_ref)
    cap, sent = out_refs[0].shape[0], far_ref.shape[0]
    rows = jnp.dot(core_expand[:, :sent], core_ref[...], preferred_element_type=jnp.float32)
    rows += jnp.dot(far_expand[:, :sent], far_ref[...], preferred_element_type=jnp.float32)
    rows = (rows + own_ref[...].astype(jnp.float32)).astype(jnp.bfloat16)
    for d, out in enumerate(out_refs):
        out[...] = rows[d * cap : (d + 1) * cap]


def unpack_both_call(expands, far, core, own, after, servers, far_first=False):
    total, width = own.shape
    return kernel_call(
        "unpack_both",
        functools.partial(unpack_both_kernel, far_first),
        [bf16(total // servers, width)] * servers,
        *expands,
        own,
        *((far, core) if far_first else (core, far)),
        after,
        flops=4 * total * far.shape[0] * width,
        in_specs=[pl.BlockSpec(memory_space=pltpu.VMEM)] * 5
        + [pl.BlockSpec(memory_space=pl.ANY)],
    )


def fill(buffer, parts):
    cap = parts[0].shape[0]
    for d, ref in enumerate(reversed(parts)):
        buffer[d * cap : (d + 1) * cap] = ref[...]


def cube(dots, width):
    positive = jnp.maximum(dots * (1.0 / width), 0.0)
    return (positive * positive * positive).astype(jnp.bfloat16)


def weigh(x, buffer, mask):
    dots = lax.dot_general(x, buffer, BOTH_LAST, preferred_element_type=jnp.float32)
    return cube(dots, x.shape[1]) * mask


def mix(x, weights, buffer):
    mixed = x.astype(jnp.float32) + jnp.dot(weights, buffer, preferred_element_type=jnp.float32)
    return normalize(mixed).astype(jnp.bfloat16)


def far_mix_kernel(servers, x_ref, turned_ref, mask_ref, *rest):
    parts, (out_ref, buffer) = rest[:servers], rest[servers:]
    fill(buffer, parts)
    rows, width = x_ref.shape
    dots = jnp.dot(buffer[...], turned_ref[...], preferred_element_type=jnp.float32).T[:rows]
    weights = cube(dots, width) * mask_ref[:rows]
    out_ref[...] = mix(x_ref[...], weights, buffer[...])


def far_mix_call(x, turned, mask, parts):
    rows, width = x.shape
    total, servers = mask.shape[1], len(parts)
    return kernel_call(
        "mix_far",
        functools.partial(far_mix_kernel, servers),
        bf16(rows, width),
        x,
        turned,
        mask,
        *reversed(parts),
        flops=4 * total * rows * width,
        scratch=[pltpu.VMEM((total, width), jnp.bfloat16)],
    )


def near_mix_kernel(servers, x_ref, mask_ref, *rest):
    parts, rest = rest[:servers], rest[servers:]
    *most_refs, core_ref, own_ref, most_ref, buffer = rest
    most_ref[...] = functools.reduce(jnp.maximum, [ref[...] for ref in most_refs])
    fill(buffer, parts)
    weights = weigh(x_ref[...], buffer[...], mask_ref[...])
    mixed = mix(x_ref[...], weights, buffer[...])
    core_ref[...] = mixed[: core_ref.shape[0]]
    own_ref[...] = mixed[core_ref.shape[0] :]


def near_mix_call(x, mask, parts, mosts):
    rows, width = x.shape
    total, servers = mask.shape[1], len(parts)
    return kernel_call(
        "mix_near",
        functools.partial(near_mix_kernel, servers),
        [bf16(rows - total, width), bf16(total, width), int32(*mosts[0].shape)],
        x,
        mask,
        *reversed(parts),
        *mosts,
        flops=4 * total * rows * width,
        scratch=[pltpu.VMEM((total, width), jnp.bfloat16)],
    )


def is_late():
    return (lax.axis_index("rep") + 1) % 4 < 2


def late_kernel(servers, x_ref, mask_ref, *rest):
    parts, (out_ref, buffer, weights) = rest[:servers], rest[servers:]

    @pl.when(is_late())
    def _():
        fill(buffer, parts)
        weights[...] = weigh(x_ref[...], buffer[...], mask_ref[...])
        for start in range(0, x_ref.shape[0], BLOCK):
            here = pl.ds(start, BLOCK)
            out_ref[here] = mix(x_ref[here], weights[here], buffer[...])


def late_call(x, mask, parts):
    rows, width = x.shape
    total, servers = mask.shape[1], len(parts)
    return kernel_call(
        "mix_whole_late",
        functools.partial(late_kernel, servers),
        bf16(rows, width),
        x,
        mask,
        *reversed(parts),
        flops=4 * total * rows * width,
        scratch=[
            pltpu.VMEM((total, width), jnp.bfloat16),
            pltpu.VMEM((rows, total), jnp.bfloat16),
        ],
    )


def mix_blocks(x_ref, mask_ref, buffer, turned, whole, out_ref, sems):
    copies = []
    turned[...] = buffer[...].T
    for start in range(0, x_ref.shape[0], BLOCK):
        here = pl.ds(start, BLOCK)
        if start % (2 * BLOCK) == 0:
            two = pl.ds(start, 2 * BLOCK)
            dots = jnp.dot(x_ref[two], turned[...], preferred_element_type=jnp.float32)
            weights = cube(dots, x_ref.shape[1]) * mask_ref[two]
        half = start % (2 * BLOCK)
        whole[here] = mix(x_ref[here], weights[half : half + BLOCK], buffer[...])
        for first in range(start, start + BLOCK, COPY):
            rows = pl.ds(first, COPY)
            copy = pltpu.make_async_copy(
                whole.at[rows], out_ref.at[rows], sems.at[first // COPY]
            )
            copy.start()
            copies.append(copy)
    for copy in copies:
        copy.wait()


def early_kernel(servers, x_ref, mask_ref, *rest):
    parts, (_, out_ref, buffer, turned, whole, sems) = rest[:servers], rest[servers:]

    @pl.when(jnp.logical_not(is_late()))
    def _():
        fill(buffer, parts)
        mix_blocks(x_ref, mask_ref, buffer, turned, whole, out_ref, sems)


def early_call(x, mask, parts, out):
    rows, width = x.shape
    total, servers = mask.shape[1], len(parts)
    return kernel_call(
        "mix_whole_early",
        functools.partial(early_kernel, servers),
        bf16(rows, width),
        x,
        mask,
        *reversed(parts),
        out,
        flops=4 * total * rows * width,
        scratch=[
            pltpu.VMEM((total, width), jnp.bfloat16),
            pltpu.VMEM((width, total), jnp.bfloat16),
            pltpu.VMEM((rows, width), jnp.bfloat16),
            pltpu.SemaphoreType.DMA((rows // COPY,)),
        ],
        in_specs=[pl.BlockSpec(memory_space=pltpu.VMEM)] * (2 + servers)
        + [pl.BlockSpec(memory_space=pl.ANY)],
        out_specs=pl.BlockSpec(memory_space=pl.ANY),
        input_output_aliases={2 + servers: 0},
    )


def last_kernel(servers, x_ref, mask_ref, *rest):
    parts, (out_ref, buffer, turned, whole, sems) = rest[:servers], rest[servers:]
    fill(buffer, parts)
    mix_blocks(x_ref, mask_ref, buffer, turned, whole, out_ref, sems)


def last_call(x, mask, parts):
    rows, width = x.shape
    total, servers = mask.shape[1], len(parts)
    return kernel_call(
        "mix",
        functools.partial(last_kernel, servers),
        pltpu.HBM((rows, width), jnp.bfloat16),
        x,
        mask,
        *reversed(parts),
        flops=4 * total * rows * width,
        moved=4 * rows * width,
        scratch=[
            pltpu.VMEM((total, width), jnp.bfloat16),
            pltpu.VMEM((width, total), jnp.bfloat16),
            pltpu.VMEM((rows, width), jnp.bfloat16),
            pltpu.SemaphoreType.DMA((rows // COPY,)),
        ],
        out_specs=pl.BlockSpec(memory_space=pltpu.HBM),
    )


def local(descriptors, request, pick):
    wanted = request[0, 0]
    rows = descriptors.shape[2]
    servers, cap = wanted.shape
    total = servers * cap
    groups = lax.axis_size("rep")
    sent = total * FIRST_SHARE[0] // FIRST_SHARE[1]
    within = [(g, g ^ 1) for g in range(groups)]
    beyond = [(g, (g + 2 * (g % 2) - 1 + groups) % groups) for g in range(groups)]

    def turn(value, d):
        return lax.ppermute(value, "clus", [(c, c ^ d) for c in range(servers)])

    def shift(value, by):
        return lax.ppermute(value, "rep", [(g, (g + by) % groups) for g in range(groups)])

    def across(value):
        return lax.ppermute(value, "rep", beyond)

    def inside(value):
        return lax.ppermute(value, "rep", within)

    def turned(parts):
        got = {d: turn(parts[d], d) for d in reversed(range(1, servers))}
        return [parts[0]] + [got[d] for d in range(1, servers)]

    def next_round(x, mask, far, near, far_turned, far_mask, near_mask, expands, parts, mosts):
        far = far_mix_call(far, far_turned, far_mask, parts)
        core, own, most = near_mix_call(near, near_mask, parts, mosts)
        y = late_call(x, mask, parts)
        last = unpack_both_call(expands, across(far), inside(core), own, y, servers)
        return early_call(x, mask, parts, y), most, turned(last)

    def in_full(x, y, mask, far, near, rest, masks, expands, most, first, last):
        late = unpack_call(expands[1], inside(rest[1]), first=sent)
        late = unpack_call(expands[0], across(rest[0]), late, first=sent)
        late = turned(list(late.reshape(servers, cap, -1)))
        first = [a + b for a, b in zip(first, late)]
        far = jnp.concatenate([far, rest[0]], axis=0)
        near = jnp.concatenate([near[:sent], rest[1], near[sent:]], axis=0)
        near_mask = jnp.concatenate([masks[1], masks[2][sent:]], axis=0)
        y, _, last = next_round(
            x, mask, far, near, masks[3], masks[0], near_mask, expands, first, [most]
        )
        return last_call(y, mask, last)

    def as_sent(x, y, mask, far, near, rest, masks, expands, most, first, last):
        return last_call(y, mask, last)

    asked = {d: turn(wanted, d) for d in reversed(range(1, servers))}
    mask, held = mask_call(pick.transpose(0, 3, 1, 2)[0], wanted)
    own_list, far_list, core_list, *expands = list_call(
        [held] + [asked[d] for d in range(1, servers)], rows
    )
    beyond_list = across(far_list)
    x = normalize_call(descriptors[0, 0])
    told, far = far_call(x, beyond_list, core_list, sent)
    core, own, near, *others, most = near_call(
        x, mask, beyond_list, own_list, told, inside(told), sent
    )
    rest, masks = others[:2], others[2:]
    first = turned(
        unpack_both_call(expands, across(far), inside(core), own, most, servers, far_first=False)
    )
    mosts, known = [most], 4
    while known < groups:
        most = functools.reduce(jnp.maximum, mosts)
        mosts = [most, shift(most, known)]
        known *= 2
    y, most, last = next_round(
        x, mask, far, near, masks[3], masks[0], masks[2], expands, first, mosts
    )
    state = x, y, mask, far, near, rest, masks, expands, most, first, last
    return lax.cond(most[0, 0] > sent, in_full, as_sent, *state)[None, None]


def solution(mesh):
    return jax.shard_map(
        local,
        mesh=mesh,
        in_specs=(
            P("rep", "clus", None, None),
            P("rep", "clus", None, None),
            P("rep", "clus", None, None),
        ),
        out_specs=P("rep", "clus", None, None),
        check_vma=False,
    )
```

```python
import functools

import jax
import jax.numpy as jnp
from jax import lax
from jax.experimental import pallas as pl
from jax.experimental.pallas import tpu as pltpu
from jax.sharding import PartitionSpec as P

LANES = 128
BLOCK = 128
COPY = 128
FIRST_SHARE = 3, 8
BOTH_LAST = (((1,), (1,)), ((), ()))


def bf16(*shape):
    return jax.ShapeDtypeStruct(shape, jnp.bfloat16)


def int32(*shape):
    return jax.ShapeDtypeStruct(shape, jnp.int32)


def kernel_call(name, kernel, outs, *args, flops, moved=0, scratch=(), mib=32, **specs):
    return pl.pallas_call(
        kernel,
        out_shape=outs,
        scratch_shapes=scratch,
        compiler_params=pltpu.CompilerParams(vmem_limit_bytes=mib * 1024 * 1024),
        cost_estimate=pl.CostEstimate(flops=flops, bytes_accessed=moved, transcendentals=0),
        name=name,
        **specs,
    )(*args)


def normalize(value):
    return value * lax.rsqrt(jnp.mean(value * value, axis=-1, keepdims=True) + 1e-06)


def normalize_kernel(x_hbm, out_ref, raw, sems):
    copies = []
    starts = range(0, raw.shape[0], BLOCK)
    for i, start in enumerate(starts):
        here = pl.ds(start, BLOCK)
        copies.append(pltpu.make_async_copy(x_hbm.at[here], raw.at[here], sems.at[i]))
        copies[-1].start()
    for copy, start in zip(copies, starts):
        copy.wait()
        here = pl.ds(start, BLOCK)
        out_ref[here] = normalize(raw[here].astype(jnp.float32)).astype(jnp.bfloat16)


def normalize_call(descriptors):
    rows, width = descriptors.shape
    return kernel_call(
        "normalize",
        normalize_kernel,
        bf16(rows, width),
        descriptors,
        flops=6 * rows * width,
        moved=4 * rows * width,
        scratch=[
            pltpu.VMEM((rows, width), jnp.bfloat16),
            pltpu.SemaphoreType.DMA((rows // BLOCK,)),
        ],
        mib=56,
        in_specs=[pl.BlockSpec(memory_space=pl.ANY)],
    )


def mask_kernel(slot_cap, pick_hbm, wanted_hbm, mask_ref, wanted_ref, pick, sems):
    copies = [
        pltpu.make_async_copy(pick_hbm, pick, sems.at[0]),
        pltpu.make_async_copy(wanted_hbm, wanted_ref, sems.at[1]),
    ]
    for copy in copies:
        copy.start()
    shape = mask_ref.shape[1], mask_ref.shape[0]
    slot = lax.broadcasted_iota(jnp.int32, shape, 0)
    slot = slot ^ (lax.axis_index("clus") * slot_cap)
    chosen = jnp.zeros(shape, jnp.float32)
    copies[0].wait()
    for k in range(pick.shape[0]):
        chosen = jnp.where(pick[k] == slot, 1.0, chosen)
    mask_ref[...] = chosen.T.astype(jnp.bfloat16)
    copies[1].wait()


def mask_call(slots, wanted):
    count, _, rows = slots.shape
    total = wanted.size
    return kernel_call(
        "mask",
        functools.partial(mask_kernel, wanted.shape[1]),
        [bf16(rows, total), pltpu.VMEM(wanted.shape, jnp.int32)],
        slots,
        wanted,
        flops=2 * count * rows * total,
        moved=2 * rows * total,
        scratch=[pltpu.VMEM(slots.shape, jnp.int32), pltpu.SemaphoreType.DMA((2,))],
        mib=56,
        in_specs=[pl.BlockSpec(memory_space=pl.ANY)] * 2,
    )


def list_kernel(rows, *refs):
    parts, refs = refs[:-5], refs[-5:]
    own_ref, far_ref, core_ref, expand_far_ref, expand_core_ref = refs
    total = own_ref.shape[1]
    lane = lax.broadcasted_iota(jnp.int32, (total, total), 1)
    sublane = lax.broadcasted_iota(jnp.int32, (total, total), 0)
    odd = lax.axis_index("rep") % 2
    lows = [(2 * odd * rows).astype(jnp.float32), ((2 - 2 * odd) * rows).astype(jnp.float32)]

    def inside(value, low):
        return (value >= low) & (value < low + rows)

    def asked(server):
        row = jnp.concatenate([ref[server, :] for ref in parts], axis=1).astype(jnp.float32)
        column = jnp.broadcast_to(row, (total, total)).T
        again = jnp.where((column == row) & (sublane < lane), 1.0, 0.0)
        return row, column, 1.0 - jnp.max(again, axis=0, keepdims=True)

    most = jnp.zeros((1, 1), jnp.float32)
    for server in range(len(parts)):
        row, _, first = asked(slice(server, server + 1))
        for low in lows:
            count = jnp.sum(jnp.where(inside(row, low), first, 0.0), axis=1, keepdims=True)
            most = jnp.maximum(most, count)
    row, column, first = asked(pl.ds(lax.axis_index("clus"), 1))
    own_ref[...] = jnp.broadcast_to(row - rows, own_ref.shape).astype(jnp.int32)
    place = lax.broadcasted_iota(jnp.int32, own_ref.shape, 0)
    for low, out_ref, expand_ref in zip(lows, (far_ref, core_ref), (expand_far_ref, expand_core_ref)):
        counted = jnp.where(inside(row, low), first, 0.0)
        rank = jnp.sum(jnp.where(row < column, counted, 0.0), axis=1, keepdims=True)
        here = inside(column, low) & (rank.astype(jnp.int32) == lane)
        expand_ref[...] = jnp.where(here, 1.0, 0.0).astype(jnp.bfloat16)
        packed = jnp.max(jnp.where(here, column - low, -1.0), axis=0, keepdims=True)
        out_ref[...] = jnp.where(place == 1, most, packed).astype(jnp.int32)


def list_call(parts, rows):
    total = parts[0].size
    return kernel_call(
        "list",
        functools.partial(list_kernel, rows),
        [int32(8, total)] * 3 + [bf16(total, total)] * 2,
        *parts,
        flops=40 * total * total,
    )


def one_hot(numbers, rows, count=None):
    total = numbers.shape[1]
    column = jnp.broadcast_to(numbers.astype(jnp.float32), (LANES, total)).T.astype(jnp.int32)
    column = column[:count]
    tiles = []
    for start in range(0, rows, LANES):
        lane = lax.broadcasted_iota(jnp.int32, column.shape, 1) + start
        tiles.append(jnp.where(column == lane, 1.0, 0.0).astype(jnp.bfloat16))
    return jnp.concatenate(tiles, axis=1)


def take(select, x):
    return jnp.dot(select, x, preferred_element_type=jnp.float32).astype(jnp.bfloat16)


def far_kernel(x_ref, beyond_ref, core_list_ref, told_ref, far_ref):
    far_ref[...] = take(one_hot(beyond_ref[0:1], *x_ref.shape[:1], far_ref.shape[0]), x_ref[...])
    place = lax.broadcasted_iota(jnp.int32, told_ref.shape, 0)
    most = jnp.maximum(core_list_ref[...], beyond_ref[...])
    told_ref[...] = jnp.where(place == 1, most, core_list_ref[...])


def far_call(x, beyond, core_list, sent):
    rows, width = x.shape
    return kernel_call(
        "pack_far",
        far_kernel,
        [int32(*core_list.shape), bf16(sent, width)],
        x,
        beyond,
        core_list,
        flops=2 * rows * sent * width,
    )


def near_kernel(x_ref, mask_ref, beyond_ref, own_list_ref, *refs):
    told_ref, within_ref, *refs = refs
    core_ref, own_ref, near_ref, rest_far_ref, rest_core_ref, *refs = refs
    far_mask_ref, core_mask_ref, near_mask_ref, far_turned_ref, most_ref, select = refs
    total, sent = own_ref.shape[0], core_ref.shape[0]
    rows = x_ref.shape[0]
    select[:total] = one_hot(within_ref[0:1], rows)
    select[total:] = one_hot(own_list_ref[0:1], rows)
    fetched = take(select[...], x_ref[...])
    core_ref[...] = fetched[:sent]
    near_ref[:sent] = fetched[:sent]
    rest_core_ref[...] = fetched[sent:total]
    own_ref[...] = fetched[total:]
    near_ref[sent:] = fetched[total:]
    pack = one_hot(beyond_ref[0:1], rows)
    far = jnp.dot(pack, x_ref[...], preferred_element_type=jnp.float32)
    rest_far_ref[...] = far[sent:].astype(jnp.bfloat16)
    far_turned_ref[...] = far.T.astype(jnp.bfloat16)
    masks = take(select[...], mask_ref[...])
    core_mask_ref[...] = masks[:total]
    near_mask_ref[:sent] = masks[:sent]
    near_mask_ref[sent:] = masks[total:]
    far_mask_ref[...] = take(pack, mask_ref[...])
    most = jnp.maximum(told_ref[...], within_ref[...])
    most_ref[...] = jnp.broadcast_to(most[1:2, :LANES], most_ref.shape)


def near_call(x, mask, beyond, own_list, told, within, sent):
    rows, width = x.shape
    total = mask.shape[1]
    return kernel_call(
        "serve_near",
        near_kernel,
        [
            bf16(sent, width),
            bf16(total, width),
            bf16(sent + total, width),
            bf16(total - sent, width),
            bf16(total - sent, width),
            bf16(total, total),
            bf16(total, total),
            bf16(sent + total, total),
            bf16(width, total),
            int32(8, LANES),
        ],
        x,
        mask,
        beyond,
        own_list,
        told,
        within,
        flops=6 * total * rows * width,
        scratch=[pltpu.VMEM((2 * total, rows), jnp.bfloat16)],
    )


def unpack_kernel(first, bases, expand_ref, far_ref, *refs):
    out_ref, sent = refs[-1], far_ref.shape[0]
    rows = jnp.dot(
        expand_ref[:, first : first + sent], far_ref[...], preferred_element_type=jnp.float32
    )
    for base_ref in refs[:bases]:
        rows += base_ref[...].astype(jnp.float32)
    out_ref[...] = rows.astype(jnp.bfloat16)


def unpack_call(expand, far, *base, first=0, after=()):
    in_vmem = [pl.BlockSpec(memory_space=pltpu.VMEM)] * (2 + len(base))
    return kernel_call(
        "unpack",
        functools.partial(unpack_kernel, first, len(base)),
        bf16(expand.shape[0], far.shape[1]),
        expand,
        far,
        *base,
        *after,
        flops=2**34,
        moved=2**25,
        in_specs=in_vmem + [pl.BlockSpec(memory_space=pl.ANY)] * len(after),
    )


def unpack_both_kernel(far_first, far_expand, core_expand, own_ref, a_ref, b_ref, _, *out_refs):
    far_ref, core_ref = (a_ref, b_ref) if far_first else (b_ref, a_ref)
    cap, sent = out_refs[0].shape[0], far_ref.shape[0]
    rows = jnp.dot(core_expand[:, :sent], core_ref[...], preferred_element_type=jnp.float32)
    rows += jnp.dot(far_expand[:, :sent], far_ref[...], preferred_element_type=jnp.float32)
    rows = (rows + own_ref[...].astype(jnp.float32)).astype(jnp.bfloat16)
    for d, out in enumerate(out_refs):
        out[...] = rows[d * cap : (d + 1) * cap]


def unpack_both_call(expands, far, core, own, after, servers, far_first=False):
    total, width = own.shape
    return kernel_call(
        "unpack_both",
        functools.partial(unpack_both_kernel, far_first),
        [bf16(total // servers, width)] * servers,
        *expands,
        own,
        *((far, core) if far_first else (core, far)),
        after,
        flops=4 * total * far.shape[0] * width,
        in_specs=[pl.BlockSpec(memory_space=pltpu.VMEM)] * 5
        + [pl.BlockSpec(memory_space=pl.ANY)],
    )


def fill(buffer, parts):
    cap = parts[0].shape[0]
    for d, ref in enumerate(reversed(parts)):
        buffer[d * cap : (d + 1) * cap] = ref[...]


def cube(dots, width):
    positive = jnp.maximum(dots * (1.0 / width), 0.0)
    return (positive * positive * positive).astype(jnp.bfloat16)


def weigh(x, buffer, mask):
    dots = lax.dot_general(x, buffer, BOTH_LAST, preferred_element_type=jnp.float32)
    return cube(dots, x.shape[1]) * mask


def mix(x, weights, buffer):
    mixed = x.astype(jnp.float32) + jnp.dot(weights, buffer, preferred_element_type=jnp.float32)
    return normalize(mixed).astype(jnp.bfloat16)


def far_mix_kernel(servers, x_ref, turned_ref, mask_ref, *rest):
    parts, (out_ref, buffer) = rest[:servers], rest[servers:]
    fill(buffer, parts)
    rows, width = x_ref.shape
    dots = jnp.dot(buffer[...], turned_ref[...], preferred_element_type=jnp.float32).T[:rows]
    weights = cube(dots, width) * mask_ref[:rows]
    out_ref[...] = mix(x_ref[...], weights, buffer[...])


def far_mix_call(x, turned, mask, parts):
    rows, width = x.shape
    total, servers = mask.shape[1], len(parts)
    return kernel_call(
        "mix_far",
        functools.partial(far_mix_kernel, servers),
        bf16(rows, width),
        x,
        turned,
        mask,
        *reversed(parts),
        flops=4 * total * rows * width,
        scratch=[pltpu.VMEM((total, width), jnp.bfloat16)],
    )


def near_mix_kernel(servers, x_ref, mask_ref, *rest):
    parts, rest = rest[:servers], rest[servers:]
    *most_refs, core_ref, own_ref, most_ref, buffer = rest
    most_ref[...] = functools.reduce(jnp.maximum, [ref[...] for ref in most_refs])
    fill(buffer, parts)
    weights = weigh(x_ref[...], buffer[...], mask_ref[...])
    mixed = mix(x_ref[...], weights, buffer[...])
    core_ref[...] = mixed[: core_ref.shape[0]]
    own_ref[...] = mixed[core_ref.shape[0] :]


def near_mix_call(x, mask, parts, mosts):
    rows, width = x.shape
    total, servers = mask.shape[1], len(parts)
    return kernel_call(
        "mix_near",
        functools.partial(near_mix_kernel, servers),
        [bf16(rows - total, width), bf16(total, width), int32(*mosts[0].shape)],
        x,
        mask,
        *reversed(parts),
        *mosts,
        flops=4 * total * rows * width,
        scratch=[pltpu.VMEM((total, width), jnp.bfloat16)],
    )


def is_late():
    return (lax.axis_index("rep") + 1) % 4 < 2


def late_kernel(servers, x_ref, mask_ref, *rest):
    parts, (out_ref, buffer, weights) = rest[:servers], rest[servers:]

    @pl.when(is_late())
    def _():
        fill(buffer, parts)
        weights[...] = weigh(x_ref[...], buffer[...], mask_ref[...])
        for start in range(0, x_ref.shape[0], BLOCK):
            here = pl.ds(start, BLOCK)
            out_ref[here] = mix(x_ref[here], weights[here], buffer[...])


def late_call(x, mask, parts):
    rows, width = x.shape
    total, servers = mask.shape[1], len(parts)
    return kernel_call(
        "mix_whole_late",
        functools.partial(late_kernel, servers),
        bf16(rows, width),
        x,
        mask,
        *reversed(parts),
        flops=4 * total * rows * width,
        scratch=[
            pltpu.VMEM((total, width), jnp.bfloat16),
            pltpu.VMEM((rows, total), jnp.bfloat16),
        ],
    )


def mix_blocks(x_ref, mask_ref, buffer, turned, whole, out_ref, sems):
    copies = []
    turned[...] = buffer[...].T
    for start in range(0, x_ref.shape[0], BLOCK):
        here = pl.ds(start, BLOCK)
        if start % (2 * BLOCK) == 0:
            two = pl.ds(start, 2 * BLOCK)
            dots = jnp.dot(x_ref[two], turned[...], preferred_element_type=jnp.float32)
            weights = cube(dots, x_ref.shape[1]) * mask_ref[two]
        half = start % (2 * BLOCK)
        whole[here] = mix(x_ref[here], weights[half : half + BLOCK], buffer[...])
        for first in range(start, start + BLOCK, COPY):
            rows = pl.ds(first, COPY)
            copy = pltpu.make_async_copy(
                whole.at[rows], out_ref.at[rows], sems.at[first // COPY]
            )
            copy.start()
            copies.append(copy)
    for copy in copies:
        copy.wait()


def early_kernel(servers, x_ref, mask_ref, *rest):
    parts, (_, out_ref, buffer, turned, whole, sems) = rest[:servers], rest[servers:]

    @pl.when(jnp.logical_not(is_late()))
    def _():
        fill(buffer, parts)
        mix_blocks(x_ref, mask_ref, buffer, turned, whole, out_ref, sems)


def early_call(x, mask, parts, out):
    rows, width = x.shape
    total, servers = mask.shape[1], len(parts)
    return kernel_call(
        "mix_whole_early",
        functools.partial(early_kernel, servers),
        bf16(rows, width),
        x,
        mask,
        *reversed(parts),
        out,
        flops=4 * total * rows * width,
        scratch=[
            pltpu.VMEM((total, width), jnp.bfloat16),
            pltpu.VMEM((width, total), jnp.bfloat16),
            pltpu.VMEM((rows, width), jnp.bfloat16),
            pltpu.SemaphoreType.DMA((rows // COPY,)),
        ],
        in_specs=[pl.BlockSpec(memory_space=pltpu.VMEM)] * (2 + servers)
        + [pl.BlockSpec(memory_space=pl.ANY)],
        out_specs=pl.BlockSpec(memory_space=pl.ANY),
        input_output_aliases={2 + servers: 0},
    )


def last_kernel(servers, x_ref, mask_ref, *rest):
    parts, (out_ref, buffer, turned, whole, sems) = rest[:servers], rest[servers:]
    fill(buffer, parts)
    mix_blocks(x_ref, mask_ref, buffer, turned, whole, out_ref, sems)


def last_call(x, mask, parts):
    rows, width = x.shape
    total, servers = mask.shape[1], len(parts)
    return kernel_call(
        "mix",
        functools.partial(last_kernel, servers),
        pltpu.HBM((rows, width), jnp.bfloat16),
        x,
        mask,
        *reversed(parts),
        flops=4 * total * rows * width,
        moved=4 * rows * width,
        scratch=[
            pltpu.VMEM((total, width), jnp.bfloat16),
            pltpu.VMEM((width, total), jnp.bfloat16),
            pltpu.VMEM((rows, width), jnp.bfloat16),
            pltpu.SemaphoreType.DMA((rows // COPY,)),
        ],
        out_specs=pl.BlockSpec(memory_space=pltpu.HBM),
    )


def local(descriptors, request, pick):
    wanted = request[0, 0]
    rows = descriptors.shape[2]
    servers, cap = wanted.shape
    total = servers * cap
    groups = lax.axis_size("rep")
    sent = total * FIRST_SHARE[0] // FIRST_SHARE[1]
    within = [(g, g ^ 1) for g in range(groups)]
    beyond = [(g, (g + 2 * (g % 2) - 1 + groups) % groups) for g in range(groups)]

    def turn(value, d):
        return lax.ppermute(value, "clus", [(c, c ^ d) for c in range(servers)])

    def shift(value, by):
        return lax.ppermute(value, "rep", [(g, (g + by) % groups) for g in range(groups)])

    def across(value):
        return lax.ppermute(value, "rep", beyond)

    def inside(value):
        return lax.ppermute(value, "rep", within)

    def turned(parts):
        got = {d: turn(parts[d], d) for d in reversed(range(1, servers))}
        return [parts[0]] + [got[d] for d in range(1, servers)]

    def next_round(x, mask, far, near, far_turned, far_mask, near_mask, expands, parts, mosts):
        far = far_mix_call(far, far_turned, far_mask, parts)
        core, own, most = near_mix_call(near, near_mask, parts, mosts)
        y = late_call(x, mask, parts)
        last = unpack_both_call(expands, across(far), inside(core), own, y, servers)
        return early_call(x, mask, parts, y), most, turned(last)

    def in_full(x, y, mask, far, near, rest, masks, expands, most, first, last):
        late = unpack_call(expands[1], inside(rest[1]), first=sent)
        late = unpack_call(expands[0], across(rest[0]), late, first=sent)
        late = turned(list(late.reshape(servers, cap, -1)))
        first = [a + b for a, b in zip(first, late)]
        far = jnp.concatenate([far, rest[0]], axis=0)
        near = jnp.concatenate([near[:sent], rest[1], near[sent:]], axis=0)
        near_mask = jnp.concatenate([masks[1], masks[2][sent:]], axis=0)
        y, _, last = next_round(
            x, mask, far, near, masks[3], masks[0], near_mask, expands, first, [most]
        )
        return last_call(y, mask, last)

    def as_sent(x, y, mask, far, near, rest, masks, expands, most, first, last):
        return last_call(y, mask, last)

    asked = {d: turn(wanted, d) for d in reversed(range(1, servers))}
    mask, held = mask_call(pick.transpose(0, 3, 1, 2)[0], wanted)
    own_list, far_list, core_list, *expands = list_call(
        [held] + [asked[d] for d in range(1, servers)], rows
    )
    beyond_list = across(far_list)
    x = normalize_call(descriptors[0, 0])
    told, far = far_call(x, beyond_list, core_list, sent)
    core, own, near, *others, most = near_call(
        x, mask, beyond_list, own_list, told, inside(told), sent
    )
    rest, masks = others[:2], others[2:]
    first = turned(
        unpack_both_call(expands, across(far), inside(core), own, most, servers, far_first=False)
    )
    mosts, known = [most], 4
    while known < groups:
        most = functools.reduce(jnp.maximum, mosts)
        mosts = [most, shift(most, known)]
        known *= 2
    y, most, last = next_round(
        x, mask, far, near, masks[3], masks[0], masks[2], expands, first, mosts
    )
    state = x, y, mask, far, near, rest, masks, expands, most, first, last
    return lax.cond(most[0, 0] > sent, in_full, as_sent, *state)[None, None]


def solution(mesh):
    return jax.shard_map(
        local,
        mesh=mesh,
        in_specs=(
            P("rep", "clus", None, None),
            P("rep", "clus", None, None),
            P("rep", "clus", None, None),
        ),
        out_specs=P("rep", "clus", None, None),
        check_vma=False,
    )
```
